32 devices in a mesh: gx: 4 (over z), gy: 8 (over y, x, core).
Axes of the slice: x: 2, y: 2, z: 4, core: 2. Of those that a mesh axis runs over, the one named last changes fastest.
Arguments:
- heat_source: float32 [8, 64, 6144], P(None, 'gx', 'gy'), may hold values from -90 to 90
- density: float32 [64, 6144], P('gx', 'gy'), may hold values from 0.3 to 1
Outputs:
- solution_field: float32 [8, 64, 6144], P(None, 'gx', 'gy')
- residual: float32 [8, 64, 6144], P(None, 'gx', 'gy')
The draws below stay inside these ranges and needn't reach their ends.
All inputs are finite; a program needn't handle non-finite values.
Results may differ from the reference program's by a relative error of at most 0.0003.
Values sent between devices are 32-bit elements; how exact they have to be, the bound alone decides.
No kernel may reach another device: no remote copies, remote signals or barrier semaphores. Data moves between devices by JAX's collectives and lax.ppermute only.
A program may use at most 64 MiB of HBM per device.

```python
import jax
import jax.numpy as jnp
import numpy as np
from jax import lax

LOADS = 8
NZ = 96
ITERS = 2
NX = 64
NY = 64


def draw_heat_source(key, part):
    first_key = jax.random.fold_in(key, 0)
    along_x = jnp.arange(NX, dtype=jnp.float32) / NX
    along_y = (jnp.arange(NY * NZ) // NZ).astype(jnp.float32) / NY
    ramp = jnp.exp(jnp.log(3.0) * along_x)[:, None] * jnp.exp(jnp.log(3.0) * along_y)[None, :]
    base = jnp.clip(jax.random.normal(first_key, (LOADS, NX, NY * NZ), jnp.float32), -6.0, 6.0)
    return (base * ramp).astype(jnp.float32)


def steps_of(rng, dims, cuts, least, top_value):
    level = 1.0
    for dim, parts in cuts:
        steps = jax.random.uniform(jax.random.fold_in(jax.random.fold_in(rng, 6), dim), (parts,), jnp.float32, least / len(cuts), top_value / len(cuts))
        level = level * jnp.repeat(jnp.exp(steps), dims[dim] // parts).reshape((-1,) + (1,) * (len(dims) - 1 - dim))
    return level


def setup_inputs(seed: int = 0) -> dict:
    streams_of = jax.random.split(jax.random.key(seed), 3)
    return {
        "heat_source": draw_heat_source(jax.random.fold_in(streams_of[2], 71), 0),
        "density": jnp.clip(0.3 + 0.7 * jax.random.uniform(streams_of[1], (NX, NY * NZ), jnp.float32) ** steps_of(streams_of[1], (NX, NY * NZ), ((0, 4), (1, 8)), -0.2, 0.2), 0.3, 1.0),
    }


KMIN = 0.001


def stiffness():
    table = np.zeros((8, 8), np.float32)
    levels = [4.0, 0.0, -1.0, -1.0]
    for first in range(8):
        for second in range(8):
            differ = first ^ second
            apart = (differ & 1) + ((differ >> 1) & 1) + ((differ >> 2) & 1)
            table[first, second] = levels[apart] / 12.0
    return table


def corners():
    return [((corner >> 2) & 1, (corner >> 1) & 1, corner & 1) for corner in range(8)]


def conductance(density):
    return KMIN + (1.0 - KMIN) * (density * density * density)


def reference(heat_source, density):
    conduct = conductance(density).reshape(NX, NY, NZ)
    k_elem = jnp.asarray(stiffness())
    offsets = corners()

    def spread(elems):
        summed = jnp.zeros((NX + 1, NY + 1, NZ + 1), jnp.float32)
        for corner, (off_x, off_y, off_z) in enumerate(offsets):
            summed = summed.at[off_x:off_x + NX, off_y:off_y + NY, off_z:off_z + NZ].add(elems[corner])
        return summed[:NX, :NY, :NZ]

    precond = spread(jnp.broadcast_to(conduct * k_elem[0, 0], (8, NX, NY, NZ)))

    def operate(field):
        padded = jnp.pad(field, ((0, 1), (0, 1), (0, 1)))
        values = jnp.stack([padded[off_x:off_x + NX, off_y:off_y + NY, off_z:off_z + NZ] for (off_x, off_y, off_z) in offsets])
        elems = jnp.einsum("nm,mabc->nabc", k_elem, values, precision=lax.Precision.HIGHEST) * conduct
        return spread(elems)

    def solve(source):
        source = source.reshape(NX, NY, NZ)
        solution = jnp.zeros((NX, NY, NZ), jnp.float32)
        residual = source
        scaled = residual / precond
        direction = scaled
        rz_sum = jnp.sum(residual * scaled)
        for step in range(ITERS):
            image = operate(direction)
            alpha = rz_sum / jnp.sum(direction * image)
            solution = solution + alpha * direction
            residual = residual - alpha * image
            scaled = residual / precond
            rz_next = jnp.sum(residual * scaled)
            direction = scaled + (rz_next / rz_sum) * direction
            rz_sum = rz_next
        return solution.reshape(NX, NY * NZ), residual.reshape(NX, NY * NZ)

    solution_all, residual_all = lax.map(solve, heat_source)
    return solution_all, residual_all
```

```python
import functools

import jax
import jax.numpy as jnp
from jax import lax
from jax.experimental import pallas as pl
from jax.experimental.pallas import tpu as pltpu
from jax.sharding import PartitionSpec as P

NZ = 96
KMIN = 0.001
LANES = 128
SUB = 8


def lane_ids(rows):
    return lax.broadcasted_iota(jnp.int32, (rows, LANES), 1)


def read_z(read, y, rows):
    start = y * NZ
    block, offset = start // LANES, start % LANES
    lane = lane_ids(rows)
    first = read(block)
    if offset:
        first = pltpu.roll(first, LANES - offset, 1)
    if offset + NZ > LANES:
        second = pltpu.roll(read(block + 1), LANES - offset, 1)
        first = jnp.where(lane < LANES - offset, first, second)
    return jnp.where(lane < NZ, first, 0.0)


def write_z(read_tile, block, rows):
    lane = lane_ids(rows)
    start = block * LANES
    out, at = None, start
    while at < start + LANES:
        y, z = at // NZ, at % NZ
        here = at - start
        piece = read_tile(y)
        shift = (here - z) % LANES
        if shift:
            piece = pltpu.roll(piece, shift, 1)
        out = piece if out is None else jnp.where(lane < here, out, piece)
        at += NZ - z
    return out


def pack_x_kernel(sizes, b_ref, d_ref, bt_ref, dt_ref, up_ref, down_ref):
    loads, nx, ny = sizes
    for load in range(loads):
        for x0 in range(0, nx, SUB):
            for y in range(ny):
                tile = read_z(
                    lambda t: b_ref[load, x0 : x0 + SUB, t * LANES : (t + 1) * LANES], y, SUB
                )
                bt_ref[pl.ds((x0 * ny + y) * loads + load, SUB, stride=ny * loads), :] = tile
    for x0 in range(0, nx, SUB):
        for y in range(ny):
            tile = read_z(lambda t: d_ref[x0 : x0 + SUB, t * LANES : (t + 1) * LANES], y, SUB)
            dt_ref[pl.ds(x0 * ny + y, SUB, stride=ny), :] = tile
    plane = ny * loads
    up_ref[: 2 * plane] = bt_ref[(nx - 2) * plane :]
    up_ref[2 * plane :] = dt_ref[(nx - 3) * ny :]
    down_ref[: 2 * plane] = bt_ref[: 2 * plane]
    down_ref[2 * plane :] = dt_ref[: 2 * ny]


def ext_rows(x, nx, plane, inner, low, high, low_planes, low_at, high_at):
    if x < 0:
        return low, low_at + (x + low_planes) * plane
    if x >= nx:
        return high, high_at + (x - nx) * plane
    return inner, x * plane


def pack_y_kernel(sizes, bt_ref, dt_ref, low_ref, high_ref, up_ref, down_ref):
    loads, nx, ny = sizes
    plane = ny * loads
    for x in range(-2, nx + 2):
        ref, row = ext_rows(x, nx, plane, bt_ref, low_ref, high_ref, 2, 0, 0)
        to = (x + 2) * 2 * loads
        up_ref[to : to + 2 * loads] = ref[row + (ny - 2) * loads : row + ny * loads]
        down_ref[to : to + 2 * loads] = ref[row : row + 2 * loads]
    base = (nx + 4) * 2 * loads
    for x in range(-3, nx + 2):
        ref, row = ext_rows(x, nx, ny, dt_ref, low_ref, high_ref, 3, 2 * plane, 2 * plane)
        to = base + (x + 3) * 3
        up_ref[to : to + 3] = ref[row + ny - 3 : row + ny]
        to = base + (x + 3) * 2
        down_ref[to : to + 2] = ref[row : row + 2]
    up_ref[base + (nx + 5) * 3 :] = jnp.zeros_like(up_ref[base + (nx + 5) * 3 :])
    down_ref[base + (nx + 5) * 2 :] = jnp.zeros_like(down_ref[base + (nx + 5) * 2 :])


def solve_kernel(
    sizes, bt_ref, dt_ref, xl_ref, xh_ref, yl_ref, yh_ref,
    q_ref, v_ref, inv_ref, sums_ref,
    dens, cond, invx, bx, zx, zs, wx, ws, qx, carry,
):
    loads, nx, ny = sizes
    plane = ny * loads
    base = (nx + 4) * 2 * loads
    for x in range(-3, nx + 2):
        ref, row = ext_rows(x, nx, ny, dt_ref, xl_ref, xh_ref, 3, 2 * plane, 2 * plane)
        dens[x + 3, 3 : 3 + ny, :] = ref[row : row + ny]
        at = base + (x + 3) * 3
        dens[x + 3, 0:3, :] = yl_ref[at : at + 3]
        at = base + (x + 3) * 2
        dens[x + 3, 3 + ny : 5 + ny, :] = yh_ref[at : at + 2]
    mx, my = nx + 4, ny + 4
    d = dens[...]
    conduct = jnp.where(d > 0.0, (KMIN + (1.0 - KMIN) * (d * d * d)) * (1.0 / 12.0), 0.0)
    pair = conduct[:-1] + conduct[1:]
    pair = pair[:, :-1, :] + pair[:, 1:, :]
    here = conduct[1:, 1:, :]
    for x in range(mx):
        total = 4.0 * (pair[x] + pltpu.roll(pair[x], 1, 1))
        inverse = jnp.where(here[x] > 0.0, 1.0 / total, 0.0)
        for y in range(my):
            row = inverse[y : y + 1, :]
            invx[x, y] = jnp.broadcast_to(row, (loads, LANES))
            if x < mx - 1 and y < my - 1:
                cond[x, y] = jnp.broadcast_to(here[x, y : y + 1, :], (loads, LANES))
        if 2 <= x < 2 + nx:
            inv_ref[(x - 2) * ny : (x - 1) * ny, :] = inverse[2 : 2 + ny, :]
    def stage(x, y, tile):
        bx[x, y] = tile
        scaled = tile * invx[x, y]
        zx[x, y] = scaled
        zs[x, y] = pltpu.roll(scaled, LANES - 1, 1)

    for x in range(mx):
        ref, row = ext_rows(x - 2, nx, plane, bt_ref, xl_ref, xh_ref, 2, 0, 0)
        for y in range(ny):
            at = row + y * loads
            stage(x, y + 2, ref[at : at + loads])
        for y in range(2):
            at = (x * 2 + y) * loads
            stage(x, y, yl_ref[at : at + loads])
            stage(x, y + 2 + ny, yh_ref[at : at + loads])

    def element_plane(a, a0, rows, low, low_s, first, emit):
        above_lo = above_hi = None
        left_lo = left_hi = None
        p0, p0s = low[a, a0], low_s[a, a0]
        p1, p1s = low[a + 1, a0], low_s[a + 1, a0]
        for step in range(rows):
            y = a0 + step
            r0, r0s = low[a, y + 1], low_s[a, y + 1]
            r1, r1s = low[a + 1, y + 1], low_s[a + 1, y + 1]
            c = cond[a, y]
            even = p0 + r1 + (r0s + p1s)
            odd = r0 + p1 + (p0s + r1s)
            t000 = c * (even + r1s)
            t110 = c * (even + p0s)
            t011 = c * (even + p1)
            t101 = c * (even + r0)
            t111 = c * (odd + p0)
            t001 = c * (odd + r1)
            t100 = c * (odd + r0s)
            t010 = c * (odd + p1s)
            if step and not first:
                lo = t000 + left_lo + carry[0, y]
                hi = t001 + left_hi + carry[1, y]
                emit(y, lo + pltpu.roll(hi, 1, 1))
            left_lo, left_hi = t010, t011
            if step:
                carry[0, y] = t100 + above_lo
                carry[1, y] = t101 + above_hi
            above_lo, above_hi = t110, t111
            p0, p0s, p1, p1s = r0, r0s, r1, r1s

    def first_pass(a, first):
        def emit(y, total):
            image = 1.25 * bx[a, y] - total
            weighted = image * invx[a, y]
            qx[a, y] = image
            wx[a, y] = weighted
            ws[a, y] = pltpu.roll(weighted, LANES - 1, 1)

        element_plane(a, 0, my - 1, zx, zs, first, emit)

    first_pass(0, True)

    @pl.loop(1, mx - 1)
    def _(a):
        first_pass(a, False)

    def second_pass(a, first, sums):
        sums = list(sums)

        def emit(y, total):
            image = qx[a, y]
            again = 1.25 * image - total
            row = pl.multiple_of(((a - 2) * ny + (y - 2)) * loads, SUB)
            q_ref[pl.ds(row, loads), :] = image
            v_ref[pl.ds(row, loads), :] = again
            scaled, weighted = zx[a, y], wx[a, y]
            sums[0] = sums[0] + bx[a, y] * scaled
            sums[1] = sums[1] + scaled * image
            sums[2] = sums[2] + image * weighted
            sums[3] = sums[3] + weighted * again

        element_plane(a, 1, my - 3, wx, ws, first, emit)
        return tuple(sums)

    zero = jnp.zeros((loads, LANES), jnp.float32)
    second_pass(1, True, (zero,) * 4)
    sums = lax.fori_loop(2, mx - 2, lambda a, s: second_pass(a, False, s), (zero,) * 4)
    lane = lane_ids(loads)
    packed = zero
    for place, part in enumerate(sums):
        packed = jnp.where(lane == place, jnp.sum(part, axis=1, keepdims=True), packed)
    sums_ref[...] = packed


def unpack_kernel(sizes, q_ref, v_ref, inv_ref, qo_ref, vo_ref, io_ref):
    loads, nx, ny = sizes
    for x0 in range(0, nx, SUB):
        for block in range(ny * NZ // LANES):
            lanes = slice(block * LANES, (block + 1) * LANES)
            io_ref[x0 : x0 + SUB, lanes] = write_z(
                lambda y: inv_ref[pl.ds(x0 * ny + y, SUB, stride=ny), :], block, SUB
            )
            for ref, out in ((q_ref, qo_ref), (v_ref, vo_ref)):
                for load in range(loads):
                    out[load, x0 : x0 + SUB, lanes] = write_z(
                        lambda y: ref[
                            pl.ds((x0 * ny + y) * loads + load, SUB, stride=ny * loads), :
                        ],
                        block,
                        SUB,
                    )


def shift(array, axis, by):
    length = lax.axis_size(axis)
    pairs = [(i, i + by) for i in range(length) if 0 <= i + by < length]
    return lax.ppermute(array, axis, pairs)


def prime_factors(number):
    factors, divisor = [], 2
    while number > 1:
        while number % divisor == 0:
            factors.append(divisor)
            number //= divisor
        divisor += 1
    return factors


def sum_over(array, axis):
    length = lax.axis_size(axis)
    stride = 1
    for factor in prime_factors(length):
        total = array
        for step in range(1, factor):
            pairs = []
            for i in range(length):
                digit = i // stride % factor
                pairs.append((i, i + ((digit + step) % factor - digit) * stride))
            total = total + lax.ppermute(array, axis, pairs)
        array = total
        stride *= factor
    return array


def per_device(heat_source, density):
    loads, nx, flat = heat_source.shape
    ny = flat // NZ
    sizes = (loads, nx, ny)
    plane = ny * loads
    f32 = jnp.float32

    def shape(*dims):
        return jax.ShapeDtypeStruct(dims, f32)

    def scratch(*dims):
        return pltpu.VMEM(dims, f32)

    params = pltpu.CompilerParams(vmem_limit_bytes=48 * 1024 * 1024)
    bt, dt, x_up, x_down = pl.pallas_call(
        functools.partial(pack_x_kernel, sizes),
        out_shape=(
            shape(nx * plane, LANES),
            shape(nx * ny, LANES),
            shape(2 * plane + 3 * ny, LANES),
            shape(2 * plane + 2 * ny, LANES),
        ),
        compiler_params=params,
    )(heat_source, density)
    x_low, x_high = shift(x_up, "gx", 1), shift(x_down, "gx", -1)
    tail = lambda width: (nx + 4) * 2 * loads + -(-(nx + 5) * width // SUB) * SUB
    y_up, y_down = pl.pallas_call(
        functools.partial(pack_y_kernel, sizes),
        out_shape=(shape(tail(3), LANES), shape(tail(2), LANES)),
        compiler_params=params,
    )(bt, dt, x_low, x_high)
    y_low, y_high = shift(y_up, "gy", 1), shift(y_down, "gy", -1)
    mx, my = nx + 4, ny + 4
    q_t, v_t, inv_t, sums = pl.pallas_call(
        functools.partial(solve_kernel, sizes),
        out_shape=(
            shape(nx * plane, LANES),
            shape(nx * plane, LANES),
            shape(nx * ny, LANES),
            shape(loads, LANES),
        ),
        scratch_shapes=[
            scratch(mx + 1, my + 1, LANES),
            scratch(mx - 1, my - 1, loads, LANES),
        ]
        + [scratch(mx, my, loads, LANES)] * 7
        + [scratch(2, my, loads, LANES)],
        compiler_params=params,
    )(bt, dt, x_low, x_high, y_low, y_high)
    totals = sum_over(sum_over(sums, "gx"), "gy")
    image, again, inverse = pl.pallas_call(
        functools.partial(unpack_kernel, sizes),
        out_shape=(shape(*heat_source.shape), shape(*heat_source.shape), shape(nx, flat)),
        compiler_params=params,
    )(q_t, v_t, inv_t)
    rz, direct, square, last = (totals[:, place] for place in range(4))
    alpha = rz / direct
    rz_next = alpha * alpha * square - rz
    beta = rz_next / rz
    grown = 1.0 + beta
    alpha_next = rz_next / (
        grown * grown * direct - 2.0 * alpha * grown * square + alpha * alpha * last
    )
    first = (alpha + alpha_next * grown)[:, None, None]
    second = (alpha_next * alpha)[:, None, None]
    solution_field = (first * heat_source - second * image) * inverse
    residual = heat_source - first * image + second * again
    return solution_field, residual


def solution(mesh):
    placed = (P(None, "gx", "gy"), P("gx", "gy"))
    return jax.shard_map(
        per_device,
        mesh=mesh,
        in_specs=placed,
        out_specs=(P(None, "gx", "gy"), P(None, "gx", "gy")),
        check_vma=False,
    )
```

```python
import functools

import jax
import jax.numpy as jnp
from jax import lax
from jax.experimental import pallas as pl
from jax.experimental.pallas import tpu as pltpu
from jax.sharding import PartitionSpec as P

NZ = 96
KMIN = 0.001
LANES = 128
SUB = 8


def lane_ids(rows):
    return lax.broadcasted_iota(jnp.int32, (rows, LANES), 1)


def read_z(read, y, rows):
    start = y * NZ
    block, offset = start // LANES, start % LANES
    lane = lane_ids(rows)
    first = read(block)
    if offset:
        first = pltpu.roll(first, LANES - offset, 1)
    if offset + NZ > LANES:
        second = pltpu.roll(read(block + 1), LANES - offset, 1)
        first = jnp.where(lane < LANES - offset, first, second)
    return jnp.where(lane < NZ, first, 0.0)


def write_z(read_tile, block, rows):
    lane = lane_ids(rows)
    start = block * LANES
    out, at = None, start
    while at < start + LANES:
        y, z = at // NZ, at % NZ
        here = at - start
        piece = read_tile(y)
        shift = (here - z) % LANES
        if shift:
            piece = pltpu.roll(piece, shift, 1)
        out = piece if out is None else jnp.where(lane < here, out, piece)
        at += NZ - z
    return out


def pack_x_kernel(sizes, b_ref, d_ref, bt_ref, dt_ref, up_ref, down_ref):
    loads, nx, ny = sizes
    for load in range(loads):
        for x0 in range(0, nx, SUB):
            for y in range(ny):
                tile = read_z(
                    lambda t: b_ref[load, x0 : x0 + SUB, t * LANES : (t + 1) * LANES], y, SUB
                )
                bt_ref[pl.ds((x0 * ny + y) * loads + load, SUB, stride=ny * loads), :] = tile
    for x0 in range(0, nx, SUB):
        for y in range(ny):
            tile = read_z(lambda t: d_ref[x0 : x0 + SUB, t * LANES : (t + 1) * LANES], y, SUB)
            dt_ref[pl.ds(x0 * ny + y, SUB, stride=ny), :] = tile
    plane = ny * loads
    up_ref[: 2 * plane] = bt_ref[(nx - 2) * plane :]
    up_ref[2 * plane :] = dt_ref[(nx - 3) * ny :]
    down_ref[: 2 * plane] = bt_ref[: 2 * plane]
    down_ref[2 * plane :] = dt_ref[: 2 * ny]


def ext_rows(x, nx, plane, inner, low, high, low_planes, low_at, high_at):
    if x < 0:
        return low, low_at + (x + low_planes) * plane
    if x >= nx:
        return high, high_at + (x - nx) * plane
    return inner, x * plane


def pack_y_kernel(sizes, bt_ref, dt_ref, low_ref, high_ref, up_ref, down_ref):
    loads, nx, ny = sizes
    plane = ny * loads
    for x in range(-2, nx + 2):
        ref, row = ext_rows(x, nx, plane, bt_ref, low_ref, high_ref, 2, 0, 0)
        to = (x + 2) * 2 * loads
        up_ref[to : to + 2 * loads] = ref[row + (ny - 2) * loads : row + ny * loads]
        down_ref[to : to + 2 * loads] = ref[row : row + 2 * loads]
    base = (nx + 4) * 2 * loads
    for x in range(-3, nx + 2):
        ref, row = ext_rows(x, nx, ny, dt_ref, low_ref, high_ref, 3, 2 * plane, 2 * plane)
        to = base + (x + 3) * 3
        up_ref[to : to + 3] = ref[row + ny - 3 : row + ny]
        to = base + (x + 3) * 2
        down_ref[to : to + 2] = ref[row : row + 2]
    up_ref[base + (nx + 5) * 3 :] = jnp.zeros_like(up_ref[base + (nx + 5) * 3 :])
    down_ref[base + (nx + 5) * 2 :] = jnp.zeros_like(down_ref[base + (nx + 5) * 2 :])


def solve_kernel(
    sizes, bt_ref, dt_ref, xl_ref, xh_ref, yl_ref, yh_ref,
    q_ref, v_ref, inv_ref, sums_ref,
    dens, cond, invx, bx, zx, zs, wx, ws, qx, carry,
):
    loads, nx, ny = sizes
    plane = ny * loads
    base = (nx + 4) * 2 * loads
    for x in range(-3, nx + 2):
        ref, row = ext_rows(x, nx, ny, dt_ref, xl_ref, xh_ref, 3, 2 * plane, 2 * plane)
        dens[x + 3, 3 : 3 + ny, :] = ref[row : row + ny]
        at = base + (x + 3) * 3
        dens[x + 3, 0:3, :] = yl_ref[at : at + 3]
        at = base + (x + 3) * 2
        dens[x + 3, 3 + ny : 5 + ny, :] = yh_ref[at : at + 2]
    mx, my = nx + 4, ny + 4
    d = dens[...]
    conduct = jnp.where(d > 0.0, (KMIN + (1.0 - KMIN) * (d * d * d)) * (1.0 / 12.0), 0.0)
    pair = conduct[:-1] + conduct[1:]
    pair = pair[:, :-1, :] + pair[:, 1:, :]
    here = conduct[1:, 1:, :]
    for x in range(mx):
        total = 4.0 * (pair[x] + pltpu.roll(pair[x], 1, 1))
        inverse = jnp.where(here[x] > 0.0, 1.0 / total, 0.0)
        for y in range(my):
            row = inverse[y : y + 1, :]
            invx[x, y] = jnp.broadcast_to(row, (loads, LANES))
            if x < mx - 1 and y < my - 1:
                cond[x, y] = jnp.broadcast_to(here[x, y : y + 1, :], (loads, LANES))
        if 2 <= x < 2 + nx:
            inv_ref[(x - 2) * ny : (x - 1) * ny, :] = inverse[2 : 2 + ny, :]
    def stage(x, y, tile):
        bx[x, y] = tile
        scaled = tile * invx[x, y]
        zx[x, y] = scaled
        zs[x, y] = pltpu.roll(scaled, LANES - 1, 1)

    for x in range(mx):
        ref, row = ext_rows(x - 2, nx, plane, bt_ref, xl_ref, xh_ref, 2, 0, 0)
        for y in range(ny):
            at = row + y * loads
            stage(x, y + 2, ref[at : at + loads])
        for y in range(2):
            at = (x * 2 + y) * loads
            stage(x, y, yl_ref[at : at + loads])
            stage(x, y + 2 + ny, yh_ref[at : at + loads])

    def element_plane(a, a0, rows, low, low_s, first, emit):
        above_lo = above_hi = None
        left_lo = left_hi = None
        p0, p0s = low[a, a0], low_s[a, a0]
        p1, p1s = low[a + 1, a0], low_s[a + 1, a0]
        for step in range(rows):
            y = a0 + step
            r0, r0s = low[a, y + 1], low_s[a, y + 1]
            r1, r1s = low[a + 1, y + 1], low_s[a + 1, y + 1]
            c = cond[a, y]
            even = p0 + r1 + (r0s + p1s)
            odd = r0 + p1 + (p0s + r1s)
            t000 = c * (even + r1s)
            t110 = c * (even + p0s)
            t011 = c * (even + p1)
            t101 = c * (even + r0)
            t111 = c * (odd + p0)
            t001 = c * (odd + r1)
            t100 = c * (odd + r0s)
            t010 = c * (odd + p1s)
            if step and not first:
                lo = t000 + left_lo + carry[0, y]
                hi = t001 + left_hi + carry[1, y]
                emit(y, lo + pltpu.roll(hi, 1, 1))
            left_lo, left_hi = t010, t011
            if step:
                carry[0, y] = t100 + above_lo
                carry[1, y] = t101 + above_hi
            above_lo, above_hi = t110, t111
            p0, p0s, p1, p1s = r0, r0s, r1, r1s

    def first_pass(a, first):
        def emit(y, total):
            image = 1.25 * bx[a, y] - total
            weighted = image * invx[a, y]
            qx[a, y] = image
            wx[a, y] = weighted
            ws[a, y] = pltpu.roll(weighted, LANES - 1, 1)

        element_plane(a, 0, my - 1, zx, zs, first, emit)

    first_pass(0, True)

    @pl.loop(1, mx - 1)
    def _(a):
        first_pass(a, False)

    def second_pass(a, first, sums):
        sums = list(sums)

        def emit(y, total):
            image = qx[a, y]
            again = 1.25 * image - total
            row = pl.multiple_of(((a - 2) * ny + (y - 2)) * loads, SUB)
            q_ref[pl.ds(row, loads), :] = image
            v_ref[pl.ds(row, loads), :] = again
            scaled, weighted = zx[a, y], wx[a, y]
            sums[0] = sums[0] + bx[a, y] * scaled
            sums[1] = sums[1] + scaled * image
            sums[2] = sums[2] + image * weighted
            sums[3] = sums[3] + weighted * again

        element_plane(a, 1, my - 3, wx, ws, first, emit)
        return tuple(sums)

    zero = jnp.zeros((loads, LANES), jnp.float32)
    second_pass(1, True, (zero,) * 4)
    sums = lax.fori_loop(2, mx - 2, lambda a, s: second_pass(a, False, s), (zero,) * 4)
    lane = lane_ids(loads)
    packed = zero
    for place, part in enumerate(sums):
        packed = jnp.where(lane == place, jnp.sum(part, axis=1, keepdims=True), packed)
    sums_ref[...] = packed


def unpack_kernel(sizes, q_ref, v_ref, inv_ref, qo_ref, vo_ref, io_ref):
    loads, nx, ny = sizes
    for x0 in range(0, nx, SUB):
        for block in range(ny * NZ // LANES):
            lanes = slice(block * LANES, (block + 1) * LANES)
            io_ref[x0 : x0 + SUB, lanes] = write_z(
                lambda y: inv_ref[pl.ds(x0 * ny + y, SUB, stride=ny), :], block, SUB
            )
            for ref, out in ((q_ref, qo_ref), (v_ref, vo_ref)):
                for load in range(loads):
                    out[load, x0 : x0 + SUB, lanes] = write_z(
                        lambda y: ref[
                            pl.ds((x0 * ny + y) * loads + load, SUB, stride=ny * loads), :
                        ],
                        block,
                        SUB,
                    )


def shift(array, axis, by):
    length = lax.axis_size(axis)
    pairs = [(i, i + by) for i in range(length) if 0 <= i + by < length]
    return lax.ppermute(array, axis, pairs)


def prime_factors(number):
    factors, divisor = [], 2
    while number > 1:
        while number % divisor == 0:
            factors.append(divisor)
            number //= divisor
        divisor += 1
    return factors


def sum_over(array, axis):
    length = lax.axis_size(axis)
    stride = 1
    for factor in prime_factors(length):
        total = array
        for step in range(1, factor):
            pairs = []
            for i in range(length):
                digit = i // stride % factor
                pairs.append((i, i + ((digit + step) % factor - digit) * stride))
            total = total + lax.ppermute(array, axis, pairs)
        array = total
        stride *= factor
    return array


def per_device(heat_source, density):
    loads, nx, flat = heat_source.shape
    ny = flat // NZ
    sizes = (loads, nx, ny)
    plane = ny * loads
    f32 = jnp.float32

    def shape(*dims):
        return jax.ShapeDtypeStruct(dims, f32)

    def scratch(*dims):
        return pltpu.VMEM(dims, f32)

    params = pltpu.CompilerParams(vmem_limit_bytes=48 * 1024 * 1024)
    bt, dt, x_up, x_down = pl.pallas_call(
        functools.partial(pack_x_kernel, sizes),
        out_shape=(
            shape(nx * plane, LANES),
            shape(nx * ny, LANES),
            shape(2 * plane + 3 * ny, LANES),
            shape(2 * plane + 2 * ny, LANES),
        ),
        compiler_params=params,
    )(heat_source, density)
    x_low, x_high = shift(x_up, "gx", 1), shift(x_down, "gx", -1)
    tail = lambda width: (nx + 4) * 2 * loads + -(-(nx + 5) * width // SUB) * SUB
    y_up, y_down = pl.pallas_call(
        functools.partial(pack_y_kernel, sizes),
        out_shape=(shape(tail(3), LANES), shape(tail(2), LANES)),
        compiler_params=params,
    )(bt, dt, x_low, x_high)
    y_low, y_high = shift(y_up, "gy", 1), shift(y_down, "gy", -1)
    mx, my = nx + 4, ny + 4
    q_t, v_t, inv_t, sums = pl.pallas_call(
        functools.partial(solve_kernel, sizes),
        out_shape=(
            shape(nx * plane, LANES),
            shape(nx * plane, LANES),
            shape(nx * ny, LANES),
            shape(loads, LANES),
        ),
        scratch_shapes=[
            scratch(mx + 1, my + 1, LANES),
            scratch(mx - 1, my - 1, loads, LANES),
        ]
        + [scratch(mx, my, loads, LANES)] * 7
        + [scratch(2, my, loads, LANES)],
        compiler_params=params,
    )(bt, dt, x_low, x_high, y_low, y_high)
    count = lax.axis_size("gx") * lax.axis_size("gy")
    spread = jnp.broadcast_to(sums[:, :4].reshape(1, -1), (count, 4 * loads))
    spread = lax.all_to_all(spread, ("gx", "gy"), 0, 0, tiled=True)
    totals = jnp.sum(spread, axis=0).reshape(loads, 4)
    image, again, inverse = pl.pallas_call(
        functools.partial(unpack_kernel, sizes),
        out_shape=(shape(*heat_source.shape), shape(*heat_source.shape), shape(nx, flat)),
        compiler_params=params,
    )(q_t, v_t, inv_t)
    rz, direct, square, last = (totals[:, place] for place in range(4))
    alpha = rz / direct
    rz_next = alpha * alpha * square - rz
    beta = rz_next / rz
    grown = 1.0 + beta
    alpha_next = rz_next / (
        grown * grown * direct - 2.0 * alpha * grown * square + alpha * alpha * last
    )
    first = (alpha + alpha_next * grown)[:, None, None]
    second = (alpha_next * alpha)[:, None, None]
    solution_field = (first * heat_source - second * image) * inverse
    residual = heat_source - first * image + second * again
    return solution_field, residual


def solution(mesh):
    placed = (P(None, "gx", "gy"), P("gx", "gy"))
    return jax.shard_map(
        per_device,
        mesh=mesh,
        in_specs=placed,
        out_specs=(P(None, "gx", "gy"), P(None, "gx", "gy")),
        check_vma=False,
    )
```

```python
import functools

import jax
import jax.numpy as jnp
from jax import lax
from jax.experimental import pallas as pl
from jax.experimental.pallas import tpu as pltpu
from jax.sharding import PartitionSpec as P

NZ = 96
KMIN = 0.001
LANES = 128
SUB = 8


def lane_ids(rows):
    return lax.broadcasted_iota(jnp.int32, (rows, LANES), 1)


def read_z(read, y, rows):
    start = y * NZ
    block, offset = start // LANES, start % LANES
    lane = lane_ids(rows)
    first = read(block)
    if offset:
        first = pltpu.roll(first, LANES - offset, 1)
    if offset + NZ > LANES:
        second = pltpu.roll(read(block + 1), LANES - offset, 1)
        first = jnp.where(lane < LANES - offset, first, second)
    return jnp.where(lane < NZ, first, 0.0)


def write_z(read_tile, block, rows):
    lane = lane_ids(rows)
    start = block * LANES
    out, at = None, start
    while at < start + LANES:
        y, z = at // NZ, at % NZ
        here = at - start
        piece = read_tile(y)
        shift = (here - z) % LANES
        if shift:
            piece = pltpu.roll(piece, shift, 1)
        out = piece if out is None else jnp.where(lane < here, out, piece)
        at += NZ - z
    return out


def pack_x_kernel(sizes, b_ref, d_ref, bt_ref, dt_ref, up_ref, down_ref):
    loads, nx, ny = sizes
    for load in range(loads):
        for x0 in range(0, nx, SUB):
            for y in range(ny):
                tile = read_z(
                    lambda t: b_ref[load, x0 : x0 + SUB, t * LANES : (t + 1) * LANES], y, SUB
                )
                bt_ref[pl.ds((x0 * ny + y) * loads + load, SUB, stride=ny * loads), :] = tile
    for x0 in range(0, nx, SUB):
        for y in range(ny):
            tile = read_z(lambda t: d_ref[x0 : x0 + SUB, t * LANES : (t + 1) * LANES], y, SUB)
            dt_ref[pl.ds(x0 * ny + y, SUB, stride=ny), :] = tile
    plane = ny * loads
    up_ref[: 2 * plane] = bt_ref[(nx - 2) * plane :]
    up_ref[2 * plane :] = dt_ref[(nx - 3) * ny :]
    down_ref[: 2 * plane] = bt_ref[: 2 * plane]
    down_ref[2 * plane :] = dt_ref[: 2 * ny]


def ext_rows(x, nx, plane, inner, low, high, low_planes, low_at, high_at):
    if x < 0:
        return low, low_at + (x + low_planes) * plane
    if x >= nx:
        return high, high_at + (x - nx) * plane
    return inner, x * plane


def pack_y_kernel(sizes, bt_ref, dt_ref, low_ref, high_ref, up_ref, down_ref):
    loads, nx, ny = sizes
    plane = ny * loads
    for x in range(-2, nx + 2):
        ref, row = ext_rows(x, nx, plane, bt_ref, low_ref, high_ref, 2, 0, 0)
        to = (x + 2) * 2 * loads
        up_ref[to : to + 2 * loads] = ref[row + (ny - 2) * loads : row + ny * loads]
        down_ref[to : to + 2 * loads] = ref[row : row + 2 * loads]
    base = (nx + 4) * 2 * loads
    for x in range(-3, nx + 2):
        ref, row = ext_rows(x, nx, ny, dt_ref, low_ref, high_ref, 3, 2 * plane, 2 * plane)
        to = base + (x + 3) * 3
        up_ref[to : to + 3] = ref[row + ny - 3 : row + ny]
        to = base + (x + 3) * 2
        down_ref[to : to + 2] = ref[row : row + 2]
    up_ref[base + (nx + 5) * 3 :] = jnp.zeros_like(up_ref[base + (nx + 5) * 3 :])
    down_ref[base + (nx + 5) * 2 :] = jnp.zeros_like(down_ref[base + (nx + 5) * 2 :])


def solve_kernel(
    sizes, bt_ref, dt_ref, xl_ref, xh_ref, yl_ref, yh_ref,
    q_ref, v_ref, inv_ref, sums_ref,
    dens, cond, invx, bx, zx, zs, wx, ws, qx, carry,
):
    loads, nx, ny = sizes
    plane = ny * loads
    base = (nx + 4) * 2 * loads
    for x in range(-3, nx + 2):
        ref, row = ext_rows(x, nx, ny, dt_ref, xl_ref, xh_ref, 3, 2 * plane, 2 * plane)
        dens[x + 3, 3 : 3 + ny, :] = ref[row : row + ny]
        at = base + (x + 3) * 3
        dens[x + 3, 0:3, :] = yl_ref[at : at + 3]
        at = base + (x + 3) * 2
        dens[x + 3, 3 + ny : 5 + ny, :] = yh_ref[at : at + 2]
    mx, my = nx + 4, ny + 4
    d = dens[...]
    conduct = jnp.where(d > 0.0, (KMIN + (1.0 - KMIN) * (d * d * d)) * (1.0 / 12.0), 0.0)
    pair = conduct[:-1] + conduct[1:]
    pair = pair[:, :-1, :] + pair[:, 1:, :]
    here = conduct[1:, 1:, :]
    for x in range(mx):
        total = 4.0 * (pair[x] + pltpu.roll(pair[x], 1, 1))
        inverse = jnp.where(here[x] > 0.0, 1.0 / total, 0.0)
        for y in range(my):
            row = inverse[y : y + 1, :]
            invx[x, y] = jnp.broadcast_to(row, (loads, LANES))
            if x < mx - 1 and y < my - 1:
                cond[x, y] = jnp.broadcast_to(here[x, y : y + 1, :], (loads, LANES))
        if 2 <= x < 2 + nx:
            inv_ref[(x - 2) * ny : (x - 1) * ny, :] = inverse[2 : 2 + ny, :]
    def stage(x, y, tile):
        bx[x, y] = tile
        scaled = tile * invx[x, y]
        zx[x, y] = scaled
        zs[x, y] = pltpu.roll(scaled, LANES - 1, 1)

    for x in range(mx):
        ref, row = ext_rows(x - 2, nx, plane, bt_ref, xl_ref, xh_ref, 2, 0, 0)
        for y in range(ny):
            at = row + y * loads
            stage(x, y + 2, ref[at : at + loads])
        for y in range(2):
            at = (x * 2 + y) * loads
            stage(x, y, yl_ref[at : at + loads])
            stage(x, y + 2 + ny, yh_ref[at : at + loads])

    def element_plane(a, a0, rows, low, low_s, first, emit):
        above_lo = above_hi = None
        left_lo = left_hi = None
        p0, p0s = low[a, a0], low_s[a, a0]
        p1, p1s = low[a + 1, a0], low_s[a + 1, a0]
        for step in range(rows):
            y = a0 + step
            r0, r0s = low[a, y + 1], low_s[a, y + 1]
            r1, r1s = low[a + 1, y + 1], low_s[a + 1, y + 1]
            c = cond[a, y]
            even = p0 + r1 + (r0s + p1s)
            odd = r0 + p1 + (p0s + r1s)
            t000 = c * (even + r1s)
            t110 = c * (even + p0s)
            t011 = c * (even + p1)
            t101 = c * (even + r0)
            t111 = c * (odd + p0)
            t001 = c * (odd + r1)
            t100 = c * (odd + r0s)
            t010 = c * (odd + p1s)
            if step and not first:
                lo = t000 + left_lo + carry[0, y]
                hi = t001 + left_hi + carry[1, y]
                emit(y, lo + pltpu.roll(hi, 1, 1))
            left_lo, left_hi = t010, t011
            if step:
                carry[0, y] = t100 + above_lo
                carry[1, y] = t101 + above_hi
            above_lo, above_hi = t110, t111
            p0, p0s, p1, p1s = r0, r0s, r1, r1s

    def first_pass(a, first):
        def emit(y, total):
            image = 1.25 * bx[a, y] - total
            weighted = image * invx[a, y]
            qx[a, y] = image
            wx[a, y] = weighted
            ws[a, y] = pltpu.roll(weighted, LANES - 1, 1)

        element_plane(a, 0, my - 1, zx, zs, first, emit)

    first_pass(0, True)

    @pl.loop(1, mx - 1)
    def _(a):
        first_pass(a, False)

    def second_pass(a, first, sums):
        sums = list(sums)

        def emit(y, total):
            image = qx[a, y]
            again = 1.25 * image - total
            row = pl.multiple_of(((a - 2) * ny + (y - 2)) * loads, SUB)
            q_ref[pl.ds(row, loads), :] = image
            v_ref[pl.ds(row, loads), :] = again
            scaled, weighted = zx[a, y], wx[a, y]
            sums[0] = sums[0] + bx[a, y] * scaled
            sums[1] = sums[1] + scaled * image
            sums[2] = sums[2] + image * weighted
            sums[3] = sums[3] + weighted * again

        element_plane(a, 1, my - 3, wx, ws, first, emit)
        return tuple(sums)

    zero = jnp.zeros((loads, LANES), jnp.float32)
    second_pass(1, True, (zero,) * 4)
    sums = lax.fori_loop(2, mx - 2, lambda a, s: second_pass(a, False, s), (zero,) * 4)
    lane = lane_ids(loads)
    packed = zero
    for place, part in enumerate(sums):
        packed = jnp.where(lane == place, jnp.sum(part, axis=1, keepdims=True), packed)
    sums_ref[...] = packed


def unpack_kernel(sizes, q_ref, v_ref, inv_ref, qo_ref, vo_ref, io_ref):
    loads, nx, ny = sizes
    for x0 in range(0, nx, SUB):
        for block in range(ny * NZ // LANES):
            lanes = slice(block * LANES, (block + 1) * LANES)
            io_ref[x0 : x0 + SUB, lanes] = write_z(
                lambda y: inv_ref[pl.ds(x0 * ny + y, SUB, stride=ny), :], block, SUB
            )
            for ref, out in ((q_ref, qo_ref), (v_ref, vo_ref)):
                for load in range(loads):
                    out[load, x0 : x0 + SUB, lanes] = write_z(
                        lambda y: ref[
                            pl.ds((x0 * ny + y) * loads + load, SUB, stride=ny * loads), :
                        ],
                        block,
                        SUB,
                    )


def shift(array, axis, by):
    length = lax.axis_size(axis)
    pairs = [(i, i + by) for i in range(length) if 0 <= i + by < length]
    return lax.ppermute(array, axis, pairs)


def prime_factors(number):
    factors, divisor = [], 2
    while number > 1:
        while number % divisor == 0:
            factors.append(divisor)
            number //= divisor
        divisor += 1
    return factors


def sum_over(array, axis):
    length = lax.axis_size(axis)
    stride = 1
    for factor in prime_factors(length):
        total = array
        for step in range(1, factor):
            pairs = []
            for i in range(length):
                digit = i // stride % factor
                pairs.append((i, i + ((digit + step) % factor - digit) * stride))
            total = total + lax.ppermute(array, axis, pairs)
        array = total
        stride *= factor
    return array


def per_device(heat_source, density):
    loads, nx, flat = heat_source.shape
    ny = flat // NZ
    sizes = (loads, nx, ny)
    plane = ny * loads
    f32 = jnp.float32

    def shape(*dims):
        return jax.ShapeDtypeStruct(dims, f32)

    def scratch(*dims):
        return pltpu.VMEM(dims, f32)

    params = pltpu.CompilerParams(vmem_limit_bytes=48 * 1024 * 1024)
    bt, dt, x_up, x_down = pl.pallas_call(
        functools.partial(pack_x_kernel, sizes),
        out_shape=(
            shape(nx * plane, LANES),
            shape(nx * ny, LANES),
            shape(2 * plane + 3 * ny, LANES),
            shape(2 * plane + 2 * ny, LANES),
        ),
        compiler_params=params,
    )(heat_source, density)
    x_low, x_high = shift(x_up, "gx", 1), shift(x_down, "gx", -1)
    tail = lambda width: (nx + 4) * 2 * loads + -(-(nx + 5) * width // SUB) * SUB
    y_up, y_down = pl.pallas_call(
        functools.partial(pack_y_kernel, sizes),
        out_shape=(shape(tail(3), LANES), shape(tail(2), LANES)),
        compiler_params=params,
    )(bt, dt, x_low, x_high)
    y_low, y_high = shift(y_up, "gy", 1), shift(y_down, "gy", -1)
    mx, my = nx + 4, ny + 4
    q_t, v_t, inv_t, sums = pl.pallas_call(
        functools.partial(solve_kernel, sizes),
        out_shape=(
            shape(nx * plane, LANES),
            shape(nx * plane, LANES),
            shape(nx * ny, LANES),
            shape(loads, LANES),
        ),
        scratch_shapes=[
            scratch(mx + 1, my + 1, LANES),
            scratch(mx - 1, my - 1, loads, LANES),
        ]
        + [scratch(mx, my, loads, LANES)] * 7
        + [scratch(2, my, loads, LANES)],
        compiler_params=params,
    )(bt, dt, x_low, x_high, y_low, y_high)
    totals = jnp.sum(lax.all_gather(sums, ("gx", "gy")), axis=0)
    image, again, inverse = pl.pallas_call(
        functools.partial(unpack_kernel, sizes),
        out_shape=(shape(*heat_source.shape), shape(*heat_source.shape), shape(nx, flat)),
        compiler_params=params,
    )(q_t, v_t, inv_t)
    rz, direct, square, last = (totals[:, place] for place in range(4))
    alpha = rz / direct
    rz_next = alpha * alpha * square - rz
    beta = rz_next / rz
    grown = 1.0 + beta
    alpha_next = rz_next / (
        grown * grown * direct - 2.0 * alpha * grown * square + alpha * alpha * last
    )
    first = (alpha + alpha_next * grown)[:, None, None]
    second = (alpha_next * alpha)[:, None, None]
    solution_field = (first * heat_source - second * image) * inverse
    residual = heat_source - first * image + second * again
    return solution_field, residual


def solution(mesh):
    placed = (P(None, "gx", "gy"), P("gx", "gy"))
    return jax.shard_map(
        per_device,
        mesh=mesh,
        in_specs=placed,
        out_specs=(P(None, "gx", "gy"), P(None, "gx", "gy")),
        check_vma=False,
    )
```

```python
import functools

import jax
import jax.numpy as jnp
from jax import lax
from jax.experimental import pallas as pl
from jax.experimental.pallas import tpu as pltpu
from jax.sharding import PartitionSpec as P

NZ = 96
KMIN = 0.001
LANES = 128
SUB = 8


def packed_count(tiles):
    return -(-tiles * NZ // LANES)


def lane_ids(rows):
    return lax.broadcasted_iota(jnp.int32, (rows, LANES), 1)


def unpack_tile(read, index, rows):
    start = index * NZ
    block, offset = start // LANES, start % LANES
    lane = lane_ids(rows)
    first = read(block)
    if offset:
        first = pltpu.roll(first, LANES - offset, 1)
    if offset + NZ > LANES:
        second = pltpu.roll(read(block + 1), LANES - offset, 1)
        first = jnp.where(lane < LANES - offset, first, second)
    return jnp.where(lane < NZ, first, 0.0)


def pack_block(read_tile, tiles, block, rows):
    lane = lane_ids(rows)
    start = block * LANES
    out, at = None, start
    while at < start + LANES and at // NZ < tiles:
        index, z = at // NZ, at % NZ
        here = at - start
        piece = read_tile(index)
        shift = (here - z) % LANES
        if shift:
            piece = pltpu.roll(piece, shift, 1)
        out = piece if out is None else jnp.where(lane < here, out, piece)
        at += NZ - z
    return out


def pack_tiles(out_ref, at, rows, tiles, read_tile):
    for block in range(packed_count(tiles)):
        out_ref[at + block * rows : at + (block + 1) * rows, :] = pack_block(
            read_tile, tiles, block, rows
        )


def unpack_tiles(ref, at, rows, tiles, write):
    for index in range(tiles):
        write(
            index,
            unpack_tile(lambda t: ref[at + t * rows : at + (t + 1) * rows, :], index, rows),
        )


class Sizes:
    def __init__(self, loads, nx, ny):
        self.loads, self.nx, self.ny = loads, nx, ny
        self.plane = ny * loads
        self.x_dens = packed_count(2 * ny) * loads
        self.x_rows = self.x_dens + 3 * ny
        self.y_dens = packed_count(2 * nx) * loads
        self.y_rows = self.y_dens + 3 * nx
        self.c_dens = packed_count(8) * loads
        self.c_rows = self.c_dens + -(-18 // SUB) * SUB
        self.pitch = -(-(ny + 6) // SUB) * SUB


def is_even(axis):
    return lax.rem(lax.axis_index(axis), 2) == 0


def pick(even, if_even, if_odd):
    return jnp.where(even, if_even, if_odd)


def pack_kernel(s, b_hbm, d_hbm, bt_ref, dt_ref, x1_ref, x2_ref, yb_ref, b_ref, d_ref, sems):
    loads, nx, ny = s.loads, s.nx, s.ny
    d_copy = pltpu.make_async_copy(d_hbm, d_ref, sems.at[loads])
    d_copy.start()
    copies = []
    for load in range(loads):
        copies.append(pltpu.make_async_copy(b_hbm.at[load], b_ref.at[load], sems.at[load]))
        copies[-1].start()
    d_copy.wait()
    for x0 in range(0, nx, SUB):
        for y in range(ny):
            tile = unpack_tile(
                lambda t: d_ref[x0 : x0 + SUB, t * LANES : (t + 1) * LANES], y, SUB
            )
            dt_ref[pl.ds(x0 * ny + y, SUB, stride=ny), :] = tile
    for load in range(loads):
        copies[load].wait()
        for x0 in range(0, nx, SUB):
            for y in range(ny):
                tile = unpack_tile(
                    lambda t: b_ref[load, x0 : x0 + SUB, t * LANES : (t + 1) * LANES], y, SUB
                )
                bt_ref[pl.ds((x0 * ny + y) * loads + load, SUB, stride=ny * loads), :] = tile
    even_x, even_y = is_even("gx"), is_even("gy")

    def tile_at(x, y):
        return bt_ref[pl.ds(pl.multiple_of((x * ny + y) * loads, SUB), loads), :]

    for ref, even in ((x1_ref, even_x), (x2_ref, jnp.logical_not(even_x))):
        x0 = pick(even, nx - 2, 0)
        pack_tiles(ref, 0, loads, 2 * ny, lambda i: tile_at(x0 + i // ny, i % ny))
        rows = pl.ds(pl.multiple_of(pick(even, nx - 3, 0) * ny, SUB), 3 * ny)
        ref[s.x_dens :, :] = dt_ref[rows, :]
    pack_face(s, jnp.logical_not(even_y), bt_ref, dt_ref, yb_ref)


def pack_face(s, upper, bt_ref, dt_ref, out_ref):
    loads, nx, ny = s.loads, s.nx, s.ny
    y0 = pick(upper, ny - 2, 0)

    def tile_at(i):
        return bt_ref[
            pl.ds(pl.multiple_of((i // 2 * ny + y0 + i % 2) * loads, SUB), loads), :
        ]

    pack_tiles(out_ref, 0, loads, 2 * nx, tile_at)
    y0 = pick(upper, ny - 3, 0)
    for dy in range(3):
        for x0 in range(0, nx, SUB):
            at = s.y_dens + dy * nx + x0
            out_ref[at : at + SUB, :] = dt_ref[pl.ds(x0 * ny + y0 + dy, SUB, stride=ny), :]


def corner_kernel(s, bt_ref, dt_ref, x1_ref, x2_ref, xt_ref, ya_ref, yc_ref):
    loads, ny = s.loads, s.ny
    for side, ref in enumerate((x1_ref, x2_ref)):

        def write(index, tile):
            at = (side * 2 * ny + index) * loads
            xt_ref[at : at + loads, :] = tile

        unpack_tiles(ref, 0, loads, 2 * ny, write)
    even_y = is_even("gy")
    pack_face(s, even_y, bt_ref, dt_ref, ya_ref)
    for out_ref, base, upper in (
        (ya_ref, s.y_rows, even_y),
        (yc_ref, 0, jnp.logical_not(even_y)),
    ):
        y0 = pick(upper, ny - 2, 0)

        def tile_at(i):
            return xt_ref[
                pl.ds(pl.multiple_of((i // 2 * ny + y0 + i % 2) * loads, SUB), loads), :
            ]

        pack_tiles(out_ref, base, loads, 8, tile_at)
        y0 = pick(upper, ny - 3, 0)
        at = base + s.c_dens
        for ref in (x1_ref, x2_ref):
            for t in range(3):
                for dy in range(3):
                    row = s.x_dens + t * ny + y0 + dy
                    out_ref[at : at + 1, :] = ref[pl.ds(row, 1), :]
                    at += 1
        end = base + s.c_rows
        out_ref[at:end, :] = jnp.zeros((end - at, LANES), jnp.float32)


def solve_kernel(
    s, bt_ref, dt_ref, xt_ref, x1_ref, x2_ref, yb_ref, ya_ref, yc_ref,
    q_ref, v_ref, inv_ref, sums_ref,
    dens, cond, invx, bx, zx, zs, wx, ws, qx, carry,
):
    loads, nx, ny, pitch = s.loads, s.nx, s.ny, s.pitch
    even_x, even_y = is_even("gx"), is_even("gy")
    xs = (pick(even_x, nx + 2, 0), pick(even_x, 0, nx + 2))
    ys = (pick(even_y, ny + 2, 0), pick(even_y, 0, ny + 2))
    xd = (pick(even_x, nx + 3, 0), pick(even_x, 0, nx + 3))
    yd = (pick(even_y, ny + 3, 0), pick(even_y, 0, ny + 3))
    faces = ((ya_ref, 0, ya_ref, s.y_rows), (yb_ref, 0, yc_ref, 0))

    for x in range(nx):
        dens[(x + 3) * pitch + 3 : (x + 3) * pitch + 3 + ny, :] = dt_ref[x * ny : (x + 1) * ny, :]
    for side, ref in enumerate((x1_ref, x2_ref)):
        for t in range(3):
            at = s.x_dens + t * ny
            to = pl.multiple_of((xd[side] + t) * pitch, SUB)
            plane = jnp.concatenate(
                [jnp.zeros((3, LANES), jnp.float32), ref[at : at + ny, :],
                 jnp.zeros((pitch - 3 - ny, LANES), jnp.float32)], axis=0
            )
            dens[pl.ds(to, pitch), :] = plane
    for side, (face, _, corner, corner_at) in enumerate(faces):
        for dy in range(3):
            for x0 in range(0, nx, SUB):
                at = s.y_dens + dy * nx + x0
                to = (x0 + 3) * pitch + yd[side] + dy
                dens[pl.ds(to, SUB, stride=pitch), :] = face[at : at + SUB, :]
        at = corner_at + s.c_dens
        for x_side in range(2):
            for t in range(3):
                for dy in range(3):
                    to = (xd[x_side] + t) * pitch + yd[side] + dy
                    dens[pl.ds(to, 1), :] = corner[at : at + 1, :]
                    at += 1

    mx, my = nx + 4, ny + 4

    def conduct_of(x):
        d = dens[x * pitch : (x + 1) * pitch, :]
        return jnp.where(d > 0.0, (KMIN + (1.0 - KMIN) * (d * d * d)) * (1.0 / 12.0), 0.0)

    before = conduct_of(0)
    for x in range(mx):
        after = conduct_of(x + 1)
        pair = before + after
        pair = pair[: pitch - 1] + pair[1:]
        here = after[1:]
        total = 4.0 * (pair + pltpu.roll(pair, 1, 1))
        inverse = jnp.where(here > 0.0, 1.0 / total, 0.0)
        for y in range(my):
            invx[x, y] = jnp.broadcast_to(inverse[y : y + 1, :], (loads, LANES))
            if x < mx - 1 and y < my - 1:
                cond[x, y] = jnp.broadcast_to(here[y : y + 1, :], (loads, LANES))
        if 2 <= x < 2 + nx:
            inv_ref[(x - 2) * ny : (x - 1) * ny, :] = inverse[2 : 2 + ny, :]
        before = after

    def stage(x, y, tile):
        bx[x, y] = tile
        scaled = tile * invx[x, y]
        zx[x, y] = scaled
        zs[x, y] = pltpu.roll(scaled, LANES - 1, 1)

    for x in range(nx):
        for y in range(ny):
            at = (x * ny + y) * loads
            stage(x + 2, y + 2, bt_ref[at : at + loads, :])
    for side in range(2):
        for dx in range(2):
            for y in range(ny):
                at = ((side * 2 + dx) * ny + y) * loads
                stage(xs[side] + dx, y + 2, xt_ref[at : at + loads, :])
    for side, (face, face_at, corner, corner_at) in enumerate(faces):
        unpack_tiles(
            face, face_at, loads, 2 * nx,
            lambda i, tile: stage(i // 2 + 2, ys[side] + i % 2, tile),
        )
        unpack_tiles(
            corner, corner_at, loads, 8,
            lambda i, tile: stage(xs[i // 4] + i // 2 % 2, ys[side] + i % 2, tile),
        )

    def element_planes(a, count, y0, columns, field, field_up, emit):
        left = [(field[a + u, y0], field_up[a + u, y0]) for u in range(count + 1)]
        old = [None] * count
        for step in range(columns):
            y = y0 + step
            right = [(field[a + u, y + 1], field_up[a + u, y + 1]) for u in range(count + 1)]
            above = (carry[0, y], carry[1, y]) if step and emit else None
            for u in range(count):
                (p0, p0s), (p1, p1s) = left[u], left[u + 1]
                (r0, r0s), (r1, r1s) = right[u], right[u + 1]
                c = cond[a + u, y]
                even = (p0 + r1) + (r0s + p1s)
                odd = (r0 + p1) + (p0s + r1s)
                lower = None
                if emit:
                    lower = (c * (odd + p1s), c * (even + p1))
                upper = (c * (even + p0s), c * (odd + p0))
                if step and emit:
                    low = (c * (even + r1s) + old[u][0][0]) + above[0]
                    high = (c * (odd + r1) + old[u][0][1]) + above[1]
                    emit(u, a + u, y, p0, low + pltpu.roll(high, 1, 1))
                if step:
                    above = (
                        c * (odd + r0s) + old[u][1][0],
                        c * (even + r0) + old[u][1][1],
                    )
                old[u] = (lower, upper)
            if step:
                carry[0, y], carry[1, y] = above
            left = right

    def first_emit(u, x, y, node, total):
        image = 1.25 * bx[x, y] - total
        weighted = image * invx[x, y]
        qx[x, y] = image
        wx[x, y] = weighted
        ws[x, y] = pltpu.roll(weighted, LANES - 1, 1)

    width = 2 if nx % 2 == 0 else 1
    element_planes(0, 1, 0, my - 1, zx, zs, None)

    @pl.loop(0, (nx + 2) // width)
    def _(i):
        element_planes(1 + i * width, width, 0, my - 1, zx, zs, first_emit)

    element_planes(1, 1, 1, ny + 1, wx, ws, None)

    def second(i, sums):
        sums = list(sums)

        def emit(u, x, y, weighted, total):
            image, source, scaled = qx[x, y], bx[x, y], zx[x, y]
            again = 1.25 * image - total
            row = pl.multiple_of(((x - 2) * ny + (y - 2)) * loads, SUB)
            q_ref[pl.ds(row, loads), :] = image
            v_ref[pl.ds(row, loads), :] = again
            change = scaled - weighted
            sums[0] = sums[0] + source * scaled
            sums[1] = sums[1] + source * change
            sums[2] = sums[2] + (source - image) * change
            sums[3] = sums[3] + (image - again) * change

        element_planes(2 + i * width, width, 1, ny + 1, wx, ws, emit)
        return tuple(sums)

    zero = jnp.zeros((loads, LANES), jnp.float32)
    sums = lax.fori_loop(0, nx // width, second, (zero,) * 4)
    lane = lane_ids(loads)
    load = lax.broadcasted_iota(jnp.int32, (loads, LANES), 0)
    packed = zero
    for place, part in enumerate(sums):
        total = jnp.sum(part, axis=1, keepdims=True)
        packed = packed + jnp.where(lane == place * loads + load, total, 0.0)
    row = jnp.sum(packed, axis=0, keepdims=True)
    sums_ref[...] = jnp.broadcast_to(row[None], sums_ref.shape)


def unpack_kernel(s, q_ref, v_ref, inv_ref, qo_ref, vo_ref, io_ref):
    loads, nx, ny = s.loads, s.nx, s.ny
    for x0 in range(0, nx, SUB):
        for block in range(packed_count(ny)):
            lanes = slice(block * LANES, (block + 1) * LANES)
            io_ref[x0 : x0 + SUB, lanes] = pack_block(
                lambda y: inv_ref[pl.ds(x0 * ny + y, SUB, stride=ny), :], ny, block, SUB
            )
            for ref, out in ((q_ref, qo_ref), (v_ref, vo_ref)):
                for load in range(loads):
                    out[load, x0 : x0 + SUB, lanes] = pack_block(
                        lambda y: ref[
                            pl.ds((x0 * ny + y) * loads + load, SUB, stride=ny * loads), :
                        ],
                        ny,
                        block,
                        SUB,
                    )


def finish_kernel(s, parts_ref, b_ref, q_ref, v_ref, inv_ref, x_hbm, r_hbm, x_ref, r_ref, sems):
    loads = s.loads
    totals = jnp.sum(parts_ref[...], axis=0)

    def part(place):
        return pltpu.roll(totals, (LANES - place * loads) % LANES, 1) if place else totals

    rz, near, square, last = (part(place) for place in range(4))
    direct = rz - near
    alpha = rz / direct
    short = -near / direct
    rz_next = short * short * rz + 2.0 * alpha * short * near + alpha * alpha * square
    beta = rz_next / rz
    grown = short + beta
    curved = (
        grown * grown * direct
        + 2.0 * alpha * grown * (near - square)
        + alpha * alpha * last
    )
    alpha_next = rz_next / curved
    first_row = alpha + alpha_next * (1.0 + beta)
    second_row = alpha_next * alpha
    inverse = inv_ref[...]
    copies = []
    for load in range(loads):
        first = first_row[:, load : load + 1]
        second = second_row[:, load : load + 1]
        source, image = b_ref[load], q_ref[load]
        x_ref[load] = (first * source - second * image) * inverse
        copies.append(pltpu.make_async_copy(x_ref.at[load], x_hbm.at[load], sems.at[0, load]))
        copies[-1].start()
        r_ref[load] = source - first * image + second * v_ref[load]
        copies.append(pltpu.make_async_copy(r_ref.at[load], r_hbm.at[load], sems.at[1, load]))
        copies[-1].start()
    for copy in copies:
        copy.wait()


def swap(array, axis, start):
    pairs = []
    for i in range(start, lax.axis_size(axis) - 1, 2):
        pairs += [(i, i + 1), (i + 1, i)]
    return lax.ppermute(array, axis, pairs)


def per_device(heat_source, density):
    loads, nx, flat = heat_source.shape
    ny = flat // NZ
    s = Sizes(loads, nx, ny)
    nodes = nx * ny * loads
    devices = lax.axis_size("gx") * lax.axis_size("gy")

    def shape(*dims):
        return jax.ShapeDtypeStruct(dims, jnp.float32)

    def scratch(*dims):
        return pltpu.VMEM(dims, jnp.float32)

    def call(kernel, out_shape, **more):
        params = pltpu.CompilerParams(vmem_limit_bytes=48 * 1024 * 1024)
        return pl.pallas_call(
            functools.partial(kernel, s), out_shape=out_shape, compiler_params=params, **more
        )

    hbm = pl.BlockSpec(memory_space=pl.ANY)
    bt, dt, x1, x2, yb = call(
        pack_kernel,
        (
            shape(nodes, LANES),
            shape(nx * ny, LANES),
            shape(s.x_rows, LANES),
            shape(s.x_rows, LANES),
            shape(s.y_rows, LANES),
        ),
        in_specs=[hbm, hbm],
        scratch_shapes=[
            scratch(loads, nx, flat),
            scratch(nx, flat),
            pltpu.SemaphoreType.DMA((loads + 1,)),
        ],
    )(heat_source, density)
    x1, x2 = swap(x1, "gx", 0), swap(x2, "gx", 1)
    yb = swap(yb, "gy", 1)
    xt, ya, yc = call(
        corner_kernel,
        (
            shape(4 * ny * loads, LANES),
            shape(s.y_rows + s.c_rows, LANES),
            shape(s.c_rows, LANES),
        ),
    )(bt, dt, x1, x2)
    ya, yc = swap(ya, "gy", 0), swap(yc, "gy", 1)
    mx, my = nx + 4, ny + 4
    field = scratch(mx, my, loads, LANES)
    q_t, v_t, inv_t, sums = call(
        solve_kernel,
        (
            shape(nodes, LANES),
            shape(nodes, LANES),
            shape(nx * ny, LANES),
            shape(devices, 1, LANES),
        ),
        scratch_shapes=[scratch((nx + 6) * s.pitch, LANES)]
        + [field] * 8
        + [scratch(2, my, loads, LANES)],
    )(bt, dt, xt, x1, x2, yb, ya, yc)
    parts = lax.all_to_all(sums, ("gx", "gy"), 0, 0, tiled=True)
    whole = shape(loads, nx, flat)
    image, again, inverse = call(unpack_kernel, (whole, whole, shape(nx, flat)))(q_t, v_t, inv_t)
    return call(
        finish_kernel,
        (whole, whole),
        out_specs=(hbm, hbm),
        scratch_shapes=[
            scratch(loads, nx, flat),
            scratch(loads, nx, flat),
            pltpu.SemaphoreType.DMA((2, loads)),
        ],
    )(parts, heat_source, image, again, inverse)


def solution(mesh):
    placed = (P(None, "gx", "gy"), P("gx", "gy"))
    return jax.shard_map(
        per_device,
        mesh=mesh,
        in_specs=placed,
        out_specs=(P(None, "gx", "gy"), P(None, "gx", "gy")),
        check_vma=False,
    )
```

```python
import functools

import jax
import jax.numpy as jnp
from jax import lax
from jax.experimental import pallas as pl
from jax.experimental.pallas import tpu as pltpu
from jax.sharding import PartitionSpec as P

NZ = 96
KMIN = 0.001
LANES = 128
SUB = 8


def packed_count(tiles):
    return -(-tiles * NZ // LANES)


def lane_ids(rows):
    return lax.broadcasted_iota(jnp.int32, (rows, LANES), 1)


def unpack_tile(read, index, rows):
    start = index * NZ
    block, offset = start // LANES, start % LANES
    lane = lane_ids(rows)
    first = read(block)
    if offset:
        first = pltpu.roll(first, LANES - offset, 1)
    if offset + NZ > LANES:
        second = pltpu.roll(read(block + 1), LANES - offset, 1)
        first = jnp.where(lane < LANES - offset, first, second)
    return jnp.where(lane < NZ, first, 0.0)


def pack_block(read_tile, tiles, block, rows):
    lane = lane_ids(rows)
    start = block * LANES
    out, at = None, start
    while at < start + LANES and at // NZ < tiles:
        index, z = at // NZ, at % NZ
        here = at - start
        piece = read_tile(index)
        shift = (here - z) % LANES
        if shift:
            piece = pltpu.roll(piece, shift, 1)
        out = piece if out is None else jnp.where(lane < here, out, piece)
        at += NZ - z
    return out


def pack_tiles(out_ref, at, rows, tiles, read_tile):
    for block in range(packed_count(tiles)):
        out_ref[at + block * rows : at + (block + 1) * rows, :] = pack_block(
            read_tile, tiles, block, rows
        )


def unpack_tiles(ref, at, rows, tiles, write):
    for index in range(tiles):
        write(
            index,
            unpack_tile(lambda t: ref[at + t * rows : at + (t + 1) * rows, :], index, rows),
        )


class Sizes:
    def __init__(self, loads, nx, ny):
        self.loads, self.nx, self.ny = loads, nx, ny
        self.plane = ny * loads
        self.x_dens = packed_count(2 * ny) * loads
        self.x_rows = self.x_dens + 3 * ny
        self.y_dens = packed_count(2 * nx) * loads
        self.y_rows = self.y_dens + 3 * nx
        self.c_dens = packed_count(8) * loads
        self.c_rows = self.c_dens + -(-18 // SUB) * SUB
        self.pitch = -(-(ny + 6) // SUB) * SUB


def is_even(axis):
    return lax.rem(lax.axis_index(axis), 2) == 0


def pick(even, if_even, if_odd):
    return jnp.where(even, if_even, if_odd)


def pack_kernel(s, b_hbm, d_hbm, bt_ref, dt_ref, x1_ref, x2_ref, yb_ref, b_ref, d_ref, sems):
    loads, nx, ny = s.loads, s.nx, s.ny
    d_copy = pltpu.make_async_copy(d_hbm, d_ref, sems.at[loads])
    d_copy.start()
    copies = []
    for load in range(loads):
        copies.append(pltpu.make_async_copy(b_hbm.at[load], b_ref.at[load], sems.at[load]))
        copies[-1].start()
    d_copy.wait()
    for x0 in range(0, nx, SUB):
        for y in range(ny):
            tile = unpack_tile(
                lambda t: d_ref[x0 : x0 + SUB, t * LANES : (t + 1) * LANES], y, SUB
            )
            dt_ref[pl.ds(x0 * ny + y, SUB, stride=ny), :] = tile
    for load in range(loads):
        copies[load].wait()
        for x0 in range(0, nx, SUB):
            for y in range(ny):
                tile = unpack_tile(
                    lambda t: b_ref[load, x0 : x0 + SUB, t * LANES : (t + 1) * LANES], y, SUB
                )
                bt_ref[pl.ds((x0 * ny + y) * loads + load, SUB, stride=ny * loads), :] = tile
    even_x, even_y = is_even("gx"), is_even("gy")

    def tile_at(x, y):
        return bt_ref[pl.ds(pl.multiple_of((x * ny + y) * loads, SUB), loads), :]

    for ref, even in ((x1_ref, even_x), (x2_ref, jnp.logical_not(even_x))):
        x0 = pick(even, nx - 2, 0)
        pack_tiles(ref, 0, loads, 2 * ny, lambda i: tile_at(x0 + i // ny, i % ny))
        rows = pl.ds(pl.multiple_of(pick(even, nx - 3, 0) * ny, SUB), 3 * ny)
        ref[s.x_dens :, :] = dt_ref[rows, :]
    pack_face(s, jnp.logical_not(even_y), bt_ref, dt_ref, yb_ref)


def pack_face(s, upper, bt_ref, dt_ref, out_ref):
    loads, nx, ny = s.loads, s.nx, s.ny
    y0 = pick(upper, ny - 2, 0)

    def tile_at(i):
        return bt_ref[
            pl.ds(pl.multiple_of((i // 2 * ny + y0 + i % 2) * loads, SUB), loads), :
        ]

    pack_tiles(out_ref, 0, loads, 2 * nx, tile_at)
    y0 = pick(upper, ny - 3, 0)
    for dy in range(3):
        for x0 in range(0, nx, SUB):
            at = s.y_dens + dy * nx + x0
            out_ref[at : at + SUB, :] = dt_ref[pl.ds(x0 * ny + y0 + dy, SUB, stride=ny), :]


def corner_kernel(s, bt_ref, dt_ref, x1_ref, x2_ref, xt_ref, ya_ref, yc_ref):
    loads, ny = s.loads, s.ny
    for side, ref in enumerate((x1_ref, x2_ref)):

        def write(index, tile):
            at = (side * 2 * ny + index) * loads
            xt_ref[at : at + loads, :] = tile

        unpack_tiles(ref, 0, loads, 2 * ny, write)
    even_y = is_even("gy")
    pack_face(s, even_y, bt_ref, dt_ref, ya_ref)
    for out_ref, base, upper in (
        (ya_ref, s.y_rows, even_y),
        (yc_ref, 0, jnp.logical_not(even_y)),
    ):
        y0 = pick(upper, ny - 2, 0)

        def tile_at(i):
            return xt_ref[
                pl.ds(pl.multiple_of((i // 2 * ny + y0 + i % 2) * loads, SUB), loads), :
            ]

        pack_tiles(out_ref, base, loads, 8, tile_at)
        y0 = pick(upper, ny - 3, 0)
        at = base + s.c_dens
        for ref in (x1_ref, x2_ref):
            for t in range(3):
                for dy in range(3):
                    row = s.x_dens + t * ny + y0 + dy
                    out_ref[at : at + 1, :] = ref[pl.ds(row, 1), :]
                    at += 1
        end = base + s.c_rows
        out_ref[at:end, :] = jnp.zeros((end - at, LANES), jnp.float32)


def solve_kernel(
    s, bt_ref, dt_ref, xt_ref, x1_ref, x2_ref, yb_ref, ya_ref, yc_ref,
    q_ref, v_ref, inv_ref, sums_ref,
    dens, cond, invx, bx, zx, zs, wx, ws, qx, carry,
):
    loads, nx, ny, pitch = s.loads, s.nx, s.ny, s.pitch
    even_x, even_y = is_even("gx"), is_even("gy")
    xs = (pick(even_x, nx + 2, 0), pick(even_x, 0, nx + 2))
    ys = (pick(even_y, ny + 2, 0), pick(even_y, 0, ny + 2))
    xd = (pick(even_x, nx + 3, 0), pick(even_x, 0, nx + 3))
    yd = (pick(even_y, ny + 3, 0), pick(even_y, 0, ny + 3))
    faces = ((ya_ref, 0, ya_ref, s.y_rows), (yb_ref, 0, yc_ref, 0))

    for x in range(nx):
        dens[(x + 3) * pitch + 3 : (x + 3) * pitch + 3 + ny, :] = dt_ref[x * ny : (x + 1) * ny, :]
    for side, ref in enumerate((x1_ref, x2_ref)):
        for t in range(3):
            at = s.x_dens + t * ny
            to = pl.multiple_of((xd[side] + t) * pitch, SUB)
            plane = jnp.concatenate(
                [jnp.zeros((3, LANES), jnp.float32), ref[at : at + ny, :],
                 jnp.zeros((pitch - 3 - ny, LANES), jnp.float32)], axis=0
            )
            dens[pl.ds(to, pitch), :] = plane
    for side, (face, _, corner, corner_at) in enumerate(faces):
        for dy in range(3):
            for x0 in range(0, nx, SUB):
                at = s.y_dens + dy * nx + x0
                to = (x0 + 3) * pitch + yd[side] + dy
                dens[pl.ds(to, SUB, stride=pitch), :] = face[at : at + SUB, :]
        at = corner_at + s.c_dens
        for x_side in range(2):
            for t in range(3):
                for dy in range(3):
                    to = (xd[x_side] + t) * pitch + yd[side] + dy
                    dens[pl.ds(to, 1), :] = corner[at : at + 1, :]
                    at += 1

    mx, my = nx + 4, ny + 4

    def conduct_of(x):
        d = dens[x * pitch : (x + 1) * pitch, :]
        return jnp.where(d > 0.0, (KMIN + (1.0 - KMIN) * (d * d * d)) * (1.0 / 12.0), 0.0)

    before = conduct_of(0)
    for x in range(mx):
        after = conduct_of(x + 1)
        pair = before + after
        pair = pair[: pitch - 1] + pair[1:]
        here = after[1:]
        total = 4.0 * (pair + pltpu.roll(pair, 1, 1))
        inverse = jnp.where(here > 0.0, 1.0 / total, 0.0)
        for y in range(my):
            invx[x, y] = jnp.broadcast_to(inverse[y : y + 1, :], (loads, LANES))
            if x < mx - 1 and y < my - 1:
                cond[x, y] = jnp.broadcast_to(here[y : y + 1, :], (loads, LANES))
        if 2 <= x < 2 + nx:
            inv_ref[(x - 2) * ny : (x - 1) * ny, :] = inverse[2 : 2 + ny, :]
        before = after

    def stage(x, y, tile):
        bx[x, y] = tile
        scaled = tile * invx[x, y]
        zx[x, y] = scaled
        zs[x, y] = pltpu.roll(scaled, LANES - 1, 1)

    for x in range(nx):
        for y in range(ny):
            at = (x * ny + y) * loads
            stage(x + 2, y + 2, bt_ref[at : at + loads, :])
    for side in range(2):
        for dx in range(2):
            for y in range(ny):
                at = ((side * 2 + dx) * ny + y) * loads
                stage(xs[side] + dx, y + 2, xt_ref[at : at + loads, :])
    for side, (face, face_at, corner, corner_at) in enumerate(faces):
        unpack_tiles(
            face, face_at, loads, 2 * nx,
            lambda i, tile: stage(i // 2 + 2, ys[side] + i % 2, tile),
        )
        unpack_tiles(
            corner, corner_at, loads, 8,
            lambda i, tile: stage(xs[i // 4] + i // 2 % 2, ys[side] + i % 2, tile),
        )

    def element_planes(a, count, y0, columns, field, field_up, emit):
        left = [(field[a + u, y0], field_up[a + u, y0]) for u in range(count + 1)]
        old = [None] * count
        for step in range(columns):
            y = y0 + step
            right = [(field[a + u, y + 1], field_up[a + u, y + 1]) for u in range(count + 1)]
            above = (carry[0, y], carry[1, y]) if step and emit else None
            for u in range(count):
                (p0, p0s), (p1, p1s) = left[u], left[u + 1]
                (r0, r0s), (r1, r1s) = right[u], right[u + 1]
                c = cond[a + u, y]
                even = (p0 + r1) + (r0s + p1s)
                odd = (r0 + p1) + (p0s + r1s)
                lower = None
                if emit:
                    lower = (c * (odd + p1s), c * (even + p1))
                upper = (c * (even + p0s), c * (odd + p0))
                if step and emit:
                    low = (c * (even + r1s) + old[u][0][0]) + above[0]
                    high = (c * (odd + r1) + old[u][0][1]) + above[1]
                    emit(u, a + u, y, p0, low + pltpu.roll(high, 1, 1))
                if step:
                    above = (
                        c * (odd + r0s) + old[u][1][0],
                        c * (even + r0) + old[u][1][1],
                    )
                old[u] = (lower, upper)
            if step:
                carry[0, y], carry[1, y] = above
            left = right

    def first_emit(u, x, y, node, total):
        image = 1.25 * bx[x, y] - total
        weighted = image * invx[x, y]
        qx[x, y] = image
        wx[x, y] = weighted
        ws[x, y] = pltpu.roll(weighted, LANES - 1, 1)

    width = 2 if nx % 2 == 0 else 1
    element_planes(0, 1, 0, my - 1, zx, zs, None)

    @pl.loop(0, (nx + 2) // width)
    def _(i):
        element_planes(1 + i * width, width, 0, my - 1, zx, zs, first_emit)

    element_planes(1, 1, 1, ny + 1, wx, ws, None)

    def second(i, sums):
        sums = list(sums)

        def emit(u, x, y, weighted, total):
            image, source, scaled = qx[x, y], bx[x, y], zx[x, y]
            again = 1.25 * image - total
            row = pl.multiple_of(((x - 2) * ny + (y - 2)) * loads, SUB)
            q_ref[pl.ds(row, loads), :] = image
            v_ref[pl.ds(row, loads), :] = again
            change = scaled - weighted
            sums[0] = sums[0] + source * scaled
            sums[1] = sums[1] + source * change
            sums[2] = sums[2] + (source - image) * change
            sums[3] = sums[3] + (image - again) * change

        element_planes(2 + i * width, width, 1, ny + 1, wx, ws, emit)
        return tuple(sums)

    zero = jnp.zeros((loads, LANES), jnp.float32)
    sums = lax.fori_loop(0, nx // width, second, (zero,) * 4)
    lane = lane_ids(loads)
    load = lax.broadcasted_iota(jnp.int32, (loads, LANES), 0)
    packed = zero
    for place, part in enumerate(sums):
        total = jnp.sum(part, axis=1, keepdims=True)
        packed = packed + jnp.where(lane == place * loads + load, total, 0.0)
    row = jnp.sum(packed, axis=0, keepdims=True)
    sums_ref[...] = jnp.broadcast_to(row[None], sums_ref.shape)


def unpack_kernel(s, q_ref, v_ref, inv_ref, qo_ref, vo_ref, io_ref):
    loads, nx, ny = s.loads, s.nx, s.ny
    for x0 in range(0, nx, SUB):
        for block in range(packed_count(ny)):
            lanes = slice(block * LANES, (block + 1) * LANES)
            io_ref[x0 : x0 + SUB, lanes] = pack_block(
                lambda y: inv_ref[pl.ds(x0 * ny + y, SUB, stride=ny), :], ny, block, SUB
            )
            for ref, out in ((q_ref, qo_ref), (v_ref, vo_ref)):
                for load in range(loads):
                    out[load, x0 : x0 + SUB, lanes] = pack_block(
                        lambda y: ref[
                            pl.ds((x0 * ny + y) * loads + load, SUB, stride=ny * loads), :
                        ],
                        ny,
                        block,
                        SUB,
                    )


def finish_kernel(s, parts_ref, b_ref, q_ref, v_ref, inv_ref, x_hbm, r_hbm, x_ref, r_ref, sems):
    loads = s.loads
    totals = jnp.sum(parts_ref[...], axis=0)

    def part(place):
        return pltpu.roll(totals, (LANES - place * loads) % LANES, 1) if place else totals

    rz, near, square, last = (part(place) for place in range(4))
    direct = rz - near
    alpha = rz / direct
    short = -near / direct
    rz_next = short * short * rz + 2.0 * alpha * short * near + alpha * alpha * square
    beta = rz_next / rz
    grown = short + beta
    curved = (
        grown * grown * direct
        + 2.0 * alpha * grown * (near - square)
        + alpha * alpha * last
    )
    alpha_next = rz_next / curved
    first_row = alpha + alpha_next * (1.0 + beta)
    second_row = alpha_next * alpha
    inverse = inv_ref[...]
    copies = []
    for load in range(loads):
        first = first_row[:, load : load + 1]
        second = second_row[:, load : load + 1]
        source, image = b_ref[load], q_ref[load]
        x_ref[load] = (first * source - second * image) * inverse
        copies.append(pltpu.make_async_copy(x_ref.at[load], x_hbm.at[load], sems.at[0, load]))
        copies[-1].start()
        r_ref[load] = source - first * image + second * v_ref[load]
        copies.append(pltpu.make_async_copy(r_ref.at[load], r_hbm.at[load], sems.at[1, load]))
        copies[-1].start()
    for copy in copies:
        copy.wait()


def swap(array, axis, start):
    pairs = []
    for i in range(start, lax.axis_size(axis) - 1, 2):
        pairs += [(i, i + 1), (i + 1, i)]
    return lax.ppermute(array, axis, pairs)


def per_device(heat_source, density):
    loads, nx, flat = heat_source.shape
    ny = flat // NZ
    s = Sizes(loads, nx, ny)
    nodes = nx * ny * loads

    def shape(*dims):
        return jax.ShapeDtypeStruct(dims, jnp.float32)

    def scratch(*dims):
        return pltpu.VMEM(dims, jnp.float32)

    def call(kernel, out_shape, **more):
        params = pltpu.CompilerParams(vmem_limit_bytes=48 * 1024 * 1024)
        return pl.pallas_call(
            functools.partial(kernel, s), out_shape=out_shape, compiler_params=params, **more
        )

    hbm = pl.BlockSpec(memory_space=pl.ANY)
    bt, dt, x1, x2, yb = call(
        pack_kernel,
        (
            shape(nodes, LANES),
            shape(nx * ny, LANES),
            shape(s.x_rows, LANES),
            shape(s.x_rows, LANES),
            shape(s.y_rows, LANES),
        ),
        in_specs=[hbm, hbm],
        scratch_shapes=[
            scratch(loads, nx, flat),
            scratch(nx, flat),
            pltpu.SemaphoreType.DMA((loads + 1,)),
        ],
    )(heat_source, density)
    x1, x2 = swap(x1, "gx", 0), swap(x2, "gx", 1)
    yb = swap(yb, "gy", 1)
    xt, ya, yc = call(
        corner_kernel,
        (
            shape(4 * ny * loads, LANES),
            shape(s.y_rows + s.c_rows, LANES),
            shape(s.c_rows, LANES),
        ),
    )(bt, dt, x1, x2)
    ya, yc = swap(ya, "gy", 0), swap(yc, "gy", 1)
    mx, my = nx + 4, ny + 4
    field = scratch(mx, my, loads, LANES)
    q_t, v_t, inv_t, sums = call(
        solve_kernel,
        (
            shape(nodes, LANES),
            shape(nodes, LANES),
            shape(nx * ny, LANES),
            shape(lax.axis_size("gy"), 1, LANES),
        ),
        scratch_shapes=[scratch((nx + 6) * s.pitch, LANES)]
        + [field] * 8
        + [scratch(2, my, loads, LANES)],
    )(bt, dt, xt, x1, x2, yb, ya, yc)
    parts = jnp.sum(lax.all_to_all(sums, "gy", 0, 0, tiled=True), axis=0, keepdims=True)
    parts = jnp.broadcast_to(parts, (lax.axis_size("gx"), 1, LANES))
    parts = lax.all_to_all(parts, "gx", 0, 0, tiled=True)
    whole = shape(loads, nx, flat)
    image, again, inverse = call(unpack_kernel, (whole, whole, shape(nx, flat)))(q_t, v_t, inv_t)
    return call(
        finish_kernel,
        (whole, whole),
        out_specs=(hbm, hbm),
        scratch_shapes=[
            scratch(loads, nx, flat),
            scratch(loads, nx, flat),
            pltpu.SemaphoreType.DMA((2, loads)),
        ],
    )(parts, heat_source, image, again, inverse)


def solution(mesh):
    placed = (P(None, "gx", "gy"), P("gx", "gy"))
    return jax.shard_map(
        per_device,
        mesh=mesh,
        in_specs=placed,
        out_specs=(P(None, "gx", "gy"), P(None, "gx", "gy")),
        check_vma=False,
    )
```

```python
import functools

import jax
import jax.numpy as jnp
from jax import lax
from jax.experimental import pallas as pl
from jax.experimental.pallas import tpu as pltpu
from jax.sharding import PartitionSpec as P

NZ = 96
KMIN = 0.001
LANES = 128
SUB = 8


def packed_count(tiles):
    return -(-tiles * NZ // LANES)


def lane_ids(rows):
    return lax.broadcasted_iota(jnp.int32, (rows, LANES), 1)


def unpack_tile(read, index, rows):
    start = index * NZ
    block, offset = start // LANES, start % LANES
    lane = lane_ids(rows)
    first = read(block)
    if offset:
        first = pltpu.roll(first, LANES - offset, 1)
    if offset + NZ > LANES:
        second = pltpu.roll(read(block + 1), LANES - offset, 1)
        first = jnp.where(lane < LANES - offset, first, second)
    return jnp.where(lane < NZ, first, 0.0)


def pack_block(read_tile, tiles, block, rows):
    lane = lane_ids(rows)
    start = block * LANES
    out, at = None, start
    while at < start + LANES and at // NZ < tiles:
        index, z = at // NZ, at % NZ
        here = at - start
        piece = read_tile(index)
        shift = (here - z) % LANES
        if shift:
            piece = pltpu.roll(piece, shift, 1)
        out = piece if out is None else jnp.where(lane < here, out, piece)
        at += NZ - z
    return out


def pack_tiles(out_ref, at, rows, tiles, read_tile):
    for block in range(packed_count(tiles)):
        out_ref[at + block * rows : at + (block + 1) * rows, :] = pack_block(
            read_tile, tiles, block, rows
        )


def unpack_tiles(ref, at, rows, tiles, write):
    for index in range(tiles):
        write(
            index,
            unpack_tile(lambda t: ref[at + t * rows : at + (t + 1) * rows, :], index, rows),
        )


class Sizes:
    def __init__(self, loads, nx, ny):
        self.loads, self.nx, self.ny = loads, nx, ny
        self.mx, self.my = nx + 4, ny + 4
        self.pitch = -(-(ny + 6) // SUB) * SUB
        self.y_dens = packed_count(2 * nx) * loads
        self.y_rows = self.y_dens + 3 * nx
        self.x_dens = packed_count(2 * self.my) * loads
        self.x_rows = self.x_dens + 3 * self.pitch


class Tiles:
    def __init__(self, ref, columns, loads):
        self.ref, self.columns, self.loads = ref, columns, loads

    def rows(self, at):
        start = (at[0] * self.columns + at[1]) * self.loads
        if not isinstance(start, int):
            start = pl.multiple_of(start, SUB)
        return pl.ds(start, self.loads)

    def __getitem__(self, at):
        return self.ref[self.rows(at), :]

    def __setitem__(self, at, tile):
        self.ref[self.rows(at), :] = tile


class Joined:
    def __init__(self, first, second, own):
        self.first, self.second, self.own = first, second, own

    def __getitem__(self, at):
        return (self.first if at[0] in self.own else self.second)[at]

    def __setitem__(self, at, tile):
        self.first[at] = tile


def is_even(axis):
    return lax.rem(lax.axis_index(axis), 2) == 0


def pick(even, if_even, if_odd):
    return jnp.where(even, if_even, if_odd)


def pack_kernel(s, b_hbm, d_hbm, bt_ref, dt_ref, y1_ref, y2_ref, b_ref, d_ref, sems):
    loads, nx, ny = s.loads, s.nx, s.ny
    d_copy = pltpu.make_async_copy(d_hbm, d_ref, sems.at[loads])
    d_copy.start()
    copies = []
    for load in range(loads):
        copies.append(pltpu.make_async_copy(b_hbm.at[load], b_ref.at[load], sems.at[load]))
        copies[-1].start()
    d_copy.wait()
    for x0 in range(0, nx, SUB):
        for y in range(ny):
            tile = unpack_tile(
                lambda t: d_ref[x0 : x0 + SUB, t * LANES : (t + 1) * LANES], y, SUB
            )
            dt_ref[pl.ds(x0 * ny + y, SUB, stride=ny), :] = tile
    for load in range(loads):
        copies[load].wait()
        for x0 in range(0, nx, SUB):
            for y in range(ny):
                tile = unpack_tile(
                    lambda t: b_ref[load, x0 : x0 + SUB, t * LANES : (t + 1) * LANES], y, SUB
                )
                bt_ref[pl.ds((x0 * ny + y) * loads + load, SUB, stride=ny * loads), :] = tile
    even_y = is_even("gy")
    pack_face(s, even_y, bt_ref, dt_ref, y1_ref)
    pack_face(s, jnp.logical_not(even_y), bt_ref, dt_ref, y2_ref)


def pack_face(s, upper, bt_ref, dt_ref, out_ref):
    loads, nx, ny = s.loads, s.nx, s.ny
    tiles = Tiles(bt_ref, ny, loads)
    y0 = pick(upper, ny - 2, 0)
    pack_tiles(out_ref, 0, loads, 2 * nx, lambda i: tiles[i // 2, y0 + i % 2])
    y0 = pick(upper, ny - 3, 0)
    for dy in range(3):
        for x0 in range(0, nx, SUB):
            at = s.y_dens + dy * nx + x0
            out_ref[at : at + SUB, :] = dt_ref[pl.ds(x0 * ny + y0 + dy, SUB, stride=ny), :]


def pack_x_kernel(s, bt_ref, dt_ref, y1_ref, y2_ref, dens_ref, x1_ref, x2_ref, edge_ref):
    loads, nx, ny, my, pitch = s.loads, s.nx, s.ny, s.my, s.pitch
    even_x, even_y = is_even("gx"), is_even("gy")
    ys = (pick(even_y, ny + 2, 0), pick(even_y, 0, ny + 2))
    yd = (pick(even_y, ny + 3, 0), pick(even_y, 0, ny + 3))
    for x in range(nx):
        at = x * pitch
        dens_ref[at + 3 : at + 3 + ny, :] = dt_ref[x * ny : (x + 1) * ny, :]
        dens_ref[at + ny + 6 : at + pitch, :] = jnp.zeros((pitch - ny - 6, LANES), jnp.float32)
    for side, ref in enumerate((y1_ref, y2_ref)):
        for dy in range(3):
            for x0 in range(0, nx, SUB):
                at = s.y_dens + dy * nx + x0
                to = x0 * pitch + yd[side] + dy
                dens_ref[pl.ds(to, SUB, stride=pitch), :] = ref[at : at + SUB, :]
    inner, edge = Tiles(bt_ref, ny, loads), Tiles(edge_ref, my, loads)
    for place, x in enumerate((0, 1, nx - 2, nx - 1)):
        for y in range(ny):
            edge[place, y + 2] = inner[x, y]
        for side, ref in enumerate((y1_ref, y2_ref)):
            for dy in range(2):
                edge[place, ys[side] + dy] = unpack_tile(
                    lambda t: ref[t * loads : (t + 1) * loads, :], 2 * x + dy, loads
                )
    for ref, upper in ((x1_ref, even_x), (x2_ref, jnp.logical_not(even_x))):
        place = pick(upper, 2, 0)
        pack_tiles(ref, 0, loads, 2 * my, lambda i: edge[place + i // my, i % my])
        rows = pl.ds(pl.multiple_of(pick(upper, nx - 3, 0) * pitch, SUB), 3 * pitch)
        ref[s.x_dens :, :] = dens_ref[rows, :]


def conduct_of(dens):
    return jnp.where(
        dens > 0.0, (KMIN + (1.0 - KMIN) * (dens * dens * dens)) * (1.0 / 12.0), 0.0
    )


def inverse_of(s, before, after):
    pair = before + after
    pair = pair[: s.pitch - 1] + pair[1:]
    total = 4.0 * (pair + pltpu.roll(pair, 1, 1))
    return jnp.where(after[1:] > 0.0, 1.0 / total, 0.0)


def spread_rows(s, field, x, values, columns):
    for y in range(columns):
        field[x, y] = jnp.broadcast_to(values[y : y + 1, :], (s.loads, LANES))


def up(tile):
    return pltpu.roll(tile, LANES - 1, 1)


def element_planes(cond, carry, a, count, y0, columns, field, field_up, emit, keep=True):
    left = [(field[a + u, y0], field_up[a + u, y0]) for u in range(count + 1)]
    old = [None] * count
    for step in range(columns):
        y = y0 + step
        right = [(field[a + u, y + 1], field_up[a + u, y + 1]) for u in range(count + 1)]
        above = (carry[0, y], carry[1, y]) if step and emit else None
        for u in range(count):
            (p0, p0s), (p1, p1s) = left[u], left[u + 1]
            (r0, r0s), (r1, r1s) = right[u], right[u + 1]
            c = cond[a + u, y]
            even = (p0 + r1) + (r0s + p1s)
            odd = (r0 + p1) + (p0s + r1s)
            pass_on = keep or u + 1 < count
            lower = upper = None
            if emit:
                lower = (c * (odd + p1s), c * (even + p1))
            if pass_on:
                upper = (c * (even + p0s), c * (odd + p0))
            if step and emit:
                low = (c * (even + r1s) + old[u][0][0]) + above[0]
                high = (c * (odd + r1) + old[u][0][1]) + above[1]
                emit(u, a + u, y, p0, low + pltpu.roll(high, 1, 1))
            if step and pass_on:
                above = (
                    c * (odd + r0s) + old[u][1][0],
                    c * (even + r0) + old[u][1][1],
                )
            old[u] = (lower, upper)
        if step and keep:
            carry[0, y], carry[1, y] = above
        left = right


def first_emit(bx, invx, qx, wx, ws):
    def emit(u, x, y, node, total):
        image = 1.25 * bx[x, y] - total
        weighted = image * invx[x, y]
        qx[x, y] = image
        wx[x, y] = weighted
        ws[x, y] = up(weighted)

    return emit


def second_emit(bx, zx, qx, vx, sums):
    def emit(u, x, y, weighted, total):
        image, source, scaled = qx[x, y], bx[x, y], zx[x, y]
        again = 1.25 * image - total
        vx[x, y] = again
        change = scaled - weighted
        sums[0] = sums[0] + source * scaled
        sums[1] = sums[1] + source * change
        sums[2] = sums[2] + (source - image) * change
        sums[3] = sums[3] + (image - again) * change

    return emit


def over_planes(start, stop, body, state):
    pairs = (stop - start) // 2
    state = lax.fori_loop(0, pairs, lambda i, st: body(start + 2 * i, 2, st), state)
    if (stop - start) % 2:
        state = body(stop - 1, 1, state)
    return state


def inner_kernel(
    s, bt_ref, dens_ref, y1_ref, y2_ref,
    cond, invx, bx, zx, zs, qx, wx, ws, vx, carry1, carry2, sums_ref,
):
    loads, nx, ny, my, pitch = s.loads, s.nx, s.ny, s.my, s.pitch
    cond, invx, bx, zx, zs, qx, wx, ws, vx, carry1, carry2 = (
        Tiles(ref, my, loads) for ref in (cond, invx, bx, zx, zs, qx, wx, ws, vx, carry1, carry2)
    )
    even_y = is_even("gy")
    ys = (pick(even_y, ny + 2, 0), pick(even_y, 0, ny + 2))
    before = None
    for x in range(nx):
        after = conduct_of(dens_ref[x * pitch : (x + 1) * pitch, :])
        spread_rows(s, cond, x + 2, after[1:], my - 1)
        if x:
            spread_rows(s, invx, x + 2, inverse_of(s, before, after), my)
        before = after

    def stage(x, y, tile):
        bx[x + 2, y] = tile
        if x:
            scaled = tile * invx[x + 2, y]
            zx[x + 2, y] = scaled
            zs[x + 2, y] = up(scaled)

    inner = Tiles(bt_ref, ny, loads)
    for x in range(nx):
        for y in range(ny):
            stage(x, y + 2, inner[x, y])
    for side, ref in enumerate((y1_ref, y2_ref)):
        unpack_tiles(
            ref, 0, loads, 2 * nx, lambda i, tile: stage(i // 2, ys[side] + i % 2, tile)
        )

    element_planes(cond, carry1, 3, 1, 0, my - 1, zx, zs, None)

    def first(a, count, state):
        emit = first_emit(bx, invx, qx, wx, ws)
        element_planes(cond, carry1, a, count, 0, my - 1, zx, zs, emit)
        return state

    over_planes(4, nx + 1, first, 0)
    element_planes(cond, carry2, 4, 1, 1, my - 3, wx, ws, None)

    def second(a, count, sums):
        sums = list(sums)
        emit = second_emit(bx, zx, qx, vx, sums)
        element_planes(cond, carry2, a, count, 1, my - 3, wx, ws, emit)
        return tuple(sums)

    zero = jnp.zeros((loads, LANES), jnp.float32)
    sums = over_planes(5, nx, second, (zero,) * 4)
    for place, part in enumerate(sums):
        sums_ref[place * loads : (place + 1) * loads, :] = part


def outer_kernel(
    s, dens_ref, x1_ref, x2_ref,
    cond1, invx1, bx1, zx1, zs1, qx1, wx1, ws1, carry1, carry2, sums1,
    q_out, v_out, inv_out, sums_ref,
    low_ref, high_ref, cond2, invx2, bx2, zx2, zs2, qx2, wx2, ws2, vx2, carry3,
):
    loads, nx, ny, mx, my, pitch = s.loads, s.nx, s.ny, s.mx, s.my, s.pitch
    even_x = is_even("gx")

    @pl.when(even_x)
    def _():
        low_ref[...] = x2_ref[...]
        high_ref[...] = x1_ref[...]

    @pl.when(jnp.logical_not(even_x))
    def _():
        low_ref[...] = x1_ref[...]
        high_ref[...] = x2_ref[...]

    def tiles(ref):
        return Tiles(ref, my, loads)

    def joined(first, second, own):
        return Joined(tiles(first), tiles(second), own)

    outside = (0, 1, nx + 2, nx + 3)
    scaled_own = outside + (2,)
    image_own = (1, 2, 3, nx + 1, nx + 2)
    cond, invx = joined(cond2, cond1, outside), joined(invx2, invx1, scaled_own)
    bx = joined(bx2, bx1, outside)
    zx, zs = joined(zx2, zx1, scaled_own), joined(zs2, zs1, scaled_own)
    qx = joined(qx2, qx1, image_own)
    wx, ws = joined(wx2, wx1, image_own), joined(ws2, ws1, image_own)
    vx, carry3 = tiles(vx2), tiles(carry3)
    carry1, carry2 = tiles(carry1), tiles(carry2)

    def conduct(ref, base, x):
        return conduct_of(ref[base + x * pitch : base + (x + 1) * pitch, :])

    low = [conduct(low_ref, s.x_dens, t) for t in range(3)] + [conduct(dens_ref, 0, 0)]
    high = [conduct(dens_ref, 0, nx - 1)] + [conduct(high_ref, s.x_dens, t) for t in range(2)]
    for x in range(3):
        inverse = inverse_of(s, low[x], low[x + 1])
        spread_rows(s, invx, x, inverse, my)
        if x < 2:
            spread_rows(s, cond, x, low[x + 1][1:], my - 1)
    inv_out[...] = inverse[2 : 2 + ny]
    for x in range(2):
        spread_rows(s, invx, nx + 2 + x, inverse_of(s, high[x], high[x + 1]), my)
    spread_rows(s, cond, nx + 2, high[1][1:], my - 1)

    def stage(x, y, tile):
        scaled = tile * invx[x, y]
        zx[x, y] = scaled
        zs[x, y] = up(scaled)

    for ref, x0 in ((low_ref, 0), (high_ref, nx + 2)):

        def write(i, tile):
            bx[x0 + i // my, i % my] = tile
            stage(x0 + i // my, i % my, tile)

        unpack_tiles(ref, 0, loads, 2 * my, write)
    for y in range(my):
        stage(2, y, bx[2, y])

    emit = first_emit(bx, invx, qx, wx, ws)
    element_planes(cond, carry3, 0, 1, 0, my - 1, zx, zs, None)
    element_planes(cond, carry3, 1, 2, 0, my - 1, zx, zs, emit)
    element_planes(cond, carry3, 3, 1, 0, my - 1, zx, zs, emit, keep=False)
    element_planes(cond, carry1, nx + 1, 2, 0, my - 1, zx, zs, emit, keep=False)
    sums = [sums1[place * loads : (place + 1) * loads, :] for place in range(4)]
    emit = second_emit(bx, zx, qx, vx, sums)
    element_planes(cond, carry3, 1, 1, 1, my - 3, wx, ws, None)
    element_planes(cond, carry3, 2, 2, 1, my - 3, wx, ws, emit)
    element_planes(cond, carry3, 4, 1, 1, my - 3, wx, ws, emit, keep=False)
    element_planes(cond, carry2, nx, 2, 1, my - 3, wx, ws, emit, keep=False)
    for field, out, planes in ((qx, q_out, image_planes(nx)), (vx, v_out, again_planes(nx))):
        out = Tiles(out, ny, loads)
        for place, x in enumerate(planes):
            for y in range(ny):
                out[place, y] = field[x, y + 2]

    lane = lane_ids(loads)
    load = lax.broadcasted_iota(jnp.int32, (loads, LANES), 0)
    packed = jnp.zeros((loads, LANES), jnp.float32)
    for place, part in enumerate(sums):
        total = jnp.sum(part, axis=1, keepdims=True)
        packed = packed + jnp.where(lane == place * loads + load, total, 0.0)
    row = jnp.sum(packed, axis=0, keepdims=True)
    sums_ref[...] = jnp.broadcast_to(row[None], sums_ref.shape)


def image_planes(nx):
    return (2, 3, nx + 1)


def again_planes(nx):
    return (2, 3, 4, nx, nx + 1)


def unpack_kernel(
    s, q1_ref, q2_ref, v1_ref, v2_ref, inv1_ref, inv2_ref, qo_ref, vo_ref, io_ref, t_ref
):
    loads, nx, ny, my = s.loads, s.nx, s.ny, s.my
    whole = Tiles(t_ref, ny, loads)
    for first, second, planes, out in (
        (q1_ref, q2_ref, image_planes(nx), qo_ref),
        (v1_ref, v2_ref, again_planes(nx), vo_ref),
    ):
        first, second = Tiles(first, my, loads), Tiles(second, ny, loads)
        for x in range(nx):
            for y in range(ny):
                if x + 2 in planes:
                    whole[x, y] = second[planes.index(x + 2), y]
                else:
                    whole[x, y] = first[x + 2, y + 2]
        for x0 in range(0, nx, SUB):
            for block in range(packed_count(ny)):
                for load in range(loads):
                    out[load, x0 : x0 + SUB, block * LANES : (block + 1) * LANES] = pack_block(
                        lambda y: t_ref[
                            pl.ds((x0 * ny + y) * loads + load, SUB, stride=ny * loads), :
                        ],
                        ny, block, SUB,
                    )
    for x0 in range(0, nx, SUB):
        for block in range(packed_count(ny)):
            io_ref[x0 : x0 + SUB, block * LANES : (block + 1) * LANES] = pack_block(
                lambda y: inv1_ref[
                    pl.ds(((x0 + 2) * my + y + 2) * loads, SUB, stride=my * loads), :
                ],
                ny, block, SUB,
            )
    for block in range(packed_count(ny)):
        io_ref[0:1, block * LANES : (block + 1) * LANES] = pack_block(
            lambda y: inv2_ref[y : y + 1, :], ny, block, 1
        )


def finish_kernel(s, parts_ref, b_ref, q_ref, v_ref, inv_ref, x_hbm, r_hbm, x_ref, r_ref, sems):
    loads = s.loads
    totals = jnp.sum(parts_ref[...], axis=0)

    def part(place):
        return pltpu.roll(totals, (LANES - place * loads) % LANES, 1) if place else totals

    rz, near, square, last = (part(place) for place in range(4))
    direct = rz - near
    alpha = rz / direct
    short = -near / direct
    rz_next = short * short * rz + 2.0 * alpha * short * near + alpha * alpha * square
    beta = rz_next / rz
    grown = short + beta
    curved = (
        grown * grown * direct
        + 2.0 * alpha * grown * (near - square)
        + alpha * alpha * last
    )
    alpha_next = rz_next / curved
    first_row = alpha + alpha_next * (1.0 + beta)
    second_row = alpha_next * alpha
    inverse = inv_ref[...]
    copies = []
    for load in range(loads):
        first = first_row[:, load : load + 1]
        second = second_row[:, load : load + 1]
        source, image = b_ref[load], q_ref[load]
        x_ref[load] = (first * source - second * image) * inverse
        copies.append(pltpu.make_async_copy(x_ref.at[load], x_hbm.at[load], sems.at[0, load]))
        copies[-1].start()
        r_ref[load] = source - first * image + second * v_ref[load]
        copies.append(pltpu.make_async_copy(r_ref.at[load], r_hbm.at[load], sems.at[1, load]))
        copies[-1].start()
    for copy in copies:
        copy.wait()


def swap(array, axis, start):
    pairs = []
    for i in range(start, lax.axis_size(axis) - 1, 2):
        pairs += [(i, i + 1), (i + 1, i)]
    return lax.ppermute(array, axis, pairs)


def per_device(heat_source, density):
    loads, nx, flat = heat_source.shape
    ny = flat // NZ
    s = Sizes(loads, nx, ny)
    nodes = nx * ny * loads
    devices = lax.axis_size("gx") * lax.axis_size("gy")

    def shape(*dims):
        return jax.ShapeDtypeStruct(dims, jnp.float32)

    def scratch(*dims):
        return pltpu.VMEM(dims, jnp.float32)

    def call(kernel, out_shape, **more):
        params = pltpu.CompilerParams(vmem_limit_bytes=48 * 1024 * 1024)
        return pl.pallas_call(
            functools.partial(kernel, s), out_shape=out_shape, compiler_params=params, **more
        )

    hbm = pl.BlockSpec(memory_space=pltpu.HBM)
    bt, dt, y1, y2 = call(
        pack_kernel,
        (
            shape(nodes, LANES),
            shape(nx * ny, LANES),
            shape(s.y_rows, LANES),
            shape(s.y_rows, LANES),
        ),
        in_specs=[hbm, hbm],
        scratch_shapes=[
            scratch(loads, nx, flat),
            scratch(nx, flat),
            pltpu.SemaphoreType.DMA((loads + 1,)),
        ],
    )(heat_source, density)
    y2, y1 = swap(y2, "gy", 1), swap(y1, "gy", 0)
    dens, x1, x2 = call(
        pack_x_kernel,
        (shape(nx * s.pitch, LANES), shape(s.x_rows, LANES), shape(s.x_rows, LANES)),
        scratch_shapes=[scratch(4 * s.my * loads, LANES)],
    )(bt, dt, y1, y2)
    x1, x2 = swap(x1, "gx", 0), swap(x2, "gx", 1)
    field = s.mx * s.my * loads
    edge = 2 * s.my * loads
    *fields, v_1, carry1, carry2, sums = call(
        inner_kernel,
        (shape(field, LANES),) * 9 + (shape(edge, LANES),) * 2 + (shape(4 * loads, LANES),),
    )(bt, dens, y1, y2)
    q_2, v_2, inv_2, sums = call(
        outer_kernel,
        (
            shape(len(image_planes(nx)) * ny * loads, LANES),
            shape(len(again_planes(nx)) * ny * loads, LANES),
            shape(ny, LANES),
            shape(devices, 1, LANES),
        ),
        scratch_shapes=[scratch(s.x_rows, LANES)] * 2
        + [scratch(field, LANES)] * 9
        + [scratch(edge, LANES)],
    )(dens, x1, x2, *fields, carry1, carry2, sums)
    parts = lax.all_to_all(sums, ("gx", "gy"), 0, 0, tiled=True)
    whole = shape(loads, nx, flat)
    image, again, inverse = call(
        unpack_kernel,
        (whole, whole, shape(nx, flat)),
        scratch_shapes=[scratch(nodes, LANES)],
    )(fields[5], q_2, v_1, v_2, fields[1], inv_2)
    return call(
        finish_kernel,
        (whole, whole),
        out_specs=(hbm, hbm),
        scratch_shapes=[
            scratch(loads, nx, flat),
            scratch(loads, nx, flat),
            pltpu.SemaphoreType.DMA((2, loads)),
        ],
    )(parts, heat_source, image, again, inverse)


def solution(mesh):
    placed = (P(None, "gx", "gy"), P("gx", "gy"))
    return jax.shard_map(
        per_device,
        mesh=mesh,
        in_specs=placed,
        out_specs=(P(None, "gx", "gy"), P(None, "gx", "gy")),
        check_vma=False,
    )
```

```python
import functools

import jax
import jax.numpy as jnp
from jax import lax
from jax.experimental import pallas as pl
from jax.experimental.pallas import tpu as pltpu
from jax.sharding import PartitionSpec as P

NZ = 96
KMIN = 0.001
LANES = 128
SUB = 8


def packed_count(tiles):
    return -(-tiles * NZ // LANES)


def lane_ids(rows):
    return lax.broadcasted_iota(jnp.int32, (rows, LANES), 1)


def unpack_tile(read, index, rows):
    start = index * NZ
    block, offset = start // LANES, start % LANES
    lane = lane_ids(rows)
    first = read(block)
    if offset:
        first = pltpu.roll(first, LANES - offset, 1)
    if offset + NZ > LANES:
        second = pltpu.roll(read(block + 1), LANES - offset, 1)
        first = jnp.where(lane < LANES - offset, first, second)
    return jnp.where(lane < NZ, first, 0.0)


def pack_block(read_tile, tiles, block, rows):
    lane = lane_ids(rows)
    start = block * LANES
    out, at = None, start
    while at < start + LANES and at // NZ < tiles:
        index, z = at // NZ, at % NZ
        here = at - start
        piece = read_tile(index)
        shift = (here - z) % LANES
        if shift:
            piece = pltpu.roll(piece, shift, 1)
        out = piece if out is None else jnp.where(lane < here, out, piece)
        at += NZ - z
    return out


def pack_tiles(out_ref, at, rows, tiles, read_tile):
    for block in range(packed_count(tiles)):
        out_ref[at + block * rows : at + (block + 1) * rows, :] = pack_block(
            read_tile, tiles, block, rows
        )


def unpack_tiles(ref, at, rows, tiles, write):
    for index in range(tiles):
        write(
            index,
            unpack_tile(lambda t: ref[at + t * rows : at + (t + 1) * rows, :], index, rows),
        )


class Sizes:
    def __init__(self, loads, nx, ny):
        self.loads, self.nx, self.ny = loads, nx, ny
        self.mx, self.my = nx + 4, ny + 4
        self.pitch = -(-(ny + 6) // SUB) * SUB
        self.y_dens = packed_count(2 * nx) * loads
        self.y_rows = self.y_dens + 3 * nx
        self.x_dens = packed_count(2 * self.my) * loads
        self.x_rows = self.x_dens + 3 * self.pitch


class Tiles:
    def __init__(self, ref, columns, loads):
        self.ref, self.columns, self.loads = ref, columns, loads

    def rows(self, at):
        start = (at[0] * self.columns + at[1]) * self.loads
        if not isinstance(start, int):
            start = pl.multiple_of(start, SUB)
        return pl.ds(start, self.loads)

    def __getitem__(self, at):
        return self.ref[self.rows(at), :]

    def __setitem__(self, at, tile):
        self.ref[self.rows(at), :] = tile


class Rows:
    def __init__(self, ref, pitch, loads):
        self.ref, self.pitch, self.loads = ref, pitch, loads

    def __getitem__(self, at):
        row = self.ref[pl.ds(at[0] * self.pitch + at[1], 1), :]
        return jnp.broadcast_to(row, (self.loads, LANES))

    def put(self, x, values):
        self.ref[x * self.pitch : x * self.pitch + values.shape[0], :] = values


class Joined:
    def __init__(self, first, second, own):
        self.first, self.second, self.own = first, second, own

    def __getitem__(self, at):
        if at[0] in self.own:
            return self.first[self.own.index(at[0]), at[1]]
        return self.second[at]

    def __setitem__(self, at, tile):
        self.first[self.own.index(at[0]), at[1]] = tile

    def put(self, x, values):
        self.first.put(self.own.index(x), values)


def is_even(axis):
    return lax.rem(lax.axis_index(axis), 2) == 0


def pick(even, if_even, if_odd):
    return jnp.where(even, if_even, if_odd)


def pack_kernel(s, b_ref, d_ref, bt_ref, dt_ref, y1_ref, y2_ref):
    loads, nx, ny = s.loads, s.nx, s.ny
    for x0 in range(0, nx, SUB):
        for y in range(ny):
            tile = unpack_tile(
                lambda t: d_ref[x0 : x0 + SUB, t * LANES : (t + 1) * LANES], y, SUB
            )
            dt_ref[pl.ds(x0 * ny + y, SUB, stride=ny), :] = tile
    for load in range(loads):
        for x0 in range(0, nx, SUB):
            for y in range(ny):
                tile = unpack_tile(
                    lambda t: b_ref[load, x0 : x0 + SUB, t * LANES : (t + 1) * LANES], y, SUB
                )
                bt_ref[pl.ds((x0 * ny + y) * loads + load, SUB, stride=ny * loads), :] = tile
    even_y = is_even("gy")
    pack_face(s, even_y, bt_ref, dt_ref, y1_ref)
    pack_face(s, jnp.logical_not(even_y), bt_ref, dt_ref, y2_ref)


def pack_face(s, upper, bt_ref, dt_ref, out_ref):
    loads, nx, ny = s.loads, s.nx, s.ny
    tiles = Tiles(bt_ref, ny, loads)
    y0 = pick(upper, ny - 2, 0)
    pack_tiles(out_ref, 0, loads, 2 * nx, lambda i: tiles[i // 2, y0 + i % 2])
    y0 = pick(upper, ny - 3, 0)
    for dy in range(3):
        for x0 in range(0, nx, SUB):
            at = s.y_dens + dy * nx + x0
            out_ref[at : at + SUB, :] = dt_ref[pl.ds(x0 * ny + y0 + dy, SUB, stride=ny), :]


def pack_x_kernel(s, bt_ref, dt_ref, y1_ref, y2_ref, dens_ref, x1_ref, x2_ref, edge_ref):
    loads, nx, ny, my, pitch = s.loads, s.nx, s.ny, s.my, s.pitch
    even_x, even_y = is_even("gx"), is_even("gy")
    ys = (pick(even_y, ny + 2, 0), pick(even_y, 0, ny + 2))
    yd = (pick(even_y, ny + 3, 0), pick(even_y, 0, ny + 3))
    for x in range(nx):
        at = x * pitch
        dens_ref[at + 3 : at + 3 + ny, :] = dt_ref[x * ny : (x + 1) * ny, :]
        dens_ref[at + ny + 6 : at + pitch, :] = jnp.zeros((pitch - ny - 6, LANES), jnp.float32)
    for side, ref in enumerate((y1_ref, y2_ref)):
        for dy in range(3):
            for x0 in range(0, nx, SUB):
                at = s.y_dens + dy * nx + x0
                to = x0 * pitch + yd[side] + dy
                dens_ref[pl.ds(to, SUB, stride=pitch), :] = ref[at : at + SUB, :]
    inner, edge = Tiles(bt_ref, ny, loads), Tiles(edge_ref, my, loads)
    for place, x in enumerate((0, 1, nx - 2, nx - 1)):
        for y in range(ny):
            edge[place, y + 2] = inner[x, y]
        for side, ref in enumerate((y1_ref, y2_ref)):
            for dy in range(2):
                edge[place, ys[side] + dy] = unpack_tile(
                    lambda t: ref[t * loads : (t + 1) * loads, :], 2 * x + dy, loads
                )
    for ref, upper in ((x1_ref, even_x), (x2_ref, jnp.logical_not(even_x))):
        place = pick(upper, 2, 0)
        pack_tiles(ref, 0, loads, 2 * my, lambda i: edge[place + i // my, i % my])
        rows = pl.ds(pl.multiple_of(pick(upper, nx - 3, 0) * pitch, SUB), 3 * pitch)
        ref[s.x_dens :, :] = dens_ref[rows, :]


def conduct_of(dens):
    return jnp.where(
        dens > 0.0, (KMIN + (1.0 - KMIN) * (dens * dens * dens)) * (1.0 / 12.0), 0.0
    )


def inverse_of(s, before, after):
    pair = before + after
    pair = pair[: s.pitch - 1] + pair[1:]
    total = 4.0 * (pair + pltpu.roll(pair, 1, 1))
    return jnp.where(after[1:] > 0.0, 1.0 / total, 0.0)


def up(tile):
    return pltpu.roll(tile, LANES - 1, 1)


def element_planes(cond, carry, a, count, y0, columns, field, emitter, keep=True):
    def loads_of(step):
        y = y0 + step
        right = [field[a + u, y + 1] for u in range(count + 1)]
        conduct = [cond[a + u, y] for u in range(count)]
        above = extra = None
        if step and emitter:
            above = (carry[0, y], carry[1, y])
            extra = [emitter.fetch(a + u, y) for u in range(count)]
        return right, conduct, above, extra

    left = [(tile, up(tile)) for tile in [field[a + u, y0] for u in range(count + 1)]]
    ahead = loads_of(0)
    old, waiting = [None] * count, []
    for step in range(columns):
        y = y0 + step
        right, conduct, above, extra = ahead
        if step + 1 < columns:
            ahead = loads_of(step + 1)
        if len(waiting) > 1:
            for into, at, tile in waiting.pop(0):
                into[at] = tile
        stores = []
        right = [(tile, up(tile)) for tile in right]
        for u in range(count):
            (p0, p0s), (p1, p1s) = left[u], left[u + 1]
            (r0, r0s), (r1, r1s) = right[u], right[u + 1]
            c = conduct[u]
            even = (p0 + r1) + (r0s + p1s)
            odd = (r0 + p1) + (p0s + r1s)
            pass_on = keep or u + 1 < count
            lower = upper = None
            if emitter:
                lower = (c * (odd + p1s), c * (even + p1))
            if pass_on:
                upper = (c * (even + p0s), c * (odd + p0))
            if step and emitter:
                low = (c * (even + r1s) + old[u][0][0]) + above[0]
                high = (c * (odd + r1) + old[u][0][1]) + above[1]
                total = low + pltpu.roll(high, 1, 1)
                stores += emitter.finish(a + u, y, p0, total, extra[u])
            if step and pass_on:
                above = (
                    c * (odd + r0s) + old[u][1][0],
                    c * (even + r0) + old[u][1][1],
                )
            old[u] = (lower, upper)
        if step and keep:
            stores += [(carry, (0, y), above[0]), (carry, (1, y), above[1])]
        waiting.append(stores)
        left = right
    for stores in waiting:
        for into, at, tile in stores:
            into[at] = tile


class First:
    def __init__(self, bx, invx, qx, wx):
        self.bx, self.invx, self.qx, self.wx = bx, invx, qx, wx

    def fetch(self, x, y):
        return self.bx[x, y], self.invx[x, y]

    def finish(self, x, y, node, total, extra):
        source, inverse = extra
        image = 1.25 * source - total
        return [(self.qx, (x, y), image), (self.wx, (x, y), image * inverse)]


class Second:
    def __init__(self, bx, zx, qx, vx, sums):
        self.bx, self.zx, self.qx, self.vx, self.sums = bx, zx, qx, vx, sums

    def fetch(self, x, y):
        return self.bx[x, y], self.zx[x, y], self.qx[x, y]

    def finish(self, x, y, weighted, total, extra):
        source, scaled, image = extra
        again = 1.25 * image - total
        change = scaled - weighted
        sums = self.sums
        sums[0] = sums[0] + source * scaled
        sums[1] = sums[1] + source * change
        sums[2] = sums[2] + (source - image) * change
        sums[3] = sums[3] + (image - again) * change
        return [(self.vx, (x, y), again)]


def over_planes(start, stop, body, state):
    pairs = (stop - start) // 2
    state = lax.fori_loop(0, pairs, lambda i, st: body(start + 2 * i, 2, st), state)
    if (stop - start) % 2:
        state = body(stop - 1, 1, state)
    return state


def inner_kernel(
    s, bt_ref, dens_ref, y1_ref, y2_ref,
    cond, invx, bx, zx, qx, wx, vx, carry1, carry2, sums_ref,
):
    loads, nx, ny, my, pitch = s.loads, s.nx, s.ny, s.my, s.pitch
    bx, zx, qx, wx, vx, carry1, carry2 = (
        Tiles(ref, my, loads) for ref in (bx, zx, qx, wx, vx, carry1, carry2)
    )
    cond, invx = Rows(cond, pitch, loads), Rows(invx, pitch, loads)
    even_y = is_even("gy")
    ys = (pick(even_y, ny + 2, 0), pick(even_y, 0, ny + 2))
    before = None
    for x in range(nx):
        after = conduct_of(dens_ref[x * pitch : (x + 1) * pitch, :])
        cond.put(x + 2, after[1:])
        if x:
            invx.put(x + 2, inverse_of(s, before, after))
        before = after

    def stage(x, y, tile):
        bx[x + 2, y] = tile
        if x:
            zx[x + 2, y] = tile * invx[x + 2, y]

    inner = Tiles(bt_ref, ny, loads)
    for x in range(nx):
        for y in range(ny):
            stage(x, y + 2, inner[x, y])
    for side, ref in enumerate((y1_ref, y2_ref)):
        unpack_tiles(
            ref, 0, loads, 2 * nx, lambda i, tile: stage(i // 2, ys[side] + i % 2, tile)
        )

    element_planes(cond, carry1, 3, 1, 0, my - 1, zx, None)

    def first(a, count, state):
        element_planes(cond, carry1, a, count, 0, my - 1, zx, First(bx, invx, qx, wx))
        return state

    over_planes(4, nx + 1, first, 0)
    element_planes(cond, carry2, 4, 1, 1, my - 3, wx, None)

    def second(a, count, sums):
        sums = list(sums)
        element_planes(cond, carry2, a, count, 1, my - 3, wx, Second(bx, zx, qx, vx, sums))
        return tuple(sums)

    zero = jnp.zeros((loads, LANES), jnp.float32)
    sums = over_planes(5, nx, second, (zero,) * 4)
    for place, part in enumerate(sums):
        sums_ref[place * loads : (place + 1) * loads, :] = part


def outer_kernel(
    s, dens_ref, x1_ref, x2_ref,
    cond1, invx1, bx1, zx1, qx1, wx1, carry1, carry2, sums1,
    q_out, v_out, inv_out, sums_ref,
    low_ref, high_ref, cond2, invx2, bx2, zx2, qx2, wx2, vx2, carry3,
):
    loads, nx, ny, mx, my, pitch = s.loads, s.nx, s.ny, s.mx, s.my, s.pitch
    even_x = is_even("gx")

    @pl.when(even_x)
    def _():
        low_ref[...] = x2_ref[...]
        high_ref[...] = x1_ref[...]

    @pl.when(jnp.logical_not(even_x))
    def _():
        low_ref[...] = x1_ref[...]
        high_ref[...] = x2_ref[...]

    def joined(first, second, own):
        return Joined(Tiles(first, my, loads), Tiles(second, my, loads), own)

    def joined_rows(first, second, own):
        return Joined(Rows(first, pitch, loads), Rows(second, pitch, loads), own)

    outside = (0, 1, nx + 2, nx + 3)
    scaled_own = outside + (2,)
    image_own = (1, 2, 3, nx + 1, nx + 2)
    cond, invx = joined_rows(cond2, cond1, outside), joined_rows(invx2, invx1, scaled_own)
    bx, zx = joined(bx2, bx1, outside), joined(zx2, zx1, scaled_own)
    qx, wx = joined(qx2, qx1, image_own), joined(wx2, wx1, image_own)
    vx = joined(vx2, vx2, again_planes(nx))
    carry1, carry2, carry3 = (Tiles(ref, my, loads) for ref in (carry1, carry2, carry3))

    def conduct(ref, base, x):
        return conduct_of(ref[base + x * pitch : base + (x + 1) * pitch, :])

    low = [conduct(low_ref, s.x_dens, t) for t in range(3)] + [conduct(dens_ref, 0, 0)]
    high = [conduct(dens_ref, 0, nx - 1)] + [conduct(high_ref, s.x_dens, t) for t in range(2)]
    for x in range(3):
        inverse = inverse_of(s, low[x], low[x + 1])
        invx.put(x, inverse)
        if x < 2:
            cond.put(x, low[x + 1][1:])
    inv_out[...] = inverse[2 : 2 + ny]
    for x in range(2):
        invx.put(nx + 2 + x, inverse_of(s, high[x], high[x + 1]))
    cond.put(nx + 2, high[1][1:])

    for ref, x0 in ((low_ref, 0), (high_ref, nx + 2)):

        def write(i, tile):
            at = x0 + i // my, i % my
            bx[at] = tile
            zx[at] = tile * invx[at]

        unpack_tiles(ref, 0, loads, 2 * my, write)
    for y in range(my):
        zx[2, y] = bx[2, y] * invx[2, y]

    emitter = First(bx, invx, qx, wx)
    element_planes(cond, carry3, 0, 1, 0, my - 1, zx, None)
    element_planes(cond, carry3, 1, 2, 0, my - 1, zx, emitter)
    element_planes(cond, carry3, 3, 1, 0, my - 1, zx, emitter, keep=False)
    element_planes(cond, carry1, nx + 1, 2, 0, my - 1, zx, emitter, keep=False)
    sums = [sums1[place * loads : (place + 1) * loads, :] for place in range(4)]
    emitter = Second(bx, zx, qx, vx, sums)
    element_planes(cond, carry3, 1, 1, 1, my - 3, wx, None)
    element_planes(cond, carry3, 2, 2, 1, my - 3, wx, emitter)
    element_planes(cond, carry3, 4, 1, 1, my - 3, wx, emitter, keep=False)
    element_planes(cond, carry2, nx, 2, 1, my - 3, wx, emitter, keep=False)
    for field, out, planes in ((qx, q_out, image_planes(nx)), (vx, v_out, again_planes(nx))):
        out = Tiles(out, ny, loads)
        for place, x in enumerate(planes):
            for y in range(ny):
                out[place, y] = field[x, y + 2]

    lane = lane_ids(loads)
    load = lax.broadcasted_iota(jnp.int32, (loads, LANES), 0)
    packed = jnp.zeros((loads, LANES), jnp.float32)
    for place, part in enumerate(sums):
        total = jnp.sum(part, axis=1, keepdims=True)
        packed = packed + jnp.where(lane == place * loads + load, total, 0.0)
    row = jnp.sum(packed, axis=0, keepdims=True)
    sums_ref[...] = jnp.broadcast_to(row[None], sums_ref.shape)


def image_planes(nx):
    return (2, 3, nx + 1)


def again_planes(nx):
    return (2, 3, 4, nx, nx + 1)


def unpack_kernel(
    s, q1_ref, q2_ref, v1_ref, v2_ref, inv1_ref, inv2_ref, qo_ref, vo_ref, io_ref, t_ref
):
    loads, nx, ny, my = s.loads, s.nx, s.ny, s.my
    whole = Tiles(t_ref, ny, loads)
    for first, second, planes, out in (
        (q1_ref, q2_ref, image_planes(nx), qo_ref),
        (v1_ref, v2_ref, again_planes(nx), vo_ref),
    ):
        first, second = Tiles(first, my, loads), Tiles(second, ny, loads)
        for x in range(nx):
            for y in range(ny):
                if x + 2 in planes:
                    whole[x, y] = second[planes.index(x + 2), y]
                else:
                    whole[x, y] = first[x + 2, y + 2]
        for x0 in range(0, nx, SUB):
            for block in range(packed_count(ny)):
                for load in range(loads):
                    out[load, x0 : x0 + SUB, block * LANES : (block + 1) * LANES] = pack_block(
                        lambda y: t_ref[
                            pl.ds((x0 * ny + y) * loads + load, SUB, stride=ny * loads), :
                        ],
                        ny, block, SUB,
                    )
    for x0 in range(0, nx, SUB):
        for block in range(packed_count(ny)):
            io_ref[x0 : x0 + SUB, block * LANES : (block + 1) * LANES] = pack_block(
                lambda y: inv1_ref[
                    pl.ds((x0 + 2) * s.pitch + y + 2, SUB, stride=s.pitch), :
                ],
                ny, block, SUB,
            )
    for block in range(packed_count(ny)):
        io_ref[0:1, block * LANES : (block + 1) * LANES] = pack_block(
            lambda y: inv2_ref[y : y + 1, :], ny, block, 1
        )


def finish_kernel(s, parts_ref, b_ref, q_ref, v_ref, inv_ref, x_hbm, r_hbm, x_ref, r_ref, sems):
    loads = s.loads
    totals = jnp.sum(parts_ref[...], axis=0)

    def part(place):
        return pltpu.roll(totals, (LANES - place * loads) % LANES, 1) if place else totals

    rz, near, square, last = (part(place) for place in range(4))
    direct = rz - near
    alpha = rz / direct
    short = -near / direct
    rz_next = short * short * rz + 2.0 * alpha * short * near + alpha * alpha * square
    beta = rz_next / rz
    grown = short + beta
    curved = (
        grown * grown * direct
        + 2.0 * alpha * grown * (near - square)
        + alpha * alpha * last
    )
    alpha_next = rz_next / curved
    first_row = alpha + alpha_next * (1.0 + beta)
    second_row = alpha_next * alpha
    inverse = inv_ref[...]
    copies = []
    for load in range(loads):
        first = first_row[:, load : load + 1]
        second = second_row[:, load : load + 1]
        source, image = b_ref[load], q_ref[load]
        x_ref[load] = (first * source - second * image) * inverse
        copies.append(pltpu.make_async_copy(x_ref.at[load], x_hbm.at[load], sems.at[0, load]))
        copies[-1].start()
        r_ref[load] = source - first * image + second * v_ref[load]
        copies.append(pltpu.make_async_copy(r_ref.at[load], r_hbm.at[load], sems.at[1, load]))
        copies[-1].start()
    for copy in copies:
        copy.wait()


def swap(array, axis, start):
    pairs = []
    for i in range(start, lax.axis_size(axis) - 1, 2):
        pairs += [(i, i + 1), (i + 1, i)]
    return lax.ppermute(array, axis, pairs)


def per_device(heat_source, density):
    loads, nx, flat = heat_source.shape
    ny = flat // NZ
    s = Sizes(loads, nx, ny)
    nodes = nx * ny * loads
    devices = lax.axis_size("gx") * lax.axis_size("gy")

    def shape(*dims):
        return jax.ShapeDtypeStruct(dims, jnp.float32)

    def scratch(*dims):
        return pltpu.VMEM(dims, jnp.float32)

    def call(kernel, out_shape, **more):
        params = pltpu.CompilerParams(vmem_limit_bytes=20 * 1024 * 1024)
        return pl.pallas_call(
            functools.partial(kernel, s), out_shape=out_shape, compiler_params=params, **more
        )

    hbm = pl.BlockSpec(memory_space=pltpu.HBM)
    bt, dt, y1, y2 = call(
        pack_kernel,
        (
            shape(nodes, LANES),
            shape(nx * ny, LANES),
            shape(s.y_rows, LANES),
            shape(s.y_rows, LANES),
        ),
    )(heat_source, density)
    y2, y1 = swap(y2, "gy", 1), swap(y1, "gy", 0)
    dens, x1, x2 = call(
        pack_x_kernel,
        (shape(nx * s.pitch, LANES), shape(s.x_rows, LANES), shape(s.x_rows, LANES)),
        scratch_shapes=[scratch(4 * s.my * loads, LANES)],
    )(bt, dt, y1, y2)
    x1, x2 = swap(x1, "gx", 0), swap(x2, "gx", 1)
    plane = s.my * loads
    rows, field = shape(s.mx * s.pitch, LANES), shape(s.mx * plane, LANES)
    edge = shape(2 * plane, LANES)
    cond, inv_1, bx, zx, q_1, w_1, v_1, carry1, carry2, sums = call(
        inner_kernel, (rows,) * 2 + (field,) * 5 + (edge,) * 2 + (shape(4 * loads, LANES),)
    )(bt, dens, y1, y2)
    q_2, v_2, inv_2, sums = call(
        outer_kernel,
        (
            shape(len(image_planes(nx)) * ny * loads, LANES),
            shape(len(again_planes(nx)) * ny * loads, LANES),
            shape(ny, LANES),
            shape(devices, 1, LANES),
        ),
        scratch_shapes=[scratch(s.x_rows, LANES)] * 2
        + [scratch(5 * s.pitch, LANES)] * 2
        + [scratch(5 * plane, LANES)] * 5
        + [scratch(2 * plane, LANES)],
    )(dens, x1, x2, cond, inv_1, bx, zx, q_1, w_1, carry1, carry2, sums)
    parts = lax.all_to_all(sums, ("gx", "gy"), 0, 0, tiled=True)
    whole = shape(loads, nx, flat)
    image, again, inverse = call(
        unpack_kernel,
        (whole, whole, shape(nx, flat)),
        scratch_shapes=[scratch(nodes, LANES)],
    )(q_1, q_2, v_1, v_2, inv_1, inv_2)
    return call(
        finish_kernel,
        (whole, whole),
        out_specs=(hbm, hbm),
        scratch_shapes=[
            scratch(loads, nx, flat),
            scratch(loads, nx, flat),
            pltpu.SemaphoreType.DMA((2, loads)),
        ],
    )(parts, heat_source, image, again, inverse)


def solution(mesh):
    placed = (P(None, "gx", "gy"), P("gx", "gy"))
    return jax.shard_map(
        per_device,
        mesh=mesh,
        in_specs=placed,
        out_specs=(P(None, "gx", "gy"), P(None, "gx", "gy")),
        check_vma=False,
    )
```

```python
import functools

import jax
import jax.numpy as jnp
from jax import lax
from jax.experimental import pallas as pl
from jax.experimental.pallas import tpu as pltpu
from jax.sharding import PartitionSpec as P

NZ = 96
KMIN = 0.001
LANES = 128
SUB = 8


def packed_count(tiles):
    return -(-tiles * NZ // LANES)


def lane_ids(rows):
    return lax.broadcasted_iota(jnp.int32, (rows, LANES), 1)


def unpack_tile(read, index, rows):
    start = index * NZ
    block, offset = start // LANES, start % LANES
    lane = lane_ids(rows)
    first = read(block)
    if offset:
        first = pltpu.roll(first, LANES - offset, 1)
    if offset + NZ > LANES:
        second = pltpu.roll(read(block + 1), LANES - offset, 1)
        first = jnp.where(lane < LANES - offset, first, second)
    return jnp.where(lane < NZ, first, 0.0)


def pack_block(read_tile, tiles, block, rows):
    lane = lane_ids(rows)
    start = block * LANES
    out, at = None, start
    while at < start + LANES and at // NZ < tiles:
        index, z = at // NZ, at % NZ
        here = at - start
        piece = read_tile(index)
        shift = (here - z) % LANES
        if shift:
            piece = pltpu.roll(piece, shift, 1)
        out = piece if out is None else jnp.where(lane < here, out, piece)
        at += NZ - z
    return out


def pack_tiles(out_ref, at, rows, tiles, read_tile):
    for block in range(packed_count(tiles)):
        out_ref[at + block * rows : at + (block + 1) * rows, :] = pack_block(
            read_tile, tiles, block, rows
        )


def unpack_tiles(ref, at, rows, tiles, write):
    for index in range(tiles):
        write(
            index,
            unpack_tile(lambda t: ref[at + t * rows : at + (t + 1) * rows, :], index, rows),
        )


class Sizes:
    def __init__(self, loads, nx, ny):
        self.loads, self.nx, self.ny = loads, nx, ny
        self.mx, self.my = nx + 4, ny + 4
        self.pitch = -(-(ny + 6) // SUB) * SUB
        self.y_dens = packed_count(2 * nx) * loads
        self.y_rows = self.y_dens + 3 * nx
        self.x_dens = packed_count(2 * self.my) * loads
        self.x_rows = self.x_dens + 3 * self.pitch


class Tiles:
    def __init__(self, ref, columns, loads):
        self.ref, self.columns, self.loads = ref, columns, loads

    def rows(self, at):
        start = (at[0] * self.columns + at[1]) * self.loads
        if not isinstance(start, int):
            start = pl.multiple_of(start, SUB)
        return pl.ds(start, self.loads)

    def __getitem__(self, at):
        return self.ref[self.rows(at), :]

    def __setitem__(self, at, tile):
        self.ref[self.rows(at), :] = tile


class Rows:
    def __init__(self, ref, pitch, loads):
        self.ref, self.pitch, self.loads = ref, pitch, loads

    def __getitem__(self, at):
        row = self.ref[pl.ds(at[0] * self.pitch + at[1], 1), :]
        return jnp.broadcast_to(row, (self.loads, LANES))

    def put(self, x, values):
        self.ref[x * self.pitch : x * self.pitch + values.shape[0], :] = values


class Joined:
    def __init__(self, first, second, own):
        self.first, self.second, self.own = first, second, own

    def __getitem__(self, at):
        if at[0] in self.own:
            return self.first[self.own.index(at[0]), at[1]]
        return self.second[at]

    def __setitem__(self, at, tile):
        self.first[self.own.index(at[0]), at[1]] = tile

    def put(self, x, values):
        self.first.put(self.own.index(x), values)


def is_even(axis):
    return lax.rem(lax.axis_index(axis), 2) == 0


def pick(even, if_even, if_odd):
    return jnp.where(even, if_even, if_odd)


def pack_kernel(s, b_hbm, d_hbm, bt_ref, dt_ref, y2_ref, b_ref, d_ref, sems):
    loads, nx, ny = s.loads, s.nx, s.ny
    d_copy = pltpu.make_async_copy(d_hbm, d_ref, sems.at[loads])
    copies = []
    for load in range(loads):
        copies.append(pltpu.make_async_copy(b_hbm.at[load], b_ref.at[load], sems.at[load]))
        copies[-1].start()
    d_copy.start()
    for load in range(loads):
        copies[load].wait()
        for x0 in range(0, nx, SUB):
            for y in range(ny):
                tile = unpack_tile(
                    lambda t: b_ref[load, x0 : x0 + SUB, t * LANES : (t + 1) * LANES], y, SUB
                )
                bt_ref[pl.ds((x0 * ny + y) * loads + load, SUB, stride=ny * loads), :] = tile
    d_copy.wait()
    for x0 in range(0, nx, SUB):
        for y in range(ny):
            tile = unpack_tile(
                lambda t: d_ref[x0 : x0 + SUB, t * LANES : (t + 1) * LANES], y, SUB
            )
            dt_ref[pl.ds(x0 * ny + y, SUB, stride=ny), :] = tile
    pack_face(s, jnp.logical_not(is_even("gy")), bt_ref, dt_ref, y2_ref)


def pack_near_kernel(s, bt_ref, dt_ref, y1_ref):
    pack_face(s, is_even("gy"), bt_ref, dt_ref, y1_ref)


def pack_face(s, upper, bt_ref, dt_ref, out_ref):
    loads, nx, ny = s.loads, s.nx, s.ny
    tiles = Tiles(bt_ref, ny, loads)
    y0 = pick(upper, ny - 2, 0)
    pack_tiles(out_ref, 0, loads, 2 * nx, lambda i: tiles[i // 2, y0 + i % 2])
    y0 = pick(upper, ny - 3, 0)
    for dy in range(3):
        for x0 in range(0, nx, SUB):
            at = s.y_dens + dy * nx + x0
            out_ref[at : at + SUB, :] = dt_ref[pl.ds(x0 * ny + y0 + dy, SUB, stride=ny), :]


def pack_x_kernel(s, bt_ref, dt_ref, y2_ref, y1_ref, dens_ref, x1_ref, x2_ref, edge_ref):
    loads, nx, ny, my, pitch = s.loads, s.nx, s.ny, s.my, s.pitch
    even_x, even_y = is_even("gx"), is_even("gy")
    ys = (pick(even_y, ny + 2, 0), pick(even_y, 0, ny + 2))
    yd = (pick(even_y, ny + 3, 0), pick(even_y, 0, ny + 3))
    for x in range(nx):
        at = x * pitch
        dens_ref[at + 3 : at + 3 + ny, :] = dt_ref[x * ny : (x + 1) * ny, :]
        dens_ref[at + ny + 6 : at + pitch, :] = jnp.zeros((pitch - ny - 6, LANES), jnp.float32)
    for side, ref in enumerate((y1_ref, y2_ref)):
        for dy in range(3):
            for x0 in range(0, nx, SUB):
                at = s.y_dens + dy * nx + x0
                to = x0 * pitch + yd[side] + dy
                dens_ref[pl.ds(to, SUB, stride=pitch), :] = ref[at : at + SUB, :]
    inner, edge = Tiles(bt_ref, ny, loads), Tiles(edge_ref, my, loads)
    for place, x in enumerate((0, 1, nx - 2, nx - 1)):
        for y in range(ny):
            edge[place, y + 2] = inner[x, y]
        for side, ref in enumerate((y1_ref, y2_ref)):
            for dy in range(2):
                edge[place, ys[side] + dy] = unpack_tile(
                    lambda t: ref[t * loads : (t + 1) * loads, :], 2 * x + dy, loads
                )
    for ref, upper in ((x1_ref, even_x), (x2_ref, jnp.logical_not(even_x))):
        place = pick(upper, 2, 0)
        pack_tiles(ref, 0, loads, 2 * my, lambda i: edge[place + i // my, i % my])
        rows = pl.ds(pl.multiple_of(pick(upper, nx - 3, 0) * pitch, SUB), 3 * pitch)
        ref[s.x_dens :, :] = dens_ref[rows, :]


def conduct_of(dens):
    return jnp.where(
        dens > 0.0, (KMIN + (1.0 - KMIN) * (dens * dens * dens)) * (1.0 / 12.0), 0.0
    )


def inverse_of(s, before, after):
    pair = before + after
    pair = pair[: s.pitch - 1] + pair[1:]
    total = 4.0 * (pair + pltpu.roll(pair, 1, 1))
    return jnp.where(after[1:] > 0.0, 1.0 / total, 0.0)


def up(tile):
    return pltpu.roll(tile, LANES - 1, 1)


def element_planes(cond, carry, a, count, y0, columns, field, emitter, keep=True):
    def loads_of(step):
        y = y0 + step
        right = [field[a + u, y + 1] for u in range(count + 1)]
        conduct = [cond[a + u, y] for u in range(count)]
        above = extra = None
        if step and emitter:
            above = (carry[0, y], carry[1, y])
            extra = [emitter.fetch(a + u, y) for u in range(count)]
        return right, conduct, above, extra

    left = [(tile, up(tile)) for tile in [field[a + u, y0] for u in range(count + 1)]]
    ahead = loads_of(0)
    old, waiting = [None] * count, []
    for step in range(columns):
        y = y0 + step
        right, conduct, above, extra = ahead
        if step + 1 < columns:
            ahead = loads_of(step + 1)
        if len(waiting) > 1:
            for into, at, tile in waiting.pop(0):
                into[at] = tile
        stores = []
        right = [(tile, up(tile)) for tile in right]
        for u in range(count):
            (p0, p0s), (p1, p1s) = left[u], left[u + 1]
            (r0, r0s), (r1, r1s) = right[u], right[u + 1]
            c = conduct[u]
            even = (p0 + r1) + (r0s + p1s)
            odd = (r0 + p1) + (p0s + r1s)
            pass_on = keep or u + 1 < count
            lower = upper = None
            if emitter:
                lower = (c * (odd + p1s), c * (even + p1))
            if pass_on:
                upper = (c * (even + p0s), c * (odd + p0))
            if step and emitter:
                low = (c * (even + r1s) + old[u][0][0]) + above[0]
                high = (c * (odd + r1) + old[u][0][1]) + above[1]
                total = low + pltpu.roll(high, 1, 1)
                stores += emitter.finish(a + u, y, p0, total, extra[u])
            if step and pass_on:
                above = (
                    c * (odd + r0s) + old[u][1][0],
                    c * (even + r0) + old[u][1][1],
                )
            old[u] = (lower, upper)
        if step and keep:
            stores += [(carry, (0, y), above[0]), (carry, (1, y), above[1])]
        waiting.append(stores)
        left = right
    for stores in waiting:
        for into, at, tile in stores:
            into[at] = tile


class First:
    def __init__(self, bx, invx, qx, wx):
        self.bx, self.invx, self.qx, self.wx = bx, invx, qx, wx

    def fetch(self, x, y):
        return self.bx[x, y], self.invx[x, y]

    def finish(self, x, y, node, total, extra):
        source, inverse = extra
        image = 1.25 * source - total
        return [(self.qx, (x, y), image), (self.wx, (x, y), image * inverse)]


class Second:
    def __init__(self, bx, zx, qx, vx, sums):
        self.bx, self.zx, self.qx, self.vx, self.sums = bx, zx, qx, vx, sums

    def fetch(self, x, y):
        return self.bx[x, y], self.zx[x, y], self.qx[x, y]

    def finish(self, x, y, weighted, total, extra):
        source, scaled, image = extra
        again = 1.25 * image - total
        change = scaled - weighted
        sums = self.sums
        sums[0] = sums[0] + source * scaled
        sums[1] = sums[1] + source * change
        sums[2] = sums[2] + (source - image) * change
        sums[3] = sums[3] + (image - again) * change
        return [(self.vx, (x, y), again)]


def over_planes(start, stop, body, state):
    pairs = (stop - start) // 2
    state = lax.fori_loop(0, pairs, lambda i, st: body(start + 2 * i, 2, st), state)
    if (stop - start) % 2:
        state = body(stop - 1, 1, state)
    return state


def image_kernel(
    s, bt_ref, dens_ref, y1_ref, y2_ref,
    cond, invx, bx, zx, qx, wx, carry1,
):
    loads, nx, ny, my, pitch = s.loads, s.nx, s.ny, s.my, s.pitch
    bx, zx, qx, wx, carry1 = (Tiles(ref, my, loads) for ref in (bx, zx, qx, wx, carry1))
    cond, invx = Rows(cond, pitch, loads), Rows(invx, pitch, loads)
    even_y = is_even("gy")
    ys = (pick(even_y, ny + 2, 0), pick(even_y, 0, ny + 2))
    before = None
    for x in range(nx):
        after = conduct_of(dens_ref[x * pitch : (x + 1) * pitch, :])
        cond.put(x + 2, after[1:])
        if x:
            invx.put(x + 2, inverse_of(s, before, after))
        before = after

    def stage(x, y, tile):
        bx[x + 2, y] = tile
        if x:
            zx[x + 2, y] = tile * invx[x + 2, y]

    inner = Tiles(bt_ref, ny, loads)
    for x in range(nx):
        for y in range(ny):
            stage(x, y + 2, inner[x, y])
    for side, ref in enumerate((y1_ref, y2_ref)):
        unpack_tiles(
            ref, 0, loads, 2 * nx, lambda i, tile: stage(i // 2, ys[side] + i % 2, tile)
        )

    element_planes(cond, carry1, 3, 1, 0, my - 1, zx, None)

    def first(a, count, state):
        element_planes(cond, carry1, a, count, 0, my - 1, zx, First(bx, invx, qx, wx))
        return state

    over_planes(4, nx + 1, first, 0)


def again_kernel(s, cond, bx, zx, qx, wx, vx, carry2, sums_ref):
    loads, nx, my = s.loads, s.nx, s.my
    bx, zx, qx, wx, vx, carry2 = (Tiles(ref, my, loads) for ref in (bx, zx, qx, wx, vx, carry2))
    cond = Rows(cond, s.pitch, loads)
    element_planes(cond, carry2, 4, 1, 1, my - 3, wx, None)

    def second(a, count, sums):
        sums = list(sums)
        element_planes(cond, carry2, a, count, 1, my - 3, wx, Second(bx, zx, qx, vx, sums))
        return tuple(sums)

    zero = jnp.zeros((loads, LANES), jnp.float32)
    sums = over_planes(5, nx, second, (zero,) * 4)
    for place, part in enumerate(sums):
        sums_ref[place * loads : (place + 1) * loads, :] = part


def outer_kernel(
    s, dens_ref, x1_ref, x2_ref,
    cond1, invx1, bx1, zx1, qx1, wx1, vx1, carry1, carry2, sums1,
    q_out, v_out, inv_out, sums_ref,
    low_ref, high_ref, cond2, invx2, bx2, zx2, qx2, wx2, vx2, carry3,
):
    loads, nx, ny, mx, my, pitch = s.loads, s.nx, s.ny, s.mx, s.my, s.pitch
    even_x = is_even("gx")

    @pl.when(even_x)
    def _():
        low_ref[...] = x2_ref[...]
        high_ref[...] = x1_ref[...]

    @pl.when(jnp.logical_not(even_x))
    def _():
        low_ref[...] = x1_ref[...]
        high_ref[...] = x2_ref[...]

    def joined(first, second, own):
        return Joined(Tiles(first, my, loads), Tiles(second, my, loads), own)

    def joined_rows(first, second, own):
        return Joined(Rows(first, pitch, loads), Rows(second, pitch, loads), own)

    outside = (0, 1, nx + 2, nx + 3)
    scaled_own = outside + (2,)
    image_own = (1, 2, 3, nx + 1, nx + 2)
    cond, invx = joined_rows(cond2, cond1, outside), joined_rows(invx2, invx1, scaled_own)
    bx, zx = joined(bx2, bx1, outside), joined(zx2, zx1, scaled_own)
    qx, wx = joined(qx2, qx1, image_own), joined(wx2, wx1, image_own)
    vx = joined(vx2, vx1, again_planes(nx))
    carry1, carry2, carry3 = (Tiles(ref, my, loads) for ref in (carry1, carry2, carry3))

    def conduct(ref, base, x):
        return conduct_of(ref[base + x * pitch : base + (x + 1) * pitch, :])

    low = [conduct(low_ref, s.x_dens, t) for t in range(3)] + [conduct(dens_ref, 0, 0)]
    high = [conduct(dens_ref, 0, nx - 1)] + [conduct(high_ref, s.x_dens, t) for t in range(2)]
    for x in range(3):
        inverse = inverse_of(s, low[x], low[x + 1])
        invx.put(x, inverse)
        if x < 2:
            cond.put(x, low[x + 1][1:])
    inv_out[...] = inverse[2 : 2 + ny]
    for x in range(2):
        invx.put(nx + 2 + x, inverse_of(s, high[x], high[x + 1]))
    cond.put(nx + 2, high[1][1:])

    for ref, x0 in ((low_ref, 0), (high_ref, nx + 2)):

        def write(i, tile):
            at = x0 + i // my, i % my
            bx[at] = tile
            zx[at] = tile * invx[at]

        unpack_tiles(ref, 0, loads, 2 * my, write)
    for y in range(my):
        zx[2, y] = bx[2, y] * invx[2, y]

    emitter = First(bx, invx, qx, wx)
    element_planes(cond, carry3, 0, 1, 0, my - 1, zx, None)
    element_planes(cond, carry3, 1, 2, 0, my - 1, zx, emitter)
    element_planes(cond, carry3, 3, 1, 0, my - 1, zx, emitter, keep=False)
    element_planes(cond, carry1, nx + 1, 2, 0, my - 1, zx, emitter, keep=False)
    sums = [sums1[place * loads : (place + 1) * loads, :] for place in range(4)]
    emitter = Second(bx, zx, qx, vx, sums)
    element_planes(cond, carry3, 1, 1, 1, my - 3, wx, None)
    element_planes(cond, carry3, 2, 2, 1, my - 3, wx, emitter)
    element_planes(cond, carry3, 4, 1, 1, my - 3, wx, emitter, keep=False)
    element_planes(cond, carry2, nx, 2, 1, my - 3, wx, emitter, keep=False)
    for field, out in ((qx, q_out), (vx, v_out)):
        out = Tiles(out, ny, loads)
        for x in range(nx):
            for y in range(ny):
                out[x, y] = field[x + 2, y + 2]

    lane = lane_ids(loads)
    load = lax.broadcasted_iota(jnp.int32, (loads, LANES), 0)
    packed = jnp.zeros((loads, LANES), jnp.float32)
    for place, part in enumerate(sums):
        total = jnp.sum(part, axis=1, keepdims=True)
        packed = packed + jnp.where(lane == place * loads + load, total, 0.0)
    row = jnp.sum(packed, axis=0, keepdims=True)
    sums_ref[...] = jnp.broadcast_to(row[None], sums_ref.shape)


def again_planes(nx):
    return (2, 3, 4, nx, nx + 1)


def unpack_kernel(s, q_ref, v_ref, inv1_ref, inv2_ref, qo_ref, vo_ref, io_ref):
    loads, nx, ny = s.loads, s.nx, s.ny
    for x0 in range(0, nx, SUB):
        for block in range(packed_count(ny)):
            lanes = slice(block * LANES, (block + 1) * LANES)
            for ref, out in ((q_ref, qo_ref), (v_ref, vo_ref)):
                for load in range(loads):
                    out[load, x0 : x0 + SUB, lanes] = pack_block(
                        lambda y: ref[
                            pl.ds((x0 * ny + y) * loads + load, SUB, stride=ny * loads), :
                        ],
                        ny, block, SUB,
                    )
            io_ref[x0 : x0 + SUB, lanes] = pack_block(
                lambda y: inv1_ref[
                    pl.ds((x0 + 2) * s.pitch + y + 2, SUB, stride=s.pitch), :
                ],
                ny, block, SUB,
            )
    for block in range(packed_count(ny)):
        io_ref[0:1, block * LANES : (block + 1) * LANES] = pack_block(
            lambda y: inv2_ref[y : y + 1, :], ny, block, 1
        )


def finish_kernel(s, parts_ref, b_ref, q_ref, v_ref, inv_ref, x_hbm, r_hbm, x_ref, r_ref, sems):
    loads = s.loads
    totals = jnp.sum(parts_ref[...], axis=0)

    def part(place):
        return pltpu.roll(totals, (LANES - place * loads) % LANES, 1) if place else totals

    rz, near, square, last = (part(place) for place in range(4))
    direct = rz - near
    alpha = rz / direct
    short = -near / direct
    rz_next = short * short * rz + 2.0 * alpha * short * near + alpha * alpha * square
    beta = rz_next / rz
    grown = short + beta
    curved = (
        grown * grown * direct
        + 2.0 * alpha * grown * (near - square)
        + alpha * alpha * last
    )
    alpha_next = rz_next / curved
    first_row = alpha + alpha_next * (1.0 + beta)
    second_row = alpha_next * alpha
    inverse = inv_ref[...]
    copies = []
    for load in range(loads):
        first = first_row[:, load : load + 1]
        second = second_row[:, load : load + 1]
        source, image = b_ref[load], q_ref[load]
        x_ref[load] = (first * source - second * image) * inverse
        copies.append(pltpu.make_async_copy(x_ref.at[load], x_hbm.at[load], sems.at[0, load]))
        copies[-1].start()
        r_ref[load] = source - first * image + second * v_ref[load]
        copies.append(pltpu.make_async_copy(r_ref.at[load], r_hbm.at[load], sems.at[1, load]))
        copies[-1].start()
    for copy in copies:
        copy.wait()


def swap(array, axis, start):
    pairs = []
    for i in range(start, lax.axis_size(axis) - 1, 2):
        pairs += [(i, i + 1), (i + 1, i)]
    return lax.ppermute(array, axis, pairs)


def per_device(heat_source, density):
    loads, nx, flat = heat_source.shape
    ny = flat // NZ
    s = Sizes(loads, nx, ny)
    nodes = nx * ny * loads
    devices = lax.axis_size("gx") * lax.axis_size("gy")

    def shape(*dims):
        return jax.ShapeDtypeStruct(dims, jnp.float32)

    def scratch(*dims):
        return pltpu.VMEM(dims, jnp.float32)

    def call(kernel, out_shape, **more):
        params = pltpu.CompilerParams(vmem_limit_bytes=20 * 1024 * 1024)
        return pl.pallas_call(
            functools.partial(kernel, s), out_shape=out_shape, compiler_params=params, **more
        )

    hbm = pl.BlockSpec(memory_space=pltpu.HBM)
    face = shape(s.y_rows, LANES)
    bt, dt, y2 = call(
        pack_kernel,
        (shape(nodes, LANES), shape(nx * ny, LANES), face),
        in_specs=[hbm, hbm],
        scratch_shapes=[
            scratch(loads, nx, flat),
            scratch(nx, flat),
            pltpu.SemaphoreType.DMA((loads + 1,)),
        ],
    )(
        pltpu.with_memory_space_constraint(heat_source, pltpu.HBM),
        pltpu.with_memory_space_constraint(density, pltpu.HBM),
    )
    y2 = swap(y2, "gy", 1)
    y1 = swap(call(pack_near_kernel, face)(bt, dt), "gy", 0)
    dens, x1, x2 = call(
        pack_x_kernel,
        (shape(nx * s.pitch, LANES), shape(s.x_rows, LANES), shape(s.x_rows, LANES)),
        scratch_shapes=[scratch(4 * s.my * loads, LANES)],
    )(bt, dt, y2, y1)
    x1 = swap(x1, "gx", 0)
    plane = s.my * loads
    rows, field = shape(s.mx * s.pitch, LANES), shape(s.mx * plane, LANES)
    edge = shape(2 * plane, LANES)
    cond, inv_1, bx, zx, q_1, w_1, carry1 = call(
        image_kernel, (rows,) * 2 + (field,) * 4 + (edge,)
    )(bt, dens, y1, y2)
    x2, w_1 = lax.optimization_barrier((x2, w_1))
    x2 = swap(x2, "gx", 1)
    v_1, carry2, sums = call(again_kernel, (field, edge, shape(4 * loads, LANES)))(
        cond, bx, zx, q_1, w_1
    )
    q_t, v_t, inv_2, sums = call(
        outer_kernel,
        (
            shape(nodes, LANES),
            shape(nodes, LANES),
            shape(ny, LANES),
            shape(devices, 1, LANES),
        ),
        scratch_shapes=[scratch(s.x_rows, LANES)] * 2
        + [scratch(5 * s.pitch, LANES)] * 2
        + [scratch(5 * plane, LANES)] * 5
        + [scratch(2 * plane, LANES)],
    )(dens, x1, x2, cond, inv_1, bx, zx, q_1, w_1, v_1, carry1, carry2, sums)
    parts = lax.all_to_all(sums, ("gx", "gy"), 0, 0, tiled=True)
    whole = shape(loads, nx, flat)
    image, again, inverse = call(unpack_kernel, (whole, whole, shape(nx, flat)))(
        q_t, v_t, inv_1, inv_2
    )
    return call(
        finish_kernel,
        (whole, whole),
        out_specs=(hbm, hbm),
        scratch_shapes=[
            scratch(loads, nx, flat),
            scratch(loads, nx, flat),
            pltpu.SemaphoreType.DMA((2, loads)),
        ],
    )(parts, heat_source, image, again, inverse)


def solution(mesh):
    placed = (P(None, "gx", "gy"), P("gx", "gy"))
    return jax.shard_map(
        per_device,
        mesh=mesh,
        in_specs=placed,
        out_specs=(P(None, "gx", "gy"), P(None, "gx", "gy")),
        check_vma=False,
    )
```

```python
import functools

import jax
import jax.numpy as jnp
from jax import lax
from jax.experimental import pallas as pl
from jax.experimental.pallas import tpu as pltpu
from jax.sharding import PartitionSpec as P

NZ = 96
KMIN = 0.001
LANES = 128
SUB = 8


def packed_count(tiles):
    return -(-tiles * NZ // LANES)


def lane_ids(rows):
    return lax.broadcasted_iota(jnp.int32, (rows, LANES), 1)


def unpack_tile(read, index, rows):
    start = index * NZ
    block, offset = start // LANES, start % LANES
    lane = lane_ids(rows)
    first = read(block)
    if offset:
        first = pltpu.roll(first, LANES - offset, 1)
    if offset + NZ > LANES:
        second = pltpu.roll(read(block + 1), LANES - offset, 1)
        first = jnp.where(lane < LANES - offset, first, second)
    return jnp.where(lane < NZ, first, 0.0)


def pack_block(read_tile, tiles, block, rows):
    lane = lane_ids(rows)
    start = block * LANES
    out, at = None, start
    while at < start + LANES and at // NZ < tiles:
        index, z = at // NZ, at % NZ
        here = at - start
        piece = read_tile(index)
        shift = (here - z) % LANES
        if shift:
            piece = pltpu.roll(piece, shift, 1)
        out = piece if out is None else jnp.where(lane < here, out, piece)
        at += NZ - z
    return out


def pack_tiles(out_ref, at, rows, tiles, read_tile):
    for block in range(packed_count(tiles)):
        out_ref[at + block * rows : at + (block + 1) * rows, :] = pack_block(
            read_tile, tiles, block, rows
        )


def unpack_tiles(ref, at, rows, tiles, write):
    for index in range(tiles):
        write(
            index,
            unpack_tile(lambda t: ref[at + t * rows : at + (t + 1) * rows, :], index, rows),
        )


class Sizes:
    def __init__(self, loads, nx, ny, count_x, count_y):
        self.loads, self.nx, self.ny = loads, nx, ny
        self.count_x, self.count_y = count_x, count_y
        self.mx, self.my = nx + 4, ny + 4
        self.pitch = -(-(ny + 6) // SUB) * SUB
        self.y_dens = packed_count(2 * nx) * loads
        self.y_rows = self.y_dens + 3 * nx
        self.x_dens = packed_count(2 * self.my) * loads
        self.x_rows = self.x_dens + 3 * self.pitch


class Tiles:
    def __init__(self, ref, columns, loads):
        self.ref, self.columns, self.loads = ref, columns, loads

    def rows(self, at):
        start = (at[0] * self.columns + at[1]) * self.loads
        if not isinstance(start, int):
            start = pl.multiple_of(start, SUB)
        return pl.ds(start, self.loads)

    def __getitem__(self, at):
        return self.ref[self.rows(at), :]

    def __setitem__(self, at, tile):
        self.ref[self.rows(at), :] = tile


class Rows:
    def __init__(self, ref, pitch, loads):
        self.ref, self.pitch, self.loads = ref, pitch, loads

    def __getitem__(self, at):
        row = self.ref[pl.ds(at[0] * self.pitch + at[1], 1), :]
        return jnp.broadcast_to(row, (self.loads, LANES))

    def put(self, x, values):
        self.ref[x * self.pitch : x * self.pitch + values.shape[0], :] = values


class Joined:
    def __init__(self, first, second, own):
        self.first, self.second, self.own = first, second, own

    def __getitem__(self, at):
        if at[0] in self.own:
            return self.first[self.own.index(at[0]), at[1]]
        return self.second[at]

    def __setitem__(self, at, tile):
        self.first[self.own.index(at[0]), at[1]] = tile

    def put(self, x, values):
        self.first.put(self.own.index(x), values)


def is_even(axis):
    return lax.rem(lax.axis_index(axis), 2) == 0


def is_alone(axis, count, start):
    place = lax.axis_index(axis)
    last = (count - start) % 2
    alone = place < start
    return jnp.logical_or(alone, place == count - 1) if last else alone


def pick(even, if_even, if_odd):
    return jnp.where(even, if_even, if_odd)


def pack_kernel(s, b_hbm, d_hbm, bt_ref, dt_ref, y2_ref, b_ref, d_ref, sems):
    loads, nx, ny = s.loads, s.nx, s.ny
    d_copy = pltpu.make_async_copy(d_hbm, d_ref, sems.at[loads])
    copies = []
    for load in range(loads):
        copies.append(pltpu.make_async_copy(b_hbm.at[load], b_ref.at[load], sems.at[load]))
        copies[-1].start()
    d_copy.start()
    for load in range(loads):
        copies[load].wait()
        for x0 in range(0, nx, SUB):
            for y in range(ny):
                tile = unpack_tile(
                    lambda t: b_ref[load, x0 : x0 + SUB, t * LANES : (t + 1) * LANES], y, SUB
                )
                bt_ref[pl.ds((x0 * ny + y) * loads + load, SUB, stride=ny * loads), :] = tile
    d_copy.wait()
    for x0 in range(0, nx, SUB):
        for y in range(ny):
            tile = unpack_tile(
                lambda t: d_ref[x0 : x0 + SUB, t * LANES : (t + 1) * LANES], y, SUB
            )
            dt_ref[pl.ds(x0 * ny + y, SUB, stride=ny), :] = tile
    pack_face(s, jnp.logical_not(is_even("gy")), bt_ref, dt_ref, y2_ref)


def pack_near_kernel(s, bt_ref, dt_ref, y1_ref):
    pack_face(s, is_even("gy"), bt_ref, dt_ref, y1_ref)


def pack_face(s, upper, bt_ref, dt_ref, out_ref):
    loads, nx, ny = s.loads, s.nx, s.ny
    tiles = Tiles(bt_ref, ny, loads)
    y0 = pick(upper, ny - 2, 0)
    pack_tiles(out_ref, 0, loads, 2 * nx, lambda i: tiles[i // 2, y0 + i % 2])
    y0 = pick(upper, ny - 3, 0)
    for dy in range(3):
        for x0 in range(0, nx, SUB):
            at = s.y_dens + dy * nx + x0
            out_ref[at : at + SUB, :] = dt_ref[pl.ds(x0 * ny + y0 + dy, SUB, stride=ny), :]


def pack_x_kernel(s, bt_ref, dt_ref, y2_ref, y1_ref, dens_ref, x1_ref, x2_ref, edge_ref):
    loads, nx, ny, my, pitch = s.loads, s.nx, s.ny, s.my, s.pitch
    even_x, even_y = is_even("gx"), is_even("gy")
    ys = (pick(even_y, ny + 2, 0), pick(even_y, 0, ny + 2))
    yd = (pick(even_y, ny + 3, 0), pick(even_y, 0, ny + 3))
    for x in range(nx):
        at = x * pitch
        dens_ref[at + 3 : at + 3 + ny, :] = dt_ref[x * ny : (x + 1) * ny, :]
        dens_ref[at + ny + 6 : at + pitch, :] = jnp.zeros((pitch - ny - 6, LANES), jnp.float32)
    for side, ref in enumerate((y1_ref, y2_ref)):
        alone = is_alone("gy", s.count_y, side)
        for dy in range(3):
            for x0 in range(0, nx, SUB):
                at = s.y_dens + dy * nx + x0
                to = x0 * pitch + yd[side] + dy
                dens_ref[pl.ds(to, SUB, stride=pitch), :] = jnp.where(
                    alone, 0.0, ref[at : at + SUB, :]
                )
    inner, edge = Tiles(bt_ref, ny, loads), Tiles(edge_ref, my, loads)
    for place, x in enumerate((0, 1, nx - 2, nx - 1)):
        for y in range(ny):
            edge[place, y + 2] = inner[x, y]
        for side, ref in enumerate((y1_ref, y2_ref)):
            for dy in range(2):
                edge[place, ys[side] + dy] = unpack_tile(
                    lambda t: ref[t * loads : (t + 1) * loads, :], 2 * x + dy, loads
                )
    for ref, upper in ((x1_ref, even_x), (x2_ref, jnp.logical_not(even_x))):
        place = pick(upper, 2, 0)
        pack_tiles(ref, 0, loads, 2 * my, lambda i: edge[place + i // my, i % my])
        rows = pl.ds(pl.multiple_of(pick(upper, nx - 3, 0) * pitch, SUB), 3 * pitch)
        ref[s.x_dens :, :] = dens_ref[rows, :]


def conduct_of(dens):
    return jnp.where(
        dens > 0.0, (KMIN + (1.0 - KMIN) * (dens * dens * dens)) * (1.0 / 12.0), 0.0
    )


def inverse_of(s, before, after):
    pair = before + after
    pair = pair[: s.pitch - 1] + pair[1:]
    total = 4.0 * (pair + pltpu.roll(pair, 1, 1))
    return jnp.where(after[1:] > 0.0, 1.0 / total, 0.0)


def up(tile):
    return pltpu.roll(tile, LANES - 1, 1)


def element_planes(cond, carry, a, count, y0, columns, field, emitter, keep=True):
    def loads_of(step):
        y = y0 + step
        right = [field[a + u, y + 1] for u in range(count + 1)]
        conduct = [cond[a + u, y] for u in range(count)]
        above = extra = None
        if step and emitter:
            above = (carry[0, y], carry[1, y])
            extra = [emitter.fetch(a + u, y) for u in range(count)]
        return right, conduct, above, extra

    left = [(tile, up(tile)) for tile in [field[a + u, y0] for u in range(count + 1)]]
    ahead = loads_of(0)
    old, waiting = [None] * count, []
    for step in range(columns):
        y = y0 + step
        right, conduct, above, extra = ahead
        if step + 1 < columns:
            ahead = loads_of(step + 1)
        if len(waiting) > 1:
            for into, at, tile in waiting.pop(0):
                into[at] = tile
        stores = []
        right = [(tile, up(tile)) for tile in right]
        for u in range(count):
            (p0, p0s), (p1, p1s) = left[u], left[u + 1]
            (r0, r0s), (r1, r1s) = right[u], right[u + 1]
            c = conduct[u]
            even = (p0 + r1) + (r0s + p1s)
            odd = (r0 + p1) + (p0s + r1s)
            pass_on = keep or u + 1 < count
            lower = upper = None
            if emitter:
                lower = (c * (odd + p1s), c * (even + p1))
            if pass_on:
                upper = (c * (even + p0s), c * (odd + p0))
            if step and emitter:
                low = (c * (even + r1s) + old[u][0][0]) + above[0]
                high = (c * (odd + r1) + old[u][0][1]) + above[1]
                total = low + pltpu.roll(high, 1, 1)
                stores += emitter.finish(a + u, y, p0, total, extra[u])
            if step and pass_on:
                above = (
                    c * (odd + r0s) + old[u][1][0],
                    c * (even + r0) + old[u][1][1],
                )
            old[u] = (lower, upper)
        if step and keep:
            stores += [(carry, (0, y), above[0]), (carry, (1, y), above[1])]
        waiting.append(stores)
        left = right
    for stores in waiting:
        for into, at, tile in stores:
            into[at] = tile


class First:
    def __init__(self, bx, invx, qx, wx):
        self.bx, self.invx, self.qx, self.wx = bx, invx, qx, wx

    def fetch(self, x, y):
        return self.bx[x, y], self.invx[x, y]

    def finish(self, x, y, node, total, extra):
        source, inverse = extra
        image = 1.25 * source - total
        return [(self.qx, (x, y), image), (self.wx, (x, y), image * inverse)]


class Second:
    def __init__(self, bx, zx, qx, vx, sums):
        self.bx, self.zx, self.qx, self.vx, self.sums = bx, zx, qx, vx, sums

    def fetch(self, x, y):
        return self.bx[x, y], self.zx[x, y], self.qx[x, y]

    def finish(self, x, y, weighted, total, extra):
        source, scaled, image = extra
        again = 1.25 * image - total
        change = scaled - weighted
        sums = self.sums
        sums[0] = sums[0] + source * scaled
        sums[1] = sums[1] + source * change
        sums[2] = sums[2] + (source - image) * change
        sums[3] = sums[3] + (image - again) * change
        return [(self.vx, (x, y), again)]


def over_planes(start, stop, body, state):
    pairs = (stop - start) // 2
    state = lax.fori_loop(0, pairs, lambda i, st: body(start + 2 * i, 2, st), state)
    if (stop - start) % 2:
        state = body(stop - 1, 1, state)
    return state


def image_kernel(
    s, bt_ref, dens_ref, y1_ref, y2_ref,
    cond, invx, bx, zx, qx, wx, carry1,
):
    loads, nx, ny, my, pitch = s.loads, s.nx, s.ny, s.my, s.pitch
    bx, zx, qx, wx, carry1 = (Tiles(ref, my, loads) for ref in (bx, zx, qx, wx, carry1))
    cond, invx = Rows(cond, pitch, loads), Rows(invx, pitch, loads)
    even_y = is_even("gy")
    ys = (pick(even_y, ny + 2, 0), pick(even_y, 0, ny + 2))
    before = None
    for x in range(nx):
        after = conduct_of(dens_ref[x * pitch : (x + 1) * pitch, :])
        cond.put(x + 2, after[1:])
        if x:
            invx.put(x + 2, inverse_of(s, before, after))
        before = after

    def stage(x, y, tile):
        bx[x + 2, y] = tile
        if x:
            zx[x + 2, y] = tile * invx[x + 2, y]

    inner = Tiles(bt_ref, ny, loads)
    for x in range(nx):
        for y in range(ny):
            stage(x, y + 2, inner[x, y])
    for side, ref in enumerate((y1_ref, y2_ref)):
        unpack_tiles(
            ref, 0, loads, 2 * nx, lambda i, tile: stage(i // 2, ys[side] + i % 2, tile)
        )

    element_planes(cond, carry1, 3, 1, 0, my - 1, zx, None)

    def first(a, count, state):
        element_planes(cond, carry1, a, count, 0, my - 1, zx, First(bx, invx, qx, wx))
        return state

    over_planes(4, nx + 1, first, 0)


def again_kernel(s, cond, bx, zx, qx, wx, vx, carry2, sums_ref):
    loads, nx, my = s.loads, s.nx, s.my
    bx, zx, qx, wx, vx, carry2 = (Tiles(ref, my, loads) for ref in (bx, zx, qx, wx, vx, carry2))
    cond = Rows(cond, s.pitch, loads)
    element_planes(cond, carry2, 4, 1, 1, my - 3, wx, None)

    def second(a, count, sums):
        sums = list(sums)
        element_planes(cond, carry2, a, count, 1, my - 3, wx, Second(bx, zx, qx, vx, sums))
        return tuple(sums)

    zero = jnp.zeros((loads, LANES), jnp.float32)
    sums = over_planes(5, nx, second, (zero,) * 4)
    for place, part in enumerate(sums):
        sums_ref[place * loads : (place + 1) * loads, :] = part


def outer_kernel(
    s, dens_ref, x1_ref, x2_ref,
    cond1, invx1, bx1, zx1, qx1, wx1, vx1, carry1, carry2, sums1,
    q_out, v_out, inv_out, sums_ref,
    low_ref, high_ref, cond2, invx2, bx2, zx2, qx2, wx2, vx2, carry3,
):
    loads, nx, ny, mx, my, pitch = s.loads, s.nx, s.ny, s.mx, s.my, s.pitch
    even_x = is_even("gx")

    def take(into, ref, start):
        into[: s.x_dens, :] = ref[: s.x_dens, :]
        dens = ref[s.x_dens :, :]
        into[s.x_dens :, :] = jnp.where(is_alone("gx", s.count_x, start), 0.0, dens)

    @pl.when(even_x)
    def _():
        take(low_ref, x2_ref, 1)
        take(high_ref, x1_ref, 0)

    @pl.when(jnp.logical_not(even_x))
    def _():
        take(low_ref, x1_ref, 0)
        take(high_ref, x2_ref, 1)

    def joined(first, second, own):
        return Joined(Tiles(first, my, loads), Tiles(second, my, loads), own)

    def joined_rows(first, second, own):
        return Joined(Rows(first, pitch, loads), Rows(second, pitch, loads), own)

    outside = (0, 1, nx + 2, nx + 3)
    scaled_own = outside + (2,)
    image_own = (1, 2, 3, nx + 1, nx + 2)
    cond, invx = joined_rows(cond2, cond1, outside), joined_rows(invx2, invx1, scaled_own)
    bx, zx = joined(bx2, bx1, outside), joined(zx2, zx1, scaled_own)
    qx, wx = joined(qx2, qx1, image_own), joined(wx2, wx1, image_own)
    vx = joined(vx2, vx1, again_planes(nx))
    carry1, carry2, carry3 = (Tiles(ref, my, loads) for ref in (carry1, carry2, carry3))

    def conduct(ref, base, x):
        return conduct_of(ref[base + x * pitch : base + (x + 1) * pitch, :])

    low = [conduct(low_ref, s.x_dens, t) for t in range(3)] + [conduct(dens_ref, 0, 0)]
    high = [conduct(dens_ref, 0, nx - 1)] + [conduct(high_ref, s.x_dens, t) for t in range(2)]
    for x in range(3):
        inverse = inverse_of(s, low[x], low[x + 1])
        invx.put(x, inverse)
        if x < 2:
            cond.put(x, low[x + 1][1:])
    inv_out[...] = inverse[2 : 2 + ny]
    for x in range(2):
        invx.put(nx + 2 + x, inverse_of(s, high[x], high[x + 1]))
    cond.put(nx + 2, high[1][1:])

    for ref, x0 in ((low_ref, 0), (high_ref, nx + 2)):

        def write(i, tile):
            at = x0 + i // my, i % my
            bx[at] = tile
            zx[at] = tile * invx[at]

        unpack_tiles(ref, 0, loads, 2 * my, write)
    for y in range(my):
        zx[2, y] = bx[2, y] * invx[2, y]

    emitter = First(bx, invx, qx, wx)
    element_planes(cond, carry3, 0, 1, 0, my - 1, zx, None)
    element_planes(cond, carry3, 1, 2, 0, my - 1, zx, emitter)
    element_planes(cond, carry3, 3, 1, 0, my - 1, zx, emitter, keep=False)
    element_planes(cond, carry1, nx + 1, 2, 0, my - 1, zx, emitter, keep=False)
    sums = [sums1[place * loads : (place + 1) * loads, :] for place in range(4)]
    emitter = Second(bx, zx, qx, vx, sums)
    element_planes(cond, carry3, 1, 1, 1, my - 3, wx, None)
    element_planes(cond, carry3, 2, 2, 1, my - 3, wx, emitter)
    element_planes(cond, carry3, 4, 1, 1, my - 3, wx, emitter, keep=False)
    element_planes(cond, carry2, nx, 2, 1, my - 3, wx, emitter, keep=False)
    for field, out in ((qx, q_out), (vx, v_out)):
        out = Tiles(out, ny, loads)
        for x in range(nx):
            for y in range(ny):
                out[x, y] = field[x + 2, y + 2]

    lane = lane_ids(loads)
    load = lax.broadcasted_iota(jnp.int32, (loads, LANES), 0)
    packed = jnp.zeros((loads, LANES), jnp.float32)
    for place, part in enumerate(sums):
        total = jnp.sum(part, axis=1, keepdims=True)
        packed = packed + jnp.where(lane == place * loads + load, total, 0.0)
    row = jnp.sum(packed, axis=0, keepdims=True)
    sums_ref[...] = jnp.broadcast_to(row[None], sums_ref.shape)


def again_planes(nx):
    return (2, 3, 4, nx, nx + 1)


def unpack_kernel(s, q_ref, v_ref, inv1_ref, inv2_ref, qo_ref, vo_ref, io_ref):
    loads, nx, ny = s.loads, s.nx, s.ny
    for x0 in range(0, nx, SUB):
        for block in range(packed_count(ny)):
            lanes = slice(block * LANES, (block + 1) * LANES)
            for ref, out in ((q_ref, qo_ref), (v_ref, vo_ref)):
                for load in range(loads):
                    out[load, x0 : x0 + SUB, lanes] = pack_block(
                        lambda y: ref[
                            pl.ds((x0 * ny + y) * loads + load, SUB, stride=ny * loads), :
                        ],
                        ny, block, SUB,
                    )
            io_ref[x0 : x0 + SUB, lanes] = pack_block(
                lambda y: inv1_ref[
                    pl.ds((x0 + 2) * s.pitch + y + 2, SUB, stride=s.pitch), :
                ],
                ny, block, SUB,
            )
    for block in range(packed_count(ny)):
        io_ref[0:1, block * LANES : (block + 1) * LANES] = pack_block(
            lambda y: inv2_ref[y : y + 1, :], ny, block, 1
        )


def finish_kernel(s, parts_ref, b_ref, q_ref, v_ref, inv_ref, x_hbm, r_hbm, x_ref, r_ref, sems):
    loads = s.loads
    totals = jnp.sum(parts_ref[...], axis=0)

    def part(place):
        return pltpu.roll(totals, (LANES - place * loads) % LANES, 1) if place else totals

    rz, near, square, last = (part(place) for place in range(4))
    direct = rz - near
    alpha = rz / direct
    short = -near / direct
    rz_next = short * short * rz + 2.0 * alpha * short * near + alpha * alpha * square
    beta = rz_next / rz
    grown = short + beta
    curved = (
        grown * grown * direct
        + 2.0 * alpha * grown * (near - square)
        + alpha * alpha * last
    )
    alpha_next = rz_next / curved
    first_row = alpha + alpha_next * (1.0 + beta)
    second_row = alpha_next * alpha
    inverse = inv_ref[...]
    copies = []
    for load in range(loads):
        first = first_row[:, load : load + 1]
        second = second_row[:, load : load + 1]
        source, image = b_ref[load], q_ref[load]
        x_ref[load] = (first * source - second * image) * inverse
        copies.append(pltpu.make_async_copy(x_ref.at[load], x_hbm.at[load], sems.at[0, load]))
        copies[-1].start()
        r_ref[load] = source - first * image + second * v_ref[load]
        copies.append(pltpu.make_async_copy(r_ref.at[load], r_hbm.at[load], sems.at[1, load]))
        copies[-1].start()
    for copy in copies:
        copy.wait()


def swap(array, axis, start):
    count = lax.axis_size(axis)
    target = list(range(count))
    for i in range(start, count - 1, 2):
        target[i], target[i + 1] = i + 1, i
    return lax.ppermute(array, axis, list(enumerate(target)))


def per_device(heat_source, density):
    loads, nx, flat = heat_source.shape
    ny = flat // NZ
    s = Sizes(loads, nx, ny, lax.axis_size("gx"), lax.axis_size("gy"))
    nodes = nx * ny * loads
    devices = lax.axis_size("gx") * lax.axis_size("gy")

    def shape(*dims):
        return jax.ShapeDtypeStruct(dims, jnp.float32)

    def scratch(*dims):
        return pltpu.VMEM(dims, jnp.float32)

    def call(kernel, out_shape, **more):
        params = pltpu.CompilerParams(vmem_limit_bytes=20 * 1024 * 1024)
        return pl.pallas_call(
            functools.partial(kernel, s), out_shape=out_shape, compiler_params=params, **more
        )

    hbm = pl.BlockSpec(memory_space=pltpu.HBM)
    face = shape(s.y_rows, LANES)
    bt, dt, y2 = call(
        pack_kernel,
        (shape(nodes, LANES), shape(nx * ny, LANES), face),
        in_specs=[hbm, hbm],
        scratch_shapes=[
            scratch(loads, nx, flat),
            scratch(nx, flat),
            pltpu.SemaphoreType.DMA((loads + 1,)),
        ],
    )(
        pltpu.with_memory_space_constraint(heat_source, pltpu.HBM),
        pltpu.with_memory_space_constraint(density, pltpu.HBM),
    )
    y2 = swap(y2, "gy", 1)
    y1 = swap(call(pack_near_kernel, face)(bt, dt), "gy", 0)
    dens, x1, x2 = call(
        pack_x_kernel,
        (shape(nx * s.pitch, LANES), shape(s.x_rows, LANES), shape(s.x_rows, LANES)),
        scratch_shapes=[scratch(4 * s.my * loads, LANES)],
    )(bt, dt, y2, y1)
    x1 = swap(x1, "gx", 0)
    plane = s.my * loads
    rows, field = shape(s.mx * s.pitch, LANES), shape(s.mx * plane, LANES)
    edge = shape(2 * plane, LANES)
    cond, inv_1, bx, zx, q_1, w_1, carry1 = call(
        image_kernel, (rows,) * 2 + (field,) * 4 + (edge,)
    )(bt, dens, y1, y2)
    x2, w_1 = lax.optimization_barrier((x2, w_1))
    x2 = swap(x2, "gx", 1)
    v_1, carry2, sums = call(again_kernel, (field, edge, shape(4 * loads, LANES)))(
        cond, bx, zx, q_1, w_1
    )
    q_t, v_t, inv_2, sums = call(
        outer_kernel,
        (
            shape(nodes, LANES),
            shape(nodes, LANES),
            shape(ny, LANES),
            shape(devices, 1, LANES),
        ),
        scratch_shapes=[scratch(s.x_rows, LANES)] * 2
        + [scratch(5 * s.pitch, LANES)] * 2
        + [scratch(5 * plane, LANES)] * 5
        + [scratch(2 * plane, LANES)],
    )(dens, x1, x2, cond, inv_1, bx, zx, q_1, w_1, v_1, carry1, carry2, sums)
    parts = lax.all_to_all(sums, ("gx", "gy"), 0, 0, tiled=True)
    whole = shape(loads, nx, flat)
    image, again, inverse = call(unpack_kernel, (whole, whole, shape(nx, flat)))(
        q_t, v_t, inv_1, inv_2
    )
    return call(
        finish_kernel,
        (whole, whole),
        out_specs=(hbm, hbm),
        scratch_shapes=[
            scratch(loads, nx, flat),
            scratch(loads, nx, flat),
            pltpu.SemaphoreType.DMA((2, loads)),
        ],
    )(parts, heat_source, image, again, inverse)


def solution(mesh):
    placed = (P(None, "gx", "gy"), P("gx", "gy"))
    return jax.shard_map(
        per_device,
        mesh=mesh,
        in_specs=placed,
        out_specs=(P(None, "gx", "gy"), P(None, "gx", "gy")),
        check_vma=False,
    )
```

```python
import functools

import jax
import jax.numpy as jnp
from jax import lax
from jax.experimental import pallas as pl
from jax.experimental.pallas import tpu as pltpu
from jax.sharding import PartitionSpec as P

NZ = 96
KMIN = 0.001
LANES = 128
SUB = 8


class Batch:
    def __init__(self, size=12):
        self.size, self.held = size, []

    def add(self, into, at, tile):
        self.held.append((into, at, tile))
        if len(self.held) >= self.size:
            self.flush()

    def flush(self):
        for into, at, tile in self.held:
            into[at] = tile
        self.held = []


def packed_count(tiles):
    return -(-tiles * NZ // LANES)


def lane_ids(rows):
    return lax.broadcasted_iota(jnp.int32, (rows, LANES), 1)


def unpack_tile(read, index, rows):
    start = index * NZ
    block, offset = start // LANES, start % LANES
    lane = lane_ids(rows)
    first = read(block)
    if offset:
        first = pltpu.roll(first, LANES - offset, 1)
    if offset + NZ > LANES:
        second = pltpu.roll(read(block + 1), LANES - offset, 1)
        first = jnp.where(lane < LANES - offset, first, second)
    return jnp.where(lane < NZ, first, 0.0)


def pack_block(read_tile, tiles, block, rows):
    lane = lane_ids(rows)
    start = block * LANES
    out, at = None, start
    while at < start + LANES and at // NZ < tiles:
        index, z = at // NZ, at % NZ
        here = at - start
        piece = read_tile(index)
        shift = (here - z) % LANES
        if shift:
            piece = pltpu.roll(piece, shift, 1)
        out = piece if out is None else jnp.where(lane < here, out, piece)
        at += NZ - z
    return out


def pack_tiles(out_ref, at, rows, tiles, read_tile):
    batch = Batch()
    for block in range(packed_count(tiles)):
        place = slice(at + block * rows, at + (block + 1) * rows), slice(None)
        batch.add(out_ref, place, pack_block(read_tile, tiles, block, rows))
    batch.flush()


def unpack_tiles(ref, at, rows, tiles, write):
    batch = Batch()
    for index in range(tiles):
        tile = unpack_tile(lambda t: ref[at + t * rows : at + (t + 1) * rows, :], index, rows)
        for store in write(index, tile):
            batch.add(*store)
    batch.flush()


class Sizes:
    def __init__(self, loads, nx, ny):
        self.loads, self.nx, self.ny = loads, nx, ny
        self.mx, self.my = nx + 4, ny + 4
        self.pitch = -(-(ny + 6) // SUB) * SUB
        self.y_dens = packed_count(2 * nx) * loads
        self.y_rows = self.y_dens + 3 * nx
        self.x_dens = packed_count(2 * self.my) * loads
        self.x_rows = self.x_dens + 3 * self.pitch


class Tiles:
    def __init__(self, ref, columns, loads):
        self.ref, self.columns, self.loads = ref, columns, loads

    def rows(self, at):
        start = (at[0] * self.columns + at[1]) * self.loads
        if not isinstance(start, int):
            start = pl.multiple_of(start, SUB)
        return pl.ds(start, self.loads)

    def __getitem__(self, at):
        return self.ref[self.rows(at), :]

    def __setitem__(self, at, tile):
        self.ref[self.rows(at), :] = tile


class Rows:
    def __init__(self, ref, pitch, loads):
        self.ref, self.pitch, self.loads = ref, pitch, loads

    def __getitem__(self, at):
        row = self.ref[pl.ds(at[0] * self.pitch + at[1], 1), :]
        return jnp.broadcast_to(row, (self.loads, LANES))

    def put(self, x, values):
        self.ref[x * self.pitch : x * self.pitch + values.shape[0], :] = values


class Joined:
    def __init__(self, first, second, own):
        self.first, self.second, self.own = first, second, own

    def __getitem__(self, at):
        if at[0] in self.own:
            return self.first[self.own.index(at[0]), at[1]]
        return self.second[at]

    def __setitem__(self, at, tile):
        self.first[self.own.index(at[0]), at[1]] = tile

    def put(self, x, values):
        self.first.put(self.own.index(x), values)


def is_even(axis):
    return lax.rem(lax.axis_index(axis), 2) == 0


def pick(even, if_even, if_odd):
    return jnp.where(even, if_even, if_odd)


def pack_kernel(s, b_hbm, d_hbm, bt_ref, dt_ref, y2_ref, b_ref, d_ref, sems):
    loads, nx, ny = s.loads, s.nx, s.ny
    d_copy = pltpu.make_async_copy(d_hbm, d_ref, sems.at[loads])
    copies = []
    for load in range(loads):
        copies.append(pltpu.make_async_copy(b_hbm.at[load], b_ref.at[load], sems.at[load]))
        copies[-1].start()
    d_copy.start()
    for load in range(loads):
        copies[load].wait()
        batch = Batch(16)
        for x0 in range(0, nx, SUB):
            for y in range(ny):
                tile = unpack_tile(
                    lambda t: b_ref[load, x0 : x0 + SUB, t * LANES : (t + 1) * LANES], y, SUB
                )
                rows = pl.ds((x0 * ny + y) * loads + load, SUB, stride=ny * loads)
                batch.add(bt_ref, (rows, slice(None)), tile)
        batch.flush()
    d_copy.wait()
    batch = Batch(16)
    for x0 in range(0, nx, SUB):
        for y in range(ny):
            tile = unpack_tile(
                lambda t: d_ref[x0 : x0 + SUB, t * LANES : (t + 1) * LANES], y, SUB
            )
            batch.add(dt_ref, (pl.ds(x0 * ny + y, SUB, stride=ny), slice(None)), tile)
    batch.flush()
    pack_face(s, jnp.logical_not(is_even("gy")), bt_ref, dt_ref, y2_ref)


def pack_near_kernel(s, bt_ref, dt_ref, y1_ref):
    pack_face(s, is_even("gy"), bt_ref, dt_ref, y1_ref)


def pack_face(s, upper, bt_ref, dt_ref, out_ref):
    loads, nx, ny = s.loads, s.nx, s.ny
    tiles = Tiles(bt_ref, ny, loads)
    y0 = pick(upper, ny - 2, 0)
    pack_tiles(out_ref, 0, loads, 2 * nx, lambda i: tiles[i // 2, y0 + i % 2])
    y0 = pick(upper, ny - 3, 0)
    batch = Batch()
    for dy in range(3):
        for x0 in range(0, nx, SUB):
            at = s.y_dens + dy * nx + x0
            tile = dt_ref[pl.ds(x0 * ny + y0 + dy, SUB, stride=ny), :]
            batch.add(out_ref, (slice(at, at + SUB), slice(None)), tile)
    batch.flush()


def pack_x_kernel(s, bt_ref, dt_ref, y2_ref, y1_ref, dens_ref, x1_ref, x2_ref, edge_ref):
    loads, nx, ny, my, pitch = s.loads, s.nx, s.ny, s.my, s.pitch
    even_x, even_y = is_even("gx"), is_even("gy")
    ys = (pick(even_y, ny + 2, 0), pick(even_y, 0, ny + 2))
    yd = (pick(even_y, ny + 3, 0), pick(even_y, 0, ny + 3))
    for x in range(nx):
        at = x * pitch
        dens_ref[at + 3 : at + 3 + ny, :] = dt_ref[x * ny : (x + 1) * ny, :]
        dens_ref[at + ny + 6 : at + pitch, :] = jnp.zeros((pitch - ny - 6, LANES), jnp.float32)
    for side, ref in enumerate((y1_ref, y2_ref)):
        for dy in range(3):
            for x0 in range(0, nx, SUB):
                at = s.y_dens + dy * nx + x0
                to = x0 * pitch + yd[side] + dy
                dens_ref[pl.ds(to, SUB, stride=pitch), :] = ref[at : at + SUB, :]
    inner, edge = Tiles(bt_ref, ny, loads), Tiles(edge_ref, my, loads)
    batch = Batch()
    for place, x in enumerate((0, 1, nx - 2, nx - 1)):
        for y in range(ny):
            batch.add(edge, (place, y + 2), inner[x, y])
        for side, ref in enumerate((y1_ref, y2_ref)):
            for dy in range(2):
                tile = unpack_tile(
                    lambda t: ref[t * loads : (t + 1) * loads, :], 2 * x + dy, loads
                )
                batch.add(edge, (place, ys[side] + dy), tile)
    batch.flush()
    for ref, upper in ((x1_ref, even_x), (x2_ref, jnp.logical_not(even_x))):
        place = pick(upper, 2, 0)
        pack_tiles(ref, 0, loads, 2 * my, lambda i: edge[place + i // my, i % my])
        rows = pl.ds(pl.multiple_of(pick(upper, nx - 3, 0) * pitch, SUB), 3 * pitch)
        ref[s.x_dens :, :] = dens_ref[rows, :]


def conduct_of(dens):
    return jnp.where(
        dens > 0.0, (KMIN + (1.0 - KMIN) * (dens * dens * dens)) * (1.0 / 12.0), 0.0
    )


def inverse_of(s, before, after):
    pair = before + after
    pair = pair[: s.pitch - 1] + pair[1:]
    total = 4.0 * (pair + pltpu.roll(pair, 1, 1))
    return jnp.where(after[1:] > 0.0, 1.0 / total, 0.0)


def up(tile):
    return pltpu.roll(tile, LANES - 1, 1)


def element_planes(cond, carry, a, count, y0, columns, field, emitter, keep=True):
    def loads_of(step):
        y = y0 + step
        right = [field[a + u, y + 1] for u in range(count + 1)]
        conduct = [cond[a + u, y] for u in range(count)]
        above = extra = None
        if step and emitter:
            above = (carry[0, y], carry[1, y])
            extra = [emitter.fetch(a + u, y) for u in range(count)]
        return right, conduct, above, extra

    left = [(tile, up(tile)) for tile in [field[a + u, y0] for u in range(count + 1)]]
    ahead = loads_of(0)
    old, waiting = [None] * count, []
    for step in range(columns):
        y = y0 + step
        right, conduct, above, extra = ahead
        if step + 1 < columns:
            ahead = loads_of(step + 1)
        if len(waiting) > 1:
            for into, at, tile in waiting.pop(0):
                into[at] = tile
        stores = []
        right = [(tile, up(tile)) for tile in right]
        for u in range(count):
            (p0, p0s), (p1, p1s) = left[u], left[u + 1]
            (r0, r0s), (r1, r1s) = right[u], right[u + 1]
            c = conduct[u]
            even = (p0 + r1) + (r0s + p1s)
            odd = (r0 + p1) + (p0s + r1s)
            pass_on = keep or u + 1 < count
            lower = upper = None
            if emitter:
                lower = (c * (odd + p1s), c * (even + p1))
            if pass_on:
                upper = (c * (even + p0s), c * (odd + p0))
            if step and emitter:
                low = (c * (even + r1s) + old[u][0][0]) + above[0]
                high = (c * (odd + r1) + old[u][0][1]) + above[1]
                total = low + pltpu.roll(high, 1, 1)
                stores += emitter.finish(a + u, y, p0, total, extra[u])
            if step and pass_on:
                above = (
                    c * (odd + r0s) + old[u][1][0],
                    c * (even + r0) + old[u][1][1],
                )
            old[u] = (lower, upper)
        if step and keep:
            stores += [(carry, (0, y), above[0]), (carry, (1, y), above[1])]
        waiting.append(stores)
        left = right
    for stores in waiting:
        for into, at, tile in stores:
            into[at] = tile


class First:
    def __init__(self, bx, invx, qx, wx):
        self.bx, self.invx, self.qx, self.wx = bx, invx, qx, wx

    def fetch(self, x, y):
        return self.bx[x, y], self.invx[x, y]

    def finish(self, x, y, node, total, extra):
        source, inverse = extra
        image = 1.25 * source - total
        return [(self.qx, (x, y), image), (self.wx, (x, y), image * inverse)]


class Second:
    def __init__(self, bx, zx, qx, vx, sums):
        self.bx, self.zx, self.qx, self.vx, self.sums = bx, zx, qx, vx, sums

    def fetch(self, x, y):
        return self.bx[x, y], self.zx[x, y], self.qx[x, y]

    def finish(self, x, y, weighted, total, extra):
        source, scaled, image = extra
        again = 1.25 * image - total
        change = scaled - weighted
        sums = self.sums
        sums[0] = sums[0] + source * scaled
        sums[1] = sums[1] + source * change
        sums[2] = sums[2] + (source - image) * change
        sums[3] = sums[3] + (image - again) * change
        return [(self.vx, (x, y), again)]


def over_planes(start, stop, body, state):
    pairs = (stop - start) // 2
    state = lax.fori_loop(0, pairs, lambda i, st: body(start + 2 * i, 2, st), state)
    if (stop - start) % 2:
        state = body(stop - 1, 1, state)
    return state


def inner_kernel(
    s, bt_ref, dens_ref, y1_ref, y2_ref,
    cond, invx, bx, zx, qx, wx, vx, carry1, carry2, sums_ref,
):
    loads, nx, ny, my, pitch = s.loads, s.nx, s.ny, s.my, s.pitch
    bx, zx, qx, wx, vx, carry1, carry2 = (
        Tiles(ref, my, loads) for ref in (bx, zx, qx, wx, vx, carry1, carry2)
    )
    cond, invx = Rows(cond, pitch, loads), Rows(invx, pitch, loads)
    even_y = is_even("gy")
    ys = (pick(even_y, ny + 2, 0), pick(even_y, 0, ny + 2))
    before = None
    for x in range(nx):
        after = conduct_of(dens_ref[x * pitch : (x + 1) * pitch, :])
        cond.put(x + 2, after[1:])
        if x:
            invx.put(x + 2, inverse_of(s, before, after))
        before = after

    def stage(x, y, tile):
        stores = [(bx, (x + 2, y), tile)]
        if x:
            stores.append((zx, (x + 2, y), tile * invx[x + 2, y]))
        return stores

    inner = Tiles(bt_ref, ny, loads)
    batch = Batch(16)
    for x in range(nx):
        for y in range(ny):
            for store in stage(x, y + 2, inner[x, y]):
                batch.add(*store)
    batch.flush()
    for side, ref in enumerate((y1_ref, y2_ref)):
        unpack_tiles(
            ref, 0, loads, 2 * nx, lambda i, tile: stage(i // 2, ys[side] + i % 2, tile)
        )

    element_planes(cond, carry1, 3, 1, 0, my - 1, zx, None)

    def first(a, count, state):
        element_planes(cond, carry1, a, count, 0, my - 1, zx, First(bx, invx, qx, wx))
        return state

    over_planes(4, nx + 1, first, 0)
    element_planes(cond, carry2, 4, 1, 1, my - 3, wx, None)

    def second(a, count, sums):
        sums = list(sums)
        element_planes(cond, carry2, a, count, 1, my - 3, wx, Second(bx, zx, qx, vx, sums))
        return tuple(sums)

    zero = jnp.zeros((loads, LANES), jnp.float32)
    sums = over_planes(5, nx, second, (zero,) * 4)
    for place, part in enumerate(sums):
        sums_ref[place * loads : (place + 1) * loads, :] = part


def outer_kernel(
    s, dens_ref, x1_ref, x2_ref,
    cond1, invx1, bx1, zx1, qx1, wx1, vx1, carry1, carry2, sums1,
    q_out, v_out, inv_out, sums_ref,
    low_ref, high_ref, cond2, invx2, bx2, zx2, qx2, wx2, vx2, carry3,
):
    loads, nx, ny, mx, my, pitch = s.loads, s.nx, s.ny, s.mx, s.my, s.pitch
    even_x = is_even("gx")

    @pl.when(even_x)
    def _():
        low_ref[...] = x2_ref[...]
        high_ref[...] = x1_ref[...]

    @pl.when(jnp.logical_not(even_x))
    def _():
        low_ref[...] = x1_ref[...]
        high_ref[...] = x2_ref[...]

    def joined(first, second, own):
        return Joined(Tiles(first, my, loads), Tiles(second, my, loads), own)

    def joined_rows(first, second, own):
        return Joined(Rows(first, pitch, loads), Rows(second, pitch, loads), own)

    outside = (0, 1, nx + 2, nx + 3)
    scaled_own = outside + (2,)
    image_own = (1, 2, 3, nx + 1, nx + 2)
    cond, invx = joined_rows(cond2, cond1, outside), joined_rows(invx2, invx1, scaled_own)
    bx, zx = joined(bx2, bx1, outside), joined(zx2, zx1, scaled_own)
    qx, wx = joined(qx2, qx1, image_own), joined(wx2, wx1, image_own)
    vx = joined(vx2, vx1, again_planes(nx))
    carry1, carry2, carry3 = (Tiles(ref, my, loads) for ref in (carry1, carry2, carry3))

    def conduct(ref, base, x):
        return conduct_of(ref[base + x * pitch : base + (x + 1) * pitch, :])

    low = [conduct(low_ref, s.x_dens, t) for t in range(3)] + [conduct(dens_ref, 0, 0)]
    high = [conduct(dens_ref, 0, nx - 1)] + [conduct(high_ref, s.x_dens, t) for t in range(2)]
    for x in range(3):
        inverse = inverse_of(s, low[x], low[x + 1])
        invx.put(x, inverse)
        if x < 2:
            cond.put(x, low[x + 1][1:])
    inv_out[...] = inverse[2 : 2 + ny]
    for x in range(2):
        invx.put(nx + 2 + x, inverse_of(s, high[x], high[x + 1]))
    cond.put(nx + 2, high[1][1:])

    for ref, x0 in ((low_ref, 0), (high_ref, nx + 2)):

        def write(i, tile):
            at = x0 + i // my, i % my
            return [(bx, at, tile), (zx, at, tile * invx[at])]

        unpack_tiles(ref, 0, loads, 2 * my, write)
    batch = Batch()
    for y in range(my):
        batch.add(zx, (2, y), bx[2, y] * invx[2, y])
    batch.flush()

    emitter = First(bx, invx, qx, wx)
    element_planes(cond, carry3, 0, 1, 0, my - 1, zx, None)
    element_planes(cond, carry3, 1, 2, 0, my - 1, zx, emitter)
    element_planes(cond, carry3, 3, 1, 0, my - 1, zx, emitter, keep=False)
    element_planes(cond, carry1, nx + 1, 2, 0, my - 1, zx, emitter, keep=False)
    sums = [sums1[place * loads : (place + 1) * loads, :] for place in range(4)]
    emitter = Second(bx, zx, qx, vx, sums)
    element_planes(cond, carry3, 1, 1, 1, my - 3, wx, None)
    element_planes(cond, carry3, 2, 2, 1, my - 3, wx, emitter)
    element_planes(cond, carry3, 4, 1, 1, my - 3, wx, emitter, keep=False)
    element_planes(cond, carry2, nx, 2, 1, my - 3, wx, emitter, keep=False)
    for field, out in ((qx, q_out), (vx, v_out)):
        out = Tiles(out, ny, loads)
        batch = Batch()
        for x in range(nx):
            for y in range(ny):
                batch.add(out, (x, y), field[x + 2, y + 2])
        batch.flush()

    lane = lane_ids(loads)
    load = lax.broadcasted_iota(jnp.int32, (loads, LANES), 0)
    packed = jnp.zeros((loads, LANES), jnp.float32)
    for place, part in enumerate(sums):
        total = jnp.sum(part, axis=1, keepdims=True)
        packed = packed + jnp.where(lane == place * loads + load, total, 0.0)
    row = jnp.sum(packed, axis=0, keepdims=True)
    sums_ref[...] = jnp.broadcast_to(row[None], sums_ref.shape)


def again_planes(nx):
    return (2, 3, 4, nx, nx + 1)


def unpack_kernel(s, q_ref, v_ref, inv1_ref, inv2_ref, qo_ref, vo_ref, io_ref):
    loads, nx, ny = s.loads, s.nx, s.ny
    batch = Batch()
    for x0 in range(0, nx, SUB):
        for ref, out in ((q_ref, qo_ref), (v_ref, vo_ref)):
            for load in range(loads):
                for block in range(packed_count(ny)):
                    tile = pack_block(
                        lambda y: ref[
                            pl.ds((x0 * ny + y) * loads + load, SUB, stride=ny * loads), :
                        ],
                        ny, block, SUB,
                    )
                    lanes = slice(block * LANES, (block + 1) * LANES)
                    batch.add(out, (load, slice(x0, x0 + SUB), lanes), tile)
        for block in range(packed_count(ny)):
            tile = pack_block(
                lambda y: inv1_ref[
                    pl.ds((x0 + 2) * s.pitch + y + 2, SUB, stride=s.pitch), :
                ],
                ny, block, SUB,
            )
            lanes = slice(block * LANES, (block + 1) * LANES)
            batch.add(io_ref, (slice(x0, x0 + SUB), lanes), tile)
    batch.flush()
    for block in range(packed_count(ny)):
        io_ref[0:1, block * LANES : (block + 1) * LANES] = pack_block(
            lambda y: inv2_ref[y : y + 1, :], ny, block, 1
        )


def finish_kernel(s, parts_ref, b_ref, q_ref, v_ref, inv_ref, x_hbm, r_hbm, x_ref, r_ref, sems):
    loads = s.loads
    totals = jnp.sum(parts_ref[...], axis=0)

    def part(place):
        return pltpu.roll(totals, (LANES - place * loads) % LANES, 1) if place else totals

    rz, near, square, last = (part(place) for place in range(4))
    direct = rz - near
    alpha = rz / direct
    short = -near / direct
    rz_next = short * short * rz + 2.0 * alpha * short * near + alpha * alpha * square
    beta = rz_next / rz
    grown = short + beta
    curved = (
        grown * grown * direct
        + 2.0 * alpha * grown * (near - square)
        + alpha * alpha * last
    )
    alpha_next = rz_next / curved
    first_row = alpha + alpha_next * (1.0 + beta)
    second_row = alpha_next * alpha
    inverse = inv_ref[...]
    copies = []
    for load in range(loads):
        first = first_row[:, load : load + 1]
        second = second_row[:, load : load + 1]
        source, image = b_ref[load], q_ref[load]
        x_ref[load] = (first * source - second * image) * inverse
        copies.append(pltpu.make_async_copy(x_ref.at[load], x_hbm.at[load], sems.at[0, load]))
        copies[-1].start()
        r_ref[load] = source - first * image + second * v_ref[load]
        copies.append(pltpu.make_async_copy(r_ref.at[load], r_hbm.at[load], sems.at[1, load]))
        copies[-1].start()
    for copy in copies:
        copy.wait()


def swap(array, axis, start):
    pairs = []
    for i in range(start, lax.axis_size(axis) - 1, 2):
        pairs += [(i, i + 1), (i + 1, i)]
    return lax.ppermute(array, axis, pairs)


def per_device(heat_source, density):
    loads, nx, flat = heat_source.shape
    ny = flat // NZ
    s = Sizes(loads, nx, ny)
    nodes = nx * ny * loads
    devices = lax.axis_size("gx") * lax.axis_size("gy")

    def shape(*dims):
        return jax.ShapeDtypeStruct(dims, jnp.float32)

    def scratch(*dims):
        return pltpu.VMEM(dims, jnp.float32)

    def call(kernel, out_shape, **more):
        params = pltpu.CompilerParams(vmem_limit_bytes=20 * 1024 * 1024)
        return pl.pallas_call(
            functools.partial(kernel, s), out_shape=out_shape, compiler_params=params, **more
        )

    hbm = pl.BlockSpec(memory_space=pltpu.HBM)
    face = shape(s.y_rows, LANES)
    bt, dt, y2 = call(
        pack_kernel,
        (shape(nodes, LANES), shape(nx * ny, LANES), face),
        in_specs=[hbm, hbm],
        scratch_shapes=[
            scratch(loads, nx, flat),
            scratch(nx, flat),
            pltpu.SemaphoreType.DMA((loads + 1,)),
        ],
    )(
        pltpu.with_memory_space_constraint(heat_source, pltpu.HBM),
        pltpu.with_memory_space_constraint(density, pltpu.HBM),
    )
    y2 = swap(y2, "gy", 1)
    y1 = swap(call(pack_near_kernel, face)(bt, dt), "gy", 0)
    dens, x1, x2 = call(
        pack_x_kernel,
        (shape(nx * s.pitch, LANES), shape(s.x_rows, LANES), shape(s.x_rows, LANES)),
        scratch_shapes=[scratch(4 * s.my * loads, LANES)],
    )(bt, dt, y2, y1)
    x1, x2 = swap(x1, "gx", 0), swap(x2, "gx", 1)
    plane = s.my * loads
    rows, field = shape(s.mx * s.pitch, LANES), shape(s.mx * plane, LANES)
    edge = shape(2 * plane, LANES)
    cond, inv_1, bx, zx, q_1, w_1, v_1, carry1, carry2, sums = call(
        inner_kernel, (rows,) * 2 + (field,) * 5 + (edge,) * 2 + (shape(4 * loads, LANES),)
    )(bt, dens, y1, y2)
    q_t, v_t, inv_2, sums = call(
        outer_kernel,
        (
            shape(nodes, LANES),
            shape(nodes, LANES),
            shape(ny, LANES),
            shape(devices, 1, LANES),
        ),
        scratch_shapes=[scratch(s.x_rows, LANES)] * 2
        + [scratch(5 * s.pitch, LANES)] * 2
        + [scratch(5 * plane, LANES)] * 5
        + [scratch(2 * plane, LANES)],
    )(dens, x1, x2, cond, inv_1, bx, zx, q_1, w_1, v_1, carry1, carry2, sums)
    parts = lax.all_to_all(sums, ("gx", "gy"), 0, 0, tiled=True)
    whole = shape(loads, nx, flat)
    image, again, inverse = call(unpack_kernel, (whole, whole, shape(nx, flat)))(
        q_t, v_t, inv_1, inv_2
    )
    return call(
        finish_kernel,
        (whole, whole),
        out_specs=(hbm, hbm),
        scratch_shapes=[
            scratch(loads, nx, flat),
            scratch(loads, nx, flat),
            pltpu.SemaphoreType.DMA((2, loads)),
        ],
    )(parts, heat_source, image, again, inverse)


def solution(mesh):
    placed = (P(None, "gx", "gy"), P("gx", "gy"))
    return jax.shard_map(
        per_device,
        mesh=mesh,
        in_specs=placed,
        out_specs=(P(None, "gx", "gy"), P(None, "gx", "gy")),
        check_vma=False,
    )
```

```python
import functools

import jax
import jax.numpy as jnp
from jax import lax
from jax.experimental import pallas as pl
from jax.experimental.pallas import tpu as pltpu
from jax.sharding import PartitionSpec as P

NZ = 96
KMIN = 0.001
LANES = 128
SUB = 8


class Batch:
    def __init__(self, size=12):
        self.size, self.held = size, []

    def add(self, into, at, tile):
        self.held.append((into, at, tile))
        if len(self.held) >= self.size:
            self.flush()

    def flush(self):
        for into, at, tile in self.held:
            into[at] = tile
        self.held = []


def packed_count(tiles):
    return -(-tiles * NZ // LANES)


def lane_ids(rows):
    return lax.broadcasted_iota(jnp.int32, (rows, LANES), 1)


def unpack_tile(read, index, rows):
    start = index * NZ
    block, offset = start // LANES, start % LANES
    lane = lane_ids(rows)
    first = read(block)
    if offset:
        first = pltpu.roll(first, LANES - offset, 1)
    if offset + NZ > LANES:
        second = pltpu.roll(read(block + 1), LANES - offset, 1)
        first = jnp.where(lane < LANES - offset, first, second)
    return jnp.where(lane < NZ, first, 0.0)


def pack_block(read_tile, tiles, block, rows):
    lane = lane_ids(rows)
    start = block * LANES
    out, at = None, start
    while at < start + LANES and at // NZ < tiles:
        index, z = at // NZ, at % NZ
        here = at - start
        piece = read_tile(index)
        shift = (here - z) % LANES
        if shift:
            piece = pltpu.roll(piece, shift, 1)
        out = piece if out is None else jnp.where(lane < here, out, piece)
        at += NZ - z
    return out


def pack_tiles(out_ref, at, rows, tiles, read_tile):
    batch = Batch()
    for block in range(packed_count(tiles)):
        place = slice(at + block * rows, at + (block + 1) * rows), slice(None)
        batch.add(out_ref, place, pack_block(read_tile, tiles, block, rows))
    batch.flush()


def unpack_tiles(ref, at, rows, tiles, write):
    batch = Batch()
    for index in range(tiles):
        tile = unpack_tile(lambda t: ref[at + t * rows : at + (t + 1) * rows, :], index, rows)
        for store in write(index, tile):
            batch.add(*store)
    batch.flush()


class Sizes:
    def __init__(self, loads, nx, ny):
        self.loads, self.nx, self.ny = loads, nx, ny
        self.mx, self.my = nx + 4, ny + 4
        self.pitch = -(-(ny + 6) // SUB) * SUB
        self.y_dens = packed_count(2 * nx) * loads
        self.y_rows = self.y_dens + 3 * nx
        self.x_dens = packed_count(2 * self.my) * loads
        self.x_rows = self.x_dens + 3 * self.pitch


class Tiles:
    def __init__(self, ref, columns, loads):
        self.ref, self.columns, self.loads = ref, columns, loads

    def rows(self, at):
        start = (at[0] * self.columns + at[1]) * self.loads
        if not isinstance(start, int):
            start = pl.multiple_of(start, SUB)
        return pl.ds(start, self.loads)

    def __getitem__(self, at):
        return self.ref[self.rows(at), :]

    def __setitem__(self, at, tile):
        self.ref[self.rows(at), :] = tile


class Rows:
    def __init__(self, ref, pitch, loads):
        self.ref, self.pitch, self.loads = ref, pitch, loads

    def __getitem__(self, at):
        row = self.ref[pl.ds(at[0] * self.pitch + at[1], 1), :]
        return jnp.broadcast_to(row, (self.loads, LANES))

    def put(self, x, values):
        self.ref[x * self.pitch : x * self.pitch + values.shape[0], :] = values


class Joined:
    def __init__(self, first, second, own):
        self.first, self.second, self.own = first, second, own

    def __getitem__(self, at):
        if at[0] in self.own:
            return self.first[self.own.index(at[0]), at[1]]
        return self.second[at]

    def __setitem__(self, at, tile):
        self.first[self.own.index(at[0]), at[1]] = tile

    def put(self, x, values):
        self.first.put(self.own.index(x), values)


def is_even(axis):
    return lax.rem(lax.axis_index(axis), 2) == 0


def pick(even, if_even, if_odd):
    return jnp.where(even, if_even, if_odd)


def pack_kernel(s, b_hbm, d_hbm, bt_ref, dt_ref, y2_ref, b_ref, d_ref, sems):
    loads, nx, ny = s.loads, s.nx, s.ny
    d_copy = pltpu.make_async_copy(d_hbm, d_ref, sems.at[0])
    d_copy.start()
    parts = 2 if loads % 2 == 0 else 1
    each = loads // parts
    copies = []
    for part in range(parts):
        some = pl.ds(part * each, each)
        copies.append(pltpu.make_async_copy(b_hbm.at[some], b_ref.at[some], sems.at[part + 1]))
        copies[-1].start()
    d_copy.wait()
    batch = Batch(16)
    for x0 in range(0, nx, SUB):
        for y in range(ny):
            tile = unpack_tile(
                lambda t: d_ref[x0 : x0 + SUB, t * LANES : (t + 1) * LANES], y, SUB
            )
            batch.add(dt_ref, (pl.ds(x0 * ny + y, SUB, stride=ny), slice(None)), tile)
    batch.flush()
    for load in range(loads):
        if load % each == 0:
            copies[load // each].wait()
        batch = Batch(16)
        for x0 in range(0, nx, SUB):
            for y in range(ny):
                tile = unpack_tile(
                    lambda t: b_ref[load, x0 : x0 + SUB, t * LANES : (t + 1) * LANES], y, SUB
                )
                rows = pl.ds((x0 * ny + y) * loads + load, SUB, stride=ny * loads)
                batch.add(bt_ref, (rows, slice(None)), tile)
        batch.flush()
    pack_face(s, jnp.logical_not(is_even("gy")), bt_ref, dt_ref, y2_ref)


def pack_near_kernel(s, bt_ref, dt_ref, y1_ref):
    pack_face(s, is_even("gy"), bt_ref, dt_ref, y1_ref)


def pack_face(s, upper, bt_ref, dt_ref, out_ref):
    loads, nx, ny = s.loads, s.nx, s.ny
    tiles = Tiles(bt_ref, ny, loads)
    y0 = pick(upper, ny - 2, 0)
    pack_tiles(out_ref, 0, loads, 2 * nx, lambda i: tiles[i // 2, y0 + i % 2])
    y0 = pick(upper, ny - 3, 0)
    batch = Batch()
    for dy in range(3):
        for x0 in range(0, nx, SUB):
            at = s.y_dens + dy * nx + x0
            tile = dt_ref[pl.ds(x0 * ny + y0 + dy, SUB, stride=ny), :]
            batch.add(out_ref, (slice(at, at + SUB), slice(None)), tile)
    batch.flush()


def open_y_kernel(s, y_ref, t_ref):
    tiles = Tiles(t_ref, 2, s.loads)
    unpack_tiles(
        y_ref, 0, s.loads, 2 * s.nx, lambda i, tile: [(tiles, (i // 2, i % 2), tile)]
    )


def open_x_kernel(s, x_ref, t_ref):
    tiles = Tiles(t_ref, s.my, s.loads)
    unpack_tiles(
        x_ref, 0, s.loads, 2 * s.my, lambda i, tile: [(tiles, (i // s.my, i % s.my), tile)]
    )


def pack_x_kernel(s, bt_ref, dt_ref, y2_ref, t2_ref, y1_ref, dens_ref, x1_ref, x2_ref, edge_ref):
    loads, nx, ny, my, pitch = s.loads, s.nx, s.ny, s.my, s.pitch
    even_x, even_y = is_even("gx"), is_even("gy")
    ys = (pick(even_y, ny + 2, 0), pick(even_y, 0, ny + 2))
    yd = (pick(even_y, ny + 3, 0), pick(even_y, 0, ny + 3))
    for x in range(nx):
        at = x * pitch
        dens_ref[at + 3 : at + 3 + ny, :] = dt_ref[x * ny : (x + 1) * ny, :]
        dens_ref[at + ny + 6 : at + pitch, :] = jnp.zeros((pitch - ny - 6, LANES), jnp.float32)
    for side, ref in enumerate((y1_ref, y2_ref)):
        for dy in range(3):
            for x0 in range(0, nx, SUB):
                at = s.y_dens + dy * nx + x0
                to = x0 * pitch + yd[side] + dy
                dens_ref[pl.ds(to, SUB, stride=pitch), :] = ref[at : at + SUB, :]
    inner, edge = Tiles(bt_ref, ny, loads), Tiles(edge_ref, my, loads)
    far = Tiles(t2_ref, 2, loads)
    batch = Batch()
    for place, x in enumerate((0, 1, nx - 2, nx - 1)):
        for y in range(ny):
            batch.add(edge, (place, y + 2), inner[x, y])
        for dy in range(2):
            tile = unpack_tile(
                lambda t: y1_ref[t * loads : (t + 1) * loads, :], 2 * x + dy, loads
            )
            batch.add(edge, (place, ys[0] + dy), tile)
            batch.add(edge, (place, ys[1] + dy), far[x, dy])
    batch.flush()
    for ref, upper in ((x1_ref, even_x), (x2_ref, jnp.logical_not(even_x))):
        place = pick(upper, 2, 0)
        pack_tiles(ref, 0, loads, 2 * my, lambda i: edge[place + i // my, i % my])
        rows = pl.ds(pl.multiple_of(pick(upper, nx - 3, 0) * pitch, SUB), 3 * pitch)
        ref[s.x_dens :, :] = dens_ref[rows, :]


def conduct_of(dens):
    return jnp.where(
        dens > 0.0, (KMIN + (1.0 - KMIN) * (dens * dens * dens)) * (1.0 / 12.0), 0.0
    )


def inverse_of(s, before, after):
    pair = before + after
    pair = pair[: s.pitch - 1] + pair[1:]
    total = 4.0 * (pair + pltpu.roll(pair, 1, 1))
    return jnp.where(after[1:] > 0.0, 1.0 / total, 0.0)


def up(tile):
    return pltpu.roll(tile, LANES - 1, 1)


def element_planes(cond, carry, a, count, y0, columns, field, emitter, keep=True):
    def loads_of(step):
        y = y0 + step
        right = [field[a + u, y + 1] for u in range(count + 1)]
        conduct = [cond[a + u, y] for u in range(count)]
        above = extra = None
        if step and emitter:
            above = (carry[0, y], carry[1, y])
            extra = [emitter.fetch(a + u, y) for u in range(count)]
        return right, conduct, above, extra

    left = [(tile, up(tile)) for tile in [field[a + u, y0] for u in range(count + 1)]]
    ahead = loads_of(0)
    old, waiting = [None] * count, []
    for step in range(columns):
        y = y0 + step
        right, conduct, above, extra = ahead
        if step + 1 < columns:
            ahead = loads_of(step + 1)
        if len(waiting) > 1:
            for into, at, tile in waiting.pop(0):
                into[at] = tile
        stores = []
        right = [(tile, up(tile)) for tile in right]
        for u in range(count):
            (p0, p0s), (p1, p1s) = left[u], left[u + 1]
            (r0, r0s), (r1, r1s) = right[u], right[u + 1]
            c = conduct[u]
            even = (p0 + r1) + (r0s + p1s)
            odd = (r0 + p1) + (p0s + r1s)
            pass_on = keep or u + 1 < count
            lower = upper = None
            if emitter:
                lower = (c * (odd + p1s), c * (even + p1))
            if pass_on:
                upper = (c * (even + p0s), c * (odd + p0))
            if step and emitter:
                low = (c * (even + r1s) + old[u][0][0]) + above[0]
                high = (c * (odd + r1) + old[u][0][1]) + above[1]
                total = low + pltpu.roll(high, 1, 1)
                stores += emitter.finish(a + u, y, p0, total, extra[u])
            if step and pass_on:
                above = (
                    c * (odd + r0s) + old[u][1][0],
                    c * (even + r0) + old[u][1][1],
                )
            old[u] = (lower, upper)
        if step and keep:
            stores += [(carry, (0, y), above[0]), (carry, (1, y), above[1])]
        waiting.append(stores)
        left = right
    for stores in waiting:
        for into, at, tile in stores:
            into[at] = tile


class First:
    def __init__(self, bx, invx, qx, wx):
        self.bx, self.invx, self.qx, self.wx = bx, invx, qx, wx

    def fetch(self, x, y):
        return self.bx[x, y], self.invx[x, y]

    def finish(self, x, y, node, total, extra):
        source, inverse = extra
        image = 1.25 * source - total
        return [(self.qx, (x, y), image), (self.wx, (x, y), image * inverse)]


class Second:
    def __init__(self, bx, zx, qx, vx, sums):
        self.bx, self.zx, self.qx, self.vx, self.sums = bx, zx, qx, vx, sums

    def fetch(self, x, y):
        return self.bx[x, y], self.zx[x, y], self.qx[x, y]

    def finish(self, x, y, weighted, total, extra):
        source, scaled, image = extra
        again = 1.25 * image - total
        change = scaled - weighted
        sums = self.sums
        sums[0] = sums[0] + source * scaled
        sums[1] = sums[1] + source * change
        sums[2] = sums[2] + (source - image) * change
        sums[3] = sums[3] + (image - again) * change
        return [(self.vx, (x, y), again)]


def over_planes(start, stop, body, state):
    pairs = (stop - start) // 2
    state = lax.fori_loop(0, pairs, lambda i, st: body(start + 2 * i, 2, st), state)
    if (stop - start) % 2:
        state = body(stop - 1, 1, state)
    return state


def inner_kernel(
    s, bt_ref, dens_ref, y1_ref, t2_ref,
    cond, invx, bx, zx, qx, wx, vx, carry1, carry2, sums_ref,
):
    loads, nx, ny, my, pitch = s.loads, s.nx, s.ny, s.my, s.pitch
    bx, zx, qx, wx, vx, carry1, carry2 = (
        Tiles(ref, my, loads) for ref in (bx, zx, qx, wx, vx, carry1, carry2)
    )
    cond, invx = Rows(cond, pitch, loads), Rows(invx, pitch, loads)
    even_y = is_even("gy")
    ys = (pick(even_y, ny + 2, 0), pick(even_y, 0, ny + 2))
    before = None
    for x in range(nx):
        after = conduct_of(dens_ref[x * pitch : (x + 1) * pitch, :])
        cond.put(x + 2, after[1:])
        if x:
            invx.put(x + 2, inverse_of(s, before, after))
        before = after

    def stage(x, y, tile):
        stores = [(bx, (x + 2, y), tile)]
        if x:
            stores.append((zx, (x + 2, y), tile * invx[x + 2, y]))
        return stores

    inner = Tiles(bt_ref, ny, loads)
    batch = Batch(16)
    for x in range(nx):
        for y in range(ny):
            for store in stage(x, y + 2, inner[x, y]):
                batch.add(*store)
    batch.flush()
    unpack_tiles(
        y1_ref, 0, loads, 2 * nx, lambda i, tile: stage(i // 2, ys[0] + i % 2, tile)
    )
    far = Tiles(t2_ref, 2, loads)
    batch = Batch(16)
    for x in range(nx):
        for dy in range(2):
            for store in stage(x, ys[1] + dy, far[x, dy]):
                batch.add(*store)
    batch.flush()

    element_planes(cond, carry1, 3, 1, 0, my - 1, zx, None)

    def first(a, count, state):
        element_planes(cond, carry1, a, count, 0, my - 1, zx, First(bx, invx, qx, wx))
        return state

    over_planes(4, nx + 1, first, 0)
    element_planes(cond, carry2, 4, 1, 1, my - 3, wx, None)

    def second(a, count, sums):
        sums = list(sums)
        element_planes(cond, carry2, a, count, 1, my - 3, wx, Second(bx, zx, qx, vx, sums))
        return tuple(sums)

    zero = jnp.zeros((loads, LANES), jnp.float32)
    sums = over_planes(5, nx, second, (zero,) * 4)
    for place, part in enumerate(sums):
        sums_ref[place * loads : (place + 1) * loads, :] = part


def outer_kernel(
    s, dens_ref, x1_ref, x2_ref, t2_ref,
    cond1, invx1, bx1, zx1, qx1, wx1, vx1, carry1, carry2, sums1,
    q_out, v_out, inv_out, sums_ref,
    low_ref, high_ref, low_d, high_d, cond2, invx2, bx2, zx2, qx2, wx2, vx2, carry3,
):
    loads, nx, ny, mx, my, pitch = s.loads, s.nx, s.ny, s.mx, s.my, s.pitch
    even_x = is_even("gx")

    def take(near, far):
        near_t, near_d = near
        far_t, far_d = far
        unpack_tiles(
            x1_ref, 0, loads, 2 * my,
            lambda i, tile: [(Tiles(near_t, my, loads), (i // my, i % my), tile)],
        )
        far_t[...] = t2_ref[...]
        near_d[...] = x1_ref[s.x_dens :, :]
        far_d[...] = x2_ref[s.x_dens :, :]

    @pl.when(even_x)
    def _():
        take((high_ref, high_d), (low_ref, low_d))

    @pl.when(jnp.logical_not(even_x))
    def _():
        take((low_ref, low_d), (high_ref, high_d))

    def joined(first, second, own):
        return Joined(Tiles(first, my, loads), Tiles(second, my, loads), own)

    def joined_rows(first, second, own):
        return Joined(Rows(first, pitch, loads), Rows(second, pitch, loads), own)

    outside = (0, 1, nx + 2, nx + 3)
    scaled_own = outside + (2,)
    image_own = (1, 2, 3, nx + 1, nx + 2)
    cond, invx = joined_rows(cond2, cond1, outside), joined_rows(invx2, invx1, scaled_own)
    bx, zx = joined(bx2, bx1, outside), joined(zx2, zx1, scaled_own)
    qx, wx = joined(qx2, qx1, image_own), joined(wx2, wx1, image_own)
    vx = joined(vx2, vx1, again_planes(nx))
    carry1, carry2, carry3 = (Tiles(ref, my, loads) for ref in (carry1, carry2, carry3))

    def conduct(ref, x):
        return conduct_of(ref[x * pitch : (x + 1) * pitch, :])

    low = [conduct(low_d, t) for t in range(3)] + [conduct(dens_ref, 0)]
    high = [conduct(dens_ref, nx - 1)] + [conduct(high_d, t) for t in range(2)]
    for x in range(3):
        inverse = inverse_of(s, low[x], low[x + 1])
        invx.put(x, inverse)
        if x < 2:
            cond.put(x, low[x + 1][1:])
    inv_out[...] = inverse[2 : 2 + ny]
    for x in range(2):
        invx.put(nx + 2 + x, inverse_of(s, high[x], high[x + 1]))
    cond.put(nx + 2, high[1][1:])

    batch = Batch(16)
    for ref, x0 in ((low_ref, 0), (high_ref, nx + 2)):
        tiles = Tiles(ref, my, loads)
        for dx in range(2):
            for y in range(my):
                tile = tiles[dx, y]
                batch.add(bx, (x0 + dx, y), tile)
                batch.add(zx, (x0 + dx, y), tile * invx[x0 + dx, y])
    for y in range(my):
        batch.add(zx, (2, y), bx[2, y] * invx[2, y])
    batch.flush()

    emitter = First(bx, invx, qx, wx)
    element_planes(cond, carry3, 0, 1, 0, my - 1, zx, None)
    element_planes(cond, carry3, 1, 2, 0, my - 1, zx, emitter)
    element_planes(cond, carry3, 3, 1, 0, my - 1, zx, emitter, keep=False)
    element_planes(cond, carry1, nx + 1, 2, 0, my - 1, zx, emitter, keep=False)
    sums = [sums1[place * loads : (place + 1) * loads, :] for place in range(4)]
    emitter = Second(bx, zx, qx, vx, sums)
    element_planes(cond, carry3, 1, 1, 1, my - 3, wx, None)
    element_planes(cond, carry3, 2, 2, 1, my - 3, wx, emitter)
    element_planes(cond, carry3, 4, 1, 1, my - 3, wx, emitter, keep=False)
    element_planes(cond, carry2, nx, 2, 1, my - 3, wx, emitter, keep=False)
    for field, out in ((qx, q_out), (vx, v_out)):
        out = Tiles(out, ny, loads)
        batch = Batch()
        for x in range(nx):
            for y in range(ny):
                batch.add(out, (x, y), field[x + 2, y + 2])
        batch.flush()

    lane = lane_ids(loads)
    load = lax.broadcasted_iota(jnp.int32, (loads, LANES), 0)
    packed = jnp.zeros((loads, LANES), jnp.float32)
    for place, part in enumerate(sums):
        total = jnp.sum(part, axis=1, keepdims=True)
        packed = packed + jnp.where(lane == place * loads + load, total, 0.0)
    row = jnp.sum(packed, axis=0, keepdims=True)
    sums_ref[...] = jnp.broadcast_to(row[None], sums_ref.shape)


def again_planes(nx):
    return (2, 3, 4, nx, nx + 1)


def unpack_kernel(s, q_ref, v_ref, inv1_ref, inv2_ref, qo_ref, vo_ref, io_ref):
    loads, nx, ny = s.loads, s.nx, s.ny
    batch = Batch()
    for x0 in range(0, nx, SUB):
        for ref, out in ((q_ref, qo_ref), (v_ref, vo_ref)):
            for load in range(loads):
                for block in range(packed_count(ny)):
                    tile = pack_block(
                        lambda y: ref[
                            pl.ds((x0 * ny + y) * loads + load, SUB, stride=ny * loads), :
                        ],
                        ny, block, SUB,
                    )
                    lanes = slice(block * LANES, (block + 1) * LANES)
                    batch.add(out, (load, slice(x0, x0 + SUB), lanes), tile)
        for block in range(packed_count(ny)):
            tile = pack_block(
                lambda y: inv1_ref[
                    pl.ds((x0 + 2) * s.pitch + y + 2, SUB, stride=s.pitch), :
                ],
                ny, block, SUB,
            )
            lanes = slice(block * LANES, (block + 1) * LANES)
            batch.add(io_ref, (slice(x0, x0 + SUB), lanes), tile)
    batch.flush()
    for block in range(packed_count(ny)):
        io_ref[0:1, block * LANES : (block + 1) * LANES] = pack_block(
            lambda y: inv2_ref[y : y + 1, :], ny, block, 1
        )


def finish_kernel(s, parts_ref, b_ref, q_ref, v_ref, inv_ref, x_hbm, r_hbm, x_ref, r_ref, sems):
    loads = s.loads
    totals = jnp.sum(parts_ref[...], axis=0)

    def part(place):
        return pltpu.roll(totals, (LANES - place * loads) % LANES, 1) if place else totals

    rz, near, square, last = (part(place) for place in range(4))
    direct = rz - near
    alpha = rz / direct
    short = -near / direct
    rz_next = short * short * rz + 2.0 * alpha * short * near + alpha * alpha * square
    beta = rz_next / rz
    grown = short + beta
    curved = (
        grown * grown * direct
        + 2.0 * alpha * grown * (near - square)
        + alpha * alpha * last
    )
    alpha_next = rz_next / curved
    first_row = alpha + alpha_next * (1.0 + beta)
    second_row = alpha_next * alpha
    inverse = inv_ref[...]
    copies = []
    for load in range(loads):
        first = first_row[:, load : load + 1]
        second = second_row[:, load : load + 1]
        source, image = b_ref[load], q_ref[load]
        x_ref[load] = (first * source - second * image) * inverse
        copies.append(pltpu.make_async_copy(x_ref.at[load], x_hbm.at[load], sems.at[0, load]))
        copies[-1].start()
        r_ref[load] = source - first * image + second * v_ref[load]
        copies.append(pltpu.make_async_copy(r_ref.at[load], r_hbm.at[load], sems.at[1, load]))
        copies[-1].start()
    for copy in copies:
        copy.wait()


def swap(array, axis, start):
    pairs = []
    for i in range(start, lax.axis_size(axis) - 1, 2):
        pairs += [(i, i + 1), (i + 1, i)]
    return lax.ppermute(array, axis, pairs)


def per_device(heat_source, density):
    loads, nx, flat = heat_source.shape
    ny = flat // NZ
    s = Sizes(loads, nx, ny)
    nodes = nx * ny * loads
    devices = lax.axis_size("gx") * lax.axis_size("gy")

    def shape(*dims):
        return jax.ShapeDtypeStruct(dims, jnp.float32)

    def scratch(*dims):
        return pltpu.VMEM(dims, jnp.float32)

    def call(kernel, out_shape, **more):
        params = pltpu.CompilerParams(vmem_limit_bytes=20 * 1024 * 1024)
        return pl.pallas_call(
            functools.partial(kernel, s), out_shape=out_shape, compiler_params=params, **more
        )

    hbm = pl.BlockSpec(memory_space=pltpu.HBM)
    face = shape(s.y_rows, LANES)
    bt, dt, y2 = call(
        pack_kernel,
        (shape(nodes, LANES), shape(nx * ny, LANES), face),
        in_specs=[hbm, hbm],
        scratch_shapes=[
            scratch(loads, nx, flat),
            scratch(nx, flat),
            pltpu.SemaphoreType.DMA((3,)),
        ],
    )(
        pltpu.with_memory_space_constraint(heat_source, pltpu.HBM),
        pltpu.with_memory_space_constraint(density, pltpu.HBM),
    )
    y2 = swap(y2, "gy", 1)
    y1 = swap(call(pack_near_kernel, face)(bt, dt), "gy", 0)
    t2 = call(open_y_kernel, shape(2 * nx * loads, LANES))(y2)
    dens, x1, x2 = call(
        pack_x_kernel,
        (shape(nx * s.pitch, LANES), shape(s.x_rows, LANES), shape(s.x_rows, LANES)),
        scratch_shapes=[scratch(4 * s.my * loads, LANES)],
    )(bt, dt, y2, t2, y1)
    x1, x2 = swap(x1, "gx", 0), swap(x2, "gx", 1)
    plane = s.my * loads
    rows, field = shape(s.mx * s.pitch, LANES), shape(s.mx * plane, LANES)
    edge = shape(2 * plane, LANES)
    cond, inv_1, bx, zx, q_1, w_1, v_1, carry1, carry2, sums = call(
        inner_kernel, (rows,) * 2 + (field,) * 5 + (edge,) * 2 + (shape(4 * loads, LANES),)
    )(bt, dens, y1, t2)
    xt2 = call(open_x_kernel, shape(2 * plane, LANES))(x2)
    q_t, v_t, inv_2, sums = call(
        outer_kernel,
        (
            shape(nodes, LANES),
            shape(nodes, LANES),
            shape(ny, LANES),
            shape(devices, 1, LANES),
        ),
        scratch_shapes=[scratch(2 * plane, LANES)] * 2
        + [scratch(3 * s.pitch, LANES)] * 2
        + [scratch(5 * s.pitch, LANES)] * 2
        + [scratch(5 * plane, LANES)] * 5
        + [scratch(2 * plane, LANES)],
    )(dens, x1, x2, xt2, cond, inv_1, bx, zx, q_1, w_1, v_1, carry1, carry2, sums)
    parts = lax.all_to_all(sums, ("gx", "gy"), 0, 0, tiled=True)
    whole = shape(loads, nx, flat)
    image, again, inverse = call(unpack_kernel, (whole, whole, shape(nx, flat)))(
        q_t, v_t, inv_1, inv_2
    )
    return call(
        finish_kernel,
        (whole, whole),
        out_specs=(hbm, hbm),
        scratch_shapes=[
            scratch(loads, nx, flat),
            scratch(loads, nx, flat),
            pltpu.SemaphoreType.DMA((2, loads)),
        ],
    )(parts, heat_source, image, again, inverse)


def solution(mesh):
    placed = (P(None, "gx", "gy"), P("gx", "gy"))
    return jax.shard_map(
        per_device,
        mesh=mesh,
        in_specs=placed,
        out_specs=(P(None, "gx", "gy"), P(None, "gx", "gy")),
        check_vma=False,
    )
```

```python
import functools

import jax
import jax.numpy as jnp
from jax import lax
from jax.experimental import pallas as pl
from jax.experimental.pallas import tpu as pltpu
from jax.sharding import PartitionSpec as P

NZ = 96
KMIN = 0.001
LANES = 128
SUB = 8


class Batch:
    def __init__(self, size=12):
        self.size, self.held = size, []

    def add(self, into, at, tile):
        self.held.append((into, at, tile))
        if len(self.held) >= self.size:
            self.flush()

    def flush(self):
        for into, at, tile in self.held:
            into[at] = tile
        self.held = []


def packed_count(tiles):
    return -(-tiles * NZ // LANES)


def lane_ids(rows):
    return lax.broadcasted_iota(jnp.int32, (rows, LANES), 1)


def unpack_tile(read, index, rows):
    start = index * NZ
    block, offset = start // LANES, start % LANES
    lane = lane_ids(rows)
    first = read(block)
    if offset:
        first = pltpu.roll(first, LANES - offset, 1)
    if offset + NZ > LANES:
        second = pltpu.roll(read(block + 1), LANES - offset, 1)
        first = jnp.where(lane < LANES - offset, first, second)
    return jnp.where(lane < NZ, first, 0.0)


def pack_block(read_tile, tiles, block, rows):
    lane = lane_ids(rows)
    start = block * LANES
    out, at = None, start
    while at < start + LANES and at // NZ < tiles:
        index, z = at // NZ, at % NZ
        here = at - start
        piece = read_tile(index)
        shift = (here - z) % LANES
        if shift:
            piece = pltpu.roll(piece, shift, 1)
        out = piece if out is None else jnp.where(lane < here, out, piece)
        at += NZ - z
    return out


def pack_tiles(out_ref, at, rows, tiles, read_tile):
    batch = Batch()
    for block in range(packed_count(tiles)):
        place = slice(at + block * rows, at + (block + 1) * rows), slice(None)
        batch.add(out_ref, place, pack_block(read_tile, tiles, block, rows))
    batch.flush()


def unpack_tiles(ref, at, rows, tiles, write):
    batch = Batch()
    for index in range(tiles):
        tile = unpack_tile(lambda t: ref[at + t * rows : at + (t + 1) * rows, :], index, rows)
        for store in write(index, tile):
            batch.add(*store)
    batch.flush()


class Sizes:
    def __init__(self, loads, nx, ny, count_x, count_y):
        self.loads, self.nx, self.ny = loads, nx, ny
        self.count_x, self.count_y = count_x, count_y
        self.mx, self.my = nx + 4, ny + 4
        self.pitch = -(-(ny + 6) // SUB) * SUB
        self.y_dens = packed_count(2 * nx) * loads
        self.y_rows = self.y_dens + 3 * nx
        self.x_dens = packed_count(2 * self.my) * loads
        self.x_rows = self.x_dens + 3 * self.pitch


class Tiles:
    def __init__(self, ref, columns, loads):
        self.ref, self.columns, self.loads = ref, columns, loads

    def rows(self, at):
        start = (at[0] * self.columns + at[1]) * self.loads
        if not isinstance(start, int):
            start = pl.multiple_of(start, SUB)
        return pl.ds(start, self.loads)

    def __getitem__(self, at):
        return self.ref[self.rows(at), :]

    def __setitem__(self, at, tile):
        self.ref[self.rows(at), :] = tile


class Rows:
    def __init__(self, ref, pitch, loads):
        self.ref, self.pitch, self.loads = ref, pitch, loads

    def __getitem__(self, at):
        row = self.ref[pl.ds(at[0] * self.pitch + at[1], 1), :]
        return jnp.broadcast_to(row, (self.loads, LANES))

    def put(self, x, values):
        self.ref[x * self.pitch : x * self.pitch + values.shape[0], :] = values


class Joined:
    def __init__(self, first, second, own):
        self.first, self.second, self.own = first, second, own

    def __getitem__(self, at):
        if at[0] in self.own:
            return self.first[self.own.index(at[0]), at[1]]
        return self.second[at]

    def __setitem__(self, at, tile):
        self.first[self.own.index(at[0]), at[1]] = tile

    def put(self, x, values):
        self.first.put(self.own.index(x), values)


def is_even(axis):
    return lax.rem(lax.axis_index(axis), 2) == 0


def is_alone(axis, count, start):
    place = lax.axis_index(axis)
    last = (count - start) % 2
    alone = place < start
    return jnp.logical_or(alone, place == count - 1) if last else alone


def pick(even, if_even, if_odd):
    return jnp.where(even, if_even, if_odd)


def pack_kernel(s, b_hbm, d_hbm, bt_ref, dt_ref, y2_ref, b_ref, d_ref, sems):
    loads, nx, ny = s.loads, s.nx, s.ny
    d_copy = pltpu.make_async_copy(d_hbm, d_ref, sems.at[0])
    d_copy.start()
    parts = 2 if loads % 2 == 0 else 1
    each = loads // parts
    copies = []
    for part in range(parts):
        some = pl.ds(part * each, each)
        copies.append(pltpu.make_async_copy(b_hbm.at[some], b_ref.at[some], sems.at[part + 1]))
        copies[-1].start()
    d_copy.wait()
    batch = Batch(16)
    for x0 in range(0, nx, SUB):
        for y in range(ny):
            tile = unpack_tile(
                lambda t: d_ref[x0 : x0 + SUB, t * LANES : (t + 1) * LANES], y, SUB
            )
            batch.add(dt_ref, (pl.ds(x0 * ny + y, SUB, stride=ny), slice(None)), tile)
    batch.flush()
    for load in range(loads):
        if load % each == 0:
            copies[load // each].wait()
        batch = Batch(16)
        for x0 in range(0, nx, SUB):
            for y in range(ny):
                tile = unpack_tile(
                    lambda t: b_ref[load, x0 : x0 + SUB, t * LANES : (t + 1) * LANES], y, SUB
                )
                rows = pl.ds((x0 * ny + y) * loads + load, SUB, stride=ny * loads)
                batch.add(bt_ref, (rows, slice(None)), tile)
        batch.flush()
    pack_face(s, jnp.logical_not(is_even("gy")), bt_ref, dt_ref, y2_ref)


def pack_near_kernel(s, bt_ref, dt_ref, y1_ref):
    pack_face(s, is_even("gy"), bt_ref, dt_ref, y1_ref)


def pack_face(s, upper, bt_ref, dt_ref, out_ref):
    loads, nx, ny = s.loads, s.nx, s.ny
    tiles = Tiles(bt_ref, ny, loads)
    y0 = pick(upper, ny - 2, 0)
    pack_tiles(out_ref, 0, loads, 2 * nx, lambda i: tiles[i // 2, y0 + i % 2])
    y0 = pick(upper, ny - 3, 0)
    batch = Batch()
    for dy in range(3):
        for x0 in range(0, nx, SUB):
            at = s.y_dens + dy * nx + x0
            tile = dt_ref[pl.ds(x0 * ny + y0 + dy, SUB, stride=ny), :]
            batch.add(out_ref, (slice(at, at + SUB), slice(None)), tile)
    batch.flush()


def open_y_kernel(s, y_ref, t_ref):
    tiles = Tiles(t_ref, 2, s.loads)
    unpack_tiles(
        y_ref, 0, s.loads, 2 * s.nx, lambda i, tile: [(tiles, (i // 2, i % 2), tile)]
    )


def open_x_kernel(s, x_ref, t_ref):
    tiles = Tiles(t_ref, s.my, s.loads)
    unpack_tiles(
        x_ref, 0, s.loads, 2 * s.my, lambda i, tile: [(tiles, (i // s.my, i % s.my), tile)]
    )


def pack_x_kernel(s, bt_ref, dt_ref, y2_ref, t2_ref, y1_ref, dens_ref, x1_ref, x2_ref, edge_ref):
    loads, nx, ny, my, pitch = s.loads, s.nx, s.ny, s.my, s.pitch
    even_x, even_y = is_even("gx"), is_even("gy")
    ys = (pick(even_y, ny + 2, 0), pick(even_y, 0, ny + 2))
    yd = (pick(even_y, ny + 3, 0), pick(even_y, 0, ny + 3))
    for x in range(nx):
        at = x * pitch
        dens_ref[at + 3 : at + 3 + ny, :] = dt_ref[x * ny : (x + 1) * ny, :]
        dens_ref[at + ny + 6 : at + pitch, :] = jnp.zeros((pitch - ny - 6, LANES), jnp.float32)
    for side, ref in enumerate((y1_ref, y2_ref)):
        alone = is_alone("gy", s.count_y, side)
        for dy in range(3):
            for x0 in range(0, nx, SUB):
                at = s.y_dens + dy * nx + x0
                to = x0 * pitch + yd[side] + dy
                dens_ref[pl.ds(to, SUB, stride=pitch), :] = jnp.where(
                    alone, 0.0, ref[at : at + SUB, :]
                )
    inner, edge = Tiles(bt_ref, ny, loads), Tiles(edge_ref, my, loads)
    far = Tiles(t2_ref, 2, loads)
    batch = Batch()
    for place, x in enumerate((0, 1, nx - 2, nx - 1)):
        for y in range(ny):
            batch.add(edge, (place, y + 2), inner[x, y])
        for dy in range(2):
            tile = unpack_tile(
                lambda t: y1_ref[t * loads : (t + 1) * loads, :], 2 * x + dy, loads
            )
            batch.add(edge, (place, ys[0] + dy), tile)
            batch.add(edge, (place, ys[1] + dy), far[x, dy])
    batch.flush()
    for ref, upper in ((x1_ref, even_x), (x2_ref, jnp.logical_not(even_x))):
        place = pick(upper, 2, 0)
        pack_tiles(ref, 0, loads, 2 * my, lambda i: edge[place + i // my, i % my])
        rows = pl.ds(pl.multiple_of(pick(upper, nx - 3, 0) * pitch, SUB), 3 * pitch)
        ref[s.x_dens :, :] = dens_ref[rows, :]


def conduct_of(dens):
    return jnp.where(
        dens > 0.0, (KMIN + (1.0 - KMIN) * (dens * dens * dens)) * (1.0 / 12.0), 0.0
    )


def inverse_of(s, before, after):
    pair = before + after
    pair = pair[: s.pitch - 1] + pair[1:]
    total = 4.0 * (pair + pltpu.roll(pair, 1, 1))
    return jnp.where(after[1:] > 0.0, 1.0 / total, 0.0)


def up(tile):
    return pltpu.roll(tile, LANES - 1, 1)


def element_planes(cond, carry, a, count, y0, columns, field, emitter, keep=True):
    def loads_of(step):
        y = y0 + step
        right = [field[a + u, y + 1] for u in range(count + 1)]
        conduct = [cond[a + u, y] for u in range(count)]
        above = extra = None
        if step and emitter:
            above = (carry[0, y], carry[1, y])
            extra = [emitter.fetch(a + u, y) for u in range(count)]
        return right, conduct, above, extra

    left = [(tile, up(tile)) for tile in [field[a + u, y0] for u in range(count + 1)]]
    ahead = loads_of(0)
    old, waiting = [None] * count, []
    for step in range(columns):
        y = y0 + step
        right, conduct, above, extra = ahead
        if step + 1 < columns:
            ahead = loads_of(step + 1)
        if len(waiting) > 1:
            for into, at, tile in waiting.pop(0):
                into[at] = tile
        stores = []
        right = [(tile, up(tile)) for tile in right]
        for u in range(count):
            (p0, p0s), (p1, p1s) = left[u], left[u + 1]
            (r0, r0s), (r1, r1s) = right[u], right[u + 1]
            c = conduct[u]
            even = (p0 + r1) + (r0s + p1s)
            odd = (r0 + p1) + (p0s + r1s)
            pass_on = keep or u + 1 < count
            lower = upper = None
            if emitter:
                lower = (c * (odd + p1s), c * (even + p1))
            if pass_on:
                upper = (c * (even + p0s), c * (odd + p0))
            if step and emitter:
                low = (c * (even + r1s) + old[u][0][0]) + above[0]
                high = (c * (odd + r1) + old[u][0][1]) + above[1]
                total = low + pltpu.roll(high, 1, 1)
                stores += emitter.finish(a + u, y, p0, total, extra[u])
            if step and pass_on:
                above = (
                    c * (odd + r0s) + old[u][1][0],
                    c * (even + r0) + old[u][1][1],
                )
            old[u] = (lower, upper)
        if step and keep:
            stores += [(carry, (0, y), above[0]), (carry, (1, y), above[1])]
        waiting.append(stores)
        left = right
    for stores in waiting:
        for into, at, tile in stores:
            into[at] = tile


class First:
    def __init__(self, bx, invx, qx, wx):
        self.bx, self.invx, self.qx, self.wx = bx, invx, qx, wx

    def fetch(self, x, y):
        return self.bx[x, y], self.invx[x, y]

    def finish(self, x, y, node, total, extra):
        source, inverse = extra
        image = 1.25 * source - total
        return [(self.qx, (x, y), image), (self.wx, (x, y), image * inverse)]


class Second:
    def __init__(self, bx, zx, qx, vx, sums):
        self.bx, self.zx, self.qx, self.vx, self.sums = bx, zx, qx, vx, sums

    def fetch(self, x, y):
        return self.bx[x, y], self.zx[x, y], self.qx[x, y]

    def finish(self, x, y, weighted, total, extra):
        source, scaled, image = extra
        again = 1.25 * image - total
        change = scaled - weighted
        sums = self.sums
        sums[0] = sums[0] + source * scaled
        sums[1] = sums[1] + source * change
        sums[2] = sums[2] + (source - image) * change
        sums[3] = sums[3] + (image - again) * change
        return [(self.vx, (x, y), again)]


def over_planes(start, stop, body, state):
    pairs = (stop - start) // 2
    state = lax.fori_loop(0, pairs, lambda i, st: body(start + 2 * i, 2, st), state)
    if (stop - start) % 2:
        state = body(stop - 1, 1, state)
    return state


def inner_kernel(
    s, bt_ref, dens_ref, y1_ref, t2_ref,
    cond, invx, bx, zx, qx, wx, vx, carry1, carry2, sums_ref,
):
    loads, nx, ny, my, pitch = s.loads, s.nx, s.ny, s.my, s.pitch
    bx, zx, qx, wx, vx, carry1, carry2 = (
        Tiles(ref, my, loads) for ref in (bx, zx, qx, wx, vx, carry1, carry2)
    )
    cond, invx = Rows(cond, pitch, loads), Rows(invx, pitch, loads)
    even_y = is_even("gy")
    ys = (pick(even_y, ny + 2, 0), pick(even_y, 0, ny + 2))
    before = None
    for x in range(nx):
        after = conduct_of(dens_ref[x * pitch : (x + 1) * pitch, :])
        cond.put(x + 2, after[1:])
        if x:
            invx.put(x + 2, inverse_of(s, before, after))
        before = after

    def stage(x, y, tile):
        stores = [(bx, (x + 2, y), tile)]
        if x:
            stores.append((zx, (x + 2, y), tile * invx[x + 2, y]))
        return stores

    inner = Tiles(bt_ref, ny, loads)
    batch = Batch(16)
    for x in range(nx):
        for y in range(ny):
            for store in stage(x, y + 2, inner[x, y]):
                batch.add(*store)
    batch.flush()
    unpack_tiles(
        y1_ref, 0, loads, 2 * nx, lambda i, tile: stage(i // 2, ys[0] + i % 2, tile)
    )
    far = Tiles(t2_ref, 2, loads)
    batch = Batch(16)
    for x in range(nx):
        for dy in range(2):
            for store in stage(x, ys[1] + dy, far[x, dy]):
                batch.add(*store)
    batch.flush()

    element_planes(cond, carry1, 3, 1, 0, my - 1, zx, None)

    def first(a, count, state):
        element_planes(cond, carry1, a, count, 0, my - 1, zx, First(bx, invx, qx, wx))
        return state

    over_planes(4, nx + 1, first, 0)
    element_planes(cond, carry2, 4, 1, 1, my - 3, wx, None)

    def second(a, count, sums):
        sums = list(sums)
        element_planes(cond, carry2, a, count, 1, my - 3, wx, Second(bx, zx, qx, vx, sums))
        return tuple(sums)

    zero = jnp.zeros((loads, LANES), jnp.float32)
    sums = over_planes(5, nx, second, (zero,) * 4)
    for place, part in enumerate(sums):
        sums_ref[place * loads : (place + 1) * loads, :] = part


def outer_kernel(
    s, dens_ref, x1_ref, x2_ref, t2_ref,
    cond1, invx1, bx1, zx1, qx1, wx1, vx1, carry1, carry2, sums1,
    q_out, v_out, inv_out, sums_ref,
    low_ref, high_ref, low_d, high_d, cond2, invx2, bx2, zx2, qx2, wx2, vx2, carry3,
):
    loads, nx, ny, mx, my, pitch = s.loads, s.nx, s.ny, s.mx, s.my, s.pitch
    even_x = is_even("gx")

    def take(near, far):
        near_t, near_d = near
        far_t, far_d = far
        unpack_tiles(
            x1_ref, 0, loads, 2 * my,
            lambda i, tile: [(Tiles(near_t, my, loads), (i // my, i % my), tile)],
        )
        far_t[...] = t2_ref[...]
        for into, ref, start in ((near_d, x1_ref, 0), (far_d, x2_ref, 1)):
            alone = is_alone("gx", s.count_x, start)
            into[...] = jnp.where(alone, 0.0, ref[s.x_dens :, :])

    @pl.when(even_x)
    def _():
        take((high_ref, high_d), (low_ref, low_d))

    @pl.when(jnp.logical_not(even_x))
    def _():
        take((low_ref, low_d), (high_ref, high_d))

    def joined(first, second, own):
        return Joined(Tiles(first, my, loads), Tiles(second, my, loads), own)

    def joined_rows(first, second, own):
        return Joined(Rows(first, pitch, loads), Rows(second, pitch, loads), own)

    outside = (0, 1, nx + 2, nx + 3)
    scaled_own = outside + (2,)
    image_own = (1, 2, 3, nx + 1, nx + 2)
    cond, invx = joined_rows(cond2, cond1, outside), joined_rows(invx2, invx1, scaled_own)
    bx, zx = joined(bx2, bx1, outside), joined(zx2, zx1, scaled_own)
    qx, wx = joined(qx2, qx1, image_own), joined(wx2, wx1, image_own)
    vx = joined(vx2, vx1, again_planes(nx))
    carry1, carry2, carry3 = (Tiles(ref, my, loads) for ref in (carry1, carry2, carry3))

    def conduct(ref, x):
        return conduct_of(ref[x * pitch : (x + 1) * pitch, :])

    low = [conduct(low_d, t) for t in range(3)] + [conduct(dens_ref, 0)]
    high = [conduct(dens_ref, nx - 1)] + [conduct(high_d, t) for t in range(2)]
    for x in range(3):
        inverse = inverse_of(s, low[x], low[x + 1])
        invx.put(x, inverse)
        if x < 2:
            cond.put(x, low[x + 1][1:])
    inv_out[...] = inverse[2 : 2 + ny]
    for x in range(2):
        invx.put(nx + 2 + x, inverse_of(s, high[x], high[x + 1]))
    cond.put(nx + 2, high[1][1:])

    batch = Batch(16)
    for ref, x0 in ((low_ref, 0), (high_ref, nx + 2)):
        tiles = Tiles(ref, my, loads)
        for dx in range(2):
            for y in range(my):
                tile = tiles[dx, y]
                batch.add(bx, (x0 + dx, y), tile)
                batch.add(zx, (x0 + dx, y), tile * invx[x0 + dx, y])
    for y in range(my):
        batch.add(zx, (2, y), bx[2, y] * invx[2, y])
    batch.flush()

    emitter = First(bx, invx, qx, wx)
    element_planes(cond, carry3, 0, 1, 0, my - 1, zx, None)
    element_planes(cond, carry3, 1, 2, 0, my - 1, zx, emitter)
    element_planes(cond, carry3, 3, 1, 0, my - 1, zx, emitter, keep=False)
    element_planes(cond, carry1, nx + 1, 2, 0, my - 1, zx, emitter, keep=False)
    sums = [sums1[place * loads : (place + 1) * loads, :] for place in range(4)]
    emitter = Second(bx, zx, qx, vx, sums)
    element_planes(cond, carry3, 1, 1, 1, my - 3, wx, None)
    element_planes(cond, carry3, 2, 2, 1, my - 3, wx, emitter)
    element_planes(cond, carry3, 4, 1, 1, my - 3, wx, emitter, keep=False)
    element_planes(cond, carry2, nx, 2, 1, my - 3, wx, emitter, keep=False)
    for field, out in ((qx, q_out), (vx, v_out)):
        out = Tiles(out, ny, loads)
        batch = Batch()
        for x in range(nx):
            for y in range(ny):
                batch.add(out, (x, y), field[x + 2, y + 2])
        batch.flush()

    lane = lane_ids(loads)
    load = lax.broadcasted_iota(jnp.int32, (loads, LANES), 0)
    packed = jnp.zeros((loads, LANES), jnp.float32)
    for place, part in enumerate(sums):
        total = jnp.sum(part, axis=1, keepdims=True)
        packed = packed + jnp.where(lane == place * loads + load, total, 0.0)
    row = jnp.sum(packed, axis=0, keepdims=True)
    sums_ref[...] = jnp.broadcast_to(row[None], sums_ref.shape)


def again_planes(nx):
    return (2, 3, 4, nx, nx + 1)


def unpack_kernel(s, q_ref, v_ref, inv1_ref, inv2_ref, qo_ref, vo_ref, io_ref):
    loads, nx, ny = s.loads, s.nx, s.ny
    batch = Batch()
    for x0 in range(0, nx, SUB):
        for ref, out in ((q_ref, qo_ref), (v_ref, vo_ref)):
            for load in range(loads):
                for block in range(packed_count(ny)):
                    tile = pack_block(
                        lambda y: ref[
                            pl.ds((x0 * ny + y) * loads + load, SUB, stride=ny * loads), :
                        ],
                        ny, block, SUB,
                    )
                    lanes = slice(block * LANES, (block + 1) * LANES)
                    batch.add(out, (load, slice(x0, x0 + SUB), lanes), tile)
        for block in range(packed_count(ny)):
            tile = pack_block(
                lambda y: inv1_ref[
                    pl.ds((x0 + 2) * s.pitch + y + 2, SUB, stride=s.pitch), :
                ],
                ny, block, SUB,
            )
            lanes = slice(block * LANES, (block + 1) * LANES)
            batch.add(io_ref, (slice(x0, x0 + SUB), lanes), tile)
    batch.flush()
    for block in range(packed_count(ny)):
        io_ref[0:1, block * LANES : (block + 1) * LANES] = pack_block(
            lambda y: inv2_ref[y : y + 1, :], ny, block, 1
        )


def finish_kernel(s, parts_ref, b_ref, q_ref, v_ref, inv_ref, x_hbm, r_hbm, x_ref, r_ref, sems):
    loads = s.loads
    totals = jnp.sum(parts_ref[...], axis=0)

    def part(place):
        return pltpu.roll(totals, (LANES - place * loads) % LANES, 1) if place else totals

    rz, near, square, last = (part(place) for place in range(4))
    direct = rz - near
    alpha = rz / direct
    short = -near / direct
    rz_next = short * short * rz + 2.0 * alpha * short * near + alpha * alpha * square
    beta = rz_next / rz
    grown = short + beta
    curved = (
        grown * grown * direct
        + 2.0 * alpha * grown * (near - square)
        + alpha * alpha * last
    )
    alpha_next = rz_next / curved
    first_row = alpha + alpha_next * (1.0 + beta)
    second_row = alpha_next * alpha
    inverse = inv_ref[...]
    copies = []
    for load in range(loads):
        first = first_row[:, load : load + 1]
        second = second_row[:, load : load + 1]
        source, image = b_ref[load], q_ref[load]
        x_ref[load] = (first * source - second * image) * inverse
        copies.append(pltpu.make_async_copy(x_ref.at[load], x_hbm.at[load], sems.at[0, load]))
        copies[-1].start()
        r_ref[load] = source - first * image + second * v_ref[load]
        copies.append(pltpu.make_async_copy(r_ref.at[load], r_hbm.at[load], sems.at[1, load]))
        copies[-1].start()
    for copy in copies:
        copy.wait()


def swap(array, axis, start):
    count = lax.axis_size(axis)
    target = list(range(count))
    for i in range(start, count - 1, 2):
        target[i], target[i + 1] = i + 1, i
    ends = [i for i in range(count) if target[i] == i]
    if len(ends) == 2:
        target[ends[0]], target[ends[1]] = ends[1], ends[0]
    return lax.ppermute(array, axis, list(enumerate(target)))


def per_device(heat_source, density):
    loads, nx, flat = heat_source.shape
    ny = flat // NZ
    s = Sizes(loads, nx, ny, lax.axis_size("gx"), lax.axis_size("gy"))
    nodes = nx * ny * loads
    devices = lax.axis_size("gx") * lax.axis_size("gy")

    def shape(*dims):
        return jax.ShapeDtypeStruct(dims, jnp.float32)

    def scratch(*dims):
        return pltpu.VMEM(dims, jnp.float32)

    def call(kernel, out_shape, **more):
        params = pltpu.CompilerParams(vmem_limit_bytes=20 * 1024 * 1024)
        return pl.pallas_call(
            functools.partial(kernel, s), out_shape=out_shape, compiler_params=params, **more
        )

    hbm = pl.BlockSpec(memory_space=pltpu.HBM)
    face = shape(s.y_rows, LANES)
    bt, dt, y2 = call(
        pack_kernel,
        (shape(nodes, LANES), shape(nx * ny, LANES), face),
        in_specs=[hbm, hbm],
        scratch_shapes=[
            scratch(loads, nx, flat),
            scratch(nx, flat),
            pltpu.SemaphoreType.DMA((3,)),
        ],
    )(
        pltpu.with_memory_space_constraint(heat_source, pltpu.HBM),
        pltpu.with_memory_space_constraint(density, pltpu.HBM),
    )
    y2 = swap(y2, "gy", 1)
    y1 = swap(call(pack_near_kernel, face)(bt, dt), "gy", 0)
    t2 = call(open_y_kernel, shape(2 * nx * loads, LANES))(y2)
    dens, x1, x2 = call(
        pack_x_kernel,
        (shape(nx * s.pitch, LANES), shape(s.x_rows, LANES), shape(s.x_rows, LANES)),
        scratch_shapes=[scratch(4 * s.my * loads, LANES)],
    )(bt, dt, y2, t2, y1)
    x1, x2 = swap(x1, "gx", 0), swap(x2, "gx", 1)
    plane = s.my * loads
    rows, field = shape(s.mx * s.pitch, LANES), shape(s.mx * plane, LANES)
    edge = shape(2 * plane, LANES)
    cond, inv_1, bx, zx, q_1, w_1, v_1, carry1, carry2, sums = call(
        inner_kernel, (rows,) * 2 + (field,) * 5 + (edge,) * 2 + (shape(4 * loads, LANES),)
    )(bt, dens, y1, t2)
    xt2 = call(open_x_kernel, shape(2 * plane, LANES))(x2)
    q_t, v_t, inv_2, sums = call(
        outer_kernel,
        (
            shape(nodes, LANES),
            shape(nodes, LANES),
            shape(ny, LANES),
            shape(devices, 1, LANES),
        ),
        scratch_shapes=[scratch(2 * plane, LANES)] * 2
        + [scratch(3 * s.pitch, LANES)] * 2
        + [scratch(5 * s.pitch, LANES)] * 2
        + [scratch(5 * plane, LANES)] * 5
        + [scratch(2 * plane, LANES)],
    )(dens, x1, x2, xt2, cond, inv_1, bx, zx, q_1, w_1, v_1, carry1, carry2, sums)
    parts = lax.all_to_all(sums, ("gx", "gy"), 0, 0, tiled=True)
    whole = shape(loads, nx, flat)
    image, again, inverse = call(unpack_kernel, (whole, whole, shape(nx, flat)))(
        q_t, v_t, inv_1, inv_2
    )
    return call(
        finish_kernel,
        (whole, whole),
        out_specs=(hbm, hbm),
        scratch_shapes=[
            scratch(loads, nx, flat),
            scratch(loads, nx, flat),
            pltpu.SemaphoreType.DMA((2, loads)),
        ],
    )(parts, heat_source, image, again, inverse)


def solution(mesh):
    placed = (P(None, "gx", "gy"), P("gx", "gy"))
    return jax.shard_map(
        per_device,
        mesh=mesh,
        in_specs=placed,
        out_specs=(P(None, "gx", "gy"), P(None, "gx", "gy")),
        check_vma=False,
    )
```

```python
import functools

import jax
import jax.numpy as jnp
import numpy as np
from jax import lax
from jax.experimental import pallas as pl
from jax.experimental.pallas import tpu as pltpu
from jax.sharding import PartitionSpec as P

NZ = 96
KMIN = 0.001
LANES = 128
SUB = 8


class Batch:
    def __init__(self, size=12):
        self.size, self.held = size, []

    def add(self, into, at, tile):
        self.held.append((into, at, tile))
        if len(self.held) >= self.size:
            self.flush()

    def flush(self):
        for into, at, tile in self.held:
            into[at] = tile
        self.held = []


def packed_count(tiles):
    return -(-tiles * NZ // LANES)


def lane_ids(rows):
    return lax.broadcasted_iota(jnp.int32, (rows, LANES), 1)


def unpack_tile(read, index, rows):
    start = index * NZ
    block, offset = start // LANES, start % LANES
    lane = lane_ids(rows)
    first = read(block)
    if offset:
        first = pltpu.roll(first, LANES - offset, 1)
    if offset + NZ > LANES:
        second = pltpu.roll(read(block + 1), LANES - offset, 1)
        first = jnp.where(lane < LANES - offset, first, second)
    return jnp.where(lane < NZ, first, 0.0)


def pack_block(read_tile, tiles, block, rows):
    lane = lane_ids(rows)
    start = block * LANES
    out, at = None, start
    while at < start + LANES and at // NZ < tiles:
        index, z = at // NZ, at % NZ
        here = at - start
        piece = read_tile(index)
        shift = (here - z) % LANES
        if shift:
            piece = pltpu.roll(piece, shift, 1)
        out = piece if out is None else jnp.where(lane < here, out, piece)
        at += NZ - z
    return out


def pack_tiles(out_ref, at, rows, tiles, read_tile):
    batch = Batch()
    for block in range(packed_count(tiles)):
        place = slice(at + block * rows, at + (block + 1) * rows), slice(None)
        batch.add(out_ref, place, pack_block(read_tile, tiles, block, rows))
    batch.flush()


def unpack_tiles(ref, at, rows, tiles, write):
    batch = Batch()
    for index in range(tiles):
        tile = unpack_tile(lambda t: ref[at + t * rows : at + (t + 1) * rows, :], index, rows)
        for store in write(index, tile):
            batch.add(*store)
    batch.flush()


class Sizes:
    def __init__(self, loads, nx, ny, count_x, count_y):
        self.loads, self.nx, self.ny = loads, nx, ny
        self.count_x, self.count_y = count_x, count_y
        self.mx, self.my = nx + 4, ny + 4
        self.pitch = -(-(ny + 6) // SUB) * SUB
        self.y_dens = packed_count(2 * nx) * loads
        self.y_rows = self.y_dens + 3 * nx
        self.x_dens = packed_count(2 * self.my) * loads
        self.x_rows = self.x_dens + 3 * self.pitch


class Tiles:
    def __init__(self, ref, columns, loads):
        self.ref, self.columns, self.loads = ref, columns, loads

    def rows(self, at):
        start = (at[0] * self.columns + at[1]) * self.loads
        if not isinstance(start, int):
            start = pl.multiple_of(start, SUB)
        return pl.ds(start, self.loads)

    def __getitem__(self, at):
        return self.ref[self.rows(at), :]

    def __setitem__(self, at, tile):
        self.ref[self.rows(at), :] = tile


class Rows:
    def __init__(self, ref, pitch, loads):
        self.ref, self.pitch, self.loads = ref, pitch, loads

    def __getitem__(self, at):
        row = self.ref[pl.ds(at[0] * self.pitch + at[1], 1), :]
        return jnp.broadcast_to(row, (self.loads, LANES))

    def put(self, x, values):
        self.ref[x * self.pitch : x * self.pitch + values.shape[0], :] = values


class Joined:
    def __init__(self, first, second, own):
        self.first, self.second, self.own = first, second, own

    def __getitem__(self, at):
        if at[0] in self.own:
            return self.first[self.own.index(at[0]), at[1]]
        return self.second[at]

    def __setitem__(self, at, tile):
        self.first[self.own.index(at[0]), at[1]] = tile

    def put(self, x, values):
        self.first.put(self.own.index(x), values)


def is_even(axis):
    return lax.rem(lax.axis_index(axis), 2) == 0


def is_alone(axis, count, start):
    place = lax.axis_index(axis)
    last = (count - start) % 2
    alone = place < start
    return jnp.logical_or(alone, place == count - 1) if last else alone


def pick(even, if_even, if_odd):
    return jnp.where(even, if_even, if_odd)


def pack_kernel(s, b_hbm, d_hbm, bt_ref, dt_ref, y2_ref, b_ref, d_ref, sems):
    loads, nx, ny = s.loads, s.nx, s.ny
    d_copy = pltpu.make_async_copy(d_hbm, d_ref, sems.at[0])
    d_copy.start()
    parts = 2 if loads % 2 == 0 else 1
    each = loads // parts
    copies = []
    for part in range(parts):
        some = pl.ds(part * each, each)
        copies.append(pltpu.make_async_copy(b_hbm.at[some], b_ref.at[some], sems.at[part + 1]))
        copies[-1].start()
    d_copy.wait()
    batch = Batch(16)
    for x0 in range(0, nx, SUB):
        for y in range(ny):
            tile = unpack_tile(
                lambda t: d_ref[x0 : x0 + SUB, t * LANES : (t + 1) * LANES], y, SUB
            )
            batch.add(dt_ref, (pl.ds(x0 * ny + y, SUB, stride=ny), slice(None)), tile)
    batch.flush()
    for load in range(loads):
        if load % each == 0:
            copies[load // each].wait()
        batch = Batch(16)
        for x0 in range(0, nx, SUB):
            for y in range(ny):
                tile = unpack_tile(
                    lambda t: b_ref[load, x0 : x0 + SUB, t * LANES : (t + 1) * LANES], y, SUB
                )
                rows = pl.ds((x0 * ny + y) * loads + load, SUB, stride=ny * loads)
                batch.add(bt_ref, (rows, slice(None)), tile)
        batch.flush()
    pack_face(s, jnp.logical_not(is_even("gy")), bt_ref, dt_ref, y2_ref)


def pack_near_kernel(s, bt_ref, dt_ref, y1_ref):
    pack_face(s, is_even("gy"), bt_ref, dt_ref, y1_ref)


def pack_face(s, upper, bt_ref, dt_ref, out_ref):
    loads, nx, ny = s.loads, s.nx, s.ny
    tiles = Tiles(bt_ref, ny, loads)
    y0 = pick(upper, ny - 2, 0)
    pack_tiles(out_ref, 0, loads, 2 * nx, lambda i: tiles[i // 2, y0 + i % 2])
    y0 = pick(upper, ny - 3, 0)
    batch = Batch()
    for dy in range(3):
        for x0 in range(0, nx, SUB):
            at = s.y_dens + dy * nx + x0
            tile = dt_ref[pl.ds(x0 * ny + y0 + dy, SUB, stride=ny), :]
            batch.add(out_ref, (slice(at, at + SUB), slice(None)), tile)
    batch.flush()


def open_y_kernel(s, y_ref, t_ref):
    tiles = Tiles(t_ref, 2, s.loads)
    unpack_tiles(
        y_ref, 0, s.loads, 2 * s.nx, lambda i, tile: [(tiles, (i // 2, i % 2), tile)]
    )


def open_x_kernel(s, x_ref, t_ref):
    tiles = Tiles(t_ref, s.my, s.loads)
    unpack_tiles(
        x_ref, 0, s.loads, 2 * s.my, lambda i, tile: [(tiles, (i // s.my, i % s.my), tile)]
    )


def pack_x_kernel(s, bt_ref, dt_ref, y2_ref, t2_ref, y1_ref, dens_ref, x1_ref, x2_ref, edge_ref):
    loads, nx, ny, my, pitch = s.loads, s.nx, s.ny, s.my, s.pitch
    even_x, even_y = is_even("gx"), is_even("gy")
    ys = (pick(even_y, ny + 2, 0), pick(even_y, 0, ny + 2))
    yd = (pick(even_y, ny + 3, 0), pick(even_y, 0, ny + 3))
    for x in range(nx):
        at = x * pitch
        dens_ref[at + 3 : at + 3 + ny, :] = dt_ref[x * ny : (x + 1) * ny, :]
        dens_ref[at + ny + 6 : at + pitch, :] = jnp.zeros((pitch - ny - 6, LANES), jnp.float32)
    for side, ref in enumerate((y1_ref, y2_ref)):
        alone = is_alone("gy", s.count_y, side)
        for dy in range(3):
            for x0 in range(0, nx, SUB):
                at = s.y_dens + dy * nx + x0
                to = x0 * pitch + yd[side] + dy
                dens_ref[pl.ds(to, SUB, stride=pitch), :] = jnp.where(
                    alone, 0.0, ref[at : at + SUB, :]
                )
    inner, edge = Tiles(bt_ref, ny, loads), Tiles(edge_ref, my, loads)
    far = Tiles(t2_ref, 2, loads)
    batch = Batch()
    for place, x in enumerate((0, 1, nx - 2, nx - 1)):
        for y in range(ny):
            batch.add(edge, (place, y + 2), inner[x, y])
        for dy in range(2):
            tile = unpack_tile(
                lambda t: y1_ref[t * loads : (t + 1) * loads, :], 2 * x + dy, loads
            )
            batch.add(edge, (place, ys[0] + dy), tile)
            batch.add(edge, (place, ys[1] + dy), far[x, dy])
    batch.flush()
    for ref, upper in ((x1_ref, even_x), (x2_ref, jnp.logical_not(even_x))):
        place = pick(upper, 2, 0)
        pack_tiles(ref, 0, loads, 2 * my, lambda i: edge[place + i // my, i % my])
        rows = pl.ds(pl.multiple_of(pick(upper, nx - 3, 0) * pitch, SUB), 3 * pitch)
        ref[s.x_dens :, :] = dens_ref[rows, :]


def conduct_of(dens):
    return jnp.where(
        dens > 0.0, (KMIN + (1.0 - KMIN) * (dens * dens * dens)) * (1.0 / 12.0), 0.0
    )


def inverse_of(s, before, after):
    pair = before + after
    pair = pair[: s.pitch - 1] + pair[1:]
    total = 4.0 * (pair + pltpu.roll(pair, 1, 1))
    return jnp.where(after[1:] > 0.0, 1.0 / total, 0.0)


def up(tile):
    return pltpu.roll(tile, LANES - 1, 1)


def element_planes(cond, carry, a, count, y0, columns, field, emitter, keep=True):
    def loads_of(step):
        y = y0 + step
        right = [field[a + u, y + 1] for u in range(count + 1)]
        conduct = [cond[a + u, y] for u in range(count)]
        above = extra = None
        if step and emitter:
            above = (carry[0, y], carry[1, y])
            extra = [emitter.fetch(a + u, y) for u in range(count)]
        return right, conduct, above, extra

    left = [(tile, up(tile)) for tile in [field[a + u, y0] for u in range(count + 1)]]
    ahead = loads_of(0)
    old, waiting = [None] * count, []
    for step in range(columns):
        y = y0 + step
        right, conduct, above, extra = ahead
        if step + 1 < columns:
            ahead = loads_of(step + 1)
        if len(waiting) > 1:
            for into, at, tile in waiting.pop(0):
                into[at] = tile
        stores = []
        right = [(tile, up(tile)) for tile in right]
        for u in range(count):
            (p0, p0s), (p1, p1s) = left[u], left[u + 1]
            (r0, r0s), (r1, r1s) = right[u], right[u + 1]
            c = conduct[u]
            even = (p0 + r1) + (r0s + p1s)
            odd = (r0 + p1) + (p0s + r1s)
            pass_on = keep or u + 1 < count
            lower = upper = None
            if emitter:
                lower = (c * (odd + p1s), c * (even + p1))
            if pass_on:
                upper = (c * (even + p0s), c * (odd + p0))
            if step and emitter:
                low = (c * (even + r1s) + old[u][0][0]) + above[0]
                high = (c * (odd + r1) + old[u][0][1]) + above[1]
                total = low + pltpu.roll(high, 1, 1)
                stores += emitter.finish(a + u, y, p0, total, extra[u])
            if step and pass_on:
                above = (
                    c * (odd + r0s) + old[u][1][0],
                    c * (even + r0) + old[u][1][1],
                )
            old[u] = (lower, upper)
        if step and keep:
            stores += [(carry, (0, y), above[0]), (carry, (1, y), above[1])]
        waiting.append(stores)
        left = right
    for stores in waiting:
        for into, at, tile in stores:
            into[at] = tile


class First:
    def __init__(self, bx, invx, qx, wx):
        self.bx, self.invx, self.qx, self.wx = bx, invx, qx, wx

    def fetch(self, x, y):
        return self.bx[x, y], self.invx[x, y]

    def finish(self, x, y, node, total, extra):
        source, inverse = extra
        image = 1.25 * source - total
        return [(self.qx, (x, y), image), (self.wx, (x, y), image * inverse)]


class Second:
    def __init__(self, bx, zx, qx, vx, sums):
        self.bx, self.zx, self.qx, self.vx, self.sums = bx, zx, qx, vx, sums

    def fetch(self, x, y):
        return self.bx[x, y], self.zx[x, y], self.qx[x, y]

    def finish(self, x, y, weighted, total, extra):
        source, scaled, image = extra
        again = 1.25 * image - total
        change = scaled - weighted
        sums = self.sums
        sums[0] = sums[0] + source * scaled
        sums[1] = sums[1] + source * change
        sums[2] = sums[2] + (source - image) * change
        sums[3] = sums[3] + (image - again) * change
        return [(self.vx, (x, y), again)]


def over_planes(start, stop, body, state):
    pairs = (stop - start) // 2
    state = lax.fori_loop(0, pairs, lambda i, st: body(start + 2 * i, 2, st), state)
    if (stop - start) % 2:
        state = body(stop - 1, 1, state)
    return state


def inner_kernel(
    s, bt_ref, dens_ref, y1_ref, t2_ref,
    cond, invx, bx, zx, qx, wx, vx, carry1, carry2, sums_ref,
):
    loads, nx, ny, my, pitch = s.loads, s.nx, s.ny, s.my, s.pitch
    bx, zx, qx, wx, vx, carry1, carry2 = (
        Tiles(ref, my, loads) for ref in (bx, zx, qx, wx, vx, carry1, carry2)
    )
    cond, invx = Rows(cond, pitch, loads), Rows(invx, pitch, loads)
    even_y = is_even("gy")
    ys = (pick(even_y, ny + 2, 0), pick(even_y, 0, ny + 2))
    before = None
    for x in range(nx):
        after = conduct_of(dens_ref[x * pitch : (x + 1) * pitch, :])
        cond.put(x + 2, after[1:])
        if x:
            invx.put(x + 2, inverse_of(s, before, after))
        before = after

    def stage(x, y, tile):
        stores = [(bx, (x + 2, y), tile)]
        if x:
            stores.append((zx, (x + 2, y), tile * invx[x + 2, y]))
        return stores

    inner = Tiles(bt_ref, ny, loads)
    batch = Batch(16)
    for x in range(nx):
        for y in range(ny):
            for store in stage(x, y + 2, inner[x, y]):
                batch.add(*store)
    batch.flush()
    unpack_tiles(
        y1_ref, 0, loads, 2 * nx, lambda i, tile: stage(i // 2, ys[0] + i % 2, tile)
    )
    far = Tiles(t2_ref, 2, loads)
    batch = Batch(16)
    for x in range(nx):
        for dy in range(2):
            for store in stage(x, ys[1] + dy, far[x, dy]):
                batch.add(*store)
    batch.flush()

    element_planes(cond, carry1, 3, 1, 0, my - 1, zx, None)

    def first(a, count, state):
        element_planes(cond, carry1, a, count, 0, my - 1, zx, First(bx, invx, qx, wx))
        return state

    over_planes(4, nx + 1, first, 0)
    element_planes(cond, carry2, 4, 1, 1, my - 3, wx, None)

    def second(a, count, sums):
        sums = list(sums)
        element_planes(cond, carry2, a, count, 1, my - 3, wx, Second(bx, zx, qx, vx, sums))
        return tuple(sums)

    zero = jnp.zeros((loads, LANES), jnp.float32)
    sums = over_planes(5, nx, second, (zero,) * 4)
    for place, part in enumerate(sums):
        sums_ref[place * loads : (place + 1) * loads, :] = part


def outer_kernel(
    s, dens_ref, x1_ref, x2_ref, t2_ref,
    cond1, invx1, bx1, zx1, qx1, wx1, vx1, carry1, carry2, sums1,
    q_out, v_out, inv_out, sums_ref,
    low_ref, high_ref, low_d, high_d, cond2, invx2, bx2, zx2, qx2, wx2, vx2, carry3,
):
    loads, nx, ny, mx, my, pitch = s.loads, s.nx, s.ny, s.mx, s.my, s.pitch
    even_x = is_even("gx")

    def take(near, far):
        near_t, near_d = near
        far_t, far_d = far
        unpack_tiles(
            x1_ref, 0, loads, 2 * my,
            lambda i, tile: [(Tiles(near_t, my, loads), (i // my, i % my), tile)],
        )
        far_t[...] = t2_ref[...]
        for into, ref, start in ((near_d, x1_ref, 0), (far_d, x2_ref, 1)):
            alone = is_alone("gx", s.count_x, start)
            into[...] = jnp.where(alone, 0.0, ref[s.x_dens :, :])

    @pl.when(even_x)
    def _():
        take((high_ref, high_d), (low_ref, low_d))

    @pl.when(jnp.logical_not(even_x))
    def _():
        take((low_ref, low_d), (high_ref, high_d))

    def joined(first, second, own):
        return Joined(Tiles(first, my, loads), Tiles(second, my, loads), own)

    def joined_rows(first, second, own):
        return Joined(Rows(first, pitch, loads), Rows(second, pitch, loads), own)

    outside = (0, 1, nx + 2, nx + 3)
    scaled_own = outside + (2,)
    image_own = (1, 2, 3, nx + 1, nx + 2)
    cond, invx = joined_rows(cond2, cond1, outside), joined_rows(invx2, invx1, scaled_own)
    bx, zx = joined(bx2, bx1, outside), joined(zx2, zx1, scaled_own)
    qx, wx = joined(qx2, qx1, image_own), joined(wx2, wx1, image_own)
    vx = joined(vx2, vx1, again_planes(nx))
    carry1, carry2, carry3 = (Tiles(ref, my, loads) for ref in (carry1, carry2, carry3))

    def conduct(ref, x):
        return conduct_of(ref[x * pitch : (x + 1) * pitch, :])

    low = [conduct(low_d, t) for t in range(3)] + [conduct(dens_ref, 0)]
    high = [conduct(dens_ref, nx - 1)] + [conduct(high_d, t) for t in range(2)]
    for x in range(3):
        inverse = inverse_of(s, low[x], low[x + 1])
        invx.put(x, inverse)
        if x < 2:
            cond.put(x, low[x + 1][1:])
    inv_out[...] = inverse[2 : 2 + ny]
    for x in range(2):
        invx.put(nx + 2 + x, inverse_of(s, high[x], high[x + 1]))
    cond.put(nx + 2, high[1][1:])

    batch = Batch(16)
    for ref, x0 in ((low_ref, 0), (high_ref, nx + 2)):
        tiles = Tiles(ref, my, loads)
        for dx in range(2):
            for y in range(my):
                tile = tiles[dx, y]
                batch.add(bx, (x0 + dx, y), tile)
                batch.add(zx, (x0 + dx, y), tile * invx[x0 + dx, y])
    for y in range(my):
        batch.add(zx, (2, y), bx[2, y] * invx[2, y])
    batch.flush()

    emitter = First(bx, invx, qx, wx)
    element_planes(cond, carry3, 0, 1, 0, my - 1, zx, None)
    element_planes(cond, carry3, 1, 2, 0, my - 1, zx, emitter)
    element_planes(cond, carry3, 3, 1, 0, my - 1, zx, emitter, keep=False)
    element_planes(cond, carry1, nx + 1, 2, 0, my - 1, zx, emitter, keep=False)
    sums = [sums1[place * loads : (place + 1) * loads, :] for place in range(4)]
    emitter = Second(bx, zx, qx, vx, sums)
    element_planes(cond, carry3, 1, 1, 1, my - 3, wx, None)
    element_planes(cond, carry3, 2, 2, 1, my - 3, wx, emitter)
    element_planes(cond, carry3, 4, 1, 1, my - 3, wx, emitter, keep=False)
    element_planes(cond, carry2, nx, 2, 1, my - 3, wx, emitter, keep=False)
    for field, out in ((qx, q_out), (vx, v_out)):
        out = Tiles(out, ny, loads)
        batch = Batch()
        for x in range(nx):
            for y in range(ny):
                batch.add(out, (x, y), field[x + 2, y + 2])
        batch.flush()

    lane = lane_ids(loads)
    load = lax.broadcasted_iota(jnp.int32, (loads, LANES), 0)
    packed = jnp.zeros((loads, LANES), jnp.float32)
    for place, part in enumerate(sums):
        total = jnp.sum(part, axis=1, keepdims=True)
        packed = packed + jnp.where(lane == place * loads + load, total, 0.0)
    row = jnp.sum(packed, axis=0, keepdims=True)
    sums_ref[...] = jnp.broadcast_to(row[None], sums_ref.shape)


def again_planes(nx):
    return (2, 3, 4, nx, nx + 1)


def unpack_kernel(s, q_ref, v_ref, inv1_ref, inv2_ref, qo_ref, vo_ref, io_ref):
    loads, nx, ny = s.loads, s.nx, s.ny
    batch = Batch()
    for x0 in range(0, nx, SUB):
        for ref, out in ((q_ref, qo_ref), (v_ref, vo_ref)):
            for load in range(loads):
                for block in range(packed_count(ny)):
                    tile = pack_block(
                        lambda y: ref[
                            pl.ds((x0 * ny + y) * loads + load, SUB, stride=ny * loads), :
                        ],
                        ny, block, SUB,
                    )
                    lanes = slice(block * LANES, (block + 1) * LANES)
                    batch.add(out, (load, slice(x0, x0 + SUB), lanes), tile)
        for block in range(packed_count(ny)):
            tile = pack_block(
                lambda y: inv1_ref[
                    pl.ds((x0 + 2) * s.pitch + y + 2, SUB, stride=s.pitch), :
                ],
                ny, block, SUB,
            )
            lanes = slice(block * LANES, (block + 1) * LANES)
            batch.add(io_ref, (slice(x0, x0 + SUB), lanes), tile)
    batch.flush()
    for block in range(packed_count(ny)):
        io_ref[0:1, block * LANES : (block + 1) * LANES] = pack_block(
            lambda y: inv2_ref[y : y + 1, :], ny, block, 1
        )


def finish_kernel(s, parts_ref, b_ref, q_ref, v_ref, inv_ref, x_hbm, r_hbm, x_ref, r_ref, sems):
    loads = s.loads
    totals = jnp.sum(parts_ref[...], axis=0)

    def part(place):
        return pltpu.roll(totals, (LANES - place * loads) % LANES, 1) if place else totals

    rz, near, square, last = (part(place) for place in range(4))
    direct = rz - near
    alpha = rz / direct
    short = -near / direct
    rz_next = short * short * rz + 2.0 * alpha * short * near + alpha * alpha * square
    beta = rz_next / rz
    grown = short + beta
    curved = (
        grown * grown * direct
        + 2.0 * alpha * grown * (near - square)
        + alpha * alpha * last
    )
    alpha_next = rz_next / curved
    first_row = alpha + alpha_next * (1.0 + beta)
    second_row = alpha_next * alpha
    inverse = inv_ref[...]
    copies = []
    for load in range(loads):
        first = first_row[:, load : load + 1]
        second = second_row[:, load : load + 1]
        source, image = b_ref[load], q_ref[load]
        x_ref[load] = (first * source - second * image) * inverse
        copies.append(pltpu.make_async_copy(x_ref.at[load], x_hbm.at[load], sems.at[0, load]))
        copies[-1].start()
        r_ref[load] = source - first * image + second * v_ref[load]
        copies.append(pltpu.make_async_copy(r_ref.at[load], r_hbm.at[load], sems.at[1, load]))
        copies[-1].start()
    for copy in copies:
        copy.wait()


def swap(array, axis, start):
    counts = {name: lax.axis_size(name) for name in ("gx", "gy")}
    other = "gy" if axis == "gx" else "gx"
    pairs = []
    for at in np.ndindex(counts["gx"], counts["gy"]):
        place = dict(zip(("gx", "gy"), at))
        partner = place[axis] + (1 if (place[axis] - start) % 2 == 0 else -1)
        if 0 <= partner < counts[axis]:
            place[axis] = partner
        elif place[other] ^ 1 < counts[other]:
            place[other] ^= 1
        pairs.append((at[0] * counts["gy"] + at[1], place["gx"] * counts["gy"] + place["gy"]))
    return lax.ppermute(array, ("gx", "gy"), pairs)


def per_device(heat_source, density):
    loads, nx, flat = heat_source.shape
    ny = flat // NZ
    s = Sizes(loads, nx, ny, lax.axis_size("gx"), lax.axis_size("gy"))
    nodes = nx * ny * loads
    devices = lax.axis_size("gx") * lax.axis_size("gy")

    def shape(*dims):
        return jax.ShapeDtypeStruct(dims, jnp.float32)

    def scratch(*dims):
        return pltpu.VMEM(dims, jnp.float32)

    def call(kernel, out_shape, **more):
        params = pltpu.CompilerParams(vmem_limit_bytes=20 * 1024 * 1024)
        return pl.pallas_call(
            functools.partial(kernel, s), out_shape=out_shape, compiler_params=params, **more
        )

    hbm = pl.BlockSpec(memory_space=pltpu.HBM)
    face = shape(s.y_rows, LANES)
    bt, dt, y2 = call(
        pack_kernel,
        (shape(nodes, LANES), shape(nx * ny, LANES), face),
        in_specs=[hbm, hbm],
        scratch_shapes=[
            scratch(loads, nx, flat),
            scratch(nx, flat),
            pltpu.SemaphoreType.DMA((3,)),
        ],
    )(
        pltpu.with_memory_space_constraint(heat_source, pltpu.HBM),
        pltpu.with_memory_space_constraint(density, pltpu.HBM),
    )
    y2 = swap(y2, "gy", 1)
    y1 = swap(call(pack_near_kernel, face)(bt, dt), "gy", 0)
    t2 = call(open_y_kernel, shape(2 * nx * loads, LANES))(y2)
    dens, x1, x2 = call(
        pack_x_kernel,
        (shape(nx * s.pitch, LANES), shape(s.x_rows, LANES), shape(s.x_rows, LANES)),
        scratch_shapes=[scratch(4 * s.my * loads, LANES)],
    )(bt, dt, y2, t2, y1)
    x1, x2 = swap(x1, "gx", 0), swap(x2, "gx", 1)
    plane = s.my * loads
    rows, field = shape(s.mx * s.pitch, LANES), shape(s.mx * plane, LANES)
    edge = shape(2 * plane, LANES)
    cond, inv_1, bx, zx, q_1, w_1, v_1, carry1, carry2, sums = call(
        inner_kernel, (rows,) * 2 + (field,) * 5 + (edge,) * 2 + (shape(4 * loads, LANES),)
    )(bt, dens, y1, t2)
    xt2 = call(open_x_kernel, shape(2 * plane, LANES))(x2)
    q_t, v_t, inv_2, sums = call(
        outer_kernel,
        (
            shape(nodes, LANES),
            shape(nodes, LANES),
            shape(ny, LANES),
            shape(devices, 1, LANES),
        ),
        scratch_shapes=[scratch(2 * plane, LANES)] * 2
        + [scratch(3 * s.pitch, LANES)] * 2
        + [scratch(5 * s.pitch, LANES)] * 2
        + [scratch(5 * plane, LANES)] * 5
        + [scratch(2 * plane, LANES)],
    )(dens, x1, x2, xt2, cond, inv_1, bx, zx, q_1, w_1, v_1, carry1, carry2, sums)
    parts = lax.all_to_all(sums, ("gx", "gy"), 0, 0, tiled=True)
    whole = shape(loads, nx, flat)
    image, again, inverse = call(unpack_kernel, (whole, whole, shape(nx, flat)))(
        q_t, v_t, inv_1, inv_2
    )
    return call(
        finish_kernel,
        (whole, whole),
        out_specs=(hbm, hbm),
        scratch_shapes=[
            scratch(loads, nx, flat),
            scratch(loads, nx, flat),
            pltpu.SemaphoreType.DMA((2, loads)),
        ],
    )(parts, heat_source, image, again, inverse)


def solution(mesh):
    placed = (P(None, "gx", "gy"), P("gx", "gy"))
    return jax.shard_map(
        per_device,
        mesh=mesh,
        in_specs=placed,
        out_specs=(P(None, "gx", "gy"), P(None, "gx", "gy")),
        check_vma=False,
    )
```

```python
import functools

import jax
import jax.numpy as jnp
import numpy as np
from jax import lax
from jax.experimental import pallas as pl
from jax.experimental.pallas import tpu as pltpu
from jax.sharding import PartitionSpec as P

NZ = 96
KMIN = 0.001
LANES = 128
SUB = 8


class Batch:
    def __init__(self, size=12):
        self.size, self.held = size, []

    def add(self, into, at, tile):
        self.held.append((into, at, tile))
        if len(self.held) >= self.size:
            self.flush()

    def flush(self):
        for into, at, tile in self.held:
            into[at] = tile
        self.held = []


def packed_count(tiles):
    return -(-tiles * NZ // LANES)


def lane_ids(rows):
    return lax.broadcasted_iota(jnp.int32, (rows, LANES), 1)


def unpack_tile(read, index, rows):
    start = index * NZ
    block, offset = start // LANES, start % LANES
    lane = lane_ids(rows)
    first = read(block)
    if offset:
        first = pltpu.roll(first, LANES - offset, 1)
    if offset + NZ > LANES:
        second = pltpu.roll(read(block + 1), LANES - offset, 1)
        first = jnp.where(lane < LANES - offset, first, second)
    return jnp.where(lane < NZ, first, 0.0)


def pack_block(read_tile, tiles, block, rows):
    lane = lane_ids(rows)
    start = block * LANES
    out, at = None, start
    while at < start + LANES and at // NZ < tiles:
        index, z = at // NZ, at % NZ
        here = at - start
        piece = read_tile(index)
        shift = (here - z) % LANES
        if shift:
            piece = pltpu.roll(piece, shift, 1)
        out = piece if out is None else jnp.where(lane < here, out, piece)
        at += NZ - z
    return out


def pack_tiles(out_ref, at, rows, tiles, read_tile):
    batch = Batch()
    for block in range(packed_count(tiles)):
        place = slice(at + block * rows, at + (block + 1) * rows), slice(None)
        batch.add(out_ref, place, pack_block(read_tile, tiles, block, rows))
    batch.flush()


def unpack_tiles(ref, at, rows, tiles, write):
    batch = Batch()
    for index in range(tiles):
        tile = unpack_tile(lambda t: ref[at + t * rows : at + (t + 1) * rows, :], index, rows)
        for store in write(index, tile):
            batch.add(*store)
    batch.flush()


class Sizes:
    def __init__(self, loads, nx, ny, count_x, count_y):
        self.loads, self.nx, self.ny = loads, nx, ny
        self.count_x, self.count_y = count_x, count_y
        self.mx, self.my = nx + 4, ny + 4
        self.pitch = -(-(ny + 6) // SUB) * SUB
        self.y_dens = packed_count(2 * nx) * loads
        self.y_rows = self.y_dens + 3 * nx
        self.x_dens = packed_count(2 * ny) * loads
        self.x_rows = self.x_dens + 3 * ny
        self.c_dens = packed_count(8) * loads
        self.c_rows = self.c_dens + -(-18 // SUB) * SUB


class Tiles:
    def __init__(self, ref, columns, loads):
        self.ref, self.columns, self.loads = ref, columns, loads

    def rows(self, at):
        start = (at[0] * self.columns + at[1]) * self.loads
        if not isinstance(start, int):
            start = pl.multiple_of(start, SUB)
        return pl.ds(start, self.loads)

    def __getitem__(self, at):
        return self.ref[self.rows(at), :]

    def __setitem__(self, at, tile):
        self.ref[self.rows(at), :] = tile


class Rows:
    def __init__(self, ref, pitch, loads):
        self.ref, self.pitch, self.loads = ref, pitch, loads

    def __getitem__(self, at):
        row = self.ref[pl.ds(at[0] * self.pitch + at[1], 1), :]
        return jnp.broadcast_to(row, (self.loads, LANES))

    def put(self, x, values):
        self.ref[x * self.pitch : x * self.pitch + values.shape[0], :] = values


class Joined:
    def __init__(self, first, second, own):
        self.first, self.second, self.own = first, second, own

    def __getitem__(self, at):
        if at[0] in self.own:
            return self.first[self.own.index(at[0]), at[1]]
        return self.second[at]

    def __setitem__(self, at, tile):
        self.first[self.own.index(at[0]), at[1]] = tile

    def put(self, x, values):
        self.first.put(self.own.index(x), values)


def is_even(axis):
    return lax.rem(lax.axis_index(axis), 2) == 0


def is_alone(axis, count, start):
    place = lax.axis_index(axis)
    last = (count - start) % 2
    alone = place < start
    return jnp.logical_or(alone, place == count - 1) if last else alone


def pick(even, if_even, if_odd):
    return jnp.where(even, if_even, if_odd)


def pack_kernel(s, b_hbm, d_hbm, bt_ref, dt_ref, y2_ref, b_ref, d_ref, sems):
    loads, nx, ny = s.loads, s.nx, s.ny
    d_copy = pltpu.make_async_copy(d_hbm, d_ref, sems.at[0])
    d_copy.start()
    parts = 2 if loads % 2 == 0 else 1
    each = loads // parts
    copies = []
    for part in range(parts):
        some = pl.ds(part * each, each)
        copies.append(pltpu.make_async_copy(b_hbm.at[some], b_ref.at[some], sems.at[part + 1]))
        copies[-1].start()
    d_copy.wait()
    batch = Batch(16)
    for x0 in range(0, nx, SUB):
        for y in range(ny):
            tile = unpack_tile(
                lambda t: d_ref[x0 : x0 + SUB, t * LANES : (t + 1) * LANES], y, SUB
            )
            batch.add(dt_ref, (pl.ds(x0 * ny + y, SUB, stride=ny), slice(None)), tile)
    batch.flush()
    for load in range(loads):
        if load % each == 0:
            copies[load // each].wait()
        batch = Batch(16)
        for x0 in range(0, nx, SUB):
            for y in range(ny):
                tile = unpack_tile(
                    lambda t: b_ref[load, x0 : x0 + SUB, t * LANES : (t + 1) * LANES], y, SUB
                )
                rows = pl.ds((x0 * ny + y) * loads + load, SUB, stride=ny * loads)
                batch.add(bt_ref, (rows, slice(None)), tile)
        batch.flush()
    pack_face(s, jnp.logical_not(is_even("gy")), bt_ref, dt_ref, y2_ref)


def pack_rest_kernel(s, bt_ref, dt_ref, y1_ref, x1_ref, x2_ref):
    even_x = is_even("gx")
    pack_x_face(s, jnp.logical_not(even_x), bt_ref, dt_ref, x2_ref)
    pack_x_face(s, even_x, bt_ref, dt_ref, x1_ref)
    pack_face(s, is_even("gy"), bt_ref, dt_ref, y1_ref)


def pack_x_face(s, upper, bt_ref, dt_ref, out_ref):
    loads, nx, ny = s.loads, s.nx, s.ny
    tiles = Tiles(bt_ref, ny, loads)
    x0 = pick(upper, nx - 2, 0)
    pack_tiles(out_ref, 0, loads, 2 * ny, lambda i: tiles[x0 + i // ny, i % ny])
    rows = pl.ds(pl.multiple_of(pick(upper, nx - 3, 0) * ny, SUB), 3 * ny)
    out_ref[s.x_dens :, :] = dt_ref[rows, :]


def pack_face(s, upper, bt_ref, dt_ref, out_ref):
    loads, nx, ny = s.loads, s.nx, s.ny
    tiles = Tiles(bt_ref, ny, loads)
    y0 = pick(upper, ny - 2, 0)
    pack_tiles(out_ref, 0, loads, 2 * nx, lambda i: tiles[i // 2, y0 + i % 2])
    y0 = pick(upper, ny - 3, 0)
    batch = Batch()
    for dy in range(3):
        for x0 in range(0, nx, SUB):
            at = s.y_dens + dy * nx + x0
            tile = dt_ref[pl.ds(x0 * ny + y0 + dy, SUB, stride=ny), :]
            batch.add(out_ref, (slice(at, at + SUB), slice(None)), tile)
    batch.flush()


def open_y_kernel(s, y_ref, t_ref):
    tiles = Tiles(t_ref, 2, s.loads)
    unpack_tiles(
        y_ref, 0, s.loads, 2 * s.nx, lambda i, tile: [(tiles, (i // 2, i % 2), tile)]
    )


def corner_kernel(s, x1_ref, x2_ref, xt_ref, c1_ref, c2_ref):
    loads, ny = s.loads, s.ny
    tiles = Tiles(xt_ref, ny, loads)
    for side, ref in enumerate((x1_ref, x2_ref)):
        unpack_tiles(
            ref, 0, loads, 2 * ny,
            lambda i, tile: [(tiles, (2 * side + i // ny, i % ny), tile)],
        )
    even_y = is_even("gy")
    for out_ref, upper in ((c2_ref, jnp.logical_not(even_y)), (c1_ref, even_y)):
        y0 = pick(upper, ny - 2, 0)
        pack_tiles(out_ref, 0, loads, 8, lambda i: tiles[i // 2, y0 + i % 2])
        y0 = pick(upper, ny - 3, 0)
        batch, at = Batch(18), s.c_dens
        for ref in (x1_ref, x2_ref):
            for t in range(3):
                for dy in range(3):
                    row = ref[pl.ds(s.x_dens + t * ny + y0 + dy, 1), :]
                    batch.add(out_ref, (slice(at, at + 1), slice(None)), row)
                    at += 1
        batch.flush()
        out_ref[at:, :] = jnp.zeros((s.c_rows - at, LANES), jnp.float32)


def join_density(s, dt_ref, y1_ref, y2_ref, dens_ref):
    nx, ny, pitch = s.nx, s.ny, s.pitch
    even_y = is_even("gy")
    yd = (pick(even_y, ny + 3, 0), pick(even_y, 0, ny + 3))
    batch = Batch(16)
    for x in range(nx):
        at = x * pitch
        batch.add(
            dens_ref, (slice(at + 3, at + 3 + ny), slice(None)), dt_ref[x * ny : (x + 1) * ny, :]
        )
    batch.flush()
    for side, ref in enumerate((y1_ref, y2_ref)):
        alone = is_alone("gy", s.count_y, side)
        for dy in range(3):
            for x0 in range(0, nx, SUB):
                at = s.y_dens + dy * nx + x0
                to = x0 * pitch + yd[side] + dy
                batch.add(
                    dens_ref,
                    (pl.ds(to, SUB, stride=pitch), slice(None)),
                    jnp.where(alone, 0.0, ref[at : at + SUB, :]),
                )
    batch.flush()


def conduct_of(dens):
    return jnp.where(
        dens > 0.0, (KMIN + (1.0 - KMIN) * (dens * dens * dens)) * (1.0 / 12.0), 0.0
    )


def inverse_of(s, before, after):
    pair = before + after
    pair = pair[: s.pitch - 1] + pair[1:]
    total = 4.0 * (pair + pltpu.roll(pair, 1, 1))
    return jnp.where(after[1:] > 0.0, 1.0 / total, 0.0)


def up(tile):
    return pltpu.roll(tile, LANES - 1, 1)


def element_planes(cond, carry, a, count, y0, columns, field, emitter, keep=True):
    def loads_of(step):
        y = y0 + step
        right = [field[a + u, y + 1] for u in range(count + 1)]
        conduct = [cond[a + u, y] for u in range(count)]
        above = extra = None
        if step and emitter:
            above = (carry[0, y], carry[1, y])
            extra = [emitter.fetch(a + u, y) for u in range(count)]
        return right, conduct, above, extra

    left = [(tile, up(tile)) for tile in [field[a + u, y0] for u in range(count + 1)]]
    ahead = loads_of(0)
    old, waiting = [None] * count, []
    for step in range(columns):
        y = y0 + step
        right, conduct, above, extra = ahead
        if step + 1 < columns:
            ahead = loads_of(step + 1)
        if len(waiting) > 1:
            for into, at, tile in waiting.pop(0):
                into[at] = tile
        stores = []
        right = [(tile, up(tile)) for tile in right]
        for u in range(count):
            (p0, p0s), (p1, p1s) = left[u], left[u + 1]
            (r0, r0s), (r1, r1s) = right[u], right[u + 1]
            c = conduct[u]
            even = (p0 + r1) + (r0s + p1s)
            odd = (r0 + p1) + (p0s + r1s)
            pass_on = keep or u + 1 < count
            lower = upper = None
            if emitter:
                lower = (c * (odd + p1s), c * (even + p1))
            if pass_on:
                upper = (c * (even + p0s), c * (odd + p0))
            if step and emitter:
                low = (c * (even + r1s) + old[u][0][0]) + above[0]
                high = (c * (odd + r1) + old[u][0][1]) + above[1]
                total = low + pltpu.roll(high, 1, 1)
                stores += emitter.finish(a + u, y, p0, total, extra[u])
            if step and pass_on:
                above = (
                    c * (odd + r0s) + old[u][1][0],
                    c * (even + r0) + old[u][1][1],
                )
            old[u] = (lower, upper)
        if step and keep:
            stores += [(carry, (0, y), above[0]), (carry, (1, y), above[1])]
        waiting.append(stores)
        left = right
    for stores in waiting:
        for into, at, tile in stores:
            into[at] = tile


class First:
    def __init__(self, bx, invx, qx, wx):
        self.bx, self.invx, self.qx, self.wx = bx, invx, qx, wx

    def fetch(self, x, y):
        return self.bx[x, y], self.invx[x, y]

    def finish(self, x, y, node, total, extra):
        source, inverse = extra
        image = 1.25 * source - total
        return [(self.qx, (x, y), image), (self.wx, (x, y), image * inverse)]


class Second:
    def __init__(self, bx, zx, qx, vx, sums):
        self.bx, self.zx, self.qx, self.vx, self.sums = bx, zx, qx, vx, sums

    def fetch(self, x, y):
        return self.bx[x, y], self.zx[x, y], self.qx[x, y]

    def finish(self, x, y, weighted, total, extra):
        source, scaled, image = extra
        again = 1.25 * image - total
        change = scaled - weighted
        sums = self.sums
        sums[0] = sums[0] + source * scaled
        sums[1] = sums[1] + source * change
        sums[2] = sums[2] + (source - image) * change
        sums[3] = sums[3] + (image - again) * change
        return [(self.vx, (x, y), again)]


def over_planes(start, stop, body, state):
    pairs = (stop - start) // 2
    state = lax.fori_loop(0, pairs, lambda i, st: body(start + 2 * i, 2, st), state)
    if (stop - start) % 2:
        state = body(stop - 1, 1, state)
    return state


def inner_kernel(
    s, bt_ref, dt_ref, y1_ref, y2_ref, t2_ref,
    dens_ref, cond, invx, bx, zx, qx, wx, vx, carry1, carry2, sums_ref,
):
    loads, nx, ny, my, pitch = s.loads, s.nx, s.ny, s.my, s.pitch
    bx, zx, qx, wx, vx, carry1, carry2 = (
        Tiles(ref, my, loads) for ref in (bx, zx, qx, wx, vx, carry1, carry2)
    )
    cond, invx = Rows(cond, pitch, loads), Rows(invx, pitch, loads)
    join_density(s, dt_ref, y1_ref, y2_ref, dens_ref)
    even_y = is_even("gy")
    ys = (pick(even_y, ny + 2, 0), pick(even_y, 0, ny + 2))
    before = None
    for x in range(nx):
        after = conduct_of(dens_ref[x * pitch : (x + 1) * pitch, :])
        cond.put(x + 2, after[1:])
        if x:
            invx.put(x + 2, inverse_of(s, before, after))
        before = after

    def stage(x, y, tile):
        stores = [(bx, (x + 2, y), tile)]
        if x:
            stores.append((zx, (x + 2, y), tile * invx[x + 2, y]))
        return stores

    inner = Tiles(bt_ref, ny, loads)
    batch = Batch(16)
    for x in range(nx):
        for y in range(ny):
            for store in stage(x, y + 2, inner[x, y]):
                batch.add(*store)
    batch.flush()
    unpack_tiles(
        y1_ref, 0, loads, 2 * nx, lambda i, tile: stage(i // 2, ys[0] + i % 2, tile)
    )
    far = Tiles(t2_ref, 2, loads)
    batch = Batch(16)
    for x in range(nx):
        for dy in range(2):
            for store in stage(x, ys[1] + dy, far[x, dy]):
                batch.add(*store)
    batch.flush()

    element_planes(cond, carry1, 3, 1, 0, my - 1, zx, None)

    def first(a, count, state):
        element_planes(cond, carry1, a, count, 0, my - 1, zx, First(bx, invx, qx, wx))
        return state

    over_planes(4, nx + 1, first, 0)
    element_planes(cond, carry2, 4, 1, 1, my - 3, wx, None)

    def second(a, count, sums):
        sums = list(sums)
        element_planes(cond, carry2, a, count, 1, my - 3, wx, Second(bx, zx, qx, vx, sums))
        return tuple(sums)

    zero = jnp.zeros((loads, LANES), jnp.float32)
    sums = over_planes(5, nx, second, (zero,) * 4)
    for place, part in enumerate(sums):
        sums_ref[place * loads : (place + 1) * loads, :] = part


def outer_kernel(
    s, dens_ref, x1_ref, x2_ref, xt_ref, c1_ref, c2_ref,
    cond1, invx1, bx1, zx1, qx1, wx1, vx1, carry1, carry2, sums1,
    q_out, v_out, inv_out, sums_ref,
    low_ref, high_ref, low_d, high_d, cond2, invx2, bx2, zx2, qx2, wx2, vx2, carry3,
):
    loads, nx, ny, mx, my, pitch = s.loads, s.nx, s.ny, s.mx, s.my, s.pitch
    even_x = is_even("gx")

    even_y = is_even("gy")
    ys = (pick(even_y, ny + 2, 0), pick(even_y, 0, ny + 2))
    yd = (pick(even_y, ny + 3, 0), pick(even_y, 0, ny + 3))

    def take(near, far):
        faces = Tiles(xt_ref, ny, loads)
        for side, (ref, (tiles_ref, into)) in enumerate(((x1_ref, near), (x2_ref, far))):
            tiles = Tiles(tiles_ref, my, loads)
            alone_x = is_alone("gx", s.count_x, side)
            batch = Batch(18)
            for dx in range(2):
                for y in range(ny):
                    batch.add(tiles, (dx, y + 2), faces[2 * side + dx, y])
            for t in range(3):
                at = s.x_dens + t * ny
                rows = jnp.where(alone_x, 0.0, ref[at : at + ny, :])
                to = t * pitch + 3
                batch.add(into, (slice(to, to + ny), slice(None)), rows)
            batch.flush()
            for end, corner in enumerate((c1_ref, c2_ref)):
                alone = jnp.logical_or(alone_x, is_alone("gy", s.count_y, end))
                for i in range(4):
                    tile = unpack_tile(
                        lambda t: corner[t * loads : (t + 1) * loads, :], 4 * side + i, loads
                    )
                    batch.add(tiles, (i // 2, ys[end] + i % 2), tile)
                for i in range(9):
                    at = s.c_dens + 9 * side + i
                    row = jnp.where(alone, 0.0, corner[at : at + 1, :])
                    to = i // 3 * pitch + yd[end] + i % 3
                    batch.add(into, (pl.ds(to, 1), slice(None)), row)
            batch.flush()

    @pl.when(even_x)
    def _():
        take((high_ref, high_d), (low_ref, low_d))

    @pl.when(jnp.logical_not(even_x))
    def _():
        take((low_ref, low_d), (high_ref, high_d))

    def joined(first, second, own):
        return Joined(Tiles(first, my, loads), Tiles(second, my, loads), own)

    def joined_rows(first, second, own):
        return Joined(Rows(first, pitch, loads), Rows(second, pitch, loads), own)

    outside = (0, 1, nx + 2, nx + 3)
    scaled_own = outside + (2,)
    image_own = (1, 2, 3, nx + 1, nx + 2)
    cond, invx = joined_rows(cond2, cond1, outside), joined_rows(invx2, invx1, scaled_own)
    bx, zx = joined(bx2, bx1, outside), joined(zx2, zx1, scaled_own)
    qx, wx = joined(qx2, qx1, image_own), joined(wx2, wx1, image_own)
    vx = joined(vx2, vx1, again_planes(nx))
    carry1, carry2, carry3 = (Tiles(ref, my, loads) for ref in (carry1, carry2, carry3))

    def conduct(ref, x):
        return conduct_of(ref[x * pitch : (x + 1) * pitch, :])

    low = [conduct(low_d, t) for t in range(3)] + [conduct(dens_ref, 0)]
    high = [conduct(dens_ref, nx - 1)] + [conduct(high_d, t) for t in range(2)]
    for x in range(3):
        inverse = inverse_of(s, low[x], low[x + 1])
        invx.put(x, inverse)
        if x < 2:
            cond.put(x, low[x + 1][1:])
    inv_out[...] = inverse[2 : 2 + ny]
    for x in range(2):
        invx.put(nx + 2 + x, inverse_of(s, high[x], high[x + 1]))
    cond.put(nx + 2, high[1][1:])

    batch = Batch(16)
    for ref, x0 in ((low_ref, 0), (high_ref, nx + 2)):
        tiles = Tiles(ref, my, loads)
        for dx in range(2):
            for y in range(my):
                tile = tiles[dx, y]
                batch.add(bx, (x0 + dx, y), tile)
                batch.add(zx, (x0 + dx, y), tile * invx[x0 + dx, y])
    for y in range(my):
        batch.add(zx, (2, y), bx[2, y] * invx[2, y])
    batch.flush()

    emitter = First(bx, invx, qx, wx)
    element_planes(cond, carry3, 0, 1, 0, my - 1, zx, None)
    element_planes(cond, carry3, 1, 2, 0, my - 1, zx, emitter)
    element_planes(cond, carry3, 3, 1, 0, my - 1, zx, emitter, keep=False)
    element_planes(cond, carry1, nx + 1, 2, 0, my - 1, zx, emitter, keep=False)
    sums = [sums1[place * loads : (place + 1) * loads, :] for place in range(4)]
    emitter = Second(bx, zx, qx, vx, sums)
    element_planes(cond, carry3, 1, 1, 1, my - 3, wx, None)
    element_planes(cond, carry3, 2, 2, 1, my - 3, wx, emitter)
    element_planes(cond, carry3, 4, 1, 1, my - 3, wx, emitter, keep=False)
    element_planes(cond, carry2, nx, 2, 1, my - 3, wx, emitter, keep=False)
    for field, out in ((qx, q_out), (vx, v_out)):
        out = Tiles(out, ny, loads)
        batch = Batch()
        for x in range(nx):
            for y in range(ny):
                batch.add(out, (x, y), field[x + 2, y + 2])
        batch.flush()

    lane = lane_ids(loads)
    load = lax.broadcasted_iota(jnp.int32, (loads, LANES), 0)
    packed = jnp.zeros((loads, LANES), jnp.float32)
    for place, part in enumerate(sums):
        total = jnp.sum(part, axis=1, keepdims=True)
        packed = packed + jnp.where(lane == place * loads + load, total, 0.0)
    row = jnp.sum(packed, axis=0, keepdims=True)
    sums_ref[...] = jnp.broadcast_to(row[None], sums_ref.shape)


def again_planes(nx):
    return (2, 3, 4, nx, nx + 1)


def unpack_kernel(s, q_ref, v_ref, inv1_ref, inv2_ref, qo_ref, vo_ref, io_ref):
    loads, nx, ny = s.loads, s.nx, s.ny
    batch = Batch()
    for x0 in range(0, nx, SUB):
        for ref, out in ((q_ref, qo_ref), (v_ref, vo_ref)):
            for load in range(loads):
                for block in range(packed_count(ny)):
                    tile = pack_block(
                        lambda y: ref[
                            pl.ds((x0 * ny + y) * loads + load, SUB, stride=ny * loads), :
                        ],
                        ny, block, SUB,
                    )
                    lanes = slice(block * LANES, (block + 1) * LANES)
                    batch.add(out, (load, slice(x0, x0 + SUB), lanes), tile)
        for block in range(packed_count(ny)):
            tile = pack_block(
                lambda y: inv1_ref[
                    pl.ds((x0 + 2) * s.pitch + y + 2, SUB, stride=s.pitch), :
                ],
                ny, block, SUB,
            )
            lanes = slice(block * LANES, (block + 1) * LANES)
            batch.add(io_ref, (slice(x0, x0 + SUB), lanes), tile)
    batch.flush()
    for block in range(packed_count(ny)):
        io_ref[0:1, block * LANES : (block + 1) * LANES] = pack_block(
            lambda y: inv2_ref[y : y + 1, :], ny, block, 1
        )


def finish_kernel(s, parts_ref, b_ref, q_ref, v_ref, inv_ref, x_hbm, r_hbm, x_ref, r_ref, sems):
    loads = s.loads
    totals = jnp.sum(parts_ref[...], axis=0)

    def part(place):
        return pltpu.roll(totals, (LANES - place * loads) % LANES, 1) if place else totals

    rz, near, square, last = (part(place) for place in range(4))
    direct = rz - near
    alpha = rz / direct
    short = -near / direct
    rz_next = short * short * rz + 2.0 * alpha * short * near + alpha * alpha * square
    beta = rz_next / rz
    grown = short + beta
    curved = (
        grown * grown * direct
        + 2.0 * alpha * grown * (near - square)
        + alpha * alpha * last
    )
    alpha_next = rz_next / curved
    first_row = alpha + alpha_next * (1.0 + beta)
    second_row = alpha_next * alpha
    inverse = inv_ref[...]
    copies = []
    for load in range(loads):
        first = first_row[:, load : load + 1]
        second = second_row[:, load : load + 1]
        source, image = b_ref[load], q_ref[load]
        x_ref[load] = (first * source - second * image) * inverse
        copies.append(pltpu.make_async_copy(x_ref.at[load], x_hbm.at[load], sems.at[0, load]))
        copies[-1].start()
        r_ref[load] = source - first * image + second * v_ref[load]
        copies.append(pltpu.make_async_copy(r_ref.at[load], r_hbm.at[load], sems.at[1, load]))
        copies[-1].start()
    for copy in copies:
        copy.wait()


def swap(array, axis, start):
    counts = {name: lax.axis_size(name) for name in ("gx", "gy")}
    other = "gy" if axis == "gx" else "gx"
    pairs = []
    for at in np.ndindex(counts["gx"], counts["gy"]):
        place = dict(zip(("gx", "gy"), at))
        partner = place[axis] + (1 if (place[axis] - start) % 2 == 0 else -1)
        if 0 <= partner < counts[axis]:
            place[axis] = partner
        elif place[other] ^ 1 < counts[other]:
            place[other] ^= 1
        pairs.append((at[0] * counts["gy"] + at[1], place["gx"] * counts["gy"] + place["gy"]))
    return lax.ppermute(array, ("gx", "gy"), pairs)


def per_device(heat_source, density):
    loads, nx, flat = heat_source.shape
    ny = flat // NZ
    s = Sizes(loads, nx, ny, lax.axis_size("gx"), lax.axis_size("gy"))
    nodes = nx * ny * loads
    devices = lax.axis_size("gx") * lax.axis_size("gy")

    def shape(*dims):
        return jax.ShapeDtypeStruct(dims, jnp.float32)

    def scratch(*dims):
        return pltpu.VMEM(dims, jnp.float32)

    def call(kernel, out_shape, **more):
        params = pltpu.CompilerParams(vmem_limit_bytes=20 * 1024 * 1024)
        return pl.pallas_call(
            functools.partial(kernel, s), out_shape=out_shape, compiler_params=params, **more
        )

    hbm = pl.BlockSpec(memory_space=pltpu.HBM)
    face = shape(s.y_rows, LANES)
    bt, dt, y2 = call(
        pack_kernel,
        (shape(nodes, LANES), shape(nx * ny, LANES), face),
        in_specs=[hbm, hbm],
        scratch_shapes=[
            scratch(loads, nx, flat),
            scratch(nx, flat),
            pltpu.SemaphoreType.DMA((3,)),
        ],
    )(
        pltpu.with_memory_space_constraint(heat_source, pltpu.HBM),
        pltpu.with_memory_space_constraint(density, pltpu.HBM),
    )
    y2 = swap(y2, "gy", 1)
    x_face, corner = shape(s.x_rows, LANES), shape(s.c_rows, LANES)
    y1, x1, x2 = call(pack_rest_kernel, (face, x_face, x_face))(bt, dt)
    x2, y1, x1 = swap(x2, "gx", 1), swap(y1, "gy", 0), swap(x1, "gx", 0)
    t2 = call(open_y_kernel, shape(2 * nx * loads, LANES))(y2)
    xt, c1, c2 = call(corner_kernel, (shape(4 * ny * loads, LANES), corner, corner))(x1, x2)
    xt, dt = lax.optimization_barrier((xt, dt))
    c2, c1 = swap(c2, "gy", 1), swap(c1, "gy", 0)
    plane = s.my * loads
    rows, field = shape(s.mx * s.pitch, LANES), shape(s.mx * plane, LANES)
    edge = shape(2 * plane, LANES)
    dens, cond, inv_1, bx, zx, q_1, w_1, v_1, carry1, carry2, sums = call(
        inner_kernel,
        (shape(nx * s.pitch, LANES),)
        + (rows,) * 2
        + (field,) * 5
        + (edge,) * 2
        + (shape(4 * loads, LANES),),
    )(bt, dt, y1, y2, t2)
    q_t, v_t, inv_2, sums = call(
        outer_kernel,
        (
            shape(nodes, LANES),
            shape(nodes, LANES),
            shape(ny, LANES),
            shape(devices, 1, LANES),
        ),
        scratch_shapes=[scratch(2 * plane, LANES)] * 2
        + [scratch(3 * s.pitch, LANES)] * 2
        + [scratch(5 * s.pitch, LANES)] * 2
        + [scratch(5 * plane, LANES)] * 5
        + [scratch(2 * plane, LANES)],
    )(dens, x1, x2, xt, c1, c2, cond, inv_1, bx, zx, q_1, w_1, v_1, carry1, carry2, sums)
    parts = lax.all_to_all(sums, ("gx", "gy"), 0, 0, tiled=True)
    whole = shape(loads, nx, flat)
    image, again, inverse = call(unpack_kernel, (whole, whole, shape(nx, flat)))(
        q_t, v_t, inv_1, inv_2
    )
    return call(
        finish_kernel,
        (whole, whole),
        out_specs=(hbm, hbm),
        scratch_shapes=[
            scratch(loads, nx, flat),
            scratch(loads, nx, flat),
            pltpu.SemaphoreType.DMA((2, loads)),
        ],
    )(parts, heat_source, image, again, inverse)


def solution(mesh):
    placed = (P(None, "gx", "gy"), P("gx", "gy"))
    return jax.shard_map(
        per_device,
        mesh=mesh,
        in_specs=placed,
        out_specs=(P(None, "gx", "gy"), P(None, "gx", "gy")),
        check_vma=False,
    )
```

```python
import functools

import jax
import jax.numpy as jnp
import numpy as np
from jax import lax
from jax.experimental import pallas as pl
from jax.experimental.pallas import tpu as pltpu
from jax.sharding import PartitionSpec as P

NZ = 96
KMIN = 0.001
LANES = 128
SUB = 8


class Batch:
    def __init__(self, size=12):
        self.size, self.held = size, []

    def add(self, into, at, tile):
        self.held.append((into, at, tile))
        if len(self.held) >= self.size:
            self.flush()

    def flush(self):
        for into, at, tile in self.held:
            into[at] = tile
        self.held = []


def packed_count(tiles):
    return -(-tiles * NZ // LANES)


def lane_ids(rows):
    return lax.broadcasted_iota(jnp.int32, (rows, LANES), 1)


def unpack_tile(read, index, rows):
    start = index * NZ
    block, offset = start // LANES, start % LANES
    lane = lane_ids(rows)
    first = read(block)
    if offset:
        first = pltpu.roll(first, LANES - offset, 1)
    if offset + NZ > LANES:
        second = pltpu.roll(read(block + 1), LANES - offset, 1)
        first = jnp.where(lane < LANES - offset, first, second)
    return jnp.where(lane < NZ, first, 0.0)


def pack_block(read_tile, tiles, block, rows):
    lane = lane_ids(rows)
    start = block * LANES
    out, at = None, start
    while at < start + LANES and at // NZ < tiles:
        index, z = at // NZ, at % NZ
        here = at - start
        piece = read_tile(index)
        shift = (here - z) % LANES
        if shift:
            piece = pltpu.roll(piece, shift, 1)
        out = piece if out is None else jnp.where(lane < here, out, piece)
        at += NZ - z
    return out


def pack_tiles(out_ref, at, rows, tiles, read_tile):
    batch = Batch()
    for block in range(packed_count(tiles)):
        place = slice(at + block * rows, at + (block + 1) * rows), slice(None)
        batch.add(out_ref, place, pack_block(read_tile, tiles, block, rows))
    batch.flush()


def unpack_tiles(ref, at, rows, tiles, write):
    batch = Batch()
    for index in range(tiles):
        tile = unpack_tile(lambda t: ref[at + t * rows : at + (t + 1) * rows, :], index, rows)
        for store in write(index, tile):
            batch.add(*store)
    batch.flush()


class Sizes:
    def __init__(self, loads, nx, ny, count_x, count_y):
        self.loads, self.nx, self.ny = loads, nx, ny
        self.count_x, self.count_y = count_x, count_y
        self.mx, self.my = nx + 4, ny + 4
        self.pitch = -(-(ny + 6) // SUB) * SUB
        self.y_dens = packed_count(2 * nx) * loads
        self.y_rows = self.y_dens + 3 * nx
        self.x_dens = packed_count(2 * ny) * loads
        self.x_rows = self.x_dens + 3 * ny
        self.c_dens = packed_count(8) * loads
        self.c_rows = self.c_dens + -(-18 // SUB) * SUB


class Tiles:
    def __init__(self, ref, columns, loads):
        self.ref, self.columns, self.loads = ref, columns, loads

    def rows(self, at):
        start = (at[0] * self.columns + at[1]) * self.loads
        if not isinstance(start, int):
            start = pl.multiple_of(start, SUB)
        return pl.ds(start, self.loads)

    def __getitem__(self, at):
        return self.ref[self.rows(at), :]

    def __setitem__(self, at, tile):
        self.ref[self.rows(at), :] = tile


class Rows:
    def __init__(self, ref, pitch, loads):
        self.ref, self.pitch, self.loads = ref, pitch, loads

    def __getitem__(self, at):
        row = self.ref[pl.ds(at[0] * self.pitch + at[1], 1), :]
        return jnp.broadcast_to(row, (self.loads, LANES))

    def put(self, x, values):
        self.ref[x * self.pitch : x * self.pitch + values.shape[0], :] = values


class Joined:
    def __init__(self, first, second, own):
        self.first, self.second, self.own = first, second, own

    def __getitem__(self, at):
        if at[0] in self.own:
            return self.first[self.own.index(at[0]), at[1]]
        return self.second[at]

    def __setitem__(self, at, tile):
        self.first[self.own.index(at[0]), at[1]] = tile

    def put(self, x, values):
        self.first.put(self.own.index(x), values)


def is_even(axis):
    return lax.rem(lax.axis_index(axis), 2) == 0


def is_alone(axis, count, start):
    place = lax.axis_index(axis)
    last = (count - start) % 2
    alone = place < start
    return jnp.logical_or(alone, place == count - 1) if last else alone


def pick(even, if_even, if_odd):
    return jnp.where(even, if_even, if_odd)


def pack_kernel(s, b_hbm, d_hbm, bt_ref, dt_ref, y2_ref, b_ref, d_ref, sems):
    loads, nx, ny = s.loads, s.nx, s.ny
    d_copy = pltpu.make_async_copy(d_hbm, d_ref, sems.at[0])
    d_copy.start()
    parts = 2 if loads % 2 == 0 else 1
    each = loads // parts
    copies = []
    for part in range(parts):
        some = pl.ds(part * each, each)
        copies.append(pltpu.make_async_copy(b_hbm.at[some], b_ref.at[some], sems.at[part + 1]))
        copies[-1].start()
    d_copy.wait()
    batch = Batch(16)
    for x0 in range(0, nx, SUB):
        for y in range(ny):
            tile = unpack_tile(
                lambda t: d_ref[x0 : x0 + SUB, t * LANES : (t + 1) * LANES], y, SUB
            )
            batch.add(dt_ref, (pl.ds(x0 * ny + y, SUB, stride=ny), slice(None)), tile)
    batch.flush()
    for load in range(loads):
        if load % each == 0:
            copies[load // each].wait()
        batch = Batch(16)
        for x0 in range(0, nx, SUB):
            for y in range(ny):
                tile = unpack_tile(
                    lambda t: b_ref[load, x0 : x0 + SUB, t * LANES : (t + 1) * LANES], y, SUB
                )
                rows = pl.ds((x0 * ny + y) * loads + load, SUB, stride=ny * loads)
                batch.add(bt_ref, (rows, slice(None)), tile)
        batch.flush()
    pack_face(s, jnp.logical_not(is_even("gy")), bt_ref, dt_ref, y2_ref)


def pack_rest_kernel(s, bt_ref, dt_ref, y1_ref, x1_ref, x2_ref):
    even_x = is_even("gx")
    pack_x_face(s, jnp.logical_not(even_x), bt_ref, dt_ref, x2_ref)
    pack_x_face(s, even_x, bt_ref, dt_ref, x1_ref)
    pack_face(s, is_even("gy"), bt_ref, dt_ref, y1_ref)


def pack_x_face(s, upper, bt_ref, dt_ref, out_ref):
    loads, nx, ny = s.loads, s.nx, s.ny
    tiles = Tiles(bt_ref, ny, loads)
    x0 = pick(upper, nx - 2, 0)
    pack_tiles(out_ref, 0, loads, 2 * ny, lambda i: tiles[x0 + i // ny, i % ny])
    rows = pl.ds(pl.multiple_of(pick(upper, nx - 3, 0) * ny, SUB), 3 * ny)
    out_ref[s.x_dens :, :] = dt_ref[rows, :]


def pack_face(s, upper, bt_ref, dt_ref, out_ref):
    loads, nx, ny = s.loads, s.nx, s.ny
    tiles = Tiles(bt_ref, ny, loads)
    y0 = pick(upper, ny - 2, 0)
    pack_tiles(out_ref, 0, loads, 2 * nx, lambda i: tiles[i // 2, y0 + i % 2])
    y0 = pick(upper, ny - 3, 0)
    batch = Batch()
    for dy in range(3):
        for x0 in range(0, nx, SUB):
            at = s.y_dens + dy * nx + x0
            tile = dt_ref[pl.ds(x0 * ny + y0 + dy, SUB, stride=ny), :]
            batch.add(out_ref, (slice(at, at + SUB), slice(None)), tile)
    batch.flush()


def open_y_kernel(s, y_ref, t_ref):
    tiles = Tiles(t_ref, 2, s.loads)
    unpack_tiles(
        y_ref, 0, s.loads, 2 * s.nx, lambda i, tile: [(tiles, (i // 2, i % 2), tile)]
    )


def corner_kernel(s, x1_ref, x2_ref, xt_ref, c1_ref, c2_ref):
    loads, ny = s.loads, s.ny
    tiles = Tiles(xt_ref, ny, loads)
    for side, ref in enumerate((x1_ref, x2_ref)):
        unpack_tiles(
            ref, 0, loads, 2 * ny,
            lambda i, tile: [(tiles, (2 * side + i // ny, i % ny), tile)],
        )
    even_y = is_even("gy")
    for out_ref, upper in ((c2_ref, jnp.logical_not(even_y)), (c1_ref, even_y)):
        y0 = pick(upper, ny - 2, 0)
        pack_tiles(out_ref, 0, loads, 8, lambda i: tiles[i // 2, y0 + i % 2])
        y0 = pick(upper, ny - 3, 0)
        batch, at = Batch(18), s.c_dens
        for ref in (x1_ref, x2_ref):
            for t in range(3):
                for dy in range(3):
                    row = ref[pl.ds(s.x_dens + t * ny + y0 + dy, 1), :]
                    batch.add(out_ref, (slice(at, at + 1), slice(None)), row)
                    at += 1
        batch.flush()
        out_ref[at:, :] = jnp.zeros((s.c_rows - at, LANES), jnp.float32)


def join_density(s, dt_ref, y1_ref, y2_ref, dens_ref):
    nx, ny, pitch = s.nx, s.ny, s.pitch
    even_y = is_even("gy")
    yd = (pick(even_y, ny + 3, 0), pick(even_y, 0, ny + 3))
    batch = Batch(16)
    for x in range(nx):
        at = x * pitch
        batch.add(
            dens_ref, (slice(at + 3, at + 3 + ny), slice(None)), dt_ref[x * ny : (x + 1) * ny, :]
        )
    batch.flush()
    for side, ref in enumerate((y1_ref, y2_ref)):
        alone = is_alone("gy", s.count_y, side)
        for dy in range(3):
            for x0 in range(0, nx, SUB):
                at = s.y_dens + dy * nx + x0
                to = x0 * pitch + yd[side] + dy
                batch.add(
                    dens_ref,
                    (pl.ds(to, SUB, stride=pitch), slice(None)),
                    jnp.where(alone, 0.0, ref[at : at + SUB, :]),
                )
    batch.flush()


def conduct_of(dens):
    return jnp.where(
        dens > 0.0, (KMIN + (1.0 - KMIN) * (dens * dens * dens)) * (1.0 / 12.0), 0.0
    )


def inverse_of(s, before, after):
    pair = before + after
    pair = pair[: s.pitch - 1] + pair[1:]
    total = 4.0 * (pair + pltpu.roll(pair, 1, 1))
    return jnp.where(after[1:] > 0.0, 1.0 / total, 0.0)


def up(tile):
    return pltpu.roll(tile, LANES - 1, 1)


def element_planes(cond, carry, a, count, y0, columns, field, emitter, keep=True):
    def loads_of(step):
        y = y0 + step
        right = [field[a + u, y + 1] for u in range(count + 1)]
        conduct = [cond[a + u, y] for u in range(count)]
        above = extra = None
        if step and emitter:
            above = (carry[0, y], carry[1, y])
            extra = [emitter.fetch(a + u, y) for u in range(count)]
        return right, conduct, above, extra

    left = [(tile, up(tile)) for tile in [field[a + u, y0] for u in range(count + 1)]]
    ahead = loads_of(0)
    old, waiting = [None] * count, []
    for step in range(columns):
        y = y0 + step
        right, conduct, above, extra = ahead
        if step + 1 < columns:
            ahead = loads_of(step + 1)
        if len(waiting) > 1:
            for into, at, tile in waiting.pop(0):
                into[at] = tile
        stores = []
        right = [(tile, up(tile)) for tile in right]
        for u in range(count):
            (p0, p0s), (p1, p1s) = left[u], left[u + 1]
            (r0, r0s), (r1, r1s) = right[u], right[u + 1]
            c = conduct[u]
            even = (p0 + r1) + (r0s + p1s)
            odd = (r0 + p1) + (p0s + r1s)
            pass_on = keep or u + 1 < count
            lower = upper = None
            if emitter:
                lower = (c * (odd + p1s), c * (even + p1))
            if pass_on:
                upper = (c * (even + p0s), c * (odd + p0))
            if step and emitter:
                low = (c * (even + r1s) + old[u][0][0]) + above[0]
                high = (c * (odd + r1) + old[u][0][1]) + above[1]
                total = low + pltpu.roll(high, 1, 1)
                stores += emitter.finish(a + u, y, p0, total, extra[u])
            if step and pass_on:
                above = (
                    c * (odd + r0s) + old[u][1][0],
                    c * (even + r0) + old[u][1][1],
                )
            old[u] = (lower, upper)
        if step and keep:
            stores += [(carry, (0, y), above[0]), (carry, (1, y), above[1])]
        waiting.append(stores)
        left = right
    for stores in waiting:
        for into, at, tile in stores:
            into[at] = tile


class First:
    def __init__(self, bx, invx, qx, wx):
        self.bx, self.invx, self.qx, self.wx = bx, invx, qx, wx

    def fetch(self, x, y):
        return self.bx[x, y], self.invx[x, y]

    def finish(self, x, y, node, total, extra):
        source, inverse = extra
        image = 1.25 * source - total
        return [(self.qx, (x, y), image), (self.wx, (x, y), image * inverse)]


class Second:
    def __init__(self, bx, zx, qx, vx, sums):
        self.bx, self.zx, self.qx, self.vx, self.sums = bx, zx, qx, vx, sums

    def fetch(self, x, y):
        return self.bx[x, y], self.zx[x, y], self.qx[x, y]

    def finish(self, x, y, weighted, total, extra):
        source, scaled, image = extra
        again = 1.25 * image - total
        change = scaled - weighted
        sums = self.sums
        sums[0] = sums[0] + source * scaled
        sums[1] = sums[1] + source * change
        sums[2] = sums[2] + (source - image) * change
        sums[3] = sums[3] + (image - again) * change
        return [(self.vx, (x, y), again)]


def over_planes(start, stop, body, state):
    pairs = (stop - start) // 2
    state = lax.fori_loop(0, pairs, lambda i, st: body(start + 2 * i, 2, st), state)
    if (stop - start) % 2:
        state = body(stop - 1, 1, state)
    return state


def inner_kernel(
    s, bt_ref, dt_ref, y1_ref, y2_ref, t2_ref,
    dens_ref, cond, invx, bx, zx, qx, wx, vx, carry1, carry2, sums_ref,
):
    loads, nx, ny, my, pitch = s.loads, s.nx, s.ny, s.my, s.pitch
    bx, zx, qx, wx, vx, carry1, carry2 = (
        Tiles(ref, my, loads) for ref in (bx, zx, qx, wx, vx, carry1, carry2)
    )
    cond, invx = Rows(cond, pitch, loads), Rows(invx, pitch, loads)
    join_density(s, dt_ref, y1_ref, y2_ref, dens_ref)
    even_y = is_even("gy")
    ys = (pick(even_y, ny + 2, 0), pick(even_y, 0, ny + 2))
    before = None
    for x in range(nx):
        after = conduct_of(dens_ref[x * pitch : (x + 1) * pitch, :])
        cond.put(x + 2, after[1:])
        if x:
            invx.put(x + 2, inverse_of(s, before, after))
        before = after

    def stage(x, y, tile):
        stores = [(bx, (x + 2, y), tile)]
        if x:
            stores.append((zx, (x + 2, y), tile * invx[x + 2, y]))
        return stores

    inner = Tiles(bt_ref, ny, loads)
    batch = Batch(16)
    for x in range(nx):
        for y in range(ny):
            for store in stage(x, y + 2, inner[x, y]):
                batch.add(*store)
    batch.flush()
    unpack_tiles(
        y1_ref, 0, loads, 2 * nx, lambda i, tile: stage(i // 2, ys[0] + i % 2, tile)
    )
    far = Tiles(t2_ref, 2, loads)
    batch = Batch(16)
    for x in range(nx):
        for dy in range(2):
            for store in stage(x, ys[1] + dy, far[x, dy]):
                batch.add(*store)
    batch.flush()

    element_planes(cond, carry1, 3, 1, 0, my - 1, zx, None)

    def first(a, count, state):
        element_planes(cond, carry1, a, count, 0, my - 1, zx, First(bx, invx, qx, wx))
        return state

    over_planes(4, nx + 1, first, 0)
    element_planes(cond, carry2, 4, 1, 1, my - 3, wx, None)

    def second(a, count, sums):
        sums = list(sums)
        element_planes(cond, carry2, a, count, 1, my - 3, wx, Second(bx, zx, qx, vx, sums))
        return tuple(sums)

    zero = jnp.zeros((loads, LANES), jnp.float32)
    sums = over_planes(5, nx, second, (zero,) * 4)
    for place, part in enumerate(sums):
        sums_ref[place * loads : (place + 1) * loads, :] = part


def outer_kernel(
    s, dens_ref, x1_ref, x2_ref, xt_ref, c1_ref, c2_ref,
    cond1, invx1, bx1, zx1, qx1, wx1, vx1, carry1, carry2, sums1,
    q_out, v_out, inv_out, sums_ref,
    low_ref, high_ref, low_d, high_d, cond2, invx2, bx2, zx2, qx2, wx2, vx2, carry3,
):
    loads, nx, ny, mx, my, pitch = s.loads, s.nx, s.ny, s.mx, s.my, s.pitch
    even_x = is_even("gx")

    even_y = is_even("gy")
    ys = (pick(even_y, ny + 2, 0), pick(even_y, 0, ny + 2))
    yd = (pick(even_y, ny + 3, 0), pick(even_y, 0, ny + 3))

    def take(near, far):
        faces = Tiles(xt_ref, ny, loads)
        for side, (ref, (tiles_ref, into)) in enumerate(((x1_ref, near), (x2_ref, far))):
            tiles = Tiles(tiles_ref, my, loads)
            alone_x = is_alone("gx", s.count_x, side)
            batch = Batch(18)
            for dx in range(2):
                for y in range(ny):
                    batch.add(tiles, (dx, y + 2), faces[2 * side + dx, y])
            for t in range(3):
                at = s.x_dens + t * ny
                rows = jnp.where(alone_x, 0.0, ref[at : at + ny, :])
                to = t * pitch + 3
                batch.add(into, (slice(to, to + ny), slice(None)), rows)
            batch.flush()
            for end, corner in enumerate((c1_ref, c2_ref)):
                alone = jnp.logical_or(alone_x, is_alone("gy", s.count_y, end))
                for i in range(4):
                    tile = unpack_tile(
                        lambda t: corner[t * loads : (t + 1) * loads, :], 4 * side + i, loads
                    )
                    batch.add(tiles, (i // 2, ys[end] + i % 2), tile)
                for i in range(9):
                    at = s.c_dens + 9 * side + i
                    row = jnp.where(alone, 0.0, corner[at : at + 1, :])
                    to = i // 3 * pitch + yd[end] + i % 3
                    batch.add(into, (pl.ds(to, 1), slice(None)), row)
            batch.flush()

    @pl.when(even_x)
    def _():
        take((high_ref, high_d), (low_ref, low_d))

    @pl.when(jnp.logical_not(even_x))
    def _():
        take((low_ref, low_d), (high_ref, high_d))

    def joined(first, second, own):
        return Joined(Tiles(first, my, loads), Tiles(second, my, loads), own)

    def joined_rows(first, second, own):
        return Joined(Rows(first, pitch, loads), Rows(second, pitch, loads), own)

    outside = (0, 1, nx + 2, nx + 3)
    scaled_own = outside + (2,)
    image_own = (1, 2, 3, nx + 1, nx + 2)
    cond, invx = joined_rows(cond2, cond1, outside), joined_rows(invx2, invx1, scaled_own)
    bx, zx = joined(bx2, bx1, outside), joined(zx2, zx1, scaled_own)
    qx, wx = joined(qx2, qx1, image_own), joined(wx2, wx1, image_own)
    vx = joined(vx2, vx1, again_planes(nx))
    carry1, carry2, carry3 = (Tiles(ref, my, loads) for ref in (carry1, carry2, carry3))

    def conduct(ref, x):
        return conduct_of(ref[x * pitch : (x + 1) * pitch, :])

    low = [conduct(low_d, t) for t in range(3)] + [conduct(dens_ref, 0)]
    high = [conduct(dens_ref, nx - 1)] + [conduct(high_d, t) for t in range(2)]
    for x in range(3):
        inverse = inverse_of(s, low[x], low[x + 1])
        invx.put(x, inverse)
        if x < 2:
            cond.put(x, low[x + 1][1:])
    inv_out[...] = inverse[2 : 2 + ny]
    for x in range(2):
        invx.put(nx + 2 + x, inverse_of(s, high[x], high[x + 1]))
    cond.put(nx + 2, high[1][1:])

    batch = Batch(16)
    for ref, x0 in ((low_ref, 0), (high_ref, nx + 2)):
        tiles = Tiles(ref, my, loads)
        for dx in range(2):
            for y in range(my):
                tile = tiles[dx, y]
                batch.add(bx, (x0 + dx, y), tile)
                batch.add(zx, (x0 + dx, y), tile * invx[x0 + dx, y])
    for y in range(my):
        batch.add(zx, (2, y), bx[2, y] * invx[2, y])
    batch.flush()

    emitter = First(bx, invx, qx, wx)
    element_planes(cond, carry3, 0, 1, 0, my - 1, zx, None)
    element_planes(cond, carry3, 1, 2, 0, my - 1, zx, emitter)
    element_planes(cond, carry3, 3, 1, 0, my - 1, zx, emitter, keep=False)
    element_planes(cond, carry1, nx + 1, 2, 0, my - 1, zx, emitter, keep=False)
    sums = [sums1[place * loads : (place + 1) * loads, :] for place in range(4)]
    emitter = Second(bx, zx, qx, vx, sums)
    element_planes(cond, carry3, 1, 1, 1, my - 3, wx, None)
    element_planes(cond, carry3, 2, 2, 1, my - 3, wx, emitter)
    element_planes(cond, carry3, 4, 1, 1, my - 3, wx, emitter, keep=False)
    element_planes(cond, carry2, nx, 2, 1, my - 3, wx, emitter, keep=False)
    for field, out in ((qx, q_out), (vx, v_out)):
        out = Tiles(out, ny, loads)
        batch = Batch()
        for x in range(nx):
            for y in range(ny):
                batch.add(out, (x, y), field[x + 2, y + 2])
        batch.flush()

    lane = lane_ids(loads)
    load = lax.broadcasted_iota(jnp.int32, (loads, LANES), 0)
    packed = jnp.zeros((loads, LANES), jnp.float32)
    for place, part in enumerate(sums):
        total = jnp.sum(part, axis=1, keepdims=True)
        packed = packed + jnp.where(lane == place * loads + load, total, 0.0)
    sums_ref[...] = jnp.sum(packed, axis=0, keepdims=True)


def again_planes(nx):
    return (2, 3, 4, nx, nx + 1)


def unpack_kernel(s, q_ref, v_ref, inv1_ref, inv2_ref, qo_ref, vo_ref, io_ref):
    loads, nx, ny = s.loads, s.nx, s.ny
    batch = Batch()
    for x0 in range(0, nx, SUB):
        for ref, out in ((q_ref, qo_ref), (v_ref, vo_ref)):
            for load in range(loads):
                for block in range(packed_count(ny)):
                    tile = pack_block(
                        lambda y: ref[
                            pl.ds((x0 * ny + y) * loads + load, SUB, stride=ny * loads), :
                        ],
                        ny, block, SUB,
                    )
                    lanes = slice(block * LANES, (block + 1) * LANES)
                    batch.add(out, (load, slice(x0, x0 + SUB), lanes), tile)
        for block in range(packed_count(ny)):
            tile = pack_block(
                lambda y: inv1_ref[
                    pl.ds((x0 + 2) * s.pitch + y + 2, SUB, stride=s.pitch), :
                ],
                ny, block, SUB,
            )
            lanes = slice(block * LANES, (block + 1) * LANES)
            batch.add(io_ref, (slice(x0, x0 + SUB), lanes), tile)
    batch.flush()
    for block in range(packed_count(ny)):
        io_ref[0:1, block * LANES : (block + 1) * LANES] = pack_block(
            lambda y: inv2_ref[y : y + 1, :], ny, block, 1
        )


def finish_kernel(s, *refs):
    *parts, b_ref, q_ref, v_ref, inv_ref, x_hbm, r_hbm, x_ref, r_ref, sems = refs
    loads = s.loads
    totals = functools.reduce(jnp.add, [ref[...] for ref in parts])

    def part(place):
        return pltpu.roll(totals, (LANES - place * loads) % LANES, 1) if place else totals

    rz, near, square, last = (part(place) for place in range(4))
    direct = rz - near
    alpha = rz / direct
    short = -near / direct
    rz_next = short * short * rz + 2.0 * alpha * short * near + alpha * alpha * square
    beta = rz_next / rz
    grown = short + beta
    curved = (
        grown * grown * direct
        + 2.0 * alpha * grown * (near - square)
        + alpha * alpha * last
    )
    alpha_next = rz_next / curved
    first_row = alpha + alpha_next * (1.0 + beta)
    second_row = alpha_next * alpha
    inverse = inv_ref[...]
    copies = []
    for load in range(loads):
        first = first_row[:, load : load + 1]
        second = second_row[:, load : load + 1]
        source, image = b_ref[load], q_ref[load]
        x_ref[load] = (first * source - second * image) * inverse
        copies.append(pltpu.make_async_copy(x_ref.at[load], x_hbm.at[load], sems.at[0, load]))
        copies[-1].start()
        r_ref[load] = source - first * image + second * v_ref[load]
        copies.append(pltpu.make_async_copy(r_ref.at[load], r_hbm.at[load], sems.at[1, load]))
        copies[-1].start()
    for copy in copies:
        copy.wait()


def radices(length):
    found = []
    while length > 1:
        small = [f for f in range(2, 9) if length % f == 0]
        factor = max(small) if small else length
        found.append(factor)
        length //= factor
    return found


def sum_rounds(row, axis):
    length, stride, rows = lax.axis_size(axis), 1, [row]
    for factor in radices(length):
        row = functools.reduce(jnp.add, rows)
        rows = [row]
        for step in range(1, factor):
            pairs = []
            for i in range(length):
                digit = i // stride % factor
                to = digit ^ step if factor & (factor - 1) == 0 else (digit + step) % factor
                pairs.append((i, i + (to - digit) * stride))
            rows.append(lax.ppermute(row, axis, pairs))
        stride *= factor
    return rows


def swap(array, axis, start):
    counts = {name: lax.axis_size(name) for name in ("gx", "gy")}
    other = "gy" if axis == "gx" else "gx"
    pairs = []
    for at in np.ndindex(counts["gx"], counts["gy"]):
        place = dict(zip(("gx", "gy"), at))
        partner = place[axis] + (1 if (place[axis] - start) % 2 == 0 else -1)
        if 0 <= partner < counts[axis]:
            place[axis] = partner
        elif place[other] ^ 1 < counts[other]:
            place[other] ^= 1
        pairs.append((at[0] * counts["gy"] + at[1], place["gx"] * counts["gy"] + place["gy"]))
    return lax.ppermute(array, ("gx", "gy"), pairs)


def per_device(heat_source, density):
    loads, nx, flat = heat_source.shape
    ny = flat // NZ
    s = Sizes(loads, nx, ny, lax.axis_size("gx"), lax.axis_size("gy"))
    nodes = nx * ny * loads

    def shape(*dims):
        return jax.ShapeDtypeStruct(dims, jnp.float32)

    def scratch(*dims):
        return pltpu.VMEM(dims, jnp.float32)

    def call(kernel, out_shape, **more):
        params = pltpu.CompilerParams(vmem_limit_bytes=20 * 1024 * 1024)
        return pl.pallas_call(
            functools.partial(kernel, s), out_shape=out_shape, compiler_params=params, **more
        )

    hbm = pl.BlockSpec(memory_space=pltpu.HBM)
    face = shape(s.y_rows, LANES)
    bt, dt, y2 = call(
        pack_kernel,
        (shape(nodes, LANES), shape(nx * ny, LANES), face),
        in_specs=[hbm, hbm],
        scratch_shapes=[
            scratch(loads, nx, flat),
            scratch(nx, flat),
            pltpu.SemaphoreType.DMA((3,)),
        ],
    )(
        pltpu.with_memory_space_constraint(heat_source, pltpu.HBM),
        pltpu.with_memory_space_constraint(density, pltpu.HBM),
    )
    y2 = swap(y2, "gy", 1)
    x_face, corner = shape(s.x_rows, LANES), shape(s.c_rows, LANES)
    y1, x1, x2 = call(pack_rest_kernel, (face, x_face, x_face))(bt, dt)
    x2, y1, x1 = swap(x2, "gx", 1), swap(y1, "gy", 0), swap(x1, "gx", 0)
    t2 = call(open_y_kernel, shape(2 * nx * loads, LANES))(y2)
    xt, c1, c2 = call(corner_kernel, (shape(4 * ny * loads, LANES), corner, corner))(x1, x2)
    xt, dt = lax.optimization_barrier((xt, dt))
    c2, c1 = swap(c2, "gy", 1), swap(c1, "gy", 0)
    plane = s.my * loads
    rows, field = shape(s.mx * s.pitch, LANES), shape(s.mx * plane, LANES)
    edge = shape(2 * plane, LANES)
    dens, cond, inv_1, bx, zx, q_1, w_1, v_1, carry1, carry2, sums = call(
        inner_kernel,
        (shape(nx * s.pitch, LANES),)
        + (rows,) * 2
        + (field,) * 5
        + (edge,) * 2
        + (shape(4 * loads, LANES),),
    )(bt, dt, y1, y2, t2)
    q_t, v_t, inv_2, sums = call(
        outer_kernel,
        (
            shape(nodes, LANES),
            shape(nodes, LANES),
            shape(ny, LANES),
            shape(1, LANES),
        ),
        scratch_shapes=[scratch(2 * plane, LANES)] * 2
        + [scratch(3 * s.pitch, LANES)] * 2
        + [scratch(5 * s.pitch, LANES)] * 2
        + [scratch(5 * plane, LANES)] * 5
        + [scratch(2 * plane, LANES)],
    )(dens, x1, x2, xt, c1, c2, cond, inv_1, bx, zx, q_1, w_1, v_1, carry1, carry2, sums)
    parts = sum_rounds(functools.reduce(jnp.add, sum_rounds(sums, "gy")), "gx")
    whole = shape(loads, nx, flat)
    image, again, inverse = call(unpack_kernel, (whole, whole, shape(nx, flat)))(
        q_t, v_t, inv_1, inv_2
    )
    return call(
        finish_kernel,
        (whole, whole),
        out_specs=(hbm, hbm),
        scratch_shapes=[
            scratch(loads, nx, flat),
            scratch(loads, nx, flat),
            pltpu.SemaphoreType.DMA((2, loads)),
        ],
    )(*parts, heat_source, image, again, inverse)


def solution(mesh):
    placed = (P(None, "gx", "gy"), P("gx", "gy"))
    return jax.shard_map(
        per_device,
        mesh=mesh,
        in_specs=placed,
        out_specs=(P(None, "gx", "gy"), P(None, "gx", "gy")),
        check_vma=False,
    )
```

```python
import functools

import jax
import jax.numpy as jnp
import numpy as np
from jax import lax
from jax.experimental import pallas as pl
from jax.experimental.pallas import tpu as pltpu
from jax.sharding import PartitionSpec as P

NZ = 96
KMIN = 0.001
LANES = 128
SUB = 8


class Batch:
    def __init__(self, size=12):
        self.size, self.held = size, []

    def add(self, into, at, tile):
        self.held.append((into, at, tile))
        if len(self.held) >= self.size:
            self.flush()

    def flush(self):
        for into, at, tile in self.held:
            into[at] = tile
        self.held = []


def packed_count(tiles):
    return -(-tiles * NZ // LANES)


def lane_ids(rows):
    return lax.broadcasted_iota(jnp.int32, (rows, LANES), 1)


def unpack_tile(read, index, rows):
    start = index * NZ
    block, offset = start // LANES, start % LANES
    lane = lane_ids(rows)
    first = read(block)
    if offset:
        first = pltpu.roll(first, LANES - offset, 1)
    if offset + NZ > LANES:
        second = pltpu.roll(read(block + 1), LANES - offset, 1)
        first = jnp.where(lane < LANES - offset, first, second)
    return jnp.where(lane < NZ, first, 0.0)


def pack_block(read_tile, tiles, block, rows):
    lane = lane_ids(rows)
    start = block * LANES
    out, at = None, start
    while at < start + LANES and at // NZ < tiles:
        index, z = at // NZ, at % NZ
        here = at - start
        piece = read_tile(index)
        shift = (here - z) % LANES
        if shift:
            piece = pltpu.roll(piece, shift, 1)
        out = piece if out is None else jnp.where(lane < here, out, piece)
        at += NZ - z
    return out


def pack_tiles(out_ref, at, rows, tiles, read_tile):
    batch = Batch()
    for block in range(packed_count(tiles)):
        place = slice(at + block * rows, at + (block + 1) * rows), slice(None)
        batch.add(out_ref, place, pack_block(read_tile, tiles, block, rows))
    batch.flush()


def unpack_tiles(ref, at, rows, tiles, write):
    batch = Batch()
    for index in range(tiles):
        tile = unpack_tile(lambda t: ref[at + t * rows : at + (t + 1) * rows, :], index, rows)
        for store in write(index, tile):
            batch.add(*store)
    batch.flush()


class Sizes:
    def __init__(self, loads, nx, ny, count_x, count_y):
        self.loads, self.nx, self.ny = loads, nx, ny
        self.count_x, self.count_y = count_x, count_y
        self.mx, self.my = nx + 4, ny + 4
        self.pitch = -(-(ny + 6) // SUB) * SUB
        self.y_dens = packed_count(2 * nx) * loads
        self.y_rows = self.y_dens + 3 * nx
        self.x_dens = packed_count(2 * ny) * loads
        self.x_rows = self.x_dens + 3 * ny
        self.c_dens = packed_count(8) * loads
        self.c_rows = self.c_dens + -(-18 // SUB) * SUB


class Tiles:
    def __init__(self, ref, columns, loads):
        self.ref, self.columns, self.loads = ref, columns, loads

    def rows(self, at):
        start = (at[0] * self.columns + at[1]) * self.loads
        if not isinstance(start, int):
            start = pl.multiple_of(start, SUB)
        return pl.ds(start, self.loads)

    def __getitem__(self, at):
        return self.ref[self.rows(at), :]

    def __setitem__(self, at, tile):
        self.ref[self.rows(at), :] = tile


class Rows:
    def __init__(self, ref, pitch, loads):
        self.ref, self.pitch, self.loads = ref, pitch, loads

    def __getitem__(self, at):
        row = self.ref[pl.ds(at[0] * self.pitch + at[1], 1), :]
        return jnp.broadcast_to(row, (self.loads, LANES))

    def put(self, x, values):
        self.ref[x * self.pitch : x * self.pitch + values.shape[0], :] = values


class Joined:
    def __init__(self, first, second, own):
        self.first, self.second, self.own = first, second, own

    def __getitem__(self, at):
        if at[0] in self.own:
            return self.first[self.own.index(at[0]), at[1]]
        return self.second[at]

    def __setitem__(self, at, tile):
        self.first[self.own.index(at[0]), at[1]] = tile

    def put(self, x, values):
        self.first.put(self.own.index(x), values)


def is_even(axis):
    return lax.rem(lax.axis_index(axis), 2) == 0


def is_alone(axis, count, start):
    place = lax.axis_index(axis)
    last = (count - start) % 2
    alone = place < start
    return jnp.logical_or(alone, place == count - 1) if last else alone


def pick(even, if_even, if_odd):
    return jnp.where(even, if_even, if_odd)


def pack_kernel(s, b_hbm, d_hbm, bt_ref, dt_ref, y2_ref, b_ref, d_ref, sems):
    loads, nx, ny = s.loads, s.nx, s.ny
    d_copy = pltpu.make_async_copy(d_hbm, d_ref, sems.at[0])
    d_copy.start()
    parts = 2 if loads % 2 == 0 else 1
    each = loads // parts
    copies = []
    for part in range(parts):
        some = pl.ds(part * each, each)
        copies.append(pltpu.make_async_copy(b_hbm.at[some], b_ref.at[some], sems.at[part + 1]))
        copies[-1].start()
    d_copy.wait()
    batch = Batch(16)
    for x0 in range(0, nx, SUB):
        for y in range(ny):
            tile = unpack_tile(
                lambda t: d_ref[x0 : x0 + SUB, t * LANES : (t + 1) * LANES], y, SUB
            )
            batch.add(dt_ref, (pl.ds(x0 * ny + y, SUB, stride=ny), slice(None)), tile)
    batch.flush()
    for load in range(loads):
        if load % each == 0:
            copies[load // each].wait()
        batch = Batch(16)
        for x0 in range(0, nx, SUB):
            for y in range(ny):
                tile = unpack_tile(
                    lambda t: b_ref[load, x0 : x0 + SUB, t * LANES : (t + 1) * LANES], y, SUB
                )
                rows = pl.ds((x0 * ny + y) * loads + load, SUB, stride=ny * loads)
                batch.add(bt_ref, (rows, slice(None)), tile)
        batch.flush()
    pack_face(s, jnp.logical_not(is_even("gy")), bt_ref, dt_ref, y2_ref)


def pack_rest_kernel(s, bt_ref, dt_ref, y1_ref, x1_ref, x2_ref):
    even_x = is_even("gx")
    pack_x_face(s, jnp.logical_not(even_x), bt_ref, dt_ref, x2_ref)
    pack_x_face(s, even_x, bt_ref, dt_ref, x1_ref)
    pack_face(s, is_even("gy"), bt_ref, dt_ref, y1_ref)


def pack_x_face(s, upper, bt_ref, dt_ref, out_ref):
    loads, nx, ny = s.loads, s.nx, s.ny
    tiles = Tiles(bt_ref, ny, loads)
    x0 = pick(upper, nx - 2, 0)
    pack_tiles(out_ref, 0, loads, 2 * ny, lambda i: tiles[x0 + i // ny, i % ny])
    rows = pl.ds(pl.multiple_of(pick(upper, nx - 3, 0) * ny, SUB), 3 * ny)
    out_ref[s.x_dens :, :] = dt_ref[rows, :]


def pack_face(s, upper, bt_ref, dt_ref, out_ref):
    loads, nx, ny = s.loads, s.nx, s.ny
    tiles = Tiles(bt_ref, ny, loads)
    y0 = pick(upper, ny - 2, 0)
    pack_tiles(out_ref, 0, loads, 2 * nx, lambda i: tiles[i // 2, y0 + i % 2])
    y0 = pick(upper, ny - 3, 0)
    batch = Batch()
    for dy in range(3):
        for x0 in range(0, nx, SUB):
            at = s.y_dens + dy * nx + x0
            tile = dt_ref[pl.ds(x0 * ny + y0 + dy, SUB, stride=ny), :]
            batch.add(out_ref, (slice(at, at + SUB), slice(None)), tile)
    batch.flush()


def open_y_kernel(s, y_ref, t_ref):
    tiles = Tiles(t_ref, 2, s.loads)
    unpack_tiles(
        y_ref, 0, s.loads, 2 * s.nx, lambda i, tile: [(tiles, (i // 2, i % 2), tile)]
    )


def open_x_kernel(s, x_ref, t_ref):
    tiles = Tiles(t_ref, s.ny, s.loads)
    unpack_tiles(
        x_ref, 0, s.loads, 2 * s.ny, lambda i, tile: [(tiles, (i // s.ny, i % s.ny), tile)]
    )


def corner_kernel(s, x2_ref, t2_ref, x1_ref, t1_ref, c1_ref, c2_ref):
    loads, ny = s.loads, s.ny
    open_x_kernel(s, x1_ref, t1_ref)
    halves = Tiles(t1_ref, ny, loads), Tiles(t2_ref, ny, loads)
    even_y = is_even("gy")
    for out_ref, upper in ((c2_ref, jnp.logical_not(even_y)), (c1_ref, even_y)):
        y0 = pick(upper, ny - 2, 0)
        pack_tiles(out_ref, 0, loads, 8, lambda i: halves[i // 4][i // 2 % 2, y0 + i % 2])
        y0 = pick(upper, ny - 3, 0)
        batch, at = Batch(18), s.c_dens
        for ref in (x1_ref, x2_ref):
            for t in range(3):
                for dy in range(3):
                    row = ref[pl.ds(s.x_dens + t * ny + y0 + dy, 1), :]
                    batch.add(out_ref, (slice(at, at + 1), slice(None)), row)
                    at += 1
        batch.flush()
        out_ref[at:, :] = jnp.zeros((s.c_rows - at, LANES), jnp.float32)


def join_density(s, dt_ref, y1_ref, y2_ref, dens_ref):
    nx, ny, pitch = s.nx, s.ny, s.pitch
    even_y = is_even("gy")
    yd = (pick(even_y, ny + 3, 0), pick(even_y, 0, ny + 3))
    batch = Batch(16)
    for x in range(nx):
        at = x * pitch
        batch.add(
            dens_ref, (slice(at + 3, at + 3 + ny), slice(None)), dt_ref[x * ny : (x + 1) * ny, :]
        )
    batch.flush()
    for side, ref in enumerate((y1_ref, y2_ref)):
        alone = is_alone("gy", s.count_y, side)
        for dy in range(3):
            for x0 in range(0, nx, SUB):
                at = s.y_dens + dy * nx + x0
                to = x0 * pitch + yd[side] + dy
                batch.add(
                    dens_ref,
                    (pl.ds(to, SUB, stride=pitch), slice(None)),
                    jnp.where(alone, 0.0, ref[at : at + SUB, :]),
                )
    batch.flush()


def conduct_of(dens):
    return jnp.where(
        dens > 0.0, (KMIN + (1.0 - KMIN) * (dens * dens * dens)) * (1.0 / 12.0), 0.0
    )


def inverse_of(s, before, after):
    pair = before + after
    pair = pair[: s.pitch - 1] + pair[1:]
    total = 4.0 * (pair + pltpu.roll(pair, 1, 1))
    return jnp.where(after[1:] > 0.0, 1.0 / total, 0.0)


def up(tile):
    return pltpu.roll(tile, LANES - 1, 1)


def element_planes(cond, carry, a, count, y0, columns, field, emitter, keep=True):
    def loads_of(step):
        y = y0 + step
        right = [field[a + u, y + 1] for u in range(count + 1)]
        conduct = [cond[a + u, y] for u in range(count)]
        above = extra = None
        if step and emitter:
            above = (carry[0, y], carry[1, y])
            extra = [emitter.fetch(a + u, y) for u in range(count)]
        return right, conduct, above, extra

    left = [(tile, up(tile)) for tile in [field[a + u, y0] for u in range(count + 1)]]
    ahead = loads_of(0)
    old, waiting = [None] * count, []
    for step in range(columns):
        y = y0 + step
        right, conduct, above, extra = ahead
        if step + 1 < columns:
            ahead = loads_of(step + 1)
        if len(waiting) > 1:
            for into, at, tile in waiting.pop(0):
                into[at] = tile
        stores = []
        right = [(tile, up(tile)) for tile in right]
        for u in range(count):
            (p0, p0s), (p1, p1s) = left[u], left[u + 1]
            (r0, r0s), (r1, r1s) = right[u], right[u + 1]
            c = conduct[u]
            even = (p0 + r1) + (r0s + p1s)
            odd = (r0 + p1) + (p0s + r1s)
            pass_on = keep or u + 1 < count
            lower = upper = None
            if emitter:
                lower = (c * (odd + p1s), c * (even + p1))
            if pass_on:
                upper = (c * (even + p0s), c * (odd + p0))
            if step and emitter:
                low = (c * (even + r1s) + old[u][0][0]) + above[0]
                high = (c * (odd + r1) + old[u][0][1]) + above[1]
                total = low + pltpu.roll(high, 1, 1)
                stores += emitter.finish(a + u, y, p0, total, extra[u])
            if step and pass_on:
                above = (
                    c * (odd + r0s) + old[u][1][0],
                    c * (even + r0) + old[u][1][1],
                )
            old[u] = (lower, upper)
        if step and keep:
            stores += [(carry, (0, y), above[0]), (carry, (1, y), above[1])]
        waiting.append(stores)
        left = right
    for stores in waiting:
        for into, at, tile in stores:
            into[at] = tile


class First:
    def __init__(self, bx, invx, qx, wx):
        self.bx, self.invx, self.qx, self.wx = bx, invx, qx, wx

    def fetch(self, x, y):
        return self.bx[x, y], self.invx[x, y]

    def finish(self, x, y, node, total, extra):
        source, inverse = extra
        image = 1.25 * source - total
        return [(self.qx, (x, y), image), (self.wx, (x, y), image * inverse)]


class Second:
    def __init__(self, bx, zx, qx, vx, sums):
        self.bx, self.zx, self.qx, self.vx, self.sums = bx, zx, qx, vx, sums

    def fetch(self, x, y):
        return self.bx[x, y], self.zx[x, y], self.qx[x, y]

    def finish(self, x, y, weighted, total, extra):
        source, scaled, image = extra
        again = 1.25 * image - total
        change = scaled - weighted
        sums = self.sums
        sums[0] = sums[0] + source * scaled
        sums[1] = sums[1] + source * change
        sums[2] = sums[2] + (source - image) * change
        sums[3] = sums[3] + (image - again) * change
        return [(self.vx, (x, y), again)]


def over_planes(start, stop, body, state):
    pairs = (stop - start) // 2
    state = lax.fori_loop(0, pairs, lambda i, st: body(start + 2 * i, 2, st), state)
    if (stop - start) % 2:
        state = body(stop - 1, 1, state)
    return state


def image_kernel(
    s, bt_ref, dt_ref, y1_ref, y2_ref, t2_ref,
    dens_ref, cond, invx, bx, zx, qx, wx, carry1,
):
    loads, nx, ny, my, pitch = s.loads, s.nx, s.ny, s.my, s.pitch
    bx, zx, qx, wx, carry1 = (Tiles(ref, my, loads) for ref in (bx, zx, qx, wx, carry1))
    cond, invx = Rows(cond, pitch, loads), Rows(invx, pitch, loads)
    join_density(s, dt_ref, y1_ref, y2_ref, dens_ref)
    even_y = is_even("gy")
    ys = (pick(even_y, ny + 2, 0), pick(even_y, 0, ny + 2))
    before = None
    for x in range(nx):
        after = conduct_of(dens_ref[x * pitch : (x + 1) * pitch, :])
        cond.put(x + 2, after[1:])
        if x:
            invx.put(x + 2, inverse_of(s, before, after))
        before = after

    def stage(x, y, tile):
        stores = [(bx, (x + 2, y), tile)]
        if x:
            stores.append((zx, (x + 2, y), tile * invx[x + 2, y]))
        return stores

    inner = Tiles(bt_ref, ny, loads)
    batch = Batch(16)
    for x in range(nx):
        for y in range(ny):
            for store in stage(x, y + 2, inner[x, y]):
                batch.add(*store)
    batch.flush()
    unpack_tiles(
        y1_ref, 0, loads, 2 * nx, lambda i, tile: stage(i // 2, ys[0] + i % 2, tile)
    )
    far = Tiles(t2_ref, 2, loads)
    batch = Batch(16)
    for x in range(nx):
        for dy in range(2):
            for store in stage(x, ys[1] + dy, far[x, dy]):
                batch.add(*store)
    batch.flush()

    element_planes(cond, carry1, 3, 1, 0, my - 1, zx, None)

    def first(a, count, state):
        element_planes(cond, carry1, a, count, 0, my - 1, zx, First(bx, invx, qx, wx))
        return state

    over_planes(4, nx + 1, first, 0)


def again_kernel(s, cond, bx, zx, qx, wx, vx, carry2, sums_ref):
    loads, nx, my = s.loads, s.nx, s.my
    bx, zx, qx, wx, vx, carry2 = (Tiles(ref, my, loads) for ref in (bx, zx, qx, wx, vx, carry2))
    cond = Rows(cond, s.pitch, loads)
    element_planes(cond, carry2, 4, 1, 1, my - 3, wx, None)

    def second(a, count, sums):
        sums = list(sums)
        element_planes(cond, carry2, a, count, 1, my - 3, wx, Second(bx, zx, qx, vx, sums))
        return tuple(sums)

    zero = jnp.zeros((loads, LANES), jnp.float32)
    sums = over_planes(5, nx, second, (zero,) * 4)
    for place, part in enumerate(sums):
        sums_ref[place * loads : (place + 1) * loads, :] = part


def outer_kernel(
    s, dens_ref, x1_ref, x2_ref, t1_ref, t2_ref, c1_ref, c2_ref,
    cond1, invx1, bx1, zx1, qx1, wx1, vx1, carry1, carry2, sums1,
    q_out, v_out, inv_out, sums_ref,
    low_ref, high_ref, low_d, high_d, cond2, invx2, bx2, zx2, qx2, wx2, vx2, carry3,
):
    loads, nx, ny, mx, my, pitch = s.loads, s.nx, s.ny, s.mx, s.my, s.pitch
    even_x = is_even("gx")

    even_y = is_even("gy")
    ys = (pick(even_y, ny + 2, 0), pick(even_y, 0, ny + 2))
    yd = (pick(even_y, ny + 3, 0), pick(even_y, 0, ny + 3))

    def take(near, far):
        faces = (x1_ref, t1_ref, near), (x2_ref, t2_ref, far)
        for side, (ref, face_ref, (tiles_ref, into)) in enumerate(faces):
            face, tiles = Tiles(face_ref, ny, loads), Tiles(tiles_ref, my, loads)
            alone_x = is_alone("gx", s.count_x, side)
            batch = Batch(18)
            for dx in range(2):
                for y in range(ny):
                    batch.add(tiles, (dx, y + 2), face[dx, y])
            for t in range(3):
                at = s.x_dens + t * ny
                rows = jnp.where(alone_x, 0.0, ref[at : at + ny, :])
                to = t * pitch + 3
                batch.add(into, (slice(to, to + ny), slice(None)), rows)
            batch.flush()
            for end, corner in enumerate((c1_ref, c2_ref)):
                alone = jnp.logical_or(alone_x, is_alone("gy", s.count_y, end))
                for i in range(4):
                    tile = unpack_tile(
                        lambda t: corner[t * loads : (t + 1) * loads, :], 4 * side + i, loads
                    )
                    batch.add(tiles, (i // 2, ys[end] + i % 2), tile)
                for i in range(9):
                    at = s.c_dens + 9 * side + i
                    row = jnp.where(alone, 0.0, corner[at : at + 1, :])
                    to = i // 3 * pitch + yd[end] + i % 3
                    batch.add(into, (pl.ds(to, 1), slice(None)), row)
            batch.flush()

    @pl.when(even_x)
    def _():
        take((high_ref, high_d), (low_ref, low_d))

    @pl.when(jnp.logical_not(even_x))
    def _():
        take((low_ref, low_d), (high_ref, high_d))

    def joined(first, second, own):
        return Joined(Tiles(first, my, loads), Tiles(second, my, loads), own)

    def joined_rows(first, second, own):
        return Joined(Rows(first, pitch, loads), Rows(second, pitch, loads), own)

    outside = (0, 1, nx + 2, nx + 3)
    scaled_own = outside + (2,)
    image_own = (1, 2, 3, nx + 1, nx + 2)
    cond, invx = joined_rows(cond2, cond1, outside), joined_rows(invx2, invx1, scaled_own)
    bx, zx = joined(bx2, bx1, outside), joined(zx2, zx1, scaled_own)
    qx, wx = joined(qx2, qx1, image_own), joined(wx2, wx1, image_own)
    vx = joined(vx2, vx1, again_planes(nx))
    carry1, carry2, carry3 = (Tiles(ref, my, loads) for ref in (carry1, carry2, carry3))

    def conduct(ref, x):
        return conduct_of(ref[x * pitch : (x + 1) * pitch, :])

    low = [conduct(low_d, t) for t in range(3)] + [conduct(dens_ref, 0)]
    high = [conduct(dens_ref, nx - 1)] + [conduct(high_d, t) for t in range(2)]
    for x in range(3):
        inverse = inverse_of(s, low[x], low[x + 1])
        invx.put(x, inverse)
        if x < 2:
            cond.put(x, low[x + 1][1:])
    inv_out[...] = inverse[2 : 2 + ny]
    for x in range(2):
        invx.put(nx + 2 + x, inverse_of(s, high[x], high[x + 1]))
    cond.put(nx + 2, high[1][1:])

    batch = Batch(16)
    for ref, x0 in ((low_ref, 0), (high_ref, nx + 2)):
        tiles = Tiles(ref, my, loads)
        for dx in range(2):
            for y in range(my):
                tile = tiles[dx, y]
                batch.add(bx, (x0 + dx, y), tile)
                batch.add(zx, (x0 + dx, y), tile * invx[x0 + dx, y])
    for y in range(my):
        batch.add(zx, (2, y), bx[2, y] * invx[2, y])
    batch.flush()

    emitter = First(bx, invx, qx, wx)
    element_planes(cond, carry3, 0, 1, 0, my - 1, zx, None)
    element_planes(cond, carry3, 1, 2, 0, my - 1, zx, emitter)
    element_planes(cond, carry3, 3, 1, 0, my - 1, zx, emitter, keep=False)
    element_planes(cond, carry1, nx + 1, 2, 0, my - 1, zx, emitter, keep=False)
    sums = [sums1[place * loads : (place + 1) * loads, :] for place in range(4)]
    emitter = Second(bx, zx, qx, vx, sums)
    element_planes(cond, carry3, 1, 1, 1, my - 3, wx, None)
    element_planes(cond, carry3, 2, 2, 1, my - 3, wx, emitter)
    element_planes(cond, carry3, 4, 1, 1, my - 3, wx, emitter, keep=False)
    element_planes(cond, carry2, nx, 2, 1, my - 3, wx, emitter, keep=False)
    for field, out in ((qx, q_out), (vx, v_out)):
        out = Tiles(out, ny, loads)
        batch = Batch()
        for x in range(nx):
            for y in range(ny):
                batch.add(out, (x, y), field[x + 2, y + 2])
        batch.flush()

    lane = lane_ids(loads)
    load = lax.broadcasted_iota(jnp.int32, (loads, LANES), 0)
    packed = jnp.zeros((loads, LANES), jnp.float32)
    for place, part in enumerate(sums):
        total = jnp.sum(part, axis=1, keepdims=True)
        packed = packed + jnp.where(lane == place * loads + load, total, 0.0)
    row = jnp.sum(packed, axis=0, keepdims=True)
    sums_ref[...] = jnp.broadcast_to(row[None], sums_ref.shape)


def again_planes(nx):
    return (2, 3, 4, nx, nx + 1)


def unpack_kernel(s, q_ref, v_ref, inv1_ref, inv2_ref, qo_ref, vo_ref, io_ref):
    loads, nx, ny = s.loads, s.nx, s.ny
    batch = Batch()
    for x0 in range(0, nx, SUB):
        for ref, out in ((q_ref, qo_ref), (v_ref, vo_ref)):
            for load in range(loads):
                for block in range(packed_count(ny)):
                    tile = pack_block(
                        lambda y: ref[
                            pl.ds((x0 * ny + y) * loads + load, SUB, stride=ny * loads), :
                        ],
                        ny, block, SUB,
                    )
                    lanes = slice(block * LANES, (block + 1) * LANES)
                    batch.add(out, (load, slice(x0, x0 + SUB), lanes), tile)
        for block in range(packed_count(ny)):
            tile = pack_block(
                lambda y: inv1_ref[
                    pl.ds((x0 + 2) * s.pitch + y + 2, SUB, stride=s.pitch), :
                ],
                ny, block, SUB,
            )
            lanes = slice(block * LANES, (block + 1) * LANES)
            batch.add(io_ref, (slice(x0, x0 + SUB), lanes), tile)
    batch.flush()
    for block in range(packed_count(ny)):
        io_ref[0:1, block * LANES : (block + 1) * LANES] = pack_block(
            lambda y: inv2_ref[y : y + 1, :], ny, block, 1
        )


def finish_kernel(s, parts_ref, b_ref, q_ref, v_ref, inv_ref, x_hbm, r_hbm, x_ref, r_ref, sems):
    loads = s.loads
    totals = jnp.sum(parts_ref[...], axis=0)

    def part(place):
        return pltpu.roll(totals, (LANES - place * loads) % LANES, 1) if place else totals

    rz, near, square, last = (part(place) for place in range(4))
    direct = rz - near
    alpha = rz / direct
    short = -near / direct
    rz_next = short * short * rz + 2.0 * alpha * short * near + alpha * alpha * square
    beta = rz_next / rz
    grown = short + beta
    curved = (
        grown * grown * direct
        + 2.0 * alpha * grown * (near - square)
        + alpha * alpha * last
    )
    alpha_next = rz_next / curved
    first_row = alpha + alpha_next * (1.0 + beta)
    second_row = alpha_next * alpha
    inverse = inv_ref[...]
    copies = []
    for load in range(loads):
        first = first_row[:, load : load + 1]
        second = second_row[:, load : load + 1]
        source, image = b_ref[load], q_ref[load]
        x_ref[load] = (first * source - second * image) * inverse
        copies.append(pltpu.make_async_copy(x_ref.at[load], x_hbm.at[load], sems.at[0, load]))
        copies[-1].start()
        r_ref[load] = source - first * image + second * v_ref[load]
        copies.append(pltpu.make_async_copy(r_ref.at[load], r_hbm.at[load], sems.at[1, load]))
        copies[-1].start()
    for copy in copies:
        copy.wait()


def swap(array, axis, start):
    counts = {name: lax.axis_size(name) for name in ("gx", "gy")}
    other = "gy" if axis == "gx" else "gx"
    pairs = []
    for at in np.ndindex(counts["gx"], counts["gy"]):
        place = dict(zip(("gx", "gy"), at))
        partner = place[axis] + (1 if (place[axis] - start) % 2 == 0 else -1)
        if 0 <= partner < counts[axis]:
            place[axis] = partner
        elif place[other] ^ 1 < counts[other]:
            place[other] ^= 1
        pairs.append((at[0] * counts["gy"] + at[1], place["gx"] * counts["gy"] + place["gy"]))
    return lax.ppermute(array, ("gx", "gy"), pairs)


def per_device(heat_source, density):
    loads, nx, flat = heat_source.shape
    ny = flat // NZ
    s = Sizes(loads, nx, ny, lax.axis_size("gx"), lax.axis_size("gy"))
    nodes = nx * ny * loads
    devices = lax.axis_size("gx") * lax.axis_size("gy")

    def shape(*dims):
        return jax.ShapeDtypeStruct(dims, jnp.float32)

    def scratch(*dims):
        return pltpu.VMEM(dims, jnp.float32)

    def call(kernel, out_shape, **more):
        params = pltpu.CompilerParams(vmem_limit_bytes=20 * 1024 * 1024)
        return pl.pallas_call(
            functools.partial(kernel, s), out_shape=out_shape, compiler_params=params, **more
        )

    hbm = pl.BlockSpec(memory_space=pltpu.HBM)
    face = shape(s.y_rows, LANES)
    bt, dt, y2 = call(
        pack_kernel,
        (shape(nodes, LANES), shape(nx * ny, LANES), face),
        in_specs=[hbm, hbm],
        scratch_shapes=[
            scratch(loads, nx, flat),
            scratch(nx, flat),
            pltpu.SemaphoreType.DMA((3,)),
        ],
    )(
        pltpu.with_memory_space_constraint(heat_source, pltpu.HBM),
        pltpu.with_memory_space_constraint(density, pltpu.HBM),
    )
    y2 = swap(y2, "gy", 1)
    x_face, corner = shape(s.x_rows, LANES), shape(s.c_rows, LANES)
    y1, x1, x2 = call(pack_rest_kernel, (face, x_face, x_face))(bt, dt)
    x2, y1, x1 = swap(x2, "gx", 1), swap(y1, "gy", 0), swap(x1, "gx", 0)
    t2 = call(open_y_kernel, shape(2 * nx * loads, LANES))(y2)
    plane = s.my * loads
    rows, field = shape(s.mx * s.pitch, LANES), shape(s.mx * plane, LANES)
    edge = shape(2 * plane, LANES)
    dens, cond, inv_1, bx, zx, q_1, w_1, carry1 = call(
        image_kernel, (shape(nx * s.pitch, LANES),) + (rows,) * 2 + (field,) * 4 + (edge,)
    )(bt, dt, y1, y2, t2)
    xt = shape(2 * ny * loads, LANES)
    x2, w_1 = lax.optimization_barrier((x2, w_1))
    xt2 = call(open_x_kernel, xt)(x2)
    xt1, c1, c2 = call(corner_kernel, (xt, corner, corner))(x2, xt2, x1)
    c2, c1 = swap(c2, "gy", 1), swap(c1, "gy", 0)
    v_1, carry2, sums = call(again_kernel, (field, edge, shape(4 * loads, LANES)))(
        cond, bx, zx, q_1, w_1
    )
    q_t, v_t, inv_2, sums = call(
        outer_kernel,
        (
            shape(nodes, LANES),
            shape(nodes, LANES),
            shape(ny, LANES),
            shape(devices, 1, LANES),
        ),
        out_specs=(pl.BlockSpec(memory_space=pltpu.VMEM),) * 4,
        scratch_shapes=[scratch(2 * plane, LANES)] * 2
        + [scratch(3 * s.pitch, LANES)] * 2
        + [scratch(5 * s.pitch, LANES)] * 2
        + [scratch(5 * plane, LANES)] * 5
        + [scratch(2 * plane, LANES)],
    )(dens, x1, x2, xt1, xt2, c1, c2, cond, inv_1, bx, zx, q_1, w_1, v_1, carry1, carry2, sums)
    parts = lax.all_to_all(sums, ("gx", "gy"), 0, 0, tiled=True)
    whole = shape(loads, nx, flat)
    image, again, inverse = call(unpack_kernel, (whole, whole, shape(nx, flat)))(
        q_t, v_t, inv_1, inv_2
    )
    return call(
        finish_kernel,
        (whole, whole),
        out_specs=(hbm, hbm),
        scratch_shapes=[
            scratch(loads, nx, flat),
            scratch(loads, nx, flat),
            pltpu.SemaphoreType.DMA((2, loads)),
        ],
    )(parts, heat_source, image, again, inverse)


def solution(mesh):
    placed = (P(None, "gx", "gy"), P("gx", "gy"))
    return jax.shard_map(
        per_device,
        mesh=mesh,
        in_specs=placed,
        out_specs=(P(None, "gx", "gy"), P(None, "gx", "gy")),
        check_vma=False,
    )
```

```python
import functools

import jax
import jax.numpy as jnp
import numpy as np
from jax import lax
from jax.experimental import pallas as pl
from jax.experimental.pallas import tpu as pltpu
from jax.sharding import PartitionSpec as P

NZ = 96
KMIN = 0.001
LANES = 128
SUB = 8


class Batch:
    def __init__(self, size=12):
        self.size, self.held = size, []

    def add(self, into, at, tile):
        self.held.append((into, at, tile))
        if len(self.held) >= self.size:
            self.flush()

    def flush(self):
        for into, at, tile in self.held:
            into[at] = tile
        self.held = []


def packed_count(tiles):
    return -(-tiles * NZ // LANES)


def lane_ids(rows):
    return lax.broadcasted_iota(jnp.int32, (rows, LANES), 1)


def unpack_tile(read, index, rows):
    start = index * NZ
    block, offset = start // LANES, start % LANES
    lane = lane_ids(rows)
    first = read(block)
    if offset:
        first = pltpu.roll(first, LANES - offset, 1)
    if offset + NZ > LANES:
        second = pltpu.roll(read(block + 1), LANES - offset, 1)
        first = jnp.where(lane < LANES - offset, first, second)
    return jnp.where(lane < NZ, first, 0.0)


def pack_block(read_tile, tiles, block, rows):
    lane = lane_ids(rows)
    start = block * LANES
    out, at = None, start
    while at < start + LANES and at // NZ < tiles:
        index, z = at // NZ, at % NZ
        here = at - start
        piece = read_tile(index)
        shift = (here - z) % LANES
        if shift:
            piece = pltpu.roll(piece, shift, 1)
        out = piece if out is None else jnp.where(lane < here, out, piece)
        at += NZ - z
    return out


def pack_tiles(out_ref, at, rows, tiles, read_tile):
    batch = Batch()
    for block in range(packed_count(tiles)):
        place = slice(at + block * rows, at + (block + 1) * rows), slice(None)
        batch.add(out_ref, place, pack_block(read_tile, tiles, block, rows))
    batch.flush()


def unpack_tiles(ref, at, rows, tiles, write):
    batch = Batch()
    for index in range(tiles):
        tile = unpack_tile(lambda t: ref[at + t * rows : at + (t + 1) * rows, :], index, rows)
        for store in write(index, tile):
            batch.add(*store)
    batch.flush()


class Sizes:
    def __init__(self, loads, nx, ny, count_x, count_y):
        self.loads, self.nx, self.ny = loads, nx, ny
        self.count_x, self.count_y = count_x, count_y
        self.mx, self.my = nx + 4, ny + 4
        self.pitch = -(-(ny + 6) // SUB) * SUB
        self.y_dens = packed_count(2 * nx) * loads
        self.y_rows = self.y_dens + 3 * nx
        self.x_dens = packed_count(2 * ny) * loads
        self.x_rows = self.x_dens + 3 * ny
        self.c_dens = packed_count(8) * loads
        self.c_rows = self.c_dens + -(-18 // SUB) * SUB


class Tiles:
    def __init__(self, ref, columns, loads):
        self.ref, self.columns, self.loads = ref, columns, loads

    def rows(self, at):
        start = (at[0] * self.columns + at[1]) * self.loads
        if not isinstance(start, int):
            start = pl.multiple_of(start, SUB)
        return pl.ds(start, self.loads)

    def __getitem__(self, at):
        return self.ref[self.rows(at), :]

    def __setitem__(self, at, tile):
        self.ref[self.rows(at), :] = tile


class Rows:
    def __init__(self, ref, pitch, loads):
        self.ref, self.pitch, self.loads = ref, pitch, loads

    def __getitem__(self, at):
        row = self.ref[pl.ds(at[0] * self.pitch + at[1], 1), :]
        return jnp.broadcast_to(row, (self.loads, LANES))

    def put(self, x, values):
        self.ref[x * self.pitch : x * self.pitch + values.shape[0], :] = values


class Joined:
    def __init__(self, first, second, own):
        self.first, self.second, self.own = first, second, own

    def __getitem__(self, at):
        if at[0] in self.own:
            return self.first[self.own.index(at[0]), at[1]]
        return self.second[at]

    def __setitem__(self, at, tile):
        self.first[self.own.index(at[0]), at[1]] = tile

    def put(self, x, values):
        self.first.put(self.own.index(x), values)


def is_even(axis):
    return lax.rem(lax.axis_index(axis), 2) == 0


def is_alone(axis, count, start):
    place = lax.axis_index(axis)
    last = (count - start) % 2
    alone = place < start
    return jnp.logical_or(alone, place == count - 1) if last else alone


def pick(even, if_even, if_odd):
    return jnp.where(even, if_even, if_odd)


def pack_kernel(s, b_hbm, d_hbm, bt_ref, dt_ref, y2_ref, b_ref, d_ref, sems):
    loads, nx, ny = s.loads, s.nx, s.ny
    d_copy = pltpu.make_async_copy(d_hbm, d_ref, sems.at[0])
    d_copy.start()
    parts = 2 if loads % 2 == 0 else 1
    each = loads // parts
    copies = []
    for part in range(parts):
        some = pl.ds(part * each, each)
        copies.append(pltpu.make_async_copy(b_hbm.at[some], b_ref.at[some], sems.at[part + 1]))
        copies[-1].start()
    d_copy.wait()
    batch = Batch(16)
    for x0 in range(0, nx, SUB):
        for y in range(ny):
            tile = unpack_tile(
                lambda t: d_ref[x0 : x0 + SUB, t * LANES : (t + 1) * LANES], y, SUB
            )
            batch.add(dt_ref, (pl.ds(x0 * ny + y, SUB, stride=ny), slice(None)), tile)
    batch.flush()
    for load in range(loads):
        if load % each == 0:
            copies[load // each].wait()
        batch = Batch(16)
        for x0 in range(0, nx, SUB):
            for y in range(ny):
                tile = unpack_tile(
                    lambda t: b_ref[load, x0 : x0 + SUB, t * LANES : (t + 1) * LANES], y, SUB
                )
                rows = pl.ds((x0 * ny + y) * loads + load, SUB, stride=ny * loads)
                batch.add(bt_ref, (rows, slice(None)), tile)
        batch.flush()
    pack_face(s, jnp.logical_not(is_even("gy")), bt_ref, dt_ref, y2_ref)


def pack_rest_kernel(s, bt_ref, dt_ref, y1_ref, x1_ref, x2_ref):
    even_x = is_even("gx")
    pack_x_face(s, jnp.logical_not(even_x), bt_ref, dt_ref, x2_ref)
    pack_x_face(s, even_x, bt_ref, dt_ref, x1_ref)
    pack_face(s, is_even("gy"), bt_ref, dt_ref, y1_ref)


def pack_x_face(s, upper, bt_ref, dt_ref, out_ref):
    loads, nx, ny = s.loads, s.nx, s.ny
    tiles = Tiles(bt_ref, ny, loads)
    x0 = pick(upper, nx - 2, 0)
    pack_tiles(out_ref, 0, loads, 2 * ny, lambda i: tiles[x0 + i // ny, i % ny])
    rows = pl.ds(pl.multiple_of(pick(upper, nx - 3, 0) * ny, SUB), 3 * ny)
    out_ref[s.x_dens :, :] = dt_ref[rows, :]


def pack_face(s, upper, bt_ref, dt_ref, out_ref):
    loads, nx, ny = s.loads, s.nx, s.ny
    tiles = Tiles(bt_ref, ny, loads)
    y0 = pick(upper, ny - 2, 0)
    pack_tiles(out_ref, 0, loads, 2 * nx, lambda i: tiles[i // 2, y0 + i % 2])
    y0 = pick(upper, ny - 3, 0)
    batch = Batch()
    for dy in range(3):
        for x0 in range(0, nx, SUB):
            at = s.y_dens + dy * nx + x0
            tile = dt_ref[pl.ds(x0 * ny + y0 + dy, SUB, stride=ny), :]
            batch.add(out_ref, (slice(at, at + SUB), slice(None)), tile)
    batch.flush()


def open_y_kernel(s, y_ref, t_ref):
    tiles = Tiles(t_ref, 2, s.loads)
    unpack_tiles(
        y_ref, 0, s.loads, 2 * s.nx, lambda i, tile: [(tiles, (i // 2, i % 2), tile)]
    )


def open_x_kernel(s, x_ref, t_ref):
    tiles = Tiles(t_ref, s.ny, s.loads)
    unpack_tiles(
        x_ref, 0, s.loads, 2 * s.ny, lambda i, tile: [(tiles, (i // s.ny, i % s.ny), tile)]
    )


def corner_kernel(s, x2_ref, t2_ref, x1_ref, t1_ref, c1_ref, c2_ref):
    loads, ny = s.loads, s.ny
    open_x_kernel(s, x1_ref, t1_ref)
    halves = Tiles(t1_ref, ny, loads), Tiles(t2_ref, ny, loads)
    even_y = is_even("gy")
    for out_ref, upper in ((c2_ref, jnp.logical_not(even_y)), (c1_ref, even_y)):
        y0 = pick(upper, ny - 2, 0)
        pack_tiles(out_ref, 0, loads, 8, lambda i: halves[i // 4][i // 2 % 2, y0 + i % 2])
        y0 = pick(upper, ny - 3, 0)
        batch, at = Batch(18), s.c_dens
        for ref in (x1_ref, x2_ref):
            for t in range(3):
                for dy in range(3):
                    row = ref[pl.ds(s.x_dens + t * ny + y0 + dy, 1), :]
                    batch.add(out_ref, (slice(at, at + 1), slice(None)), row)
                    at += 1
        batch.flush()
        out_ref[at:, :] = jnp.zeros((s.c_rows - at, LANES), jnp.float32)


def join_density(s, dt_ref, y1_ref, y2_ref, dens_ref):
    nx, ny, pitch = s.nx, s.ny, s.pitch
    even_y = is_even("gy")
    yd = (pick(even_y, ny + 3, 0), pick(even_y, 0, ny + 3))
    batch = Batch(16)
    for x in range(nx):
        at = x * pitch
        batch.add(
            dens_ref, (slice(at + 3, at + 3 + ny), slice(None)), dt_ref[x * ny : (x + 1) * ny, :]
        )
    batch.flush()
    for side, ref in enumerate((y1_ref, y2_ref)):
        alone = is_alone("gy", s.count_y, side)
        for dy in range(3):
            for x0 in range(0, nx, SUB):
                at = s.y_dens + dy * nx + x0
                to = x0 * pitch + yd[side] + dy
                batch.add(
                    dens_ref,
                    (pl.ds(to, SUB, stride=pitch), slice(None)),
                    jnp.where(alone, 0.0, ref[at : at + SUB, :]),
                )
    batch.flush()


def conduct_of(dens):
    return jnp.where(
        dens > 0.0, (KMIN + (1.0 - KMIN) * (dens * dens * dens)) * (1.0 / 12.0), 0.0
    )


def inverse_of(s, before, after):
    pair = before + after
    pair = pair[: s.pitch - 1] + pair[1:]
    total = 4.0 * (pair + pltpu.roll(pair, 1, 1))
    return jnp.where(after[1:] > 0.0, 1.0 / total, 0.0)


def up(tile):
    return pltpu.roll(tile, LANES - 1, 1)


def element_planes(cond, carry, a, count, y0, columns, field, emitter, keep=True):
    def loads_of(step):
        y = y0 + step
        right = [field[a + u, y + 1] for u in range(count + 1)]
        conduct = [cond[a + u, y] for u in range(count)]
        above = extra = None
        if step and emitter:
            above = (carry[0, y], carry[1, y])
            extra = [emitter.fetch(a + u, y) for u in range(count)]
        return right, conduct, above, extra

    left = [(tile, up(tile)) for tile in [field[a + u, y0] for u in range(count + 1)]]
    ahead = loads_of(0)
    old, waiting = [None] * count, []
    for step in range(columns):
        y = y0 + step
        right, conduct, above, extra = ahead
        if step + 1 < columns:
            ahead = loads_of(step + 1)
        if len(waiting) > 1:
            for into, at, tile in waiting.pop(0):
                into[at] = tile
        stores = []
        right = [(tile, up(tile)) for tile in right]
        for u in range(count):
            (p0, p0s), (p1, p1s) = left[u], left[u + 1]
            (r0, r0s), (r1, r1s) = right[u], right[u + 1]
            c = conduct[u]
            even = (p0 + r1) + (r0s + p1s)
            odd = (r0 + p1) + (p0s + r1s)
            pass_on = keep or u + 1 < count
            lower = upper = None
            if emitter:
                lower = (c * (odd + p1s), c * (even + p1))
            if pass_on:
                upper = (c * (even + p0s), c * (odd + p0))
            if step and emitter:
                low = (c * (even + r1s) + old[u][0][0]) + above[0]
                high = (c * (odd + r1) + old[u][0][1]) + above[1]
                total = low + pltpu.roll(high, 1, 1)
                stores += emitter.finish(a + u, y, p0, total, extra[u])
            if step and pass_on:
                above = (
                    c * (odd + r0s) + old[u][1][0],
                    c * (even + r0) + old[u][1][1],
                )
            old[u] = (lower, upper)
        if step and keep:
            stores += [(carry, (0, y), above[0]), (carry, (1, y), above[1])]
        waiting.append(stores)
        left = right
    for stores in waiting:
        for into, at, tile in stores:
            into[at] = tile


class First:
    def __init__(self, bx, invx, qx, wx):
        self.bx, self.invx, self.qx, self.wx = bx, invx, qx, wx

    def fetch(self, x, y):
        return self.bx[x, y], self.invx[x, y]

    def finish(self, x, y, node, total, extra):
        source, inverse = extra
        image = 1.25 * source - total
        return [(self.qx, (x, y), image), (self.wx, (x, y), image * inverse)]


class Second:
    def __init__(self, bx, zx, qx, q_out, v_out, sums):
        self.bx, self.zx, self.qx, self.sums = bx, zx, qx, sums
        self.q_out, self.v_out = q_out, v_out

    def fetch(self, x, y):
        return self.bx[x, y], self.zx[x, y], self.qx[x, y]

    def finish(self, x, y, weighted, total, extra):
        source, scaled, image = extra
        again = 1.25 * image - total
        change = scaled - weighted
        sums = self.sums
        sums[0] = sums[0] + source * scaled
        sums[1] = sums[1] + source * change
        sums[2] = sums[2] + (source - image) * change
        sums[3] = sums[3] + (image - again) * change
        at = x - 2, y - 2
        return [(self.q_out, at, image), (self.v_out, at, again)]


def over_planes(start, stop, body, state):
    pairs = (stop - start) // 2
    state = lax.fori_loop(0, pairs, lambda i, st: body(start + 2 * i, 2, st), state)
    if (stop - start) % 2:
        state = body(stop - 1, 1, state)
    return state


def inner_kernel(
    s, bt_ref, dt_ref, y1_ref, y2_ref, t2_ref,
    dens_ref, cond, invx, bx, zx, qx, wx, q_out, v_out, carry1, carry2, sums_ref,
):
    loads, nx, ny, my, pitch = s.loads, s.nx, s.ny, s.my, s.pitch
    bx, zx, qx, wx, carry1, carry2 = (
        Tiles(ref, my, loads) for ref in (bx, zx, qx, wx, carry1, carry2)
    )
    q_out, v_out = Tiles(q_out, ny, loads), Tiles(v_out, ny, loads)
    cond, invx = Rows(cond, pitch, loads), Rows(invx, pitch, loads)
    join_density(s, dt_ref, y1_ref, y2_ref, dens_ref)
    even_y = is_even("gy")
    ys = (pick(even_y, ny + 2, 0), pick(even_y, 0, ny + 2))
    before = None
    for x in range(nx):
        after = conduct_of(dens_ref[x * pitch : (x + 1) * pitch, :])
        cond.put(x + 2, after[1:])
        if x:
            invx.put(x + 2, inverse_of(s, before, after))
        before = after

    def stage(x, y, tile):
        stores = [(bx, (x + 2, y), tile)]
        if x:
            stores.append((zx, (x + 2, y), tile * invx[x + 2, y]))
        return stores

    inner = Tiles(bt_ref, ny, loads)
    batch = Batch(16)
    for x in range(nx):
        for y in range(ny):
            for store in stage(x, y + 2, inner[x, y]):
                batch.add(*store)
    batch.flush()
    unpack_tiles(
        y1_ref, 0, loads, 2 * nx, lambda i, tile: stage(i // 2, ys[0] + i % 2, tile)
    )
    far = Tiles(t2_ref, 2, loads)
    batch = Batch(16)
    for x in range(nx):
        for dy in range(2):
            for store in stage(x, ys[1] + dy, far[x, dy]):
                batch.add(*store)
    batch.flush()

    element_planes(cond, carry1, 3, 1, 0, my - 1, zx, None)

    def first(a, count, state):
        element_planes(cond, carry1, a, count, 0, my - 1, zx, First(bx, invx, qx, wx))
        return state

    over_planes(4, nx + 1, first, 0)
    element_planes(cond, carry2, 4, 1, 1, my - 3, wx, None)

    def second(a, count, sums):
        sums = list(sums)
        emitter = Second(bx, zx, qx, q_out, v_out, sums)
        element_planes(cond, carry2, a, count, 1, my - 3, wx, emitter)
        return tuple(sums)

    zero = jnp.zeros((loads, LANES), jnp.float32)
    sums = over_planes(5, nx, second, (zero,) * 4)
    for place, part in enumerate(sums):
        sums_ref[place * loads : (place + 1) * loads, :] = part


def outer_kernel(
    s, dens_ref, x1_ref, x2_ref, t1_ref, t2_ref, c1_ref, c2_ref,
    cond1, invx1, bx1, zx1, qx1, wx1, carry1, carry2, sums1,
    q_out, v_out, inv_out, sums_ref,
    low_ref, high_ref, low_d, high_d, cond2, invx2, bx2, zx2, qx2, wx2, carry3,
):
    loads, nx, ny, mx, my, pitch = s.loads, s.nx, s.ny, s.mx, s.my, s.pitch
    even_x = is_even("gx")

    even_y = is_even("gy")
    ys = (pick(even_y, ny + 2, 0), pick(even_y, 0, ny + 2))
    yd = (pick(even_y, ny + 3, 0), pick(even_y, 0, ny + 3))

    def take(near, far):
        faces = (x1_ref, t1_ref, near), (x2_ref, t2_ref, far)
        for side, (ref, face_ref, (tiles_ref, into)) in enumerate(faces):
            face, tiles = Tiles(face_ref, ny, loads), Tiles(tiles_ref, my, loads)
            alone_x = is_alone("gx", s.count_x, side)
            batch = Batch(18)
            for dx in range(2):
                for y in range(ny):
                    batch.add(tiles, (dx, y + 2), face[dx, y])
            for t in range(3):
                at = s.x_dens + t * ny
                rows = jnp.where(alone_x, 0.0, ref[at : at + ny, :])
                to = t * pitch + 3
                batch.add(into, (slice(to, to + ny), slice(None)), rows)
            batch.flush()
            for end, corner in enumerate((c1_ref, c2_ref)):
                alone = jnp.logical_or(alone_x, is_alone("gy", s.count_y, end))
                for i in range(4):
                    tile = unpack_tile(
                        lambda t: corner[t * loads : (t + 1) * loads, :], 4 * side + i, loads
                    )
                    batch.add(tiles, (i // 2, ys[end] + i % 2), tile)
                for i in range(9):
                    at = s.c_dens + 9 * side + i
                    row = jnp.where(alone, 0.0, corner[at : at + 1, :])
                    to = i // 3 * pitch + yd[end] + i % 3
                    batch.add(into, (pl.ds(to, 1), slice(None)), row)
            batch.flush()

    @pl.when(even_x)
    def _():
        take((high_ref, high_d), (low_ref, low_d))

    @pl.when(jnp.logical_not(even_x))
    def _():
        take((low_ref, low_d), (high_ref, high_d))

    def joined(first, second, own):
        return Joined(Tiles(first, my, loads), Tiles(second, my, loads), own)

    def joined_rows(first, second, own):
        return Joined(Rows(first, pitch, loads), Rows(second, pitch, loads), own)

    outside = (0, 1, nx + 2, nx + 3)
    scaled_own = outside + (2,)
    image_own = (1, 2, 3, nx + 1, nx + 2)
    cond, invx = joined_rows(cond2, cond1, outside), joined_rows(invx2, invx1, scaled_own)
    bx, zx = joined(bx2, bx1, outside), joined(zx2, zx1, scaled_own)
    qx, wx = joined(qx2, qx1, image_own), joined(wx2, wx1, image_own)
    own = [x - 2 for x in outer_planes(nx)]
    q_out, v_out = (Joined(Tiles(ref, ny, loads), None, own) for ref in (q_out, v_out))
    carry1, carry2, carry3 = (Tiles(ref, my, loads) for ref in (carry1, carry2, carry3))

    def conduct(ref, x):
        return conduct_of(ref[x * pitch : (x + 1) * pitch, :])

    low = [conduct(low_d, t) for t in range(3)] + [conduct(dens_ref, 0)]
    high = [conduct(dens_ref, nx - 1)] + [conduct(high_d, t) for t in range(2)]
    for x in range(3):
        inverse = inverse_of(s, low[x], low[x + 1])
        invx.put(x, inverse)
        if x < 2:
            cond.put(x, low[x + 1][1:])
    inv_out[...] = inverse[2 : 2 + ny]
    for x in range(2):
        invx.put(nx + 2 + x, inverse_of(s, high[x], high[x + 1]))
    cond.put(nx + 2, high[1][1:])

    batch = Batch(16)
    for ref, x0 in ((low_ref, 0), (high_ref, nx + 2)):
        tiles = Tiles(ref, my, loads)
        for dx in range(2):
            for y in range(my):
                tile = tiles[dx, y]
                batch.add(bx, (x0 + dx, y), tile)
                batch.add(zx, (x0 + dx, y), tile * invx[x0 + dx, y])
    for y in range(my):
        batch.add(zx, (2, y), bx[2, y] * invx[2, y])
    batch.flush()

    emitter = First(bx, invx, qx, wx)
    element_planes(cond, carry3, 0, 1, 0, my - 1, zx, None)
    element_planes(cond, carry3, 1, 2, 0, my - 1, zx, emitter)
    element_planes(cond, carry3, 3, 1, 0, my - 1, zx, emitter, keep=False)
    element_planes(cond, carry1, nx + 1, 2, 0, my - 1, zx, emitter, keep=False)
    sums = [sums1[place * loads : (place + 1) * loads, :] for place in range(4)]
    emitter = Second(bx, zx, qx, q_out, v_out, sums)
    element_planes(cond, carry3, 1, 1, 1, my - 3, wx, None)
    element_planes(cond, carry3, 2, 2, 1, my - 3, wx, emitter)
    element_planes(cond, carry3, 4, 1, 1, my - 3, wx, emitter, keep=False)
    element_planes(cond, carry2, nx, 2, 1, my - 3, wx, emitter, keep=False)
    lane = lane_ids(loads)
    load = lax.broadcasted_iota(jnp.int32, (loads, LANES), 0)
    packed = jnp.zeros((loads, LANES), jnp.float32)
    for place, part in enumerate(sums):
        total = jnp.sum(part, axis=1, keepdims=True)
        packed = packed + jnp.where(lane == place * loads + load, total, 0.0)
    row = jnp.sum(packed, axis=0, keepdims=True)
    sums_ref[...] = jnp.broadcast_to(row[None], sums_ref.shape)


def outer_planes(nx):
    return (2, 3, 4, nx, nx + 1)


def unpack_kernel(
    s, q1_ref, q2_ref, v1_ref, v2_ref, inv1_ref, inv2_ref, qo_ref, vo_ref, io_ref, q_ref, v_ref
):
    loads, nx, ny = s.loads, s.nx, s.ny
    batch = Batch()
    planes = outer_planes(nx)
    for first, second, whole in ((q1_ref, q2_ref, q_ref), (v1_ref, v2_ref, v_ref)):
        first, second = Tiles(first, ny, loads), Tiles(second, ny, loads)
        whole = Tiles(whole, ny, loads)
        for x in range(nx):
            for y in range(ny):
                if x + 2 in planes:
                    batch.add(whole, (x, y), second[planes.index(x + 2), y])
                else:
                    batch.add(whole, (x, y), first[x, y])
    batch.flush()
    batch = Batch()
    for x0 in range(0, nx, SUB):
        for ref, out in ((q_ref, qo_ref), (v_ref, vo_ref)):
            for load in range(loads):
                for block in range(packed_count(ny)):
                    tile = pack_block(
                        lambda y: ref[
                            pl.ds((x0 * ny + y) * loads + load, SUB, stride=ny * loads), :
                        ],
                        ny, block, SUB,
                    )
                    lanes = slice(block * LANES, (block + 1) * LANES)
                    batch.add(out, (load, slice(x0, x0 + SUB), lanes), tile)
        for block in range(packed_count(ny)):
            tile = pack_block(
                lambda y: inv1_ref[
                    pl.ds((x0 + 2) * s.pitch + y + 2, SUB, stride=s.pitch), :
                ],
                ny, block, SUB,
            )
            lanes = slice(block * LANES, (block + 1) * LANES)
            batch.add(io_ref, (slice(x0, x0 + SUB), lanes), tile)
    batch.flush()
    for block in range(packed_count(ny)):
        io_ref[0:1, block * LANES : (block + 1) * LANES] = pack_block(
            lambda y: inv2_ref[y : y + 1, :], ny, block, 1
        )


def finish_kernel(s, parts_ref, b_ref, q_ref, v_ref, inv_ref, x_hbm, r_hbm, x_ref, r_ref, sems):
    loads = s.loads
    totals = jnp.sum(parts_ref[...], axis=0)

    def part(place):
        return pltpu.roll(totals, (LANES - place * loads) % LANES, 1) if place else totals

    rz, near, square, last = (part(place) for place in range(4))
    direct = rz - near
    alpha = rz / direct
    short = -near / direct
    rz_next = short * short * rz + 2.0 * alpha * short * near + alpha * alpha * square
    beta = rz_next / rz
    grown = short + beta
    curved = (
        grown * grown * direct
        + 2.0 * alpha * grown * (near - square)
        + alpha * alpha * last
    )
    alpha_next = rz_next / curved
    first_row = alpha + alpha_next * (1.0 + beta)
    second_row = alpha_next * alpha
    inverse = inv_ref[...]
    copies = []
    for load in range(loads):
        first = first_row[:, load : load + 1]
        second = second_row[:, load : load + 1]
        source, image = b_ref[load], q_ref[load]
        x_ref[load] = (first * source - second * image) * inverse
        copies.append(pltpu.make_async_copy(x_ref.at[load], x_hbm.at[load], sems.at[0, load]))
        copies[-1].start()
        r_ref[load] = source - first * image + second * v_ref[load]
        copies.append(pltpu.make_async_copy(r_ref.at[load], r_hbm.at[load], sems.at[1, load]))
        copies[-1].start()
    for copy in copies:
        copy.wait()


def swap(array, axis, start):
    counts = {name: lax.axis_size(name) for name in ("gx", "gy")}
    other = "gy" if axis == "gx" else "gx"
    pairs = []
    for at in np.ndindex(counts["gx"], counts["gy"]):
        place = dict(zip(("gx", "gy"), at))
        partner = place[axis] + (1 if (place[axis] - start) % 2 == 0 else -1)
        if 0 <= partner < counts[axis]:
            place[axis] = partner
        elif place[other] ^ 1 < counts[other]:
            place[other] ^= 1
        pairs.append((at[0] * counts["gy"] + at[1], place["gx"] * counts["gy"] + place["gy"]))
    return lax.ppermute(array, ("gx", "gy"), pairs)


def per_device(heat_source, density):
    loads, nx, flat = heat_source.shape
    ny = flat // NZ
    s = Sizes(loads, nx, ny, lax.axis_size("gx"), lax.axis_size("gy"))
    nodes = nx * ny * loads
    devices = lax.axis_size("gx") * lax.axis_size("gy")

    def shape(*dims):
        return jax.ShapeDtypeStruct(dims, jnp.float32)

    def scratch(*dims):
        return pltpu.VMEM(dims, jnp.float32)

    def call(kernel, out_shape, **more):
        params = pltpu.CompilerParams(vmem_limit_bytes=20 * 1024 * 1024)
        return pl.pallas_call(
            functools.partial(kernel, s), out_shape=out_shape, compiler_params=params, **more
        )

    hbm = pl.BlockSpec(memory_space=pltpu.HBM)
    face = shape(s.y_rows, LANES)
    bt, dt, y2 = call(
        pack_kernel,
        (shape(nodes, LANES), shape(nx * ny, LANES), face),
        in_specs=[hbm, hbm],
        scratch_shapes=[
            scratch(loads, nx, flat),
            scratch(nx, flat),
            pltpu.SemaphoreType.DMA((3,)),
        ],
    )(
        pltpu.with_memory_space_constraint(heat_source, pltpu.HBM),
        pltpu.with_memory_space_constraint(density, pltpu.HBM),
    )
    y2 = swap(y2, "gy", 1)
    x_face, corner = shape(s.x_rows, LANES), shape(s.c_rows, LANES)
    y1, x1, x2 = call(pack_rest_kernel, (face, x_face, x_face))(bt, dt)
    x2, y1, x1 = swap(x2, "gx", 1), swap(y1, "gy", 0), swap(x1, "gx", 0)
    t2 = call(open_y_kernel, shape(2 * nx * loads, LANES))(y2)
    xt = shape(2 * ny * loads, LANES)
    xt2 = call(open_x_kernel, xt)(x2)
    xt1, c1, c2 = call(corner_kernel, (xt, corner, corner))(x2, xt2, x1)
    xt1, dt = lax.optimization_barrier((xt1, dt))
    c2, c1 = swap(c2, "gy", 1), swap(c1, "gy", 0)
    plane = s.my * loads
    rows, field = shape(s.mx * s.pitch, LANES), shape(s.mx * plane, LANES)
    edge = shape(2 * plane, LANES)
    inside = shape(nodes, LANES)
    dens, cond, inv_1, bx, zx, q_x, w_x, q_1, v_1, carry1, carry2, sums = call(
        inner_kernel,
        (shape(nx * s.pitch, LANES),)
        + (rows,) * 2
        + (field,) * 4
        + (inside,) * 2
        + (edge,) * 2
        + (shape(4 * loads, LANES),),
    )(bt, dt, y1, y2, t2)
    ends = shape(len(outer_planes(nx)) * ny * loads, LANES)
    q_2, v_2, inv_2, sums = call(
        outer_kernel,
        (ends, ends, shape(ny, LANES), shape(devices, 1, LANES)),
        scratch_shapes=[scratch(2 * plane, LANES)] * 2
        + [scratch(3 * s.pitch, LANES)] * 2
        + [scratch(5 * s.pitch, LANES)] * 2
        + [scratch(5 * plane, LANES)] * 4
        + [scratch(2 * plane, LANES)],
    )(dens, x1, x2, xt1, xt2, c1, c2, cond, inv_1, bx, zx, q_x, w_x, carry1, carry2, sums)
    parts = lax.all_to_all(sums, ("gx", "gy"), 0, 0, tiled=True)
    whole = shape(loads, nx, flat)
    image, again, inverse = call(
        unpack_kernel,
        (whole, whole, shape(nx, flat)),
        scratch_shapes=[scratch(nodes, LANES)] * 2,
    )(q_1, q_2, v_1, v_2, inv_1, inv_2)
    return call(
        finish_kernel,
        (whole, whole),
        out_specs=(hbm, hbm),
        scratch_shapes=[
            scratch(loads, nx, flat),
            scratch(loads, nx, flat),
            pltpu.SemaphoreType.DMA((2, loads)),
        ],
    )(parts, heat_source, image, again, inverse)


def solution(mesh):
    placed = (P(None, "gx", "gy"), P("gx", "gy"))
    return jax.shard_map(
        per_device,
        mesh=mesh,
        in_specs=placed,
        out_specs=(P(None, "gx", "gy"), P(None, "gx", "gy")),
        check_vma=False,
    )
```

```python
import functools

import jax
import jax.numpy as jnp
import numpy as np
from jax import lax
from jax.experimental import pallas as pl
from jax.experimental.pallas import tpu as pltpu
from jax.sharding import PartitionSpec as P

NZ = 96
KMIN = 0.001
LANES = 128
SUB = 8


class Batch:
    def __init__(self, size=12):
        self.size, self.held = size, []

    def add(self, into, at, tile):
        self.held.append((into, at, tile))
        if len(self.held) >= self.size:
            self.flush()

    def flush(self):
        for into, at, tile in self.held:
            into[at] = tile
        self.held = []


def packed_count(tiles):
    return -(-tiles * NZ // LANES)


def lane_ids(rows):
    return lax.broadcasted_iota(jnp.int32, (rows, LANES), 1)


def unpack_tile(read, index, rows):
    start = index * NZ
    block, offset = start // LANES, start % LANES
    lane = lane_ids(rows)
    first = read(block)
    if offset:
        first = pltpu.roll(first, LANES - offset, 1)
    if offset + NZ > LANES:
        second = pltpu.roll(read(block + 1), LANES - offset, 1)
        first = jnp.where(lane < LANES - offset, first, second)
    return jnp.where(lane < NZ, first, 0.0)


def pack_block(read_tile, tiles, block, rows):
    lane = lane_ids(rows)
    start = block * LANES
    out, at = None, start
    while at < start + LANES and at // NZ < tiles:
        index, z = at // NZ, at % NZ
        here = at - start
        piece = read_tile(index)
        shift = (here - z) % LANES
        if shift:
            piece = pltpu.roll(piece, shift, 1)
        out = piece if out is None else jnp.where(lane < here, out, piece)
        at += NZ - z
    return out


def pack_tiles(out_ref, at, rows, tiles, read_tile):
    batch = Batch()
    for block in range(packed_count(tiles)):
        place = slice(at + block * rows, at + (block + 1) * rows), slice(None)
        batch.add(out_ref, place, pack_block(read_tile, tiles, block, rows))
    batch.flush()


def unpack_tiles(ref, at, rows, tiles, write):
    batch = Batch()
    for index in range(tiles):
        tile = unpack_tile(lambda t: ref[at + t * rows : at + (t + 1) * rows, :], index, rows)
        for store in write(index, tile):
            batch.add(*store)
    batch.flush()


class Sizes:
    def __init__(self, loads, nx, ny, count_x, count_y):
        self.loads, self.nx, self.ny = loads, nx, ny
        self.count_x, self.count_y = count_x, count_y
        self.mx, self.my = nx + 4, ny + 4
        self.pitch = -(-(ny + 6) // SUB) * SUB
        self.y_dens = packed_count(2 * nx) * loads
        self.y_rows = self.y_dens + 3 * nx
        self.x_dens = packed_count(2 * ny) * loads
        self.x_rows = self.x_dens + 3 * ny
        self.c_dens = packed_count(8) * loads
        self.c_rows = self.c_dens + -(-18 // SUB) * SUB


class Tiles:
    def __init__(self, ref, columns, loads):
        self.ref, self.columns, self.loads = ref, columns, loads

    def rows(self, at):
        start = (at[0] * self.columns + at[1]) * self.loads
        if not isinstance(start, int):
            start = pl.multiple_of(start, SUB)
        return pl.ds(start, self.loads)

    def __getitem__(self, at):
        return self.ref[self.rows(at), :]

    def __setitem__(self, at, tile):
        self.ref[self.rows(at), :] = tile


class Rows:
    def __init__(self, ref, pitch, loads):
        self.ref, self.pitch, self.loads = ref, pitch, loads

    def __getitem__(self, at):
        row = self.ref[pl.ds(at[0] * self.pitch + at[1], 1), :]
        return jnp.broadcast_to(row, (self.loads, LANES))

    def put(self, x, values):
        self.ref[x * self.pitch : x * self.pitch + values.shape[0], :] = values


class Joined:
    def __init__(self, first, second, own):
        self.first, self.second, self.own = first, second, own

    def __getitem__(self, at):
        if at[0] in self.own:
            return self.first[self.own.index(at[0]), at[1]]
        return self.second[at]

    def __setitem__(self, at, tile):
        self.first[self.own.index(at[0]), at[1]] = tile

    def put(self, x, values):
        self.first.put(self.own.index(x), values)


def is_even(axis):
    return lax.rem(lax.axis_index(axis), 2) == 0


def is_alone(axis, count, start):
    place = lax.axis_index(axis)
    last = (count - start) % 2
    alone = place < start
    return jnp.logical_or(alone, place == count - 1) if last else alone


def pick(even, if_even, if_odd):
    return jnp.where(even, if_even, if_odd)


def pack_kernel(s, b_hbm, d_hbm, bt_ref, dt_ref, x1_ref, x2_ref, b_ref, d_ref, sems):
    loads, nx, ny = s.loads, s.nx, s.ny
    d_copy = pltpu.make_async_copy(d_hbm, d_ref, sems.at[0])
    d_copy.start()
    parts = 2 if loads % 2 == 0 else 1
    each = loads // parts
    copies = []
    for part in range(parts):
        some = pl.ds(part * each, each)
        copies.append(pltpu.make_async_copy(b_hbm.at[some], b_ref.at[some], sems.at[part + 1]))
        copies[-1].start()
    d_copy.wait()
    batch = Batch(16)
    for x0 in range(0, nx, SUB):
        for y in range(ny):
            tile = unpack_tile(
                lambda t: d_ref[x0 : x0 + SUB, t * LANES : (t + 1) * LANES], y, SUB
            )
            batch.add(dt_ref, (pl.ds(x0 * ny + y, SUB, stride=ny), slice(None)), tile)
    batch.flush()
    for load in range(loads):
        if load % each == 0:
            copies[load // each].wait()
        batch = Batch(16)
        for x0 in range(0, nx, SUB):
            for y in range(ny):
                tile = unpack_tile(
                    lambda t: b_ref[load, x0 : x0 + SUB, t * LANES : (t + 1) * LANES], y, SUB
                )
                rows = pl.ds((x0 * ny + y) * loads + load, SUB, stride=ny * loads)
                batch.add(bt_ref, (rows, slice(None)), tile)
        batch.flush()
    even_x = is_even("gx")
    pack_x_face(s, jnp.logical_not(even_x), bt_ref, dt_ref, x2_ref)
    pack_x_face(s, even_x, bt_ref, dt_ref, x1_ref)


def pack_y_kernel(s, bt_ref, dt_ref, y1_ref, y2_ref):
    even_y = is_even("gy")
    pack_y_face(s, jnp.logical_not(even_y), bt_ref, dt_ref, y2_ref)
    pack_y_face(s, even_y, bt_ref, dt_ref, y1_ref)


def pack_x_face(s, upper, bt_ref, dt_ref, out_ref):
    loads, nx, ny = s.loads, s.nx, s.ny
    tiles = Tiles(bt_ref, ny, loads)
    x0 = pick(upper, nx - 2, 0)
    pack_tiles(out_ref, 0, loads, 2 * ny, lambda i: tiles[x0 + i // ny, i % ny])
    rows = pl.ds(pl.multiple_of(pick(upper, nx - 3, 0) * ny, SUB), 3 * ny)
    out_ref[s.x_dens :, :] = dt_ref[rows, :]


def pack_y_face(s, upper, bt_ref, dt_ref, out_ref):
    loads, nx, ny = s.loads, s.nx, s.ny
    tiles = Tiles(bt_ref, ny, loads)
    y0 = pick(upper, ny - 2, 0)
    pack_tiles(out_ref, 0, loads, 2 * nx, lambda i: tiles[i // 2, y0 + i % 2])
    y0 = pick(upper, ny - 3, 0)
    batch = Batch()
    for dy in range(3):
        for x0 in range(0, nx, SUB):
            at = s.y_dens + dy * nx + x0
            tile = dt_ref[pl.ds(x0 * ny + y0 + dy, SUB, stride=ny), :]
            batch.add(out_ref, (slice(at, at + SUB), slice(None)), tile)
    batch.flush()


def open_y_kernel(s, y_ref, t_ref):
    tiles = Tiles(t_ref, 2, s.loads)
    unpack_tiles(
        y_ref, 0, s.loads, 2 * s.nx, lambda i, tile: [(tiles, (i // 2, i % 2), tile)]
    )


def open_x_kernel(s, x_ref, t_ref):
    tiles = Tiles(t_ref, s.ny, s.loads)
    unpack_tiles(
        x_ref, 0, s.loads, 2 * s.ny, lambda i, tile: [(tiles, (i // s.ny, i % s.ny), tile)]
    )


def corner_kernel(s, x2_ref, t2_ref, x1_ref, t1_ref, c1_ref, c2_ref):
    loads, ny = s.loads, s.ny
    open_x_kernel(s, x1_ref, t1_ref)
    halves = Tiles(t1_ref, ny, loads), Tiles(t2_ref, ny, loads)
    even_y = is_even("gy")
    for out_ref, upper in ((c2_ref, jnp.logical_not(even_y)), (c1_ref, even_y)):
        y0 = pick(upper, ny - 2, 0)
        pack_tiles(out_ref, 0, loads, 8, lambda i: halves[i // 4][i // 2 % 2, y0 + i % 2])
        y0 = pick(upper, ny - 3, 0)
        batch, at = Batch(18), s.c_dens
        for ref in (x1_ref, x2_ref):
            for t in range(3):
                for dy in range(3):
                    row = ref[pl.ds(s.x_dens + t * ny + y0 + dy, 1), :]
                    batch.add(out_ref, (slice(at, at + 1), slice(None)), row)
                    at += 1
        batch.flush()
        out_ref[at:, :] = jnp.zeros((s.c_rows - at, LANES), jnp.float32)


def join_density(s, dt_ref, y1_ref, y2_ref, dens_ref):
    nx, ny, pitch = s.nx, s.ny, s.pitch
    even_y = is_even("gy")
    yd = (pick(even_y, ny + 3, 0), pick(even_y, 0, ny + 3))
    batch = Batch(16)
    for x in range(nx):
        at = x * pitch
        batch.add(
            dens_ref, (slice(at + 3, at + 3 + ny), slice(None)), dt_ref[x * ny : (x + 1) * ny, :]
        )
    batch.flush()
    for side, ref in enumerate((y1_ref, y2_ref)):
        alone = is_alone("gy", s.count_y, side)
        for dy in range(3):
            for x0 in range(0, nx, SUB):
                at = s.y_dens + dy * nx + x0
                to = x0 * pitch + yd[side] + dy
                batch.add(
                    dens_ref,
                    (pl.ds(to, SUB, stride=pitch), slice(None)),
                    jnp.where(alone, 0.0, ref[at : at + SUB, :]),
                )
    batch.flush()


def conduct_of(dens):
    return jnp.where(
        dens > 0.0, (KMIN + (1.0 - KMIN) * (dens * dens * dens)) * (1.0 / 12.0), 0.0
    )


def inverse_of(s, before, after):
    pair = before + after
    pair = pair[: s.pitch - 1] + pair[1:]
    total = 4.0 * (pair + pltpu.roll(pair, 1, 1))
    return jnp.where(after[1:] > 0.0, 1.0 / total, 0.0)


def up(tile):
    return pltpu.roll(tile, LANES - 1, 1)


def element_planes(cond, carry, a, count, y0, columns, field, emitter, keep=True):
    def loads_of(step):
        y = y0 + step
        right = [field[a + u, y + 1] for u in range(count + 1)]
        conduct = [cond[a + u, y] for u in range(count)]
        above = extra = None
        if step and emitter:
            above = (carry[0, y], carry[1, y])
            extra = [emitter.fetch(a + u, y) for u in range(count)]
        return right, conduct, above, extra

    left = [(tile, up(tile)) for tile in [field[a + u, y0] for u in range(count + 1)]]
    ahead = loads_of(0)
    old, waiting = [None] * count, []
    for step in range(columns):
        y = y0 + step
        right, conduct, above, extra = ahead
        if step + 1 < columns:
            ahead = loads_of(step + 1)
        if len(waiting) > 1:
            for into, at, tile in waiting.pop(0):
                into[at] = tile
        stores = []
        right = [(tile, up(tile)) for tile in right]
        for u in range(count):
            (p0, p0s), (p1, p1s) = left[u], left[u + 1]
            (r0, r0s), (r1, r1s) = right[u], right[u + 1]
            c = conduct[u]
            even = (p0 + r1) + (r0s + p1s)
            odd = (r0 + p1) + (p0s + r1s)
            pass_on = keep or u + 1 < count
            lower = upper = None
            if emitter:
                lower = (c * (odd + p1s), c * (even + p1))
            if pass_on:
                upper = (c * (even + p0s), c * (odd + p0))
            if step and emitter:
                low = (c * (even + r1s) + old[u][0][0]) + above[0]
                high = (c * (odd + r1) + old[u][0][1]) + above[1]
                total = low + pltpu.roll(high, 1, 1)
                stores += emitter.finish(a + u, y, p0, total, extra[u])
            if step and pass_on:
                above = (
                    c * (odd + r0s) + old[u][1][0],
                    c * (even + r0) + old[u][1][1],
                )
            old[u] = (lower, upper)
        if step and keep:
            stores += [(carry, (0, y), above[0]), (carry, (1, y), above[1])]
        waiting.append(stores)
        left = right
    for stores in waiting:
        for into, at, tile in stores:
            into[at] = tile


class First:
    def __init__(self, bx, invx, qx, wx):
        self.bx, self.invx, self.qx, self.wx = bx, invx, qx, wx

    def fetch(self, x, y):
        return self.bx[x, y], self.invx[x, y]

    def finish(self, x, y, node, total, extra):
        source, inverse = extra
        image = 1.25 * source - total
        return [(self.qx, (x, y), image), (self.wx, (x, y), image * inverse)]


class Second:
    def __init__(self, bx, zx, qx, q_out, v_out, sums):
        self.bx, self.zx, self.qx, self.sums = bx, zx, qx, sums
        self.q_out, self.v_out = q_out, v_out

    def fetch(self, x, y):
        return self.bx[x, y], self.zx[x, y], self.qx[x, y]

    def finish(self, x, y, weighted, total, extra):
        source, scaled, image = extra
        again = 1.25 * image - total
        change = scaled - weighted
        sums = self.sums
        sums[0] = sums[0] + source * scaled
        sums[1] = sums[1] + source * change
        sums[2] = sums[2] + (source - image) * change
        sums[3] = sums[3] + (image - again) * change
        at = x - 2, y - 2
        return [(self.q_out, at, image), (self.v_out, at, again)]


def over_planes(start, stop, body, state):
    pairs = (stop - start) // 2
    state = lax.fori_loop(0, pairs, lambda i, st: body(start + 2 * i, 2, st), state)
    if (stop - start) % 2:
        state = body(stop - 1, 1, state)
    return state


def inner_kernel(
    s, bt_ref, dt_ref, y1_ref, y2_ref, t2_ref,
    dens_ref, cond, invx, bx, zx, qx, wx, q_out, v_out, carry1, carry2, sums_ref,
):
    loads, nx, ny, my, pitch = s.loads, s.nx, s.ny, s.my, s.pitch
    bx, zx, qx, wx, carry1, carry2 = (
        Tiles(ref, my, loads) for ref in (bx, zx, qx, wx, carry1, carry2)
    )
    q_out, v_out = Tiles(q_out, ny, loads), Tiles(v_out, ny, loads)
    cond, invx = Rows(cond, pitch, loads), Rows(invx, pitch, loads)
    join_density(s, dt_ref, y1_ref, y2_ref, dens_ref)
    even_y = is_even("gy")
    ys = (pick(even_y, ny + 2, 0), pick(even_y, 0, ny + 2))
    before = None
    for x in range(nx):
        after = conduct_of(dens_ref[x * pitch : (x + 1) * pitch, :])
        cond.put(x + 2, after[1:])
        if x:
            invx.put(x + 2, inverse_of(s, before, after))
        before = after

    def stage(x, y, tile):
        stores = [(bx, (x + 2, y), tile)]
        if x:
            stores.append((zx, (x + 2, y), tile * invx[x + 2, y]))
        return stores

    inner = Tiles(bt_ref, ny, loads)
    batch = Batch(16)
    for x in range(nx):
        for y in range(ny):
            for store in stage(x, y + 2, inner[x, y]):
                batch.add(*store)
    batch.flush()
    unpack_tiles(
        y1_ref, 0, loads, 2 * nx, lambda i, tile: stage(i // 2, ys[0] + i % 2, tile)
    )
    far = Tiles(t2_ref, 2, loads)
    batch = Batch(16)
    for x in range(nx):
        for dy in range(2):
            for store in stage(x, ys[1] + dy, far[x, dy]):
                batch.add(*store)
    batch.flush()

    element_planes(cond, carry1, 3, 1, 0, my - 1, zx, None)

    def first(a, count, state):
        element_planes(cond, carry1, a, count, 0, my - 1, zx, First(bx, invx, qx, wx))
        return state

    over_planes(4, nx + 1, first, 0)
    element_planes(cond, carry2, 4, 1, 1, my - 3, wx, None)

    def second(a, count, sums):
        sums = list(sums)
        emitter = Second(bx, zx, qx, q_out, v_out, sums)
        element_planes(cond, carry2, a, count, 1, my - 3, wx, emitter)
        return tuple(sums)

    zero = jnp.zeros((loads, LANES), jnp.float32)
    sums = over_planes(5, nx, second, (zero,) * 4)
    for place, part in enumerate(sums):
        sums_ref[place * loads : (place + 1) * loads, :] = part


def outer_kernel(
    s, dens_ref, x1_ref, x2_ref, t1_ref, t2_ref, c1_ref, c2_ref,
    cond1, invx1, bx1, zx1, qx1, wx1, carry1, carry2, sums1,
    q_out, v_out, inv_out, sums_ref,
    low_ref, high_ref, low_d, high_d, cond2, invx2, bx2, zx2, qx2, wx2, carry3,
):
    loads, nx, ny, mx, my, pitch = s.loads, s.nx, s.ny, s.mx, s.my, s.pitch
    even_x = is_even("gx")

    even_y = is_even("gy")
    ys = (pick(even_y, ny + 2, 0), pick(even_y, 0, ny + 2))
    yd = (pick(even_y, ny + 3, 0), pick(even_y, 0, ny + 3))

    def take(near, far):
        faces = (x1_ref, t1_ref, near), (x2_ref, t2_ref, far)
        for side, (ref, face_ref, (tiles_ref, into)) in enumerate(faces):
            face, tiles = Tiles(face_ref, ny, loads), Tiles(tiles_ref, my, loads)
            alone_x = is_alone("gx", s.count_x, side)
            batch = Batch(18)
            for dx in range(2):
                for y in range(ny):
                    batch.add(tiles, (dx, y + 2), face[dx, y])
            for t in range(3):
                at = s.x_dens + t * ny
                rows = jnp.where(alone_x, 0.0, ref[at : at + ny, :])
                to = t * pitch + 3
                batch.add(into, (slice(to, to + ny), slice(None)), rows)
            batch.flush()
            for end, corner in enumerate((c1_ref, c2_ref)):
                alone = jnp.logical_or(alone_x, is_alone("gy", s.count_y, end))
                for i in range(4):
                    tile = unpack_tile(
                        lambda t: corner[t * loads : (t + 1) * loads, :], 4 * side + i, loads
                    )
                    batch.add(tiles, (i // 2, ys[end] + i % 2), tile)
                for i in range(9):
                    at = s.c_dens + 9 * side + i
                    row = jnp.where(alone, 0.0, corner[at : at + 1, :])
                    to = i // 3 * pitch + yd[end] + i % 3
                    batch.add(into, (pl.ds(to, 1), slice(None)), row)
            batch.flush()

    @pl.when(even_x)
    def _():
        take((high_ref, high_d), (low_ref, low_d))

    @pl.when(jnp.logical_not(even_x))
    def _():
        take((low_ref, low_d), (high_ref, high_d))

    def joined(first, second, own):
        return Joined(Tiles(first, my, loads), Tiles(second, my, loads), own)

    def joined_rows(first, second, own):
        return Joined(Rows(first, pitch, loads), Rows(second, pitch, loads), own)

    outside = (0, 1, nx + 2, nx + 3)
    scaled_own = outside + (2,)
    image_own = (1, 2, 3, nx + 1, nx + 2)
    cond, invx = joined_rows(cond2, cond1, outside), joined_rows(invx2, invx1, scaled_own)
    bx, zx = joined(bx2, bx1, outside), joined(zx2, zx1, scaled_own)
    qx, wx = joined(qx2, qx1, image_own), joined(wx2, wx1, image_own)
    own = [x - 2 for x in outer_planes(nx)]
    q_out, v_out = (Joined(Tiles(ref, ny, loads), None, own) for ref in (q_out, v_out))
    carry1, carry2, carry3 = (Tiles(ref, my, loads) for ref in (carry1, carry2, carry3))

    def conduct(ref, x):
        return conduct_of(ref[x * pitch : (x + 1) * pitch, :])

    low = [conduct(low_d, t) for t in range(3)] + [conduct(dens_ref, 0)]
    high = [conduct(dens_ref, nx - 1)] + [conduct(high_d, t) for t in range(2)]
    for x in range(3):
        inverse = inverse_of(s, low[x], low[x + 1])
        invx.put(x, inverse)
        if x < 2:
            cond.put(x, low[x + 1][1:])
    inv_out[...] = inverse[2 : 2 + ny]
    for x in range(2):
        invx.put(nx + 2 + x, inverse_of(s, high[x], high[x + 1]))
    cond.put(nx + 2, high[1][1:])

    batch = Batch(16)
    for ref, x0 in ((low_ref, 0), (high_ref, nx + 2)):
        tiles = Tiles(ref, my, loads)
        for dx in range(2):
            for y in range(my):
                tile = tiles[dx, y]
                batch.add(bx, (x0 + dx, y), tile)
                batch.add(zx, (x0 + dx, y), tile * invx[x0 + dx, y])
    for y in range(my):
        batch.add(zx, (2, y), bx[2, y] * invx[2, y])
    batch.flush()

    emitter = First(bx, invx, qx, wx)
    element_planes(cond, carry3, 0, 1, 0, my - 1, zx, None)
    element_planes(cond, carry3, 1, 2, 0, my - 1, zx, emitter)
    element_planes(cond, carry3, 3, 1, 0, my - 1, zx, emitter, keep=False)
    element_planes(cond, carry1, nx + 1, 2, 0, my - 1, zx, emitter, keep=False)
    sums = [sums1[place * loads : (place + 1) * loads, :] for place in range(4)]
    emitter = Second(bx, zx, qx, q_out, v_out, sums)
    element_planes(cond, carry3, 1, 1, 1, my - 3, wx, None)
    element_planes(cond, carry3, 2, 2, 1, my - 3, wx, emitter)
    element_planes(cond, carry3, 4, 1, 1, my - 3, wx, emitter, keep=False)
    element_planes(cond, carry2, nx, 2, 1, my - 3, wx, emitter, keep=False)
    lane = lane_ids(loads)
    load = lax.broadcasted_iota(jnp.int32, (loads, LANES), 0)
    packed = jnp.zeros((loads, LANES), jnp.float32)
    for place, part in enumerate(sums):
        total = jnp.sum(part, axis=1, keepdims=True)
        packed = packed + jnp.where(lane == place * loads + load, total, 0.0)
    row = jnp.sum(packed, axis=0, keepdims=True)
    sums_ref[...] = jnp.broadcast_to(row[None], sums_ref.shape)


def outer_planes(nx):
    return (2, 3, 4, nx, nx + 1)


def unpack_kernel(
    s, q1_ref, q2_ref, v1_ref, v2_ref, inv1_ref, inv2_ref, qo_ref, vo_ref, io_ref, q_ref, v_ref
):
    loads, nx, ny = s.loads, s.nx, s.ny
    batch = Batch()
    planes = outer_planes(nx)
    for first, second, whole in ((q1_ref, q2_ref, q_ref), (v1_ref, v2_ref, v_ref)):
        first, second = Tiles(first, ny, loads), Tiles(second, ny, loads)
        whole = Tiles(whole, ny, loads)
        for x in range(nx):
            for y in range(ny):
                if x + 2 in planes:
                    batch.add(whole, (x, y), second[planes.index(x + 2), y])
                else:
                    batch.add(whole, (x, y), first[x, y])
    batch.flush()
    batch = Batch()
    for x0 in range(0, nx, SUB):
        for ref, out in ((q_ref, qo_ref), (v_ref, vo_ref)):
            for load in range(loads):
                for block in range(packed_count(ny)):
                    tile = pack_block(
                        lambda y: ref[
                            pl.ds((x0 * ny + y) * loads + load, SUB, stride=ny * loads), :
                        ],
                        ny, block, SUB,
                    )
                    lanes = slice(block * LANES, (block + 1) * LANES)
                    batch.add(out, (load, slice(x0, x0 + SUB), lanes), tile)
        for block in range(packed_count(ny)):
            tile = pack_block(
                lambda y: inv1_ref[
                    pl.ds((x0 + 2) * s.pitch + y + 2, SUB, stride=s.pitch), :
                ],
                ny, block, SUB,
            )
            lanes = slice(block * LANES, (block + 1) * LANES)
            batch.add(io_ref, (slice(x0, x0 + SUB), lanes), tile)
    batch.flush()
    for block in range(packed_count(ny)):
        io_ref[0:1, block * LANES : (block + 1) * LANES] = pack_block(
            lambda y: inv2_ref[y : y + 1, :], ny, block, 1
        )


def finish_kernel(s, parts_ref, b_ref, q_ref, v_ref, inv_ref, x_hbm, r_hbm, x_ref, r_ref, sems):
    loads = s.loads
    totals = jnp.sum(parts_ref[...], axis=0)

    def part(place):
        return pltpu.roll(totals, (LANES - place * loads) % LANES, 1) if place else totals

    rz, near, square, last = (part(place) for place in range(4))
    direct = rz - near
    alpha = rz / direct
    short = -near / direct
    rz_next = short * short * rz + 2.0 * alpha * short * near + alpha * alpha * square
    beta = rz_next / rz
    grown = short + beta
    curved = (
        grown * grown * direct
        + 2.0 * alpha * grown * (near - square)
        + alpha * alpha * last
    )
    alpha_next = rz_next / curved
    first_row = alpha + alpha_next * (1.0 + beta)
    second_row = alpha_next * alpha
    inverse = inv_ref[...]
    copies = []
    for load in range(loads):
        first = first_row[:, load : load + 1]
        second = second_row[:, load : load + 1]
        source, image = b_ref[load], q_ref[load]
        x_ref[load] = (first * source - second * image) * inverse
        copies.append(pltpu.make_async_copy(x_ref.at[load], x_hbm.at[load], sems.at[0, load]))
        copies[-1].start()
        r_ref[load] = source - first * image + second * v_ref[load]
        copies.append(pltpu.make_async_copy(r_ref.at[load], r_hbm.at[load], sems.at[1, load]))
        copies[-1].start()
    for copy in copies:
        copy.wait()


def swap(array, axis, start):
    counts = {name: lax.axis_size(name) for name in ("gx", "gy")}
    other = "gy" if axis == "gx" else "gx"
    pairs = []
    for at in np.ndindex(counts["gx"], counts["gy"]):
        place = dict(zip(("gx", "gy"), at))
        partner = place[axis] + (1 if (place[axis] - start) % 2 == 0 else -1)
        if 0 <= partner < counts[axis]:
            place[axis] = partner
        elif place[other] ^ 1 < counts[other]:
            place[other] ^= 1
        pairs.append((at[0] * counts["gy"] + at[1], place["gx"] * counts["gy"] + place["gy"]))
    return lax.ppermute(array, ("gx", "gy"), pairs)


def per_device(heat_source, density):
    loads, nx, flat = heat_source.shape
    ny = flat // NZ
    s = Sizes(loads, nx, ny, lax.axis_size("gx"), lax.axis_size("gy"))
    nodes = nx * ny * loads
    devices = lax.axis_size("gx") * lax.axis_size("gy")

    def shape(*dims):
        return jax.ShapeDtypeStruct(dims, jnp.float32)

    def scratch(*dims):
        return pltpu.VMEM(dims, jnp.float32)

    def call(kernel, out_shape, **more):
        params = pltpu.CompilerParams(vmem_limit_bytes=20 * 1024 * 1024)
        return pl.pallas_call(
            functools.partial(kernel, s), out_shape=out_shape, compiler_params=params, **more
        )

    hbm = pl.BlockSpec(memory_space=pltpu.HBM)
    y_face, x_face, corner = (shape(rows, LANES) for rows in (s.y_rows, s.x_rows, s.c_rows))
    bt, dt, x1, x2 = call(
        pack_kernel,
        (shape(nodes, LANES), shape(nx * ny, LANES), x_face, x_face),
        in_specs=[hbm, hbm],
        scratch_shapes=[
            scratch(loads, nx, flat),
            scratch(nx, flat),
            pltpu.SemaphoreType.DMA((3,)),
        ],
    )(
        pltpu.with_memory_space_constraint(heat_source, pltpu.HBM),
        pltpu.with_memory_space_constraint(density, pltpu.HBM),
    )
    x2, x1 = swap(x2, "gx", 1), swap(x1, "gx", 0)
    y1, y2 = call(pack_y_kernel, (y_face, y_face))(bt, dt)
    y2, y1 = swap(y2, "gy", 1), swap(y1, "gy", 0)
    t2 = call(open_y_kernel, shape(2 * nx * loads, LANES))(y2)
    xt = shape(2 * ny * loads, LANES)
    xt2 = call(open_x_kernel, xt)(x2)
    xt1, c1, c2 = call(
        corner_kernel,
        (xt, corner, corner),
        cost_estimate=pl.CostEstimate(flops=2 * 10**9, transcendentals=0, bytes_accessed=0),
    )(x2, xt2, x1)
    xt1, dt = lax.optimization_barrier((xt1, dt))
    c2, c1 = swap(c2, "gy", 1), swap(c1, "gy", 0)
    plane = s.my * loads
    rows, field = shape(s.mx * s.pitch, LANES), shape(s.mx * plane, LANES)
    edge = shape(2 * plane, LANES)
    inside = shape(nodes, LANES)
    dens, cond, inv_1, bx, zx, q_x, w_x, q_1, v_1, carry1, carry2, sums = call(
        inner_kernel,
        (shape(nx * s.pitch, LANES),)
        + (rows,) * 2
        + (field,) * 4
        + (inside,) * 2
        + (edge,) * 2
        + (shape(4 * loads, LANES),),
    )(bt, dt, y1, y2, t2)
    ends = shape(len(outer_planes(nx)) * ny * loads, LANES)
    q_2, v_2, inv_2, sums = call(
        outer_kernel,
        (ends, ends, shape(ny, LANES), shape(devices, 1, LANES)),
        scratch_shapes=[scratch(2 * plane, LANES)] * 2
        + [scratch(3 * s.pitch, LANES)] * 2
        + [scratch(5 * s.pitch, LANES)] * 2
        + [scratch(5 * plane, LANES)] * 4
        + [scratch(2 * plane, LANES)],
    )(dens, x1, x2, xt1, xt2, c1, c2, cond, inv_1, bx, zx, q_x, w_x, carry1, carry2, sums)
    parts = lax.all_to_all(sums, ("gx", "gy"), 0, 0, tiled=True)
    whole = shape(loads, nx, flat)
    image, again, inverse = call(
        unpack_kernel,
        (whole, whole, shape(nx, flat)),
        scratch_shapes=[scratch(nodes, LANES)] * 2,
    )(q_1, q_2, v_1, v_2, inv_1, inv_2)
    return call(
        finish_kernel,
        (whole, whole),
        out_specs=(hbm, hbm),
        scratch_shapes=[
            scratch(loads, nx, flat),
            scratch(loads, nx, flat),
            pltpu.SemaphoreType.DMA((2, loads)),
        ],
    )(parts, heat_source, image, again, inverse)


def solution(mesh):
    placed = (P(None, "gx", "gy"), P("gx", "gy"))
    return jax.shard_map(
        per_device,
        mesh=mesh,
        in_specs=placed,
        out_specs=(P(None, "gx", "gy"), P(None, "gx", "gy")),
        check_vma=False,
    )
```

```python
import functools

import jax
import jax.numpy as jnp
import numpy as np
from jax import lax
from jax.experimental import pallas as pl
from jax.experimental.pallas import tpu as pltpu
from jax.sharding import PartitionSpec as P

NZ = 96
KMIN = 0.001
LANES = 128
SUB = 8


class Batch:
    def __init__(self, size=12):
        self.size, self.held = size, []

    def add(self, into, at, tile):
        self.held.append((into, at, tile))
        if len(self.held) >= self.size:
            self.flush()

    def flush(self):
        for into, at, tile in self.held:
            into[at] = tile
        self.held = []


def packed_count(tiles):
    return -(-tiles * NZ // LANES)


def lane_ids(rows):
    return lax.broadcasted_iota(jnp.int32, (rows, LANES), 1)


def unpack_tile(read, index, rows):
    start = index * NZ
    block, offset = start // LANES, start % LANES
    lane = lane_ids(rows)
    first = read(block)
    if offset:
        first = pltpu.roll(first, LANES - offset, 1)
    if offset + NZ > LANES:
        second = pltpu.roll(read(block + 1), LANES - offset, 1)
        first = jnp.where(lane < LANES - offset, first, second)
    return jnp.where(lane < NZ, first, 0.0)


def pack_block(read_tile, tiles, block, rows):
    lane = lane_ids(rows)
    start = block * LANES
    out, at = None, start
    while at < start + LANES and at // NZ < tiles:
        index, z = at // NZ, at % NZ
        here = at - start
        piece = read_tile(index)
        shift = (here - z) % LANES
        if shift:
            piece = pltpu.roll(piece, shift, 1)
        out = piece if out is None else jnp.where(lane < here, out, piece)
        at += NZ - z
    return out


def pack_tiles(out_ref, at, rows, tiles, read_tile):
    batch = Batch()
    for block in range(packed_count(tiles)):
        place = slice(at + block * rows, at + (block + 1) * rows), slice(None)
        batch.add(out_ref, place, pack_block(read_tile, tiles, block, rows))
    batch.flush()


def unpack_tiles(ref, at, rows, tiles, write):
    batch = Batch()
    for index in range(tiles):
        tile = unpack_tile(lambda t: ref[at + t * rows : at + (t + 1) * rows, :], index, rows)
        for store in write(index, tile):
            batch.add(*store)
    batch.flush()


class Sizes:
    def __init__(self, loads, nx, ny, count_x, count_y):
        self.loads, self.nx, self.ny = loads, nx, ny
        self.count_x, self.count_y = count_x, count_y
        self.mx, self.my = nx + 4, ny + 4
        self.pitch = -(-(ny + 6) // SUB) * SUB
        self.y_dens = packed_count(2 * nx) * loads
        self.y_rows = self.y_dens + 3 * nx
        self.x_dens = packed_count(2 * ny) * loads
        self.x_rows = self.x_dens + 3 * ny
        self.c_dens = packed_count(8) * loads
        self.c_rows = self.c_dens + -(-18 // SUB) * SUB


class Tiles:
    def __init__(self, ref, columns, loads):
        self.ref, self.columns, self.loads = ref, columns, loads

    def rows(self, at):
        start = (at[0] * self.columns + at[1]) * self.loads
        if not isinstance(start, int):
            start = pl.multiple_of(start, SUB)
        return pl.ds(start, self.loads)

    def __getitem__(self, at):
        return self.ref[self.rows(at), :]

    def __setitem__(self, at, tile):
        self.ref[self.rows(at), :] = tile


class Rows:
    def __init__(self, ref, pitch, loads):
        self.ref, self.pitch, self.loads = ref, pitch, loads

    def __getitem__(self, at):
        row = self.ref[pl.ds(at[0] * self.pitch + at[1], 1), :]
        return jnp.broadcast_to(row, (self.loads, LANES))

    def put(self, x, values):
        self.ref[x * self.pitch : x * self.pitch + values.shape[0], :] = values


class Joined:
    def __init__(self, first, second, own):
        self.first, self.second, self.own = first, second, own

    def __getitem__(self, at):
        if at[0] in self.own:
            return self.first[self.own.index(at[0]), at[1]]
        return self.second[at]

    def __setitem__(self, at, tile):
        self.first[self.own.index(at[0]), at[1]] = tile

    def put(self, x, values):
        self.first.put(self.own.index(x), values)


class Inside:
    def __init__(self, inner, own, outer):
        self.inner, self.own, self.outer = inner, own, outer

    def __getitem__(self, at):
        if at[1] in self.own:
            return self.inner[at[0] - 2, at[1] - 2]
        return self.outer[at]

    def __setitem__(self, at, tile):
        self.outer[at] = tile


def is_even(axis):
    return lax.rem(lax.axis_index(axis), 2) == 0


def is_alone(axis, count, start):
    place = lax.axis_index(axis)
    last = (count - start) % 2
    alone = place < start
    return jnp.logical_or(alone, place == count - 1) if last else alone


def pick(even, if_even, if_odd):
    return jnp.where(even, if_even, if_odd)


def pack_x_kernel(s, b_hbm, d_hbm, b_ref, dt_ref, x1_ref, x2_ref, d_ref, sems):
    loads, nx, ny = s.loads, s.nx, s.ny
    blocks = packed_count(ny)
    d_copy = pltpu.make_async_copy(d_hbm, d_ref, sems.at[blocks])
    d_copy.start()
    copies = []
    for block in range(blocks):
        lanes = pl.ds(block * LANES, LANES)
        copies.append(
            pltpu.make_async_copy(b_hbm.at[:, lanes], b_ref.at[block], sems.at[block])
        )
        copies[-1].start()
    d_copy.wait()
    batch = Batch(16)
    for x0 in range(0, nx, SUB):
        for y in range(ny):
            tile = unpack_tile(
                lambda t: d_ref[x0 : x0 + SUB, t * LANES : (t + 1) * LANES], y, SUB
            )
            batch.add(dt_ref, (pl.ds(x0 * ny + y, SUB, stride=ny), slice(None)), tile)
    batch.flush()
    even_x = is_even("gx")
    for ref, upper in ((x2_ref, jnp.logical_not(even_x)), (x1_ref, even_x)):
        rows = pl.ds(pl.multiple_of(pick(upper, nx - 3, 0) * ny, SUB), 3 * ny)
        ref[s.x_dens :, :] = dt_ref[rows, :]
    for copy in copies:
        copy.wait()
    batch = Batch()
    for ref, upper in ((x2_ref, jnp.logical_not(even_x)), (x1_ref, even_x)):
        x0 = pick(upper, nx - 2, 0)
        for dx in range(2):
            for block in range(blocks):
                tile = b_ref[block, pl.ds(x0 + dx, loads, stride=nx), :]
                at = (dx * blocks + block) * loads
                batch.add(ref, (slice(at, at + loads), slice(None)), tile)
    batch.flush()


def pack_y_kernel(s, b_ref, dt_ref, bt_ref, y1_ref, y2_ref):
    loads, nx, ny = s.loads, s.nx, s.ny
    batch = Batch(16)
    for load in range(loads):
        for x0 in range(0, nx, SUB):
            at = load * nx + x0
            for y in range(ny):
                tile = unpack_tile(
                    lambda t: b_ref[t, at : at + SUB, :], y, SUB
                )
                rows = pl.ds((x0 * ny + y) * loads + load, SUB, stride=ny * loads)
                batch.add(bt_ref, (rows, slice(None)), tile)
    batch.flush()
    even_y = is_even("gy")
    pack_y_face(s, jnp.logical_not(even_y), bt_ref, dt_ref, y2_ref)
    pack_y_face(s, even_y, bt_ref, dt_ref, y1_ref)


def pack_y_face(s, upper, bt_ref, dt_ref, out_ref):
    loads, nx, ny = s.loads, s.nx, s.ny
    tiles = Tiles(bt_ref, ny, loads)
    y0 = pick(upper, ny - 2, 0)
    pack_tiles(out_ref, 0, loads, 2 * nx, lambda i: tiles[i // 2, y0 + i % 2])
    y0 = pick(upper, ny - 3, 0)
    batch = Batch()
    for dy in range(3):
        for x0 in range(0, nx, SUB):
            at = s.y_dens + dy * nx + x0
            tile = dt_ref[pl.ds(x0 * ny + y0 + dy, SUB, stride=ny), :]
            batch.add(out_ref, (slice(at, at + SUB), slice(None)), tile)
    batch.flush()


def open_y_kernel(s, y_ref, t_ref):
    tiles = Tiles(t_ref, 2, s.loads)
    unpack_tiles(
        y_ref, 0, s.loads, 2 * s.nx, lambda i, tile: [(tiles, (i // 2, i % 2), tile)]
    )


def open_x_kernel(s, x_ref, t_ref):
    tiles = Tiles(t_ref, s.ny, s.loads)
    unpack_tiles(
        x_ref, 0, s.loads, 2 * s.ny, lambda i, tile: [(tiles, (i // s.ny, i % s.ny), tile)]
    )


def corner_kernel(s, x2_ref, t2_ref, x1_ref, t1_ref, c1_ref, c2_ref):
    loads, ny = s.loads, s.ny
    open_x_kernel(s, x1_ref, t1_ref)
    halves = Tiles(t1_ref, ny, loads), Tiles(t2_ref, ny, loads)
    even_y = is_even("gy")
    for out_ref, upper in ((c2_ref, jnp.logical_not(even_y)), (c1_ref, even_y)):
        y0 = pick(upper, ny - 2, 0)
        pack_tiles(out_ref, 0, loads, 8, lambda i: halves[i // 4][i // 2 % 2, y0 + i % 2])
        y0 = pick(upper, ny - 3, 0)
        batch, at = Batch(18), s.c_dens
        for ref in (x1_ref, x2_ref):
            for t in range(3):
                for dy in range(3):
                    row = ref[pl.ds(s.x_dens + t * ny + y0 + dy, 1), :]
                    batch.add(out_ref, (slice(at, at + 1), slice(None)), row)
                    at += 1
        batch.flush()
        out_ref[at:, :] = jnp.zeros((s.c_rows - at, LANES), jnp.float32)


def join_density(s, dt_ref, y1_ref, y2_ref, dens_ref):
    nx, ny, pitch = s.nx, s.ny, s.pitch
    even_y = is_even("gy")
    yd = (pick(even_y, ny + 3, 0), pick(even_y, 0, ny + 3))
    batch = Batch(16)
    for x in range(nx):
        at = x * pitch
        batch.add(
            dens_ref, (slice(at + 3, at + 3 + ny), slice(None)), dt_ref[x * ny : (x + 1) * ny, :]
        )
    batch.flush()
    for side, ref in enumerate((y1_ref, y2_ref)):
        alone = is_alone("gy", s.count_y, side)
        for dy in range(3):
            for x0 in range(0, nx, SUB):
                at = s.y_dens + dy * nx + x0
                to = x0 * pitch + yd[side] + dy
                batch.add(
                    dens_ref,
                    (pl.ds(to, SUB, stride=pitch), slice(None)),
                    jnp.where(alone, 0.0, ref[at : at + SUB, :]),
                )
    batch.flush()


def conduct_of(dens):
    return jnp.where(
        dens > 0.0, (KMIN + (1.0 - KMIN) * (dens * dens * dens)) * (1.0 / 12.0), 0.0
    )


def inverse_of(s, before, after):
    pair = before + after
    pair = pair[: s.pitch - 1] + pair[1:]
    total = 4.0 * (pair + pltpu.roll(pair, 1, 1))
    return jnp.where(after[1:] > 0.0, 1.0 / total, 0.0)


def up(tile):
    return pltpu.roll(tile, LANES - 1, 1)


def element_planes(cond, carry, a, count, y0, columns, field, emitter, keep=True):
    def loads_of(step):
        y = y0 + step
        right = [field[a + u, y + 1] for u in range(count + 1)]
        conduct = [cond[a + u, y] for u in range(count)]
        above = extra = None
        if step and emitter:
            above = (carry[0, y], carry[1, y])
            extra = [emitter.fetch(a + u, y) for u in range(count)]
        return right, conduct, above, extra

    left = [(tile, up(tile)) for tile in [field[a + u, y0] for u in range(count + 1)]]
    ahead = loads_of(0)
    old, waiting = [None] * count, []
    for step in range(columns):
        y = y0 + step
        right, conduct, above, extra = ahead
        if step + 1 < columns:
            ahead = loads_of(step + 1)
        if len(waiting) > 1:
            for into, at, tile in waiting.pop(0):
                into[at] = tile
        stores = []
        right = [(tile, up(tile)) for tile in right]
        for u in range(count):
            (p0, p0s), (p1, p1s) = left[u], left[u + 1]
            (r0, r0s), (r1, r1s) = right[u], right[u + 1]
            c = conduct[u]
            even = (p0 + r1) + (r0s + p1s)
            odd = (r0 + p1) + (p0s + r1s)
            pass_on = keep or u + 1 < count
            lower = upper = None
            if emitter:
                lower = (c * (odd + p1s), c * (even + p1))
            if pass_on:
                upper = (c * (even + p0s), c * (odd + p0))
            if step and emitter:
                low = (c * (even + r1s) + old[u][0][0]) + above[0]
                high = (c * (odd + r1) + old[u][0][1]) + above[1]
                total = low + pltpu.roll(high, 1, 1)
                stores += emitter.finish(a + u, y, p0, total, extra[u])
            if step and pass_on:
                above = (
                    c * (odd + r0s) + old[u][1][0],
                    c * (even + r0) + old[u][1][1],
                )
            old[u] = (lower, upper)
        if step and keep:
            stores += [(carry, (0, y), above[0]), (carry, (1, y), above[1])]
        waiting.append(stores)
        left = right
    for stores in waiting:
        for into, at, tile in stores:
            into[at] = tile


class First:
    def __init__(self, bx, invx, qx, wx):
        self.bx, self.invx, self.qx, self.wx = bx, invx, qx, wx

    def fetch(self, x, y):
        return self.bx[x, y], self.invx[x, y]

    def finish(self, x, y, node, total, extra):
        source, inverse = extra
        image = 1.25 * source - total
        return [(self.qx, (x, y), image), (self.wx, (x, y), image * inverse)]


class Second:
    def __init__(self, bx, zx, qx, q_out, v_out, sums):
        self.bx, self.zx, self.qx, self.sums = bx, zx, qx, sums
        self.q_out, self.v_out = q_out, v_out

    def fetch(self, x, y):
        return self.bx[x, y], self.zx[x, y], self.qx[x, y]

    def finish(self, x, y, weighted, total, extra):
        source, scaled, image = extra
        again = 1.25 * image - total
        change = scaled - weighted
        sums = self.sums
        sums[0] = sums[0] + source * scaled
        sums[1] = sums[1] + source * change
        sums[2] = sums[2] + (source - image) * change
        sums[3] = sums[3] + (image - again) * change
        at = x - 2, y - 2
        return [(self.q_out, at, image), (self.v_out, at, again)]


def over_planes(start, stop, body, state):
    pairs = (stop - start) // 2
    state = lax.fori_loop(0, pairs, lambda i, st: body(start + 2 * i, 2, st), state)
    if (stop - start) % 2:
        state = body(stop - 1, 1, state)
    return state


def inside_fields(s, bt_ref, zt_ref, bx, zx):
    brick = (Tiles(ref, s.ny, s.loads) for ref in (bt_ref, zt_ref))
    starts = (2, 3)
    return tuple(
        Inside(inner, range(start, s.ny + 2), outer)
        for inner, start, outer in zip(brick, starts, (bx, zx))
    )


def scale_kernel(s, bt_ref, dt_ref, zt_ref, inv_ref):
    loads, nx, ny = s.loads, s.nx, s.ny
    inner, scaled = Tiles(bt_ref, ny, loads), Tiles(zt_ref, ny, loads)
    inverse = Rows(inv_ref, ny, loads)
    before = conduct_of(dt_ref[0:ny, :])
    for x in range(1, nx):
        after = conduct_of(dt_ref[x * ny : (x + 1) * ny, :])
        pair = before + after
        pair = pair[: ny - 1] + pair[1:]
        total = 4.0 * (pair + pltpu.roll(pair, 1, 1))
        inverse.put(x, jnp.where(after[1:] > 0.0, 1.0 / total, 0.0))
        before = after
    batch = Batch(16)
    for x in range(1, nx):
        for y in range(1, ny):
            batch.add(scaled, (x, y), inner[x, y] * inverse[x, y - 1])
    batch.flush()


def inner_kernel(
    s, bt_ref, zt_ref, dt_ref, y1_ref, y2_ref, t1_ref,
    dens_ref, cond, invx, bx, zx, qx, wx, q_out, v_out, carry1, carry2, sums_ref,
):
    loads, nx, ny, my, pitch = s.loads, s.nx, s.ny, s.my, s.pitch
    bx, zx, qx, wx, carry1, carry2 = (
        Tiles(ref, my, loads) for ref in (bx, zx, qx, wx, carry1, carry2)
    )
    q_out, v_out = Tiles(q_out, ny, loads), Tiles(v_out, ny, loads)
    cond, invx = Rows(cond, pitch, loads), Rows(invx, pitch, loads)
    join_density(s, dt_ref, y1_ref, y2_ref, dens_ref)
    even_y = is_even("gy")
    ys = (pick(even_y, ny + 2, 0), pick(even_y, 0, ny + 2))
    before = None
    for x in range(nx):
        after = conduct_of(dens_ref[x * pitch : (x + 1) * pitch, :])
        cond.put(x + 2, after[1:])
        if x:
            invx.put(x + 2, inverse_of(s, before, after))
        before = after

    bx, zx = inside_fields(s, bt_ref, zt_ref, bx, zx)

    def stage(x, y, tile):
        stores = [(bx, (x + 2, y), tile)]
        if x:
            stores.append((zx, (x + 2, y), tile * invx[x + 2, y]))
        return stores

    batch = Batch(16)
    for x in range(1, nx):
        batch.add(zx, (x + 2, 2), bx[x + 2, 2] * invx[x + 2, 2])
    batch.flush()
    unpack_tiles(
        y2_ref, 0, loads, 2 * nx, lambda i, tile: stage(i // 2, ys[1] + i % 2, tile)
    )
    near = Tiles(t1_ref, 2, loads)
    batch = Batch(16)
    for x in range(nx):
        for dy in range(2):
            for store in stage(x, ys[0] + dy, near[x, dy]):
                batch.add(*store)
    batch.flush()

    element_planes(cond, carry1, 3, 1, 0, my - 1, zx, None)

    def first(a, count, state):
        element_planes(cond, carry1, a, count, 0, my - 1, zx, First(bx, invx, qx, wx))
        return state

    over_planes(4, nx + 1, first, 0)
    element_planes(cond, carry2, 4, 1, 1, my - 3, wx, None)

    def second(a, count, sums):
        sums = list(sums)
        emitter = Second(bx, zx, qx, q_out, v_out, sums)
        element_planes(cond, carry2, a, count, 1, my - 3, wx, emitter)
        return tuple(sums)

    zero = jnp.zeros((loads, LANES), jnp.float32)
    sums = over_planes(5, nx, second, (zero,) * 4)
    for place, part in enumerate(sums):
        sums_ref[place * loads : (place + 1) * loads, :] = part


def outer_kernel(
    s, bt_ref, zt_ref, dens_ref, x1_ref, x2_ref, t1_ref, t2_ref, c1_ref, c2_ref,
    cond1, invx1, bx1, zx1, qx1, wx1, carry1, carry2, sums1,
    q_out, v_out, inv_out, sums_ref,
    low_ref, high_ref, low_d, high_d, cond2, invx2, bx2, zx2, qx2, wx2, carry3,
):
    loads, nx, ny, mx, my, pitch = s.loads, s.nx, s.ny, s.mx, s.my, s.pitch
    even_x = is_even("gx")

    even_y = is_even("gy")
    ys = (pick(even_y, ny + 2, 0), pick(even_y, 0, ny + 2))
    yd = (pick(even_y, ny + 3, 0), pick(even_y, 0, ny + 3))

    def take(near, far):
        faces = (x1_ref, t1_ref, near), (x2_ref, t2_ref, far)
        for side, (ref, face_ref, (tiles_ref, into)) in enumerate(faces):
            face, tiles = Tiles(face_ref, ny, loads), Tiles(tiles_ref, my, loads)
            alone_x = is_alone("gx", s.count_x, side)
            batch = Batch(18)
            for dx in range(2):
                for y in range(ny):
                    batch.add(tiles, (dx, y + 2), face[dx, y])
            for t in range(3):
                at = s.x_dens + t * ny
                rows = jnp.where(alone_x, 0.0, ref[at : at + ny, :])
                to = t * pitch + 3
                batch.add(into, (slice(to, to + ny), slice(None)), rows)
            batch.flush()
            for end, corner in enumerate((c1_ref, c2_ref)):
                alone = jnp.logical_or(alone_x, is_alone("gy", s.count_y, end))
                for i in range(4):
                    tile = unpack_tile(
                        lambda t: corner[t * loads : (t + 1) * loads, :], 4 * side + i, loads
                    )
                    batch.add(tiles, (i // 2, ys[end] + i % 2), tile)
                for i in range(9):
                    at = s.c_dens + 9 * side + i
                    row = jnp.where(alone, 0.0, corner[at : at + 1, :])
                    to = i // 3 * pitch + yd[end] + i % 3
                    batch.add(into, (pl.ds(to, 1), slice(None)), row)
            batch.flush()

    @pl.when(even_x)
    def _():
        take((high_ref, high_d), (low_ref, low_d))

    @pl.when(jnp.logical_not(even_x))
    def _():
        take((low_ref, low_d), (high_ref, high_d))

    def joined(first, second, own):
        return Joined(Tiles(first, my, loads), Tiles(second, my, loads), own)

    def joined_rows(first, second, own):
        return Joined(Rows(first, pitch, loads), Rows(second, pitch, loads), own)

    outside = (0, 1, nx + 2, nx + 3)
    scaled_own = outside + (2,)
    image_own = (1, 2, 3, nx + 1, nx + 2)
    cond, invx = joined_rows(cond2, cond1, outside), joined_rows(invx2, invx1, scaled_own)
    bx1, zx1 = inside_fields(
        s, bt_ref, zt_ref, Tiles(bx1, my, loads), Tiles(zx1, my, loads)
    )
    bx = Joined(Tiles(bx2, my, loads), bx1, outside)
    zx = Joined(Tiles(zx2, my, loads), zx1, scaled_own)
    qx, wx = joined(qx2, qx1, image_own), joined(wx2, wx1, image_own)
    own = [x - 2 for x in outer_planes(nx)]
    q_out, v_out = (Joined(Tiles(ref, ny, loads), None, own) for ref in (q_out, v_out))
    carry1, carry2, carry3 = (Tiles(ref, my, loads) for ref in (carry1, carry2, carry3))

    def conduct(ref, x):
        return conduct_of(ref[x * pitch : (x + 1) * pitch, :])

    low = [conduct(low_d, t) for t in range(3)] + [conduct(dens_ref, 0)]
    high = [conduct(dens_ref, nx - 1)] + [conduct(high_d, t) for t in range(2)]
    for x in range(3):
        inverse = inverse_of(s, low[x], low[x + 1])
        invx.put(x, inverse)
        if x < 2:
            cond.put(x, low[x + 1][1:])
    inv_out[...] = inverse[2 : 2 + ny]
    for x in range(2):
        invx.put(nx + 2 + x, inverse_of(s, high[x], high[x + 1]))
    cond.put(nx + 2, high[1][1:])

    batch = Batch(16)
    for ref, x0 in ((low_ref, 0), (high_ref, nx + 2)):
        tiles = Tiles(ref, my, loads)
        for dx in range(2):
            for y in range(my):
                tile = tiles[dx, y]
                batch.add(bx, (x0 + dx, y), tile)
                batch.add(zx, (x0 + dx, y), tile * invx[x0 + dx, y])
    for y in range(my):
        batch.add(zx, (2, y), bx[2, y] * invx[2, y])
    batch.flush()

    emitter = First(bx, invx, qx, wx)
    element_planes(cond, carry3, 0, 1, 0, my - 1, zx, None)
    element_planes(cond, carry3, 1, 2, 0, my - 1, zx, emitter)
    element_planes(cond, carry3, 3, 1, 0, my - 1, zx, emitter, keep=False)
    element_planes(cond, carry1, nx + 1, 2, 0, my - 1, zx, emitter, keep=False)
    sums = [sums1[place * loads : (place + 1) * loads, :] for place in range(4)]
    emitter = Second(bx, zx, qx, q_out, v_out, sums)
    element_planes(cond, carry3, 1, 1, 1, my - 3, wx, None)
    element_planes(cond, carry3, 2, 2, 1, my - 3, wx, emitter)
    element_planes(cond, carry3, 4, 1, 1, my - 3, wx, emitter, keep=False)
    element_planes(cond, carry2, nx, 2, 1, my - 3, wx, emitter, keep=False)
    lane = lane_ids(loads)
    load = lax.broadcasted_iota(jnp.int32, (loads, LANES), 0)
    packed = jnp.zeros((loads, LANES), jnp.float32)
    for place, part in enumerate(sums):
        total = jnp.sum(part, axis=1, keepdims=True)
        packed = packed + jnp.where(lane == place * loads + load, total, 0.0)
    row = jnp.sum(packed, axis=0, keepdims=True)
    sums_ref[...] = jnp.broadcast_to(row[None], sums_ref.shape)


def outer_planes(nx):
    return (2, 3, 4, nx, nx + 1)


def unpack_kernel(
    s, q1_ref, q2_ref, v1_ref, v2_ref, inv1_ref, inv2_ref, qo_ref, vo_ref, io_ref, q_ref, v_ref
):
    loads, nx, ny = s.loads, s.nx, s.ny
    batch = Batch()
    planes = outer_planes(nx)
    for first, second, whole in ((q1_ref, q2_ref, q_ref), (v1_ref, v2_ref, v_ref)):
        first, second = Tiles(first, ny, loads), Tiles(second, ny, loads)
        whole = Tiles(whole, ny, loads)
        for x in range(nx):
            for y in range(ny):
                if x + 2 in planes:
                    batch.add(whole, (x, y), second[planes.index(x + 2), y])
                else:
                    batch.add(whole, (x, y), first[x, y])
    batch.flush()
    batch = Batch()
    for x0 in range(0, nx, SUB):
        for ref, out in ((q_ref, qo_ref), (v_ref, vo_ref)):
            for load in range(loads):
                for block in range(packed_count(ny)):
                    tile = pack_block(
                        lambda y: ref[
                            pl.ds((x0 * ny + y) * loads + load, SUB, stride=ny * loads), :
                        ],
                        ny, block, SUB,
                    )
                    lanes = slice(block * LANES, (block + 1) * LANES)
                    batch.add(out, (load, slice(x0, x0 + SUB), lanes), tile)
        for block in range(packed_count(ny)):
            tile = pack_block(
                lambda y: inv1_ref[
                    pl.ds((x0 + 2) * s.pitch + y + 2, SUB, stride=s.pitch), :
                ],
                ny, block, SUB,
            )
            lanes = slice(block * LANES, (block + 1) * LANES)
            batch.add(io_ref, (slice(x0, x0 + SUB), lanes), tile)
    batch.flush()
    for block in range(packed_count(ny)):
        io_ref[0:1, block * LANES : (block + 1) * LANES] = pack_block(
            lambda y: inv2_ref[y : y + 1, :], ny, block, 1
        )


def finish_kernel(s, parts_ref, b_ref, q_ref, v_ref, inv_ref, x_hbm, r_hbm, x_ref, r_ref, sems):
    loads = s.loads
    totals = jnp.sum(parts_ref[...], axis=0)

    def part(place):
        return pltpu.roll(totals, (LANES - place * loads) % LANES, 1) if place else totals

    rz, near, square, last = (part(place) for place in range(4))
    direct = rz - near
    alpha = rz / direct
    short = -near / direct
    rz_next = short * short * rz + 2.0 * alpha * short * near + alpha * alpha * square
    beta = rz_next / rz
    grown = short + beta
    curved = (
        grown * grown * direct
        + 2.0 * alpha * grown * (near - square)
        + alpha * alpha * last
    )
    alpha_next = rz_next / curved
    first_row = alpha + alpha_next * (1.0 + beta)
    second_row = alpha_next * alpha
    inverse = inv_ref[...]
    copies = []
    for load in range(loads):
        first = first_row[:, load : load + 1]
        second = second_row[:, load : load + 1]
        source, image = b_ref[load], q_ref[load]
        x_ref[load] = (first * source - second * image) * inverse
        copies.append(pltpu.make_async_copy(x_ref.at[load], x_hbm.at[load], sems.at[0, load]))
        copies[-1].start()
        r_ref[load] = source - first * image + second * v_ref[load]
        copies.append(pltpu.make_async_copy(r_ref.at[load], r_hbm.at[load], sems.at[1, load]))
        copies[-1].start()
    for copy in copies:
        copy.wait()


def swap(array, axis, start):
    counts = {name: lax.axis_size(name) for name in ("gx", "gy")}
    other = "gy" if axis == "gx" else "gx"
    pairs = []
    for at in np.ndindex(counts["gx"], counts["gy"]):
        place = dict(zip(("gx", "gy"), at))
        partner = place[axis] + (1 if (place[axis] - start) % 2 == 0 else -1)
        if 0 <= partner < counts[axis]:
            place[axis] = partner
        elif place[other] ^ 1 < counts[other]:
            place[other] ^= 1
        pairs.append((at[0] * counts["gy"] + at[1], place["gx"] * counts["gy"] + place["gy"]))
    return lax.ppermute(array, ("gx", "gy"), pairs)


def per_device(heat_source, density):
    loads, nx, flat = heat_source.shape
    ny = flat // NZ
    s = Sizes(loads, nx, ny, lax.axis_size("gx"), lax.axis_size("gy"))
    nodes = nx * ny * loads
    devices = lax.axis_size("gx") * lax.axis_size("gy")

    def shape(*dims):
        return jax.ShapeDtypeStruct(dims, jnp.float32)

    def scratch(*dims):
        return pltpu.VMEM(dims, jnp.float32)

    def call(kernel, out_shape, **more):
        params = pltpu.CompilerParams(vmem_limit_bytes=20 * 1024 * 1024)
        return pl.pallas_call(
            functools.partial(kernel, s), out_shape=out_shape, compiler_params=params, **more
        )

    hbm = pl.BlockSpec(memory_space=pltpu.HBM)
    y_face, x_face, corner = (shape(rows, LANES) for rows in (s.y_rows, s.x_rows, s.c_rows))
    b, dt, x1, x2 = call(
        pack_x_kernel,
        (shape(packed_count(ny), loads * nx, LANES), shape(nx * ny, LANES), x_face, x_face),
        in_specs=[hbm, hbm],
        scratch_shapes=[scratch(nx, flat), pltpu.SemaphoreType.DMA((packed_count(ny) + 1,))],
    )(
        pltpu.with_memory_space_constraint(heat_source.reshape(loads * nx, flat), pltpu.HBM),
        pltpu.with_memory_space_constraint(density, pltpu.HBM),
    )
    x2, x1 = swap(x2, "gx", 1), swap(x1, "gx", 0)
    bt, y1, y2 = call(pack_y_kernel, (shape(nodes, LANES), y_face, y_face))(b, dt)
    y2, y1 = swap(y2, "gy", 1), swap(y1, "gy", 0)
    t1 = call(open_y_kernel, shape(2 * nx * loads, LANES))(y1)
    xt = shape(2 * ny * loads, LANES)
    xt2 = call(open_x_kernel, xt)(x2)
    xt2, dt_later = lax.optimization_barrier((xt2, dt))
    zt = call(
        scale_kernel, shape(nodes, LANES), scratch_shapes=[scratch(nx * ny, LANES)]
    )(bt, dt_later)
    xt1, c1, c2 = call(
        corner_kernel,
        (xt, corner, corner),
        cost_estimate=pl.CostEstimate(flops=2 * 10**9, transcendentals=0, bytes_accessed=0),
    )(x2, xt2, x1)
    xt1, dt = lax.optimization_barrier((xt1, dt))
    c2, c1 = swap(c2, "gy", 1), swap(c1, "gy", 0)
    plane = s.my * loads
    rows, field = shape(s.mx * s.pitch, LANES), shape(s.mx * plane, LANES)
    edge = shape(2 * plane, LANES)
    inside = shape(nodes, LANES)
    dens, cond, inv_1, bx, zx, q_x, w_x, q_1, v_1, carry1, carry2, sums = call(
        inner_kernel,
        (shape(nx * s.pitch, LANES),)
        + (rows,) * 2
        + (field,) * 4
        + (inside,) * 2
        + (edge,) * 2
        + (shape(4 * loads, LANES),),
    )(bt, zt, dt, y1, y2, t1)
    ends = shape(len(outer_planes(nx)) * ny * loads, LANES)
    q_2, v_2, inv_2, sums = call(
        outer_kernel,
        (ends, ends, shape(ny, LANES), shape(devices, 1, LANES)),
        scratch_shapes=[scratch(2 * plane, LANES)] * 2
        + [scratch(3 * s.pitch, LANES)] * 2
        + [scratch(5 * s.pitch, LANES)] * 2
        + [scratch(5 * plane, LANES)] * 4
        + [scratch(2 * plane, LANES)],
    )(bt, zt, dens, x1, x2, xt1, xt2, c1, c2, cond, inv_1, bx, zx, q_x, w_x, carry1, carry2, sums)
    parts = lax.all_to_all(sums, ("gx", "gy"), 0, 0, tiled=True)
    whole = shape(loads, nx, flat)
    image, again, inverse = call(
        unpack_kernel,
        (whole, whole, shape(nx, flat)),
        scratch_shapes=[scratch(nodes, LANES)] * 2,
    )(q_1, q_2, v_1, v_2, inv_1, inv_2)
    return call(
        finish_kernel,
        (whole, whole),
        out_specs=(hbm, hbm),
        scratch_shapes=[
            scratch(loads, nx, flat),
            scratch(loads, nx, flat),
            pltpu.SemaphoreType.DMA((2, loads)),
        ],
    )(parts, heat_source, image, again, inverse)


def solution(mesh):
    placed = (P(None, "gx", "gy"), P("gx", "gy"))
    return jax.shard_map(
        per_device,
        mesh=mesh,
        in_specs=placed,
        out_specs=(P(None, "gx", "gy"), P(None, "gx", "gy")),
        check_vma=False,
    )
```

```python
import functools

import jax
import jax.numpy as jnp
import numpy as np
from jax import lax
from jax.experimental import pallas as pl
from jax.experimental.pallas import tpu as pltpu
from jax.sharding import PartitionSpec as P

NZ = 96
KMIN = 0.001
LANES = 128
SUB = 8


class Batch:
    def __init__(self, size=12):
        self.size, self.held = size, []

    def add(self, into, at, tile):
        self.held.append((into, at, tile))
        if len(self.held) >= self.size:
            self.flush()

    def flush(self):
        for into, at, tile in self.held:
            into[at] = tile
        self.held = []


def packed_count(tiles):
    return -(-tiles * NZ // LANES)


def lane_ids(rows):
    return lax.broadcasted_iota(jnp.int32, (rows, LANES), 1)


def unpack_tile(read, index, rows):
    start = index * NZ
    block, offset = start // LANES, start % LANES
    lane = lane_ids(rows)
    first = read(block)
    if offset:
        first = pltpu.roll(first, LANES - offset, 1)
    if offset + NZ > LANES:
        second = pltpu.roll(read(block + 1), LANES - offset, 1)
        first = jnp.where(lane < LANES - offset, first, second)
    return jnp.where(lane < NZ, first, 0.0)


def pack_block(read_tile, tiles, block, rows):
    lane = lane_ids(rows)
    start = block * LANES
    out, at = None, start
    while at < start + LANES and at // NZ < tiles:
        index, z = at // NZ, at % NZ
        here = at - start
        piece = read_tile(index)
        shift = (here - z) % LANES
        if shift:
            piece = pltpu.roll(piece, shift, 1)
        out = piece if out is None else jnp.where(lane < here, out, piece)
        at += NZ - z
    return out


def pack_tiles(out_ref, at, rows, tiles, read_tile):
    batch = Batch()
    for block in range(packed_count(tiles)):
        place = slice(at + block * rows, at + (block + 1) * rows), slice(None)
        batch.add(out_ref, place, pack_block(read_tile, tiles, block, rows))
    batch.flush()


def unpack_tiles(ref, at, rows, tiles, write):
    batch = Batch()
    for index in range(tiles):
        tile = unpack_tile(lambda t: ref[at + t * rows : at + (t + 1) * rows, :], index, rows)
        for store in write(index, tile):
            batch.add(*store)
    batch.flush()


class Sizes:
    def __init__(self, loads, nx, ny, count_x, count_y):
        self.loads, self.nx, self.ny = loads, nx, ny
        self.count_x, self.count_y = count_x, count_y
        self.mx, self.my = nx + 4, ny + 4
        self.pitch = -(-(ny + 6) // SUB) * SUB
        self.y_dens = packed_count(2 * nx) * loads
        self.y_rows = self.y_dens + 3 * nx
        self.x_dens = packed_count(2 * ny) * loads
        self.x_rows = self.x_dens + 3 * ny
        self.c_dens = packed_count(4) * loads
        self.c_rows = self.c_dens + -(-9 // SUB) * SUB


class Tiles:
    def __init__(self, ref, columns, loads):
        self.ref, self.columns, self.loads = ref, columns, loads

    def rows(self, at):
        start = (at[0] * self.columns + at[1]) * self.loads
        if not isinstance(start, int):
            start = pl.multiple_of(start, SUB)
        return pl.ds(start, self.loads)

    def __getitem__(self, at):
        return self.ref[self.rows(at), :]

    def __setitem__(self, at, tile):
        self.ref[self.rows(at), :] = tile


class Rows:
    def __init__(self, ref, pitch, loads):
        self.ref, self.pitch, self.loads = ref, pitch, loads

    def __getitem__(self, at):
        row = self.ref[pl.ds(at[0] * self.pitch + at[1], 1), :]
        return jnp.broadcast_to(row, (self.loads, LANES))

    def put(self, x, values):
        self.ref[x * self.pitch : x * self.pitch + values.shape[0], :] = values


class Joined:
    def __init__(self, first, second, own):
        self.first, self.second, self.own = first, second, own

    def __getitem__(self, at):
        if at[0] in self.own:
            return self.first[self.own.index(at[0]), at[1]]
        return self.second[at]

    def __setitem__(self, at, tile):
        self.first[self.own.index(at[0]), at[1]] = tile

    def put(self, x, values):
        self.first.put(self.own.index(x), values)


class Inside:
    def __init__(self, inner, own, outer):
        self.inner, self.own, self.outer = inner, own, outer

    def __getitem__(self, at):
        if at[1] in self.own:
            return self.inner[at[0] - 2, at[1] - 2]
        return self.outer[at]

    def __setitem__(self, at, tile):
        self.outer[at] = tile


def is_even(axis):
    return lax.rem(lax.axis_index(axis), 2) == 0


def is_alone(axis, count, start):
    place = lax.axis_index(axis)
    last = (count - start) % 2
    alone = place < start
    return jnp.logical_or(alone, place == count - 1) if last else alone


def pick(even, if_even, if_odd):
    return jnp.where(even, if_even, if_odd)


def pack_kernel(s, b_hbm, d_hbm, bt_ref, dt_ref, y2_ref, b_ref, d_ref, sems):
    loads, nx, ny = s.loads, s.nx, s.ny
    d_copy = pltpu.make_async_copy(d_hbm, d_ref, sems.at[0])
    d_copy.start()
    parts = 2 if loads % 2 == 0 else 1
    each = loads // parts
    copies = []
    for part in range(parts):
        some = pl.ds(part * each, each)
        copies.append(pltpu.make_async_copy(b_hbm.at[some], b_ref.at[some], sems.at[part + 1]))
        copies[-1].start()
    d_copy.wait()
    batch = Batch(16)
    for x0 in range(0, nx, SUB):
        for y in range(ny):
            tile = unpack_tile(
                lambda t: d_ref[x0 : x0 + SUB, t * LANES : (t + 1) * LANES], y, SUB
            )
            batch.add(dt_ref, (pl.ds(x0 * ny + y, SUB, stride=ny), slice(None)), tile)
    batch.flush()
    for load in range(loads):
        if load % each == 0:
            copies[load // each].wait()
        batch = Batch(16)
        for x0 in range(0, nx, SUB):
            for y in range(ny):
                tile = unpack_tile(
                    lambda t: b_ref[load, x0 : x0 + SUB, t * LANES : (t + 1) * LANES], y, SUB
                )
                rows = pl.ds((x0 * ny + y) * loads + load, SUB, stride=ny * loads)
                batch.add(bt_ref, (rows, slice(None)), tile)
        batch.flush()
    pack_y_face(s, jnp.logical_not(is_even("gy")), bt_ref, dt_ref, y2_ref)


def pack_rest_kernel(s, bt_ref, dt_ref, y1_ref, x1_ref, x2_ref, *corners):
    even_x, even_y = is_even("gx"), is_even("gy")
    upper_x, upper_y = ((even, jnp.logical_not(even)) for even in (even_x, even_y))
    pack_y_face(s, even_y, bt_ref, dt_ref, y1_ref)
    pack_x_face(s, upper_x[1], bt_ref, dt_ref, x2_ref)
    pack_x_face(s, upper_x[0], bt_ref, dt_ref, x1_ref)
    for place, ref in enumerate(corners):
        pack_corner(s, upper_x[place // 2], upper_y[place % 2], bt_ref, dt_ref, ref)


def pack_corner(s, upper_x, upper_y, bt_ref, dt_ref, out_ref):
    loads, nx, ny = s.loads, s.nx, s.ny
    tiles = Tiles(bt_ref, ny, loads)
    x0, y0 = pick(upper_x, nx - 2, 0), pick(upper_y, ny - 2, 0)
    pack_tiles(out_ref, 0, loads, 4, lambda i: tiles[x0 + i // 2, y0 + i % 2])
    x0, y0 = pick(upper_x, nx - 3, 0), pick(upper_y, ny - 3, 0)
    batch = Batch()
    for i in range(9):
        row = dt_ref[pl.ds((x0 + i // 3) * ny + y0 + i % 3, 1), :]
        batch.add(out_ref, (slice(s.c_dens + i, s.c_dens + i + 1), slice(None)), row)
    batch.flush()
    out_ref[s.c_dens + 9 :, :] = jnp.zeros((s.c_rows - s.c_dens - 9, LANES), jnp.float32)


def pack_x_face(s, upper, bt_ref, dt_ref, out_ref):
    loads, nx, ny = s.loads, s.nx, s.ny
    tiles = Tiles(bt_ref, ny, loads)
    x0 = pick(upper, nx - 2, 0)
    pack_tiles(out_ref, 0, loads, 2 * ny, lambda i: tiles[x0 + i // ny, i % ny])
    rows = pl.ds(pl.multiple_of(pick(upper, nx - 3, 0) * ny, SUB), 3 * ny)
    out_ref[s.x_dens :, :] = dt_ref[rows, :]


def pack_y_face(s, upper, bt_ref, dt_ref, out_ref):
    loads, nx, ny = s.loads, s.nx, s.ny
    tiles = Tiles(bt_ref, ny, loads)
    y0 = pick(upper, ny - 2, 0)
    pack_tiles(out_ref, 0, loads, 2 * nx, lambda i: tiles[i // 2, y0 + i % 2])
    y0 = pick(upper, ny - 3, 0)
    batch = Batch()
    for dy in range(3):
        for x0 in range(0, nx, SUB):
            at = s.y_dens + dy * nx + x0
            tile = dt_ref[pl.ds(x0 * ny + y0 + dy, SUB, stride=ny), :]
            batch.add(out_ref, (slice(at, at + SUB), slice(None)), tile)
    batch.flush()


def open_y_kernel(s, y_ref, t_ref):
    tiles = Tiles(t_ref, 2, s.loads)
    unpack_tiles(
        y_ref, 0, s.loads, 2 * s.nx, lambda i, tile: [(tiles, (i // 2, i % 2), tile)]
    )


def open_x_kernel(s, x1_ref, x2_ref, t1_ref, t2_ref):
    for x_ref, t_ref in ((x1_ref, t1_ref), (x2_ref, t2_ref)):
        tiles = Tiles(t_ref, s.ny, s.loads)
        unpack_tiles(
            x_ref, 0, s.loads, 2 * s.ny,
            lambda i, tile: [(tiles, (i // s.ny, i % s.ny), tile)],
        )


def join_density(s, dt_ref, y1_ref, y2_ref, dens_ref):
    nx, ny, pitch = s.nx, s.ny, s.pitch
    even_y = is_even("gy")
    yd = (pick(even_y, ny + 3, 0), pick(even_y, 0, ny + 3))
    batch = Batch(16)
    for x in range(nx):
        at = x * pitch
        batch.add(
            dens_ref, (slice(at + 3, at + 3 + ny), slice(None)), dt_ref[x * ny : (x + 1) * ny, :]
        )
    batch.flush()
    for side, ref in enumerate((y1_ref, y2_ref)):
        alone = is_alone("gy", s.count_y, side)
        for dy in range(3):
            for x0 in range(0, nx, SUB):
                at = s.y_dens + dy * nx + x0
                to = x0 * pitch + yd[side] + dy
                batch.add(
                    dens_ref,
                    (pl.ds(to, SUB, stride=pitch), slice(None)),
                    jnp.where(alone, 0.0, ref[at : at + SUB, :]),
                )
    batch.flush()


def conduct_of(dens):
    return jnp.where(
        dens > 0.0, (KMIN + (1.0 - KMIN) * (dens * dens * dens)) * (1.0 / 12.0), 0.0
    )


def inverse_of(s, before, after):
    pair = before + after
    pair = pair[: s.pitch - 1] + pair[1:]
    total = 4.0 * (pair + pltpu.roll(pair, 1, 1))
    return jnp.where(after[1:] > 0.0, 1.0 / total, 0.0)


def up(tile):
    return pltpu.roll(tile, LANES - 1, 1)


def element_planes(cond, carry, a, count, y0, columns, field, emitter, keep=True):
    def loads_of(step):
        y = y0 + step
        right = [field[a + u, y + 1] for u in range(count + 1)]
        conduct = [cond[a + u, y] for u in range(count)]
        above = extra = None
        if step and emitter:
            above = (carry[0, y], carry[1, y])
            extra = [emitter.fetch(a + u, y) for u in range(count)]
        return right, conduct, above, extra

    left = [(tile, up(tile)) for tile in [field[a + u, y0] for u in range(count + 1)]]
    ahead = loads_of(0)
    old, waiting = [None] * count, []
    for step in range(columns):
        y = y0 + step
        right, conduct, above, extra = ahead
        if step + 1 < columns:
            ahead = loads_of(step + 1)
        if len(waiting) > 1:
            for into, at, tile in waiting.pop(0):
                into[at] = tile
        stores = []
        right = [(tile, up(tile)) for tile in right]
        for u in range(count):
            (p0, p0s), (p1, p1s) = left[u], left[u + 1]
            (r0, r0s), (r1, r1s) = right[u], right[u + 1]
            c = conduct[u]
            even = (p0 + r1) + (r0s + p1s)
            odd = (r0 + p1) + (p0s + r1s)
            pass_on = keep or u + 1 < count
            lower = upper = None
            if emitter:
                lower = (c * (odd + p1s), c * (even + p1))
            if pass_on:
                upper = (c * (even + p0s), c * (odd + p0))
            if step and emitter:
                low = (c * (even + r1s) + old[u][0][0]) + above[0]
                high = (c * (odd + r1) + old[u][0][1]) + above[1]
                total = low + pltpu.roll(high, 1, 1)
                stores += emitter.finish(a + u, y, p0, total, extra[u])
            if step and pass_on:
                above = (
                    c * (odd + r0s) + old[u][1][0],
                    c * (even + r0) + old[u][1][1],
                )
            old[u] = (lower, upper)
        if step and keep:
            stores += [(carry, (0, y), above[0]), (carry, (1, y), above[1])]
        waiting.append(stores)
        left = right
    for stores in waiting:
        for into, at, tile in stores:
            into[at] = tile


class First:
    def __init__(self, bx, invx, qx, wx):
        self.bx, self.invx, self.qx, self.wx = bx, invx, qx, wx

    def fetch(self, x, y):
        return self.bx[x, y], self.invx[x, y]

    def finish(self, x, y, node, total, extra):
        source, inverse = extra
        image = 1.25 * source - total
        return [(self.qx, (x, y), image), (self.wx, (x, y), image * inverse)]


class Second:
    def __init__(self, bx, zx, qx, q_out, v_out, sums):
        self.bx, self.zx, self.qx, self.sums = bx, zx, qx, sums
        self.q_out, self.v_out = q_out, v_out

    def fetch(self, x, y):
        return self.bx[x, y], self.zx[x, y], self.qx[x, y]

    def finish(self, x, y, weighted, total, extra):
        source, scaled, image = extra
        again = 1.25 * image - total
        change = scaled - weighted
        sums = self.sums
        sums[0] = sums[0] + source * scaled
        sums[1] = sums[1] + source * change
        sums[2] = sums[2] + (source - image) * change
        sums[3] = sums[3] + (image - again) * change
        at = x - 2, y - 2
        return [(self.q_out, at, image), (self.v_out, at, again)]


def over_planes(start, stop, body, state):
    pairs = (stop - start) // 2
    state = lax.fori_loop(0, pairs, lambda i, st: body(start + 2 * i, 2, st), state)
    if (stop - start) % 2:
        state = body(stop - 1, 1, state)
    return state


def inside_fields(s, bt_ref, zt_ref, bx, zx):
    brick = (Tiles(ref, s.ny, s.loads) for ref in (bt_ref, zt_ref))
    starts = (2, 3)
    return tuple(
        Inside(inner, range(start, s.ny + 2), outer)
        for inner, start, outer in zip(brick, starts, (bx, zx))
    )


def scale_kernel(s, bt_ref, dt_ref, zt_ref, inv_ref):
    loads, nx, ny = s.loads, s.nx, s.ny
    inner, scaled = Tiles(bt_ref, ny, loads), Tiles(zt_ref, ny, loads)
    inverse = Rows(inv_ref, ny, loads)
    before = conduct_of(dt_ref[0:ny, :])
    for x in range(1, nx):
        after = conduct_of(dt_ref[x * ny : (x + 1) * ny, :])
        pair = before + after
        pair = pair[: ny - 1] + pair[1:]
        total = 4.0 * (pair + pltpu.roll(pair, 1, 1))
        inverse.put(x, jnp.where(after[1:] > 0.0, 1.0 / total, 0.0))
        before = after
    batch = Batch(16)
    for x in range(1, nx):
        for y in range(1, ny):
            batch.add(scaled, (x, y), inner[x, y] * inverse[x, y - 1])
    batch.flush()


def inner_kernel(
    s, bt_ref, zt_ref, dt_ref, y1_ref, y2_ref, t1_ref,
    dens_ref, cond, invx, bx, zx, qx, wx, q_out, v_out, carry1, carry2, sums_ref,
):
    loads, nx, ny, my, pitch = s.loads, s.nx, s.ny, s.my, s.pitch
    bx, zx, qx, wx, carry1, carry2 = (
        Tiles(ref, my, loads) for ref in (bx, zx, qx, wx, carry1, carry2)
    )
    q_out, v_out = Tiles(q_out, ny, loads), Tiles(v_out, ny, loads)
    cond, invx = Rows(cond, pitch, loads), Rows(invx, pitch, loads)
    join_density(s, dt_ref, y1_ref, y2_ref, dens_ref)
    even_y = is_even("gy")
    ys = (pick(even_y, ny + 2, 0), pick(even_y, 0, ny + 2))
    before = None
    for x in range(nx):
        after = conduct_of(dens_ref[x * pitch : (x + 1) * pitch, :])
        cond.put(x + 2, after[1:])
        if x:
            invx.put(x + 2, inverse_of(s, before, after))
        before = after

    bx, zx = inside_fields(s, bt_ref, zt_ref, bx, zx)

    def stage(x, y, tile):
        stores = [(bx, (x + 2, y), tile)]
        if x:
            stores.append((zx, (x + 2, y), tile * invx[x + 2, y]))
        return stores

    batch = Batch(16)
    for x in range(1, nx):
        batch.add(zx, (x + 2, 2), bx[x + 2, 2] * invx[x + 2, 2])
    batch.flush()
    unpack_tiles(
        y2_ref, 0, loads, 2 * nx, lambda i, tile: stage(i // 2, ys[1] + i % 2, tile)
    )
    near = Tiles(t1_ref, 2, loads)
    batch = Batch(16)
    for x in range(nx):
        for dy in range(2):
            for store in stage(x, ys[0] + dy, near[x, dy]):
                batch.add(*store)
    batch.flush()

    element_planes(cond, carry1, 3, 1, 0, my - 1, zx, None)

    def first(a, count, state):
        element_planes(cond, carry1, a, count, 0, my - 1, zx, First(bx, invx, qx, wx))
        return state

    over_planes(4, nx + 1, first, 0)
    element_planes(cond, carry2, 4, 1, 1, my - 3, wx, None)

    def second(a, count, sums):
        sums = list(sums)
        emitter = Second(bx, zx, qx, q_out, v_out, sums)
        element_planes(cond, carry2, a, count, 1, my - 3, wx, emitter)
        return tuple(sums)

    zero = jnp.zeros((loads, LANES), jnp.float32)
    sums = over_planes(5, nx, second, (zero,) * 4)
    for place, part in enumerate(sums):
        sums_ref[place * loads : (place + 1) * loads, :] = part


def outer_kernel(
    s, bt_ref, zt_ref, dens_ref, x1_ref, x2_ref, t1_ref, t2_ref,
    c11_ref, c12_ref, c21_ref, c22_ref,
    cond1, invx1, bx1, zx1, qx1, wx1, carry1, carry2, sums1,
    q_out, v_out, inv_out, sums_ref,
    low_ref, high_ref, low_d, high_d, cond2, invx2, bx2, zx2, qx2, wx2, carry3,
):
    loads, nx, ny, mx, my, pitch = s.loads, s.nx, s.ny, s.mx, s.my, s.pitch
    even_x = is_even("gx")

    even_y = is_even("gy")
    ys = (pick(even_y, ny + 2, 0), pick(even_y, 0, ny + 2))
    yd = (pick(even_y, ny + 3, 0), pick(even_y, 0, ny + 3))

    def take(near, far):
        faces = (x1_ref, t1_ref, near), (x2_ref, t2_ref, far)
        for side, (ref, face_ref, (tiles_ref, into)) in enumerate(faces):
            face, tiles = Tiles(face_ref, ny, loads), Tiles(tiles_ref, my, loads)
            alone_x = is_alone("gx", s.count_x, side)
            batch = Batch(18)
            for dx in range(2):
                for y in range(ny):
                    batch.add(tiles, (dx, y + 2), face[dx, y])
            for t in range(3):
                at = s.x_dens + t * ny
                rows = jnp.where(alone_x, 0.0, ref[at : at + ny, :])
                to = t * pitch + 3
                batch.add(into, (slice(to, to + ny), slice(None)), rows)
            batch.flush()
            corners = ((c11_ref, c12_ref), (c21_ref, c22_ref))[side]
            for end, corner in enumerate(corners):
                alone = jnp.logical_or(alone_x, is_alone("gy", s.count_y, end))
                for i in range(4):
                    tile = unpack_tile(
                        lambda t: corner[t * loads : (t + 1) * loads, :], i, loads
                    )
                    batch.add(tiles, (i // 2, ys[end] + i % 2), tile)
                for i in range(9):
                    at = s.c_dens + i
                    row = jnp.where(alone, 0.0, corner[at : at + 1, :])
                    to = i // 3 * pitch + yd[end] + i % 3
                    batch.add(into, (pl.ds(to, 1), slice(None)), row)
            batch.flush()

    @pl.when(even_x)
    def _():
        take((high_ref, high_d), (low_ref, low_d))

    @pl.when(jnp.logical_not(even_x))
    def _():
        take((low_ref, low_d), (high_ref, high_d))

    def joined(first, second, own):
        return Joined(Tiles(first, my, loads), Tiles(second, my, loads), own)

    def joined_rows(first, second, own):
        return Joined(Rows(first, pitch, loads), Rows(second, pitch, loads), own)

    outside = (0, 1, nx + 2, nx + 3)
    scaled_own = outside + (2,)
    image_own = (1, 2, 3, nx + 1, nx + 2)
    cond, invx = joined_rows(cond2, cond1, outside), joined_rows(invx2, invx1, scaled_own)
    bx1, zx1 = inside_fields(
        s, bt_ref, zt_ref, Tiles(bx1, my, loads), Tiles(zx1, my, loads)
    )
    bx = Joined(Tiles(bx2, my, loads), bx1, outside)
    zx = Joined(Tiles(zx2, my, loads), zx1, scaled_own)
    qx, wx = joined(qx2, qx1, image_own), joined(wx2, wx1, image_own)
    own = [x - 2 for x in outer_planes(nx)]
    q_out, v_out = (Joined(Tiles(ref, ny, loads), None, own) for ref in (q_out, v_out))
    carry1, carry2, carry3 = (Tiles(ref, my, loads) for ref in (carry1, carry2, carry3))

    def conduct(ref, x):
        return conduct_of(ref[x * pitch : (x + 1) * pitch, :])

    low = [conduct(low_d, t) for t in range(3)] + [conduct(dens_ref, 0)]
    high = [conduct(dens_ref, nx - 1)] + [conduct(high_d, t) for t in range(2)]
    for x in range(3):
        inverse = inverse_of(s, low[x], low[x + 1])
        invx.put(x, inverse)
        if x < 2:
            cond.put(x, low[x + 1][1:])
    inv_out[...] = inverse[2 : 2 + ny]
    for x in range(2):
        invx.put(nx + 2 + x, inverse_of(s, high[x], high[x + 1]))
    cond.put(nx + 2, high[1][1:])

    batch = Batch(16)
    for ref, x0 in ((low_ref, 0), (high_ref, nx + 2)):
        tiles = Tiles(ref, my, loads)
        for dx in range(2):
            for y in range(my):
                tile = tiles[dx, y]
                batch.add(bx, (x0 + dx, y), tile)
                batch.add(zx, (x0 + dx, y), tile * invx[x0 + dx, y])
    for y in range(my):
        batch.add(zx, (2, y), bx[2, y] * invx[2, y])
    batch.flush()

    emitter = First(bx, invx, qx, wx)
    element_planes(cond, carry3, 0, 1, 0, my - 1, zx, None)
    element_planes(cond, carry3, 1, 2, 0, my - 1, zx, emitter)
    element_planes(cond, carry3, 3, 1, 0, my - 1, zx, emitter, keep=False)
    element_planes(cond, carry1, nx + 1, 2, 0, my - 1, zx, emitter, keep=False)
    sums = [sums1[place * loads : (place + 1) * loads, :] for place in range(4)]
    emitter = Second(bx, zx, qx, q_out, v_out, sums)
    element_planes(cond, carry3, 1, 1, 1, my - 3, wx, None)
    element_planes(cond, carry3, 2, 2, 1, my - 3, wx, emitter)
    element_planes(cond, carry3, 4, 1, 1, my - 3, wx, emitter, keep=False)
    element_planes(cond, carry2, nx, 2, 1, my - 3, wx, emitter, keep=False)
    lane = lane_ids(loads)
    load = lax.broadcasted_iota(jnp.int32, (loads, LANES), 0)
    packed = jnp.zeros((loads, LANES), jnp.float32)
    for place, part in enumerate(sums):
        total = jnp.sum(part, axis=1, keepdims=True)
        packed = packed + jnp.where(lane == place * loads + load, total, 0.0)
    row = jnp.sum(packed, axis=0, keepdims=True)
    sums_ref[...] = jnp.broadcast_to(row[None], sums_ref.shape)


def outer_planes(nx):
    return (2, 3, 4, nx, nx + 1)


def unpack_kernel(
    s, q1_ref, q2_ref, v1_ref, v2_ref, inv1_ref, inv2_ref, qo_ref, vo_ref, io_ref, q_ref, v_ref
):
    loads, nx, ny = s.loads, s.nx, s.ny
    batch = Batch()
    planes = outer_planes(nx)
    for first, second, whole in ((q1_ref, q2_ref, q_ref), (v1_ref, v2_ref, v_ref)):
        first, second = Tiles(first, ny, loads), Tiles(second, ny, loads)
        whole = Tiles(whole, ny, loads)
        for x in range(nx):
            for y in range(ny):
                if x + 2 in planes:
                    batch.add(whole, (x, y), second[planes.index(x + 2), y])
                else:
                    batch.add(whole, (x, y), first[x, y])
    batch.flush()
    batch = Batch()
    for x0 in range(0, nx, SUB):
        for ref, out in ((q_ref, qo_ref), (v_ref, vo_ref)):
            for load in range(loads):
                for block in range(packed_count(ny)):
                    tile = pack_block(
                        lambda y: ref[
                            pl.ds((x0 * ny + y) * loads + load, SUB, stride=ny * loads), :
                        ],
                        ny, block, SUB,
                    )
                    lanes = slice(block * LANES, (block + 1) * LANES)
                    batch.add(out, (load, slice(x0, x0 + SUB), lanes), tile)
        for block in range(packed_count(ny)):
            tile = pack_block(
                lambda y: inv1_ref[
                    pl.ds((x0 + 2) * s.pitch + y + 2, SUB, stride=s.pitch), :
                ],
                ny, block, SUB,
            )
            lanes = slice(block * LANES, (block + 1) * LANES)
            batch.add(io_ref, (slice(x0, x0 + SUB), lanes), tile)
    batch.flush()
    for block in range(packed_count(ny)):
        io_ref[0:1, block * LANES : (block + 1) * LANES] = pack_block(
            lambda y: inv2_ref[y : y + 1, :], ny, block, 1
        )


def finish_kernel(s, parts_ref, b_ref, q_ref, v_ref, inv_ref, x_hbm, r_hbm, x_ref, r_ref, sems):
    loads = s.loads
    totals = jnp.sum(parts_ref[...], axis=0)

    def part(place):
        return pltpu.roll(totals, (LANES - place * loads) % LANES, 1) if place else totals

    rz, near, square, last = (part(place) for place in range(4))
    direct = rz - near
    alpha = rz / direct
    short = -near / direct
    rz_next = short * short * rz + 2.0 * alpha * short * near + alpha * alpha * square
    beta = rz_next / rz
    grown = short + beta
    curved = (
        grown * grown * direct
        + 2.0 * alpha * grown * (near - square)
        + alpha * alpha * last
    )
    alpha_next = rz_next / curved
    first_row = alpha + alpha_next * (1.0 + beta)
    second_row = alpha_next * alpha
    inverse = inv_ref[...]
    copies = []
    for load in range(loads):
        first = first_row[:, load : load + 1]
        second = second_row[:, load : load + 1]
        source, image = b_ref[load], q_ref[load]
        x_ref[load] = (first * source - second * image) * inverse
        copies.append(pltpu.make_async_copy(x_ref.at[load], x_hbm.at[load], sems.at[0, load]))
        copies[-1].start()
        r_ref[load] = source - first * image + second * v_ref[load]
        copies.append(pltpu.make_async_copy(r_ref.at[load], r_hbm.at[load], sems.at[1, load]))
        copies[-1].start()
    for copy in copies:
        copy.wait()


def swap(array, start_x=None, start_y=None):
    count_x, count_y = lax.axis_size("gx"), lax.axis_size("gy")

    def partner(place, start, count):
        if start is None:
            return place
        to = place + (1 if (place - start) % 2 == 0 else -1)
        return to if 0 <= to < count else None

    pairs = []
    for x, y in np.ndindex(count_x, count_y):
        to_x, to_y = partner(x, start_x, count_x), partner(y, start_y, count_y)
        if to_x is None and to_y is None:
            to_x, to_y = x, y
            if partner(count_x - 1 - x, start_x, count_x) is None:
                to_x = count_x - 1 - x
        elif to_x is None:
            to_x = x
            if start_y is None and y ^ 1 < count_y:
                to_y = y ^ 1
        elif to_y is None:
            to_y = y
            if start_x is None and x ^ 1 < count_x:
                to_x = x ^ 1
        pairs.append((x * count_y + y, to_x * count_y + to_y))
    return lax.ppermute(array, ("gx", "gy"), pairs)


def per_device(heat_source, density):
    loads, nx, flat = heat_source.shape
    ny = flat // NZ
    s = Sizes(loads, nx, ny, lax.axis_size("gx"), lax.axis_size("gy"))
    nodes = nx * ny * loads
    devices = lax.axis_size("gx") * lax.axis_size("gy")

    def shape(*dims):
        return jax.ShapeDtypeStruct(dims, jnp.float32)

    def scratch(*dims):
        return pltpu.VMEM(dims, jnp.float32)

    def call(kernel, out_shape, **more):
        params = pltpu.CompilerParams(vmem_limit_bytes=20 * 1024 * 1024)
        return pl.pallas_call(
            functools.partial(kernel, s), out_shape=out_shape, compiler_params=params, **more
        )

    hbm = pl.BlockSpec(memory_space=pltpu.HBM)
    y_face, x_face, corner = (shape(rows, LANES) for rows in (s.y_rows, s.x_rows, s.c_rows))
    bt, dt, y2 = call(
        pack_kernel,
        (shape(nodes, LANES), shape(nx * ny, LANES), y_face),
        in_specs=[hbm, hbm],
        scratch_shapes=[
            scratch(loads, nx, flat),
            scratch(nx, flat),
            pltpu.SemaphoreType.DMA((3,)),
        ],
    )(
        pltpu.with_memory_space_constraint(heat_source, pltpu.HBM),
        pltpu.with_memory_space_constraint(density, pltpu.HBM),
    )
    y2 = swap(y2, start_y=1)
    y1, x1, x2, *corners = call(pack_rest_kernel, (y_face, x_face, x_face) + (corner,) * 4)(bt, dt)
    y1, x2, x1 = swap(y1, start_y=0), swap(x2, start_x=1), swap(x1, start_x=0)
    corners = [swap(part, place // 2, place % 2) for place, part in enumerate(corners)]
    t1 = call(open_y_kernel, shape(2 * nx * loads, LANES))(y1)
    zt = call(
        scale_kernel, shape(nodes, LANES), scratch_shapes=[scratch(nx * ny, LANES)]
    )(bt, dt)
    xt = shape(2 * ny * loads, LANES)
    xt1, xt2 = call(open_x_kernel, (xt, xt))(x1, x2)
    plane = s.my * loads
    rows, field = shape(s.mx * s.pitch, LANES), shape(s.mx * plane, LANES)
    edge = shape(2 * plane, LANES)
    inside = shape(nodes, LANES)
    dens, cond, inv_1, bx, zx, q_x, w_x, q_1, v_1, carry1, carry2, sums = call(
        inner_kernel,
        (shape(nx * s.pitch, LANES),)
        + (rows,) * 2
        + (field,) * 4
        + (inside,) * 2
        + (edge,) * 2
        + (shape(4 * loads, LANES),),
    )(bt, zt, dt, y1, y2, t1)
    ends = shape(len(outer_planes(nx)) * ny * loads, LANES)
    q_2, v_2, inv_2, sums = call(
        outer_kernel,
        (ends, ends, shape(ny, LANES), shape(devices, 1, LANES)),
        scratch_shapes=[scratch(2 * plane, LANES)] * 2
        + [scratch(3 * s.pitch, LANES)] * 2
        + [scratch(5 * s.pitch, LANES)] * 2
        + [scratch(5 * plane, LANES)] * 4
        + [scratch(2 * plane, LANES)],
    )(bt, zt, dens, x1, x2, xt1, xt2, *corners, cond, inv_1, bx, zx, q_x, w_x, carry1, carry2, sums)
    parts = lax.all_to_all(sums, ("gx", "gy"), 0, 0, tiled=True)
    whole = shape(loads, nx, flat)
    image, again, inverse = call(
        unpack_kernel,
        (whole, whole, shape(nx, flat)),
        scratch_shapes=[scratch(nodes, LANES)] * 2,
    )(q_1, q_2, v_1, v_2, inv_1, inv_2)
    return call(
        finish_kernel,
        (whole, whole),
        out_specs=(hbm, hbm),
        scratch_shapes=[
            scratch(loads, nx, flat),
            scratch(loads, nx, flat),
            pltpu.SemaphoreType.DMA((2, loads)),
        ],
    )(parts, heat_source, image, again, inverse)


def solution(mesh):
    placed = (P(None, "gx", "gy"), P("gx", "gy"))
    return jax.shard_map(
        per_device,
        mesh=mesh,
        in_specs=placed,
        out_specs=(P(None, "gx", "gy"), P(None, "gx", "gy")),
        check_vma=False,
    )
```

```python
import functools

import jax
import jax.numpy as jnp
import numpy as np
from jax import lax
from jax.experimental import pallas as pl
from jax.experimental.pallas import tpu as pltpu
from jax.sharding import PartitionSpec as P

NZ = 96
KMIN = 0.001
LANES = 128
SUB = 8


class Batch:
    def __init__(self, size=12):
        self.size, self.held = size, []

    def add(self, into, at, tile):
        self.held.append((into, at, tile))
        if len(self.held) >= self.size:
            self.flush()

    def flush(self):
        for into, at, tile in self.held:
            into[at] = tile
        self.held = []


def packed_count(tiles):
    return -(-tiles * NZ // LANES)


def lane_ids(rows):
    return lax.broadcasted_iota(jnp.int32, (rows, LANES), 1)


def unpack_tile(read, index, rows):
    start = index * NZ
    block, offset = start // LANES, start % LANES
    lane = lane_ids(rows)
    first = read(block)
    if offset:
        first = pltpu.roll(first, LANES - offset, 1)
    if offset + NZ > LANES:
        second = pltpu.roll(read(block + 1), LANES - offset, 1)
        first = jnp.where(lane < LANES - offset, first, second)
    return jnp.where(lane < NZ, first, 0.0)


def pack_block(read_tile, tiles, block, rows):
    lane = lane_ids(rows)
    start = block * LANES
    out, at = None, start
    while at < start + LANES and at // NZ < tiles:
        index, z = at // NZ, at % NZ
        here = at - start
        piece = read_tile(index)
        shift = (here - z) % LANES
        if shift:
            piece = pltpu.roll(piece, shift, 1)
        out = piece if out is None else jnp.where(lane < here, out, piece)
        at += NZ - z
    return out


def pack_tiles(out_ref, at, rows, tiles, read_tile):
    batch = Batch()
    for block in range(packed_count(tiles)):
        place = slice(at + block * rows, at + (block + 1) * rows), slice(None)
        batch.add(out_ref, place, pack_block(read_tile, tiles, block, rows))
    batch.flush()


def unpack_tiles(ref, at, rows, tiles, write):
    batch = Batch()
    for index in range(tiles):
        tile = unpack_tile(lambda t: ref[at + t * rows : at + (t + 1) * rows, :], index, rows)
        for store in write(index, tile):
            batch.add(*store)
    batch.flush()


class Sizes:
    def __init__(self, loads, nx, ny, count_x, count_y):
        self.loads, self.nx, self.ny = loads, nx, ny
        self.count_x, self.count_y = count_x, count_y
        self.mx, self.my = nx + 4, ny + 4
        self.pitch = -(-(ny + 6) // SUB) * SUB
        self.y_dens = packed_count(2 * nx) * loads
        self.y_rows = self.y_dens + 3 * nx
        self.x_dens = packed_count(2 * ny) * loads
        self.x_rows = self.x_dens + 3 * ny
        self.c_dens = packed_count(8) * loads
        self.c_rows = self.c_dens + -(-18 // SUB) * SUB


class Tiles:
    def __init__(self, ref, columns, loads):
        self.ref, self.columns, self.loads = ref, columns, loads

    def rows(self, at):
        start = (at[0] * self.columns + at[1]) * self.loads
        if not isinstance(start, int):
            start = pl.multiple_of(start, SUB)
        return pl.ds(start, self.loads)

    def __getitem__(self, at):
        return self.ref[self.rows(at), :]

    def __setitem__(self, at, tile):
        self.ref[self.rows(at), :] = tile


class Rows:
    def __init__(self, ref, pitch, loads):
        self.ref, self.pitch, self.loads = ref, pitch, loads

    def __getitem__(self, at):
        row = self.ref[pl.ds(at[0] * self.pitch + at[1], 1), :]
        return jnp.broadcast_to(row, (self.loads, LANES))

    def put(self, x, values):
        self.ref[x * self.pitch : x * self.pitch + values.shape[0], :] = values


class Joined:
    def __init__(self, first, second, own):
        self.first, self.second, self.own = first, second, own

    def __getitem__(self, at):
        if at[0] in self.own:
            return self.first[self.own.index(at[0]), at[1]]
        return self.second[at]

    def __setitem__(self, at, tile):
        self.first[self.own.index(at[0]), at[1]] = tile

    def put(self, x, values):
        self.first.put(self.own.index(x), values)


class Inside:
    def __init__(self, inner, own, outer):
        self.inner, self.own, self.outer = inner, own, outer

    def __getitem__(self, at):
        if at[1] in self.own:
            return self.inner[at[0] - 2, at[1] - 2]
        return self.outer[at]

    def __setitem__(self, at, tile):
        self.outer[at] = tile


def is_even(axis):
    return lax.rem(lax.axis_index(axis), 2) == 0


def is_alone(axis, count, start):
    place = lax.axis_index(axis)
    last = (count - start) % 2
    alone = place < start
    return jnp.logical_or(alone, place == count - 1) if last else alone


def pick(even, if_even, if_odd):
    return jnp.where(even, if_even, if_odd)


def pack_x_kernel(s, b_hbm, d_hbm, b_ref, dt_ref, x1_ref, x2_ref, d_ref, sems):
    loads, nx, ny = s.loads, s.nx, s.ny
    blocks = packed_count(ny)
    d_copy = pltpu.make_async_copy(d_hbm, d_ref, sems.at[blocks])
    d_copy.start()
    copies = []
    for block in range(blocks):
        lanes = pl.ds(block * LANES, LANES)
        copies.append(
            pltpu.make_async_copy(b_hbm.at[:, lanes], b_ref.at[block], sems.at[block])
        )
        copies[-1].start()
    d_copy.wait()
    batch = Batch(16)
    for x0 in range(0, nx, SUB):
        for y in range(ny):
            tile = unpack_tile(
                lambda t: d_ref[x0 : x0 + SUB, t * LANES : (t + 1) * LANES], y, SUB
            )
            batch.add(dt_ref, (pl.ds(x0 * ny + y, SUB, stride=ny), slice(None)), tile)
    batch.flush()
    even_x = is_even("gx")
    for ref, upper in ((x2_ref, jnp.logical_not(even_x)), (x1_ref, even_x)):
        rows = pl.ds(pl.multiple_of(pick(upper, nx - 3, 0) * ny, SUB), 3 * ny)
        ref[s.x_dens :, :] = dt_ref[rows, :]
    for copy in copies:
        copy.wait()
    batch = Batch()
    for ref, upper in ((x2_ref, jnp.logical_not(even_x)), (x1_ref, even_x)):
        x0 = pick(upper, nx - 2, 0)
        for dx in range(2):
            for block in range(blocks):
                tile = b_ref[block, pl.ds(x0 + dx, loads, stride=nx), :]
                at = (dx * blocks + block) * loads
                batch.add(ref, (slice(at, at + loads), slice(None)), tile)
    batch.flush()


def pack_y_kernel(s, b_ref, dt_ref, bt_ref, y1_ref, y2_ref):
    loads, nx, ny = s.loads, s.nx, s.ny
    batch = Batch(16)
    for load in range(loads):
        for x0 in range(0, nx, SUB):
            at = load * nx + x0
            for y in range(ny):
                tile = unpack_tile(
                    lambda t: b_ref[t, at : at + SUB, :], y, SUB
                )
                rows = pl.ds((x0 * ny + y) * loads + load, SUB, stride=ny * loads)
                batch.add(bt_ref, (rows, slice(None)), tile)
    batch.flush()
    even_y = is_even("gy")
    pack_y_face(s, jnp.logical_not(even_y), bt_ref, dt_ref, y2_ref)
    pack_y_face(s, even_y, bt_ref, dt_ref, y1_ref)


def pack_y_face(s, upper, bt_ref, dt_ref, out_ref):
    loads, nx, ny = s.loads, s.nx, s.ny
    tiles = Tiles(bt_ref, ny, loads)
    y0 = pick(upper, ny - 2, 0)
    pack_tiles(out_ref, 0, loads, 2 * nx, lambda i: tiles[i // 2, y0 + i % 2])
    y0 = pick(upper, ny - 3, 0)
    batch = Batch()
    for dy in range(3):
        for x0 in range(0, nx, SUB):
            at = s.y_dens + dy * nx + x0
            tile = dt_ref[pl.ds(x0 * ny + y0 + dy, SUB, stride=ny), :]
            batch.add(out_ref, (slice(at, at + SUB), slice(None)), tile)
    batch.flush()


def open_y_kernel(s, y_ref, t_ref):
    tiles = Tiles(t_ref, 2, s.loads)
    unpack_tiles(
        y_ref, 0, s.loads, 2 * s.nx, lambda i, tile: [(tiles, (i // 2, i % 2), tile)]
    )


def open_x_kernel(s, x_ref, t_ref):
    tiles = Tiles(t_ref, s.ny, s.loads)
    unpack_tiles(
        x_ref, 0, s.loads, 2 * s.ny, lambda i, tile: [(tiles, (i // s.ny, i % s.ny), tile)]
    )


def corner_kernel(s, x2_ref, t2_ref, x1_ref, t1_ref, c1_ref, c2_ref):
    loads, ny = s.loads, s.ny
    open_x_kernel(s, x1_ref, t1_ref)
    halves = Tiles(t1_ref, ny, loads), Tiles(t2_ref, ny, loads)
    even_y = is_even("gy")
    for out_ref, upper in ((c2_ref, jnp.logical_not(even_y)), (c1_ref, even_y)):
        y0 = pick(upper, ny - 2, 0)
        pack_tiles(out_ref, 0, loads, 8, lambda i: halves[i // 4][i // 2 % 2, y0 + i % 2])
        y0 = pick(upper, ny - 3, 0)
        batch, at = Batch(18), s.c_dens
        for ref in (x1_ref, x2_ref):
            for t in range(3):
                for dy in range(3):
                    row = ref[pl.ds(s.x_dens + t * ny + y0 + dy, 1), :]
                    batch.add(out_ref, (slice(at, at + 1), slice(None)), row)
                    at += 1
        batch.flush()
        out_ref[at:, :] = jnp.zeros((s.c_rows - at, LANES), jnp.float32)


def join_density(s, dt_ref, y1_ref, y2_ref, dens_ref):
    nx, ny, pitch = s.nx, s.ny, s.pitch
    even_y = is_even("gy")
    yd = (pick(even_y, ny + 3, 0), pick(even_y, 0, ny + 3))
    batch = Batch(16)
    for x in range(nx):
        at = x * pitch
        batch.add(
            dens_ref, (slice(at + 3, at + 3 + ny), slice(None)), dt_ref[x * ny : (x + 1) * ny, :]
        )
    batch.flush()
    for side, ref in enumerate((y1_ref, y2_ref)):
        alone = is_alone("gy", s.count_y, side)
        for dy in range(3):
            for x0 in range(0, nx, SUB):
                at = s.y_dens + dy * nx + x0
                to = x0 * pitch + yd[side] + dy
                batch.add(
                    dens_ref,
                    (pl.ds(to, SUB, stride=pitch), slice(None)),
                    jnp.where(alone, 0.0, ref[at : at + SUB, :]),
                )
    batch.flush()


def conduct_of(dens):
    return jnp.where(
        dens > 0.0, (KMIN + (1.0 - KMIN) * (dens * dens * dens)) * (1.0 / 12.0), 0.0
    )


def inverse_of(s, before, after):
    pair = before + after
    pair = pair[: s.pitch - 1] + pair[1:]
    total = 4.0 * (pair + pltpu.roll(pair, 1, 1))
    return jnp.where(after[1:] > 0.0, 1.0 / total, 0.0)


def up(tile):
    return pltpu.roll(tile, LANES - 1, 1)


def element_planes(cond, carry, a, count, y0, columns, field, field_up, emitter, keep=True):
    def loads_of(step):
        y = y0 + step
        right = [(field[a + u, y + 1], field_up[a + u, y + 1]) for u in range(count + 1)]
        conduct = [cond[a + u, y] for u in range(count)]
        above = extra = None
        if step and emitter:
            above = (carry[0, y], carry[1, y])
            extra = [emitter.fetch(a + u, y) for u in range(count)]
        return right, conduct, above, extra

    left = [(field[a + u, y0], field_up[a + u, y0]) for u in range(count + 1)]
    ahead = loads_of(0)
    old, waiting = [None] * count, []
    for step in range(columns):
        y = y0 + step
        right, conduct, above, extra = ahead
        if step + 1 < columns:
            ahead = loads_of(step + 1)
        if len(waiting) > 1:
            for into, at, tile in waiting.pop(0):
                into[at] = tile
        stores = []
        for u in range(count):
            (p0, p0s), (p1, p1s) = left[u], left[u + 1]
            (r0, r0s), (r1, r1s) = right[u], right[u + 1]
            c = conduct[u]
            even = (p0 + r1) + (r0s + p1s)
            odd = (r0 + p1) + (p0s + r1s)
            pass_on = keep or u + 1 < count
            lower = upper = None
            if emitter:
                lower = (c * (odd + p1s), c * (even + p1))
            if pass_on:
                upper = (c * (even + p0s), c * (odd + p0))
            if step and emitter:
                low = (c * (even + r1s) + old[u][0][0]) + above[0]
                high = (c * (odd + r1) + old[u][0][1]) + above[1]
                total = low + pltpu.roll(high, 1, 1)
                stores += emitter.finish(a + u, y, p0, total, extra[u])
            if step and pass_on:
                above = (
                    c * (odd + r0s) + old[u][1][0],
                    c * (even + r0) + old[u][1][1],
                )
            old[u] = (lower, upper)
        if step and keep:
            stores += [(carry, (0, y), above[0]), (carry, (1, y), above[1])]
        waiting.append(stores)
        left = right
    for stores in waiting:
        for into, at, tile in stores:
            into[at] = tile


class First:
    def __init__(self, bx, invx, qx, wx, wu):
        self.bx, self.invx, self.qx, self.wx, self.wu = bx, invx, qx, wx, wu

    def fetch(self, x, y):
        return self.bx[x, y], self.invx[x, y]

    def finish(self, x, y, node, total, extra):
        source, inverse = extra
        image = 1.25 * source - total
        weighted = image * inverse
        at = x, y
        return [(self.qx, at, image), (self.wx, at, weighted), (self.wu, at, up(weighted))]


class Second:
    def __init__(self, bx, zx, qx, q_out, v_out, sums):
        self.bx, self.zx, self.qx, self.sums = bx, zx, qx, sums
        self.q_out, self.v_out = q_out, v_out

    def fetch(self, x, y):
        return self.bx[x, y], self.zx[x, y], self.qx[x, y]

    def finish(self, x, y, weighted, total, extra):
        source, scaled, image = extra
        again = 1.25 * image - total
        change = scaled - weighted
        sums = self.sums
        sums[0] = sums[0] + source * scaled
        sums[1] = sums[1] + source * change
        sums[2] = sums[2] + (source - image) * change
        sums[3] = sums[3] + (image - again) * change
        at = x - 2, y - 2
        return [(self.q_out, at, image), (self.v_out, at, again)]


def over_planes(start, stop, body, state):
    pairs = (stop - start) // 2
    state = lax.fori_loop(0, pairs, lambda i, st: body(start + 2 * i, 2, st), state)
    if (stop - start) % 2:
        state = body(stop - 1, 1, state)
    return state


def inside_fields(s, bt_ref, zt_ref, ut_ref, bx, zx, zu):
    brick = (Tiles(ref, s.ny, s.loads) for ref in (bt_ref, zt_ref, ut_ref))
    starts = (2, 3, 3)
    return tuple(
        Inside(inner, range(start, s.ny + 2), outer)
        for inner, start, outer in zip(brick, starts, (bx, zx, zu))
    )


def scale_kernel(s, bt_ref, dt_ref, zt_ref, ut_ref, inv_ref):
    loads, nx, ny = s.loads, s.nx, s.ny
    inner, scaled, shifted = (Tiles(ref, ny, loads) for ref in (bt_ref, zt_ref, ut_ref))
    inverse = Rows(inv_ref, ny, loads)
    before = conduct_of(dt_ref[0:ny, :])
    for x in range(1, nx):
        after = conduct_of(dt_ref[x * ny : (x + 1) * ny, :])
        pair = before + after
        pair = pair[: ny - 1] + pair[1:]
        total = 4.0 * (pair + pltpu.roll(pair, 1, 1))
        inverse.put(x, jnp.where(after[1:] > 0.0, 1.0 / total, 0.0))
        before = after
    batch = Batch(16)
    for x in range(1, nx):
        for y in range(1, ny):
            tile = inner[x, y] * inverse[x, y - 1]
            batch.add(scaled, (x, y), tile)
            batch.add(shifted, (x, y), up(tile))
    batch.flush()


def inner_kernel(
    s, bt_ref, zt_ref, ut_ref, dt_ref, y1_ref, y2_ref, t1_ref,
    dens_ref, cond, invx, bx, zx, zu, qx, wx, wu, q_out, v_out, carry1, carry2, sums_ref,
):
    loads, nx, ny, my, pitch = s.loads, s.nx, s.ny, s.my, s.pitch
    bx, zx, zu, qx, wx, wu, carry1, carry2 = (
        Tiles(ref, my, loads) for ref in (bx, zx, zu, qx, wx, wu, carry1, carry2)
    )
    q_out, v_out = Tiles(q_out, ny, loads), Tiles(v_out, ny, loads)
    cond, invx = Rows(cond, pitch, loads), Rows(invx, pitch, loads)
    join_density(s, dt_ref, y1_ref, y2_ref, dens_ref)
    even_y = is_even("gy")
    ys = (pick(even_y, ny + 2, 0), pick(even_y, 0, ny + 2))
    before = None
    for x in range(nx):
        after = conduct_of(dens_ref[x * pitch : (x + 1) * pitch, :])
        cond.put(x + 2, after[1:])
        if x:
            invx.put(x + 2, inverse_of(s, before, after))
        before = after

    bx, zx, zu = inside_fields(s, bt_ref, zt_ref, ut_ref, bx, zx, zu)

    def stage(x, y, tile):
        stores = [(bx, (x + 2, y), tile)]
        if x:
            scaled = tile * invx[x + 2, y]
            stores += [(zx, (x + 2, y), scaled), (zu, (x + 2, y), up(scaled))]
        return stores

    batch = Batch(16)
    for x in range(1, nx):
        scaled = bx[x + 2, 2] * invx[x + 2, 2]
        batch.add(zx, (x + 2, 2), scaled)
        batch.add(zu, (x + 2, 2), up(scaled))
    batch.flush()
    unpack_tiles(
        y2_ref, 0, loads, 2 * nx, lambda i, tile: stage(i // 2, ys[1] + i % 2, tile)
    )
    near = Tiles(t1_ref, 2, loads)
    batch = Batch(16)
    for x in range(nx):
        for dy in range(2):
            for store in stage(x, ys[0] + dy, near[x, dy]):
                batch.add(*store)
    batch.flush()

    element_planes(cond, carry1, 3, 1, 0, my - 1, zx, zu, None)

    def first(a, count, state):
        emitter = First(bx, invx, qx, wx, wu)
        element_planes(cond, carry1, a, count, 0, my - 1, zx, zu, emitter)
        return state

    over_planes(4, nx + 1, first, 0)
    element_planes(cond, carry2, 4, 1, 1, my - 3, wx, wu, None)

    def second(a, count, sums):
        sums = list(sums)
        emitter = Second(bx, zx, qx, q_out, v_out, sums)
        element_planes(cond, carry2, a, count, 1, my - 3, wx, wu, emitter)
        return tuple(sums)

    zero = jnp.zeros((loads, LANES), jnp.float32)
    sums = over_planes(5, nx, second, (zero,) * 4)
    for place, part in enumerate(sums):
        sums_ref[place * loads : (place + 1) * loads, :] = part


def outer_kernel(
    s, bt_ref, zt_ref, ut_ref, dens_ref, x1_ref, x2_ref, t1_ref, t2_ref, c1_ref, c2_ref,
    cond1, invx1, bx1, zx1, zu1, qx1, wx1, wu1, carry1, carry2, sums1,
    q_out, v_out, inv_out, sums_ref,
    low_ref, high_ref, low_d, high_d, cond2, invx2, bx2, zx2, zu2, qx2, wx2, wu2, carry3,
):
    loads, nx, ny, mx, my, pitch = s.loads, s.nx, s.ny, s.mx, s.my, s.pitch
    even_x = is_even("gx")

    even_y = is_even("gy")
    ys = (pick(even_y, ny + 2, 0), pick(even_y, 0, ny + 2))
    yd = (pick(even_y, ny + 3, 0), pick(even_y, 0, ny + 3))

    def take(near, far):
        faces = (x1_ref, t1_ref, near), (x2_ref, t2_ref, far)
        for side, (ref, face_ref, (tiles_ref, into)) in enumerate(faces):
            face, tiles = Tiles(face_ref, ny, loads), Tiles(tiles_ref, my, loads)
            alone_x = is_alone("gx", s.count_x, side)
            batch = Batch(18)
            for dx in range(2):
                for y in range(ny):
                    batch.add(tiles, (dx, y + 2), face[dx, y])
            for t in range(3):
                at = s.x_dens + t * ny
                rows = jnp.where(alone_x, 0.0, ref[at : at + ny, :])
                to = t * pitch + 3
                batch.add(into, (slice(to, to + ny), slice(None)), rows)
            batch.flush()
            for end, corner in enumerate((c1_ref, c2_ref)):
                alone = jnp.logical_or(alone_x, is_alone("gy", s.count_y, end))
                for i in range(4):
                    tile = unpack_tile(
                        lambda t: corner[t * loads : (t + 1) * loads, :], 4 * side + i, loads
                    )
                    batch.add(tiles, (i // 2, ys[end] + i % 2), tile)
                for i in range(9):
                    at = s.c_dens + 9 * side + i
                    row = jnp.where(alone, 0.0, corner[at : at + 1, :])
                    to = i // 3 * pitch + yd[end] + i % 3
                    batch.add(into, (pl.ds(to, 1), slice(None)), row)
            batch.flush()

    @pl.when(even_x)
    def _():
        take((high_ref, high_d), (low_ref, low_d))

    @pl.when(jnp.logical_not(even_x))
    def _():
        take((low_ref, low_d), (high_ref, high_d))

    def joined(first, second, own):
        return Joined(Tiles(first, my, loads), Tiles(second, my, loads), own)

    def joined_rows(first, second, own):
        return Joined(Rows(first, pitch, loads), Rows(second, pitch, loads), own)

    outside = (0, 1, nx + 2, nx + 3)
    scaled_own = outside + (2,)
    image_own = (1, 2, 3, nx + 1, nx + 2)
    cond, invx = joined_rows(cond2, cond1, outside), joined_rows(invx2, invx1, scaled_own)
    bx1, zx1, zu1 = inside_fields(
        s, bt_ref, zt_ref, ut_ref, *(Tiles(ref, my, loads) for ref in (bx1, zx1, zu1))
    )
    bx = Joined(Tiles(bx2, my, loads), bx1, outside)
    zx = Joined(Tiles(zx2, my, loads), zx1, scaled_own)
    zu = Joined(Tiles(zu2, my, loads), zu1, scaled_own)
    qx, wx = joined(qx2, qx1, image_own), joined(wx2, wx1, image_own)
    wu = joined(wu2, wu1, image_own)
    own = [x - 2 for x in outer_planes(nx)]
    q_out, v_out = (Joined(Tiles(ref, ny, loads), None, own) for ref in (q_out, v_out))
    carry1, carry2, carry3 = (Tiles(ref, my, loads) for ref in (carry1, carry2, carry3))

    def conduct(ref, x):
        return conduct_of(ref[x * pitch : (x + 1) * pitch, :])

    low = [conduct(low_d, t) for t in range(3)] + [conduct(dens_ref, 0)]
    high = [conduct(dens_ref, nx - 1)] + [conduct(high_d, t) for t in range(2)]
    for x in range(3):
        inverse = inverse_of(s, low[x], low[x + 1])
        invx.put(x, inverse)
        if x < 2:
            cond.put(x, low[x + 1][1:])
    inv_out[...] = inverse[2 : 2 + ny]
    for x in range(2):
        invx.put(nx + 2 + x, inverse_of(s, high[x], high[x + 1]))
    cond.put(nx + 2, high[1][1:])

    batch = Batch(16)
    for ref, x0 in ((low_ref, 0), (high_ref, nx + 2)):
        tiles = Tiles(ref, my, loads)
        for dx in range(2):
            for y in range(my):
                tile = tiles[dx, y]
                batch.add(bx, (x0 + dx, y), tile)
                scaled = tile * invx[x0 + dx, y]
                batch.add(zx, (x0 + dx, y), scaled)
                batch.add(zu, (x0 + dx, y), up(scaled))
    for y in range(my):
        scaled = bx[2, y] * invx[2, y]
        batch.add(zx, (2, y), scaled)
        batch.add(zu, (2, y), up(scaled))
    batch.flush()

    emitter = First(bx, invx, qx, wx, wu)
    element_planes(cond, carry3, 0, 1, 0, my - 1, zx, zu, None)
    element_planes(cond, carry3, 1, 2, 0, my - 1, zx, zu, emitter)
    element_planes(cond, carry3, 3, 1, 0, my - 1, zx, zu, emitter, keep=False)
    element_planes(cond, carry1, nx + 1, 2, 0, my - 1, zx, zu, emitter, keep=False)
    sums = [sums1[place * loads : (place + 1) * loads, :] for place in range(4)]
    emitter = Second(bx, zx, qx, q_out, v_out, sums)
    element_planes(cond, carry3, 1, 1, 1, my - 3, wx, wu, None)
    element_planes(cond, carry3, 2, 2, 1, my - 3, wx, wu, emitter)
    element_planes(cond, carry3, 4, 1, 1, my - 3, wx, wu, emitter, keep=False)
    element_planes(cond, carry2, nx, 2, 1, my - 3, wx, wu, emitter, keep=False)
    lane = lane_ids(loads)
    load = lax.broadcasted_iota(jnp.int32, (loads, LANES), 0)
    packed = jnp.zeros((loads, LANES), jnp.float32)
    for place, part in enumerate(sums):
        total = jnp.sum(part, axis=1, keepdims=True)
        packed = packed + jnp.where(lane == place * loads + load, total, 0.0)
    row = jnp.sum(packed, axis=0, keepdims=True)
    sums_ref[...] = jnp.broadcast_to(row[None], sums_ref.shape)


def outer_planes(nx):
    return (2, 3, 4, nx, nx + 1)


def unpack_kernel(
    s, q1_ref, q2_ref, v1_ref, v2_ref, inv1_ref, inv2_ref, qo_ref, vo_ref, io_ref, q_ref, v_ref
):
    loads, nx, ny = s.loads, s.nx, s.ny
    batch = Batch()
    planes = outer_planes(nx)
    for first, second, whole in ((q1_ref, q2_ref, q_ref), (v1_ref, v2_ref, v_ref)):
        first, second = Tiles(first, ny, loads), Tiles(second, ny, loads)
        whole = Tiles(whole, ny, loads)
        for x in range(nx):
            for y in range(ny):
                if x + 2 in planes:
                    batch.add(whole, (x, y), second[planes.index(x + 2), y])
                else:
                    batch.add(whole, (x, y), first[x, y])
    batch.flush()
    batch = Batch()
    for x0 in range(0, nx, SUB):
        for ref, out in ((q_ref, qo_ref), (v_ref, vo_ref)):
            for load in range(loads):
                for block in range(packed_count(ny)):
                    tile = pack_block(
                        lambda y: ref[
                            pl.ds((x0 * ny + y) * loads + load, SUB, stride=ny * loads), :
                        ],
                        ny, block, SUB,
                    )
                    lanes = slice(block * LANES, (block + 1) * LANES)
                    batch.add(out, (load, slice(x0, x0 + SUB), lanes), tile)
        for block in range(packed_count(ny)):
            tile = pack_block(
                lambda y: inv1_ref[
                    pl.ds((x0 + 2) * s.pitch + y + 2, SUB, stride=s.pitch), :
                ],
                ny, block, SUB,
            )
            lanes = slice(block * LANES, (block + 1) * LANES)
            batch.add(io_ref, (slice(x0, x0 + SUB), lanes), tile)
    batch.flush()
    for block in range(packed_count(ny)):
        io_ref[0:1, block * LANES : (block + 1) * LANES] = pack_block(
            lambda y: inv2_ref[y : y + 1, :], ny, block, 1
        )


def finish_kernel(s, parts_ref, b_ref, q_ref, v_ref, inv_ref, x_hbm, r_hbm, x_ref, r_ref, sems):
    loads = s.loads
    totals = jnp.sum(parts_ref[...], axis=0)

    def part(place):
        return pltpu.roll(totals, (LANES - place * loads) % LANES, 1) if place else totals

    rz, near, square, last = (part(place) for place in range(4))
    direct = rz - near
    alpha = rz / direct
    short = -near / direct
    rz_next = short * short * rz + 2.0 * alpha * short * near + alpha * alpha * square
    beta = rz_next / rz
    grown = short + beta
    curved = (
        grown * grown * direct
        + 2.0 * alpha * grown * (near - square)
        + alpha * alpha * last
    )
    alpha_next = rz_next / curved
    first_row = alpha + alpha_next * (1.0 + beta)
    second_row = alpha_next * alpha
    inverse = inv_ref[...]
    copies = []
    for load in range(loads):
        first = first_row[:, load : load + 1]
        second = second_row[:, load : load + 1]
        source, image = b_ref[load], q_ref[load]
        x_ref[load] = (first * source - second * image) * inverse
        copies.append(pltpu.make_async_copy(x_ref.at[load], x_hbm.at[load], sems.at[0, load]))
        copies[-1].start()
        r_ref[load] = source - first * image + second * v_ref[load]
        copies.append(pltpu.make_async_copy(r_ref.at[load], r_hbm.at[load], sems.at[1, load]))
        copies[-1].start()
    for copy in copies:
        copy.wait()


def swap(array, axis, start):
    counts = {name: lax.axis_size(name) for name in ("gx", "gy")}
    other = "gy" if axis == "gx" else "gx"
    pairs = []
    for at in np.ndindex(counts["gx"], counts["gy"]):
        place = dict(zip(("gx", "gy"), at))
        partner = place[axis] + (1 if (place[axis] - start) % 2 == 0 else -1)
        if 0 <= partner < counts[axis]:
            place[axis] = partner
        elif place[other] ^ 1 < counts[other]:
            place[other] ^= 1
        pairs.append((at[0] * counts["gy"] + at[1], place["gx"] * counts["gy"] + place["gy"]))
    return lax.ppermute(array, ("gx", "gy"), pairs)


def per_device(heat_source, density):
    loads, nx, flat = heat_source.shape
    ny = flat // NZ
    s = Sizes(loads, nx, ny, lax.axis_size("gx"), lax.axis_size("gy"))
    nodes = nx * ny * loads
    devices = lax.axis_size("gx") * lax.axis_size("gy")

    def shape(*dims):
        return jax.ShapeDtypeStruct(dims, jnp.float32)

    def scratch(*dims):
        return pltpu.VMEM(dims, jnp.float32)

    def call(kernel, out_shape, **more):
        params = pltpu.CompilerParams(vmem_limit_bytes=20 * 1024 * 1024)
        return pl.pallas_call(
            functools.partial(kernel, s), out_shape=out_shape, compiler_params=params, **more
        )

    hbm = pl.BlockSpec(memory_space=pltpu.HBM)
    y_face, x_face, corner = (shape(rows, LANES) for rows in (s.y_rows, s.x_rows, s.c_rows))
    b, dt, x1, x2 = call(
        pack_x_kernel,
        (shape(packed_count(ny), loads * nx, LANES), shape(nx * ny, LANES), x_face, x_face),
        in_specs=[hbm, hbm],
        scratch_shapes=[scratch(nx, flat), pltpu.SemaphoreType.DMA((packed_count(ny) + 1,))],
    )(
        pltpu.with_memory_space_constraint(heat_source.reshape(loads * nx, flat), pltpu.HBM),
        pltpu.with_memory_space_constraint(density, pltpu.HBM),
    )
    x2, x1 = swap(x2, "gx", 1), swap(x1, "gx", 0)
    bt, y1, y2 = call(pack_y_kernel, (shape(nodes, LANES), y_face, y_face))(b, dt)
    y2, y1 = swap(y2, "gy", 1), swap(y1, "gy", 0)
    t1 = call(open_y_kernel, shape(2 * nx * loads, LANES))(y1)
    xt = shape(2 * ny * loads, LANES)
    xt2 = call(open_x_kernel, xt)(x2)
    xt2, dt_later = lax.optimization_barrier((xt2, dt))
    inside = shape(nodes, LANES)
    zt, ut = call(
        scale_kernel, (inside, inside), scratch_shapes=[scratch(nx * ny, LANES)]
    )(bt, dt_later)
    xt1, c1, c2 = call(
        corner_kernel,
        (xt, corner, corner),
        cost_estimate=pl.CostEstimate(flops=2 * 10**9, transcendentals=0, bytes_accessed=0),
    )(x2, xt2, x1)
    xt1, dt = lax.optimization_barrier((xt1, dt))
    c2, c1 = swap(c2, "gy", 1), swap(c1, "gy", 0)
    plane = s.my * loads
    rows, field = shape(s.mx * s.pitch, LANES), shape(s.mx * plane, LANES)
    edge = shape(2 * plane, LANES)
    dens, cond, inv_1, bx, zx, zu, q_x, w_x, w_u, q_1, v_1, carry1, carry2, sums = call(
        inner_kernel,
        (shape(nx * s.pitch, LANES),)
        + (rows,) * 2
        + (field,) * 6
        + (inside,) * 2
        + (edge,) * 2
        + (shape(4 * loads, LANES),),
    )(bt, zt, ut, dt, y1, y2, t1)
    ends = shape(len(outer_planes(nx)) * ny * loads, LANES)
    q_2, v_2, inv_2, sums = call(
        outer_kernel,
        (ends, ends, shape(ny, LANES), shape(devices, 1, LANES)),
        scratch_shapes=[scratch(2 * plane, LANES)] * 2
        + [scratch(3 * s.pitch, LANES)] * 2
        + [scratch(5 * s.pitch, LANES)] * 2
        + [scratch(5 * plane, LANES)] * 6
        + [scratch(2 * plane, LANES)],
    )(bt, zt, ut, dens, x1, x2, xt1, xt2, c1, c2, cond, inv_1, bx, zx, zu, q_x, w_x, w_u, carry1, carry2, sums)
    parts = lax.all_to_all(sums, ("gx", "gy"), 0, 0, tiled=True)
    whole = shape(loads, nx, flat)
    image, again, inverse = call(
        unpack_kernel,
        (whole, whole, shape(nx, flat)),
        scratch_shapes=[scratch(nodes, LANES)] * 2,
    )(q_1, q_2, v_1, v_2, inv_1, inv_2)
    return call(
        finish_kernel,
        (whole, whole),
        out_specs=(hbm, hbm),
        scratch_shapes=[
            scratch(loads, nx, flat),
            scratch(loads, nx, flat),
            pltpu.SemaphoreType.DMA((2, loads)),
        ],
    )(parts, heat_source, image, again, inverse)


def solution(mesh):
    placed = (P(None, "gx", "gy"), P("gx", "gy"))
    return jax.shard_map(
        per_device,
        mesh=mesh,
        in_specs=placed,
        out_specs=(P(None, "gx", "gy"), P(None, "gx", "gy")),
        check_vma=False,
    )
```

```python
import functools

import jax
import jax.numpy as jnp
import numpy as np
from jax import lax
from jax.experimental import pallas as pl
from jax.experimental.pallas import tpu as pltpu
from jax.sharding import PartitionSpec as P

NZ = 96
KMIN = 0.001
LANES = 128
SUB = 8


class Batch:
    def __init__(self, size=12):
        self.size, self.held = size, []

    def add(self, into, at, tile):
        self.held.append((into, at, tile))
        if len(self.held) >= self.size:
            self.flush()

    def flush(self):
        for into, at, tile in self.held:
            into[at] = tile
        self.held = []


def packed_count(tiles):
    return -(-tiles * NZ // LANES)


def lane_ids(rows):
    return lax.broadcasted_iota(jnp.int32, (rows, LANES), 1)


def unpack_tile(read, index, rows):
    start = index * NZ
    block, offset = start // LANES, start % LANES
    lane = lane_ids(rows)
    first = read(block)
    if offset:
        first = pltpu.roll(first, LANES - offset, 1)
    if offset + NZ > LANES:
        second = pltpu.roll(read(block + 1), LANES - offset, 1)
        first = jnp.where(lane < LANES - offset, first, second)
    return jnp.where(lane < NZ, first, 0.0)


def pack_block(read_tile, tiles, block, rows):
    lane = lane_ids(rows)
    start = block * LANES
    out, at = None, start
    while at < start + LANES and at // NZ < tiles:
        index, z = at // NZ, at % NZ
        here = at - start
        piece = read_tile(index)
        shift = (here - z) % LANES
        if shift:
            piece = pltpu.roll(piece, shift, 1)
        out = piece if out is None else jnp.where(lane < here, out, piece)
        at += NZ - z
    return out


def pack_tiles(out_ref, at, rows, tiles, read_tile):
    batch = Batch()
    for block in range(packed_count(tiles)):
        place = slice(at + block * rows, at + (block + 1) * rows), slice(None)
        batch.add(out_ref, place, pack_block(read_tile, tiles, block, rows))
    batch.flush()


def unpack_tiles(ref, at, rows, tiles, write):
    batch = Batch()
    for index in range(tiles):
        tile = unpack_tile(lambda t: ref[at + t * rows : at + (t + 1) * rows, :], index, rows)
        for store in write(index, tile):
            batch.add(*store)
    batch.flush()


class Sizes:
    def __init__(self, loads, nx, ny, count_x, count_y):
        self.loads, self.nx, self.ny = loads, nx, ny
        self.count_x, self.count_y = count_x, count_y
        self.mx, self.my = nx + 4, ny + 4
        self.pitch = -(-(ny + 6) // SUB) * SUB
        self.y_dens = packed_count(2 * nx) * loads
        self.y_rows = self.y_dens + 3 * nx
        self.x_dens = packed_count(2 * ny) * loads
        self.x_rows = self.x_dens + 3 * ny
        self.c_dens = packed_count(8) * loads
        self.c_rows = self.c_dens + -(-18 // SUB) * SUB


class Tiles:
    def __init__(self, ref, columns, loads):
        self.ref, self.columns, self.loads = ref, columns, loads

    def rows(self, at):
        start = (at[0] * self.columns + at[1]) * self.loads
        if not isinstance(start, int):
            start = pl.multiple_of(start, SUB)
        return pl.ds(start, self.loads)

    def __getitem__(self, at):
        return self.ref[self.rows(at), :]

    def __setitem__(self, at, tile):
        self.ref[self.rows(at), :] = tile


class Rows:
    def __init__(self, ref, pitch, loads):
        self.ref, self.pitch, self.loads = ref, pitch, loads

    def __getitem__(self, at):
        row = self.ref[pl.ds(at[0] * self.pitch + at[1], 1), :]
        return jnp.broadcast_to(row, (self.loads, LANES))

    def put(self, x, values):
        self.ref[x * self.pitch : x * self.pitch + values.shape[0], :] = values


class Joined:
    def __init__(self, first, second, own):
        self.first, self.second, self.own = first, second, own

    def __getitem__(self, at):
        if at[0] in self.own:
            return self.first[self.own.index(at[0]), at[1]]
        return self.second[at]

    def __setitem__(self, at, tile):
        self.first[self.own.index(at[0]), at[1]] = tile

    def put(self, x, values):
        self.first.put(self.own.index(x), values)


class Halves:
    def __init__(self, outer_ref, middle_ref, ny, loads):
        self.edge = (0, 1, ny - 2, ny - 1)
        self.outer, self.middle = Tiles(outer_ref, 4, loads), Tiles(middle_ref, ny - 4, loads)

    def __getitem__(self, at):
        if at[1] in self.edge:
            return self.outer[at[0], self.edge.index(at[1])]
        return self.middle[at[0], at[1] - 2]


class Inside:
    def __init__(self, inner, own, outer):
        self.inner, self.own, self.outer = inner, own, outer

    def __getitem__(self, at):
        if at[1] in self.own:
            return self.inner[at[0] - 2, at[1] - 2]
        return self.outer[at]

    def __setitem__(self, at, tile):
        self.outer[at] = tile


def is_even(axis):
    return lax.rem(lax.axis_index(axis), 2) == 0


def is_alone(axis, count, start):
    place = lax.axis_index(axis)
    last = (count - start) % 2
    alone = place < start
    return jnp.logical_or(alone, place == count - 1) if last else alone


def pick(even, if_even, if_odd):
    return jnp.where(even, if_even, if_odd)


def pack_x_kernel(s, b_hbm, d_hbm, b_ref, dt_ref, x1_ref, x2_ref, d_ref, sems):
    loads, nx, ny = s.loads, s.nx, s.ny
    blocks = packed_count(ny)
    d_copy = pltpu.make_async_copy(d_hbm, d_ref, sems.at[blocks])
    d_copy.start()
    copies = []
    for block in range(blocks):
        lanes = pl.ds(block * LANES, LANES)
        copies.append(
            pltpu.make_async_copy(b_hbm.at[:, lanes], b_ref.at[block], sems.at[block])
        )
        copies[-1].start()
    d_copy.wait()
    batch = Batch(16)
    for x0 in range(0, nx, SUB):
        for y in range(ny):
            tile = unpack_tile(
                lambda t: d_ref[x0 : x0 + SUB, t * LANES : (t + 1) * LANES], y, SUB
            )
            batch.add(dt_ref, (pl.ds(x0 * ny + y, SUB, stride=ny), slice(None)), tile)
    batch.flush()
    even_x = is_even("gx")
    for ref, upper in ((x2_ref, jnp.logical_not(even_x)), (x1_ref, even_x)):
        rows = pl.ds(pl.multiple_of(pick(upper, nx - 3, 0) * ny, SUB), 3 * ny)
        ref[s.x_dens :, :] = dt_ref[rows, :]
    for copy in copies:
        copy.wait()
    batch = Batch()
    for ref, upper in ((x2_ref, jnp.logical_not(even_x)), (x1_ref, even_x)):
        x0 = pick(upper, nx - 2, 0)
        for dx in range(2):
            for block in range(blocks):
                tile = b_ref[block, pl.ds(x0 + dx, loads, stride=nx), :]
                at = (dx * blocks + block) * loads
                batch.add(ref, (slice(at, at + loads), slice(None)), tile)
    batch.flush()


def lay_out(s, b_ref, columns, out_ref):
    loads, nx, count = s.loads, s.nx, len(columns)
    batch = Batch(16)
    for load in range(loads):
        for x0 in range(0, nx, SUB):
            at = load * nx + x0
            for place, y in enumerate(columns):
                tile = unpack_tile(lambda t: b_ref[t, at : at + SUB, :], y, SUB)
                rows = pl.ds((x0 * count + place) * loads + load, SUB, stride=count * loads)
                batch.add(out_ref, (rows, slice(None)), tile)
    batch.flush()


def pack_y_kernel(s, b_ref, dt_ref, be_ref, y1_ref, y2_ref):
    lay_out(s, b_ref, (0, 1, s.ny - 2, s.ny - 1), be_ref)
    even_y = is_even("gy")
    pack_y_face(s, jnp.logical_not(even_y), be_ref, dt_ref, y2_ref)
    pack_y_face(s, even_y, be_ref, dt_ref, y1_ref)


def pack_y_face(s, upper, be_ref, dt_ref, out_ref):
    loads, nx, ny = s.loads, s.nx, s.ny
    tiles = Tiles(be_ref, 4, loads)
    y0 = pick(upper, 2, 0)
    pack_tiles(out_ref, 0, loads, 2 * nx, lambda i: tiles[i // 2, y0 + i % 2])
    y0 = pick(upper, ny - 3, 0)
    batch = Batch()
    for dy in range(3):
        for x0 in range(0, nx, SUB):
            at = s.y_dens + dy * nx + x0
            tile = dt_ref[pl.ds(x0 * ny + y0 + dy, SUB, stride=ny), :]
            batch.add(out_ref, (slice(at, at + SUB), slice(None)), tile)
    batch.flush()


def open_y_kernel(s, y_ref, t_ref):
    tiles = Tiles(t_ref, 2, s.loads)
    unpack_tiles(
        y_ref, 0, s.loads, 2 * s.nx, lambda i, tile: [(tiles, (i // 2, i % 2), tile)]
    )


def open_x_kernel(s, x_ref, t_ref):
    tiles = Tiles(t_ref, s.ny, s.loads)
    unpack_tiles(
        x_ref, 0, s.loads, 2 * s.ny, lambda i, tile: [(tiles, (i // s.ny, i % s.ny), tile)]
    )


def corner_kernel(s, x2_ref, t2_ref, x1_ref, t1_ref, c1_ref, c2_ref):
    loads, ny = s.loads, s.ny
    open_x_kernel(s, x1_ref, t1_ref)
    halves = Tiles(t1_ref, ny, loads), Tiles(t2_ref, ny, loads)
    even_y = is_even("gy")
    for out_ref, upper in ((c2_ref, jnp.logical_not(even_y)), (c1_ref, even_y)):
        y0 = pick(upper, ny - 2, 0)
        pack_tiles(out_ref, 0, loads, 8, lambda i: halves[i // 4][i // 2 % 2, y0 + i % 2])
        y0 = pick(upper, ny - 3, 0)
        batch, at = Batch(18), s.c_dens
        for ref in (x1_ref, x2_ref):
            for t in range(3):
                for dy in range(3):
                    row = ref[pl.ds(s.x_dens + t * ny + y0 + dy, 1), :]
                    batch.add(out_ref, (slice(at, at + 1), slice(None)), row)
                    at += 1
        batch.flush()
        out_ref[at:, :] = jnp.zeros((s.c_rows - at, LANES), jnp.float32)


def join_density(s, dt_ref, y1_ref, y2_ref, dens_ref):
    nx, ny, pitch = s.nx, s.ny, s.pitch
    even_y = is_even("gy")
    yd = (pick(even_y, ny + 3, 0), pick(even_y, 0, ny + 3))
    batch = Batch(16)
    for x in range(nx):
        at = x * pitch
        batch.add(
            dens_ref, (slice(at + 3, at + 3 + ny), slice(None)), dt_ref[x * ny : (x + 1) * ny, :]
        )
    batch.flush()
    for side, ref in enumerate((y1_ref, y2_ref)):
        alone = is_alone("gy", s.count_y, side)
        for dy in range(3):
            for x0 in range(0, nx, SUB):
                at = s.y_dens + dy * nx + x0
                to = x0 * pitch + yd[side] + dy
                batch.add(
                    dens_ref,
                    (pl.ds(to, SUB, stride=pitch), slice(None)),
                    jnp.where(alone, 0.0, ref[at : at + SUB, :]),
                )
    batch.flush()


def conduct_of(dens):
    return jnp.where(
        dens > 0.0, (KMIN + (1.0 - KMIN) * (dens * dens * dens)) * (1.0 / 12.0), 0.0
    )


def inverse_of(s, before, after):
    pair = before + after
    pair = pair[: s.pitch - 1] + pair[1:]
    total = 4.0 * (pair + pltpu.roll(pair, 1, 1))
    return jnp.where(after[1:] > 0.0, 1.0 / total, 0.0)


def up(tile):
    return pltpu.roll(tile, LANES - 1, 1)


def element_planes(cond, carry, a, count, y0, columns, field, field_up, emitter, keep=True):
    def loads_of(step):
        y = y0 + step
        right = [(field[a + u, y + 1], field_up[a + u, y + 1]) for u in range(count + 1)]
        conduct = [cond[a + u, y] for u in range(count)]
        above = extra = None
        if step and emitter:
            above = (carry[0, y], carry[1, y])
            extra = [emitter.fetch(a + u, y) for u in range(count)]
        return right, conduct, above, extra

    left = [(field[a + u, y0], field_up[a + u, y0]) for u in range(count + 1)]
    ahead = loads_of(0)
    old, waiting = [None] * count, []
    for step in range(columns):
        y = y0 + step
        right, conduct, above, extra = ahead
        if step + 1 < columns:
            ahead = loads_of(step + 1)
        if len(waiting) > 1:
            for into, at, tile in waiting.pop(0):
                into[at] = tile
        stores = []
        for u in range(count):
            (p0, p0s), (p1, p1s) = left[u], left[u + 1]
            (r0, r0s), (r1, r1s) = right[u], right[u + 1]
            c = conduct[u]
            even = (p0 + r1) + (r0s + p1s)
            odd = (r0 + p1) + (p0s + r1s)
            pass_on = keep or u + 1 < count
            lower = upper = None
            if emitter:
                lower = (c * (odd + p1s), c * (even + p1))
            if pass_on:
                upper = (c * (even + p0s), c * (odd + p0))
            if step and emitter:
                low = (c * (even + r1s) + old[u][0][0]) + above[0]
                high = (c * (odd + r1) + old[u][0][1]) + above[1]
                total = low + pltpu.roll(high, 1, 1)
                stores += emitter.finish(a + u, y, p0, total, extra[u])
            if step and pass_on:
                above = (
                    c * (odd + r0s) + old[u][1][0],
                    c * (even + r0) + old[u][1][1],
                )
            old[u] = (lower, upper)
        if step and keep:
            stores += [(carry, (0, y), above[0]), (carry, (1, y), above[1])]
        waiting.append(stores)
        left = right
    for stores in waiting:
        for into, at, tile in stores:
            into[at] = tile


class First:
    def __init__(self, bx, invx, qx, wx, wu):
        self.bx, self.invx, self.qx, self.wx, self.wu = bx, invx, qx, wx, wu

    def fetch(self, x, y):
        return self.bx[x, y], self.invx[x, y]

    def finish(self, x, y, node, total, extra):
        source, inverse = extra
        image = 1.25 * source - total
        weighted = image * inverse
        at = x, y
        return [(self.qx, at, image), (self.wx, at, weighted), (self.wu, at, up(weighted))]


class Second:
    def __init__(self, bx, zx, qx, q_out, v_out, sums):
        self.bx, self.zx, self.qx, self.sums = bx, zx, qx, sums
        self.q_out, self.v_out = q_out, v_out

    def fetch(self, x, y):
        return self.bx[x, y], self.zx[x, y], self.qx[x, y]

    def finish(self, x, y, weighted, total, extra):
        source, scaled, image = extra
        again = 1.25 * image - total
        change = scaled - weighted
        sums = self.sums
        sums[0] = sums[0] + source * scaled
        sums[1] = sums[1] + source * change
        sums[2] = sums[2] + (source - image) * change
        sums[3] = sums[3] + (image - again) * change
        at = x - 2, y - 2
        return [(self.q_out, at, image), (self.v_out, at, again)]


def over_planes(start, stop, body, state):
    pairs = (stop - start) // 2
    state = lax.fori_loop(0, pairs, lambda i, st: body(start + 2 * i, 2, st), state)
    if (stop - start) % 2:
        state = body(stop - 1, 1, state)
    return state


def inside_fields(s, be_ref, bm_ref, zt_ref, ut_ref, bx, zx, zu):
    brick = [Halves(be_ref, bm_ref, s.ny, s.loads)]
    brick += [Tiles(ref, s.ny, s.loads) for ref in (zt_ref, ut_ref)]
    starts = (2, 3, 3)
    return tuple(
        Inside(inner, range(start, s.ny + 2), outer)
        for inner, start, outer in zip(brick, starts, (bx, zx, zu))
    )


def scale_kernel(
    s, b_ref, be_ref, dt_ref, bm_ref, zt_ref, ut_ref, ct_ref, it_ref, cond_ref, inv_ref
):
    loads, nx, ny = s.loads, s.nx, s.ny
    lay_out(s, b_ref, range(2, ny - 2), bm_ref)
    inner = Halves(be_ref, bm_ref, ny, loads)
    scaled, shifted, cond_t, inv_t = (
        Tiles(ref, ny, loads) for ref in (zt_ref, ut_ref, ct_ref, it_ref)
    )
    cond, inverse = Rows(cond_ref, ny, loads), Rows(inv_ref, ny, loads)
    before = None
    for x in range(nx):
        after = conduct_of(dt_ref[x * ny : (x + 1) * ny, :])
        cond.put(x, after)
        if x:
            pair = before + after
            pair = pair[: ny - 1] + pair[1:]
            total = 4.0 * (pair + pltpu.roll(pair, 1, 1))
            inverse.put(x, jnp.where(after[1:] > 0.0, 1.0 / total, 0.0))
        before = after
    batch = Batch(16)
    for x in range(nx):
        for y in range(ny):
            batch.add(cond_t, (x, y), cond[x, y])
            if x and y:
                row = inverse[x, y - 1]
                tile = inner[x, y] * row
                batch.add(inv_t, (x, y), row)
                batch.add(scaled, (x, y), tile)
                batch.add(shifted, (x, y), up(tile))
    batch.flush()


def inner_kernel(
    s, be_ref, bm_ref, zt_ref, ut_ref, ct_ref, it_ref, dt_ref, y1_ref, y2_ref, t1_ref,
    dens_ref, cond, invx, bx, zx, zu, qx, wx, wu, q_out, v_out, carry1, carry2, sums_ref,
):
    loads, nx, ny, my, pitch = s.loads, s.nx, s.ny, s.my, s.pitch
    bx, zx, zu, qx, wx, wu, carry1, carry2 = (
        Tiles(ref, my, loads) for ref in (bx, zx, zu, qx, wx, wu, carry1, carry2)
    )
    q_out, v_out = Tiles(q_out, ny, loads), Tiles(v_out, ny, loads)
    cond, invx = Rows(cond, pitch, loads), Rows(invx, pitch, loads)
    join_density(s, dt_ref, y1_ref, y2_ref, dens_ref)
    even_y = is_even("gy")
    ys = (pick(even_y, ny + 2, 0), pick(even_y, 0, ny + 2))
    before = None
    for x in range(nx):
        after = conduct_of(dens_ref[x * pitch : (x + 1) * pitch, :])
        cond.put(x + 2, after[1:])
        if x:
            invx.put(x + 2, inverse_of(s, before, after))
        before = after

    bx, zx, zu = inside_fields(s, be_ref, bm_ref, zt_ref, ut_ref, bx, zx, zu)

    def stage(x, y, tile):
        stores = [(bx, (x + 2, y), tile)]
        if x:
            scaled = tile * invx[x + 2, y]
            stores += [(zx, (x + 2, y), scaled), (zu, (x + 2, y), up(scaled))]
        return stores

    batch = Batch(16)
    for x in range(1, nx):
        scaled = bx[x + 2, 2] * invx[x + 2, 2]
        batch.add(zx, (x + 2, 2), scaled)
        batch.add(zu, (x + 2, 2), up(scaled))
    batch.flush()
    unpack_tiles(
        y2_ref, 0, loads, 2 * nx, lambda i, tile: stage(i // 2, ys[1] + i % 2, tile)
    )
    near = Tiles(t1_ref, 2, loads)
    batch = Batch(16)
    for x in range(nx):
        for dy in range(2):
            for store in stage(x, ys[0] + dy, near[x, dy]):
                batch.add(*store)
    batch.flush()

    cond = Inside(Tiles(ct_ref, ny, loads), range(2, ny + 2), cond)
    invx = Inside(Tiles(it_ref, ny, loads), range(3, ny + 2), invx)
    element_planes(cond, carry1, 3, 1, 0, my - 1, zx, zu, None)

    def first(a, count, state):
        emitter = First(bx, invx, qx, wx, wu)
        element_planes(cond, carry1, a, count, 0, my - 1, zx, zu, emitter)
        return state

    over_planes(4, nx + 1, first, 0)
    element_planes(cond, carry2, 4, 1, 1, my - 3, wx, wu, None)

    def second(a, count, sums):
        sums = list(sums)
        emitter = Second(bx, zx, qx, q_out, v_out, sums)
        element_planes(cond, carry2, a, count, 1, my - 3, wx, wu, emitter)
        return tuple(sums)

    zero = jnp.zeros((loads, LANES), jnp.float32)
    sums = over_planes(5, nx, second, (zero,) * 4)
    for place, part in enumerate(sums):
        sums_ref[place * loads : (place + 1) * loads, :] = part


def outer_kernel(
    s, be_ref, bm_ref, zt_ref, ut_ref, dens_ref, x1_ref, x2_ref, t1_ref, t2_ref, c1_ref, c2_ref,
    cond1, invx1, bx1, zx1, zu1, qx1, wx1, wu1, carry1, carry2, sums1,
    q_out, v_out, inv_out, sums_ref,
    low_ref, high_ref, low_d, high_d, cond2, invx2, bx2, zx2, zu2, qx2, wx2, wu2, carry3,
):
    loads, nx, ny, mx, my, pitch = s.loads, s.nx, s.ny, s.mx, s.my, s.pitch
    even_x = is_even("gx")

    even_y = is_even("gy")
    ys = (pick(even_y, ny + 2, 0), pick(even_y, 0, ny + 2))
    yd = (pick(even_y, ny + 3, 0), pick(even_y, 0, ny + 3))

    def take(near, far):
        faces = (x1_ref, t1_ref, near), (x2_ref, t2_ref, far)
        for side, (ref, face_ref, (tiles_ref, into)) in enumerate(faces):
            face, tiles = Tiles(face_ref, ny, loads), Tiles(tiles_ref, my, loads)
            alone_x = is_alone("gx", s.count_x, side)
            batch = Batch(18)
            for dx in range(2):
                for y in range(ny):
                    batch.add(tiles, (dx, y + 2), face[dx, y])
            for t in range(3):
                at = s.x_dens + t * ny
                rows = jnp.where(alone_x, 0.0, ref[at : at + ny, :])
                to = t * pitch + 3
                batch.add(into, (slice(to, to + ny), slice(None)), rows)
            batch.flush()
            for end, corner in enumerate((c1_ref, c2_ref)):
                alone = jnp.logical_or(alone_x, is_alone("gy", s.count_y, end))
                for i in range(4):
                    tile = unpack_tile(
                        lambda t: corner[t * loads : (t + 1) * loads, :], 4 * side + i, loads
                    )
                    batch.add(tiles, (i // 2, ys[end] + i % 2), tile)
                for i in range(9):
                    at = s.c_dens + 9 * side + i
                    row = jnp.where(alone, 0.0, corner[at : at + 1, :])
                    to = i // 3 * pitch + yd[end] + i % 3
                    batch.add(into, (pl.ds(to, 1), slice(None)), row)
            batch.flush()

    @pl.when(even_x)
    def _():
        take((high_ref, high_d), (low_ref, low_d))

    @pl.when(jnp.logical_not(even_x))
    def _():
        take((low_ref, low_d), (high_ref, high_d))

    def joined(first, second, own):
        return Joined(Tiles(first, my, loads), Tiles(second, my, loads), own)

    def joined_rows(first, second, own):
        return Joined(Rows(first, pitch, loads), Rows(second, pitch, loads), own)

    outside = (0, 1, nx + 2, nx + 3)
    scaled_own = outside + (2,)
    image_own = (1, 2, 3, nx + 1, nx + 2)
    cond, invx = joined_rows(cond2, cond1, outside), joined_rows(invx2, invx1, scaled_own)
    bx1, zx1, zu1 = inside_fields(
        s, be_ref, bm_ref, zt_ref, ut_ref, *(Tiles(ref, my, loads) for ref in (bx1, zx1, zu1))
    )
    bx = Joined(Tiles(bx2, my, loads), bx1, outside)
    zx = Joined(Tiles(zx2, my, loads), zx1, scaled_own)
    zu = Joined(Tiles(zu2, my, loads), zu1, scaled_own)
    qx, wx = joined(qx2, qx1, image_own), joined(wx2, wx1, image_own)
    wu = joined(wu2, wu1, image_own)
    own = [x - 2 for x in outer_planes(nx)]
    q_out, v_out = (Joined(Tiles(ref, ny, loads), None, own) for ref in (q_out, v_out))
    carry1, carry2, carry3 = (Tiles(ref, my, loads) for ref in (carry1, carry2, carry3))

    def conduct(ref, x):
        return conduct_of(ref[x * pitch : (x + 1) * pitch, :])

    low = [conduct(low_d, t) for t in range(3)] + [conduct(dens_ref, 0)]
    high = [conduct(dens_ref, nx - 1)] + [conduct(high_d, t) for t in range(2)]
    for x in range(3):
        inverse = inverse_of(s, low[x], low[x + 1])
        invx.put(x, inverse)
        if x < 2:
            cond.put(x, low[x + 1][1:])
    inv_out[...] = inverse[2 : 2 + ny]
    for x in range(2):
        invx.put(nx + 2 + x, inverse_of(s, high[x], high[x + 1]))
    cond.put(nx + 2, high[1][1:])

    batch = Batch(16)
    for ref, x0 in ((low_ref, 0), (high_ref, nx + 2)):
        tiles = Tiles(ref, my, loads)
        for dx in range(2):
            for y in range(my):
                tile = tiles[dx, y]
                batch.add(bx, (x0 + dx, y), tile)
                scaled = tile * invx[x0 + dx, y]
                batch.add(zx, (x0 + dx, y), scaled)
                batch.add(zu, (x0 + dx, y), up(scaled))
    for y in range(my):
        scaled = bx[2, y] * invx[2, y]
        batch.add(zx, (2, y), scaled)
        batch.add(zu, (2, y), up(scaled))
    batch.flush()

    emitter = First(bx, invx, qx, wx, wu)
    element_planes(cond, carry3, 0, 1, 0, my - 1, zx, zu, None)
    element_planes(cond, carry3, 1, 2, 0, my - 1, zx, zu, emitter)
    element_planes(cond, carry3, 3, 1, 0, my - 1, zx, zu, emitter, keep=False)
    element_planes(cond, carry1, nx + 1, 2, 0, my - 1, zx, zu, emitter, keep=False)
    sums = [sums1[place * loads : (place + 1) * loads, :] for place in range(4)]
    emitter = Second(bx, zx, qx, q_out, v_out, sums)
    element_planes(cond, carry3, 1, 1, 1, my - 3, wx, wu, None)
    element_planes(cond, carry3, 2, 2, 1, my - 3, wx, wu, emitter)
    element_planes(cond, carry3, 4, 1, 1, my - 3, wx, wu, emitter, keep=False)
    element_planes(cond, carry2, nx, 2, 1, my - 3, wx, wu, emitter, keep=False)
    lane = lane_ids(loads)
    load = lax.broadcasted_iota(jnp.int32, (loads, LANES), 0)
    packed = jnp.zeros((loads, LANES), jnp.float32)
    for place, part in enumerate(sums):
        total = jnp.sum(part, axis=1, keepdims=True)
        packed = packed + jnp.where(lane == place * loads + load, total, 0.0)
    row = jnp.sum(packed, axis=0, keepdims=True)
    sums_ref[...] = jnp.broadcast_to(row[None], sums_ref.shape)


def outer_planes(nx):
    return (2, 3, 4, nx, nx + 1)


def unpack_kernel(
    s, q1_ref, q2_ref, v1_ref, v2_ref, inv1_ref, inv2_ref, qo_ref, vo_ref, io_ref, q_ref, v_ref
):
    loads, nx, ny = s.loads, s.nx, s.ny
    batch = Batch()
    planes = outer_planes(nx)
    for first, second, whole in ((q1_ref, q2_ref, q_ref), (v1_ref, v2_ref, v_ref)):
        first, second = Tiles(first, ny, loads), Tiles(second, ny, loads)
        whole = Tiles(whole, ny, loads)
        for x in range(nx):
            for y in range(ny):
                if x + 2 in planes:
                    batch.add(whole, (x, y), second[planes.index(x + 2), y])
                else:
                    batch.add(whole, (x, y), first[x, y])
    batch.flush()
    batch = Batch()
    for x0 in range(0, nx, SUB):
        for ref, out in ((q_ref, qo_ref), (v_ref, vo_ref)):
            for load in range(loads):
                for block in range(packed_count(ny)):
                    tile = pack_block(
                        lambda y: ref[
                            pl.ds((x0 * ny + y) * loads + load, SUB, stride=ny * loads), :
                        ],
                        ny, block, SUB,
                    )
                    lanes = slice(block * LANES, (block + 1) * LANES)
                    batch.add(out, (load, slice(x0, x0 + SUB), lanes), tile)
        for block in range(packed_count(ny)):
            tile = pack_block(
                lambda y: inv1_ref[
                    pl.ds((x0 + 2) * s.pitch + y + 2, SUB, stride=s.pitch), :
                ],
                ny, block, SUB,
            )
            lanes = slice(block * LANES, (block + 1) * LANES)
            batch.add(io_ref, (slice(x0, x0 + SUB), lanes), tile)
    batch.flush()
    for block in range(packed_count(ny)):
        io_ref[0:1, block * LANES : (block + 1) * LANES] = pack_block(
            lambda y: inv2_ref[y : y + 1, :], ny, block, 1
        )


def finish_kernel(s, parts_ref, b_ref, q_ref, v_ref, inv_ref, x_hbm, r_hbm, x_ref, r_ref, sems):
    loads = s.loads
    totals = jnp.sum(parts_ref[...], axis=0)

    def part(place):
        return pltpu.roll(totals, (LANES - place * loads) % LANES, 1) if place else totals

    rz, near, square, last = (part(place) for place in range(4))
    direct = rz - near
    alpha = rz / direct
    short = -near / direct
    rz_next = short * short * rz + 2.0 * alpha * short * near + alpha * alpha * square
    beta = rz_next / rz
    grown = short + beta
    curved = (
        grown * grown * direct
        + 2.0 * alpha * grown * (near - square)
        + alpha * alpha * last
    )
    alpha_next = rz_next / curved
    first_row = alpha + alpha_next * (1.0 + beta)
    second_row = alpha_next * alpha
    inverse = inv_ref[...]
    copies = []
    for load in range(loads):
        first = first_row[:, load : load + 1]
        second = second_row[:, load : load + 1]
        source, image = b_ref[load], q_ref[load]
        x_ref[load] = (first * source - second * image) * inverse
        copies.append(pltpu.make_async_copy(x_ref.at[load], x_hbm.at[load], sems.at[0, load]))
        copies[-1].start()
        r_ref[load] = source - first * image + second * v_ref[load]
        copies.append(pltpu.make_async_copy(r_ref.at[load], r_hbm.at[load], sems.at[1, load]))
        copies[-1].start()
    for copy in copies:
        copy.wait()


def swap(array, axis, start):
    counts = {name: lax.axis_size(name) for name in ("gx", "gy")}
    other = "gy" if axis == "gx" else "gx"
    pairs = []
    for at in np.ndindex(counts["gx"], counts["gy"]):
        place = dict(zip(("gx", "gy"), at))
        partner = place[axis] + (1 if (place[axis] - start) % 2 == 0 else -1)
        if 0 <= partner < counts[axis]:
            place[axis] = partner
        elif place[other] ^ 1 < counts[other]:
            place[other] ^= 1
        pairs.append((at[0] * counts["gy"] + at[1], place["gx"] * counts["gy"] + place["gy"]))
    return lax.ppermute(array, ("gx", "gy"), pairs)


def per_device(heat_source, density):
    loads, nx, flat = heat_source.shape
    ny = flat // NZ
    s = Sizes(loads, nx, ny, lax.axis_size("gx"), lax.axis_size("gy"))
    nodes = nx * ny * loads
    devices = lax.axis_size("gx") * lax.axis_size("gy")

    def shape(*dims):
        return jax.ShapeDtypeStruct(dims, jnp.float32)

    def scratch(*dims):
        return pltpu.VMEM(dims, jnp.float32)

    def call(kernel, out_shape, **more):
        params = pltpu.CompilerParams(vmem_limit_bytes=20 * 1024 * 1024)
        return pl.pallas_call(
            functools.partial(kernel, s), out_shape=out_shape, compiler_params=params, **more
        )

    hbm = pl.BlockSpec(memory_space=pltpu.HBM)
    y_face, x_face, corner = (shape(rows, LANES) for rows in (s.y_rows, s.x_rows, s.c_rows))
    b, dt, x1, x2 = call(
        pack_x_kernel,
        (shape(packed_count(ny), loads * nx, LANES), shape(nx * ny, LANES), x_face, x_face),
        in_specs=[hbm, hbm],
        scratch_shapes=[scratch(nx, flat), pltpu.SemaphoreType.DMA((packed_count(ny) + 1,))],
    )(
        pltpu.with_memory_space_constraint(heat_source.reshape(loads * nx, flat), pltpu.HBM),
        pltpu.with_memory_space_constraint(density, pltpu.HBM),
    )
    x2, x1 = swap(x2, "gx", 1), swap(x1, "gx", 0)
    outer_columns = shape(nx * 4 * loads, LANES)
    be, y1, y2 = call(pack_y_kernel, (outer_columns, y_face, y_face))(b, dt)
    y2, y1 = swap(y2, "gy", 1), swap(y1, "gy", 0)
    t1 = call(open_y_kernel, shape(2 * nx * loads, LANES))(y1)
    xt = shape(2 * ny * loads, LANES)
    xt2 = call(open_x_kernel, xt)(x2)
    xt2, dt_later = lax.optimization_barrier((xt2, dt))
    inside = shape(nodes, LANES)
    bm, zt, ut, ct, it = call(
        scale_kernel,
        (shape(nx * (ny - 4) * loads, LANES),) + (inside,) * 4,
        scratch_shapes=[scratch(nx * ny, LANES)] * 2,
    )(b, be, dt_later)
    xt1, c1, c2 = call(
        corner_kernel,
        (xt, corner, corner),
        cost_estimate=pl.CostEstimate(flops=2 * 10**9, transcendentals=0, bytes_accessed=0),
    )(x2, xt2, x1)
    xt1, dt = lax.optimization_barrier((xt1, dt))
    c2, c1 = swap(c2, "gy", 1), swap(c1, "gy", 0)
    plane = s.my * loads
    rows, field = shape(s.mx * s.pitch, LANES), shape(s.mx * plane, LANES)
    edge = shape(2 * plane, LANES)
    dens, cond, inv_1, bx, zx, zu, q_x, w_x, w_u, q_1, v_1, carry1, carry2, sums = call(
        inner_kernel,
        (shape(nx * s.pitch, LANES),)
        + (rows,) * 2
        + (field,) * 6
        + (inside,) * 2
        + (edge,) * 2
        + (shape(4 * loads, LANES),),
    )(be, bm, zt, ut, ct, it, dt, y1, y2, t1)
    ends = shape(len(outer_planes(nx)) * ny * loads, LANES)
    q_2, v_2, inv_2, sums = call(
        outer_kernel,
        (ends, ends, shape(ny, LANES), shape(devices, 1, LANES)),
        scratch_shapes=[scratch(2 * plane, LANES)] * 2
        + [scratch(3 * s.pitch, LANES)] * 2
        + [scratch(5 * s.pitch, LANES)] * 2
        + [scratch(5 * plane, LANES)] * 6
        + [scratch(2 * plane, LANES)],
    )(be, bm, zt, ut, dens, x1, x2, xt1, xt2, c1, c2, cond, inv_1, bx, zx, zu, q_x, w_x, w_u, carry1, carry2, sums)
    parts = lax.all_to_all(sums, ("gx", "gy"), 0, 0, tiled=True)
    whole = shape(loads, nx, flat)
    image, again, inverse = call(
        unpack_kernel,
        (whole, whole, shape(nx, flat)),
        scratch_shapes=[scratch(nodes, LANES)] * 2,
    )(q_1, q_2, v_1, v_2, inv_1, inv_2)
    return call(
        finish_kernel,
        (whole, whole),
        out_specs=(hbm, hbm),
        scratch_shapes=[
            scratch(loads, nx, flat),
            scratch(loads, nx, flat),
            pltpu.SemaphoreType.DMA((2, loads)),
        ],
    )(parts, heat_source, image, again, inverse)


def solution(mesh):
    placed = (P(None, "gx", "gy"), P("gx", "gy"))
    return jax.shard_map(
        per_device,
        mesh=mesh,
        in_specs=placed,
        out_specs=(P(None, "gx", "gy"), P(None, "gx", "gy")),
        check_vma=False,
    )
```

```python
import functools

import jax
import jax.numpy as jnp
import numpy as np
from jax import lax
from jax.experimental import pallas as pl
from jax.experimental.pallas import tpu as pltpu
from jax.sharding import PartitionSpec as P

NZ = 96
KMIN = 0.001
LANES = 128
SUB = 8


class Batch:
    def __init__(self, size=12):
        self.size, self.held = size, []

    def add(self, into, at, tile):
        self.held.append((into, at, tile))
        if len(self.held) >= self.size:
            self.flush()

    def flush(self):
        for into, at, tile in self.held:
            into[at] = tile
        self.held = []


def packed_count(tiles):
    return -(-tiles * NZ // LANES)


def lane_ids(rows):
    return lax.broadcasted_iota(jnp.int32, (rows, LANES), 1)


def unpack_tile(read, index, rows):
    start = index * NZ
    block, offset = start // LANES, start % LANES
    lane = lane_ids(rows)
    first = read(block)
    if offset:
        first = pltpu.roll(first, LANES - offset, 1)
    if offset + NZ > LANES:
        second = pltpu.roll(read(block + 1), LANES - offset, 1)
        first = jnp.where(lane < LANES - offset, first, second)
    return jnp.where(lane < NZ, first, 0.0)


def pack_block(read_tile, tiles, block, rows):
    lane = lane_ids(rows)
    start = block * LANES
    out, at = None, start
    while at < start + LANES and at // NZ < tiles:
        index, z = at // NZ, at % NZ
        here = at - start
        piece = read_tile(index)
        shift = (here - z) % LANES
        if shift:
            piece = pltpu.roll(piece, shift, 1)
        out = piece if out is None else jnp.where(lane < here, out, piece)
        at += NZ - z
    return out


def pack_tiles(out_ref, at, rows, tiles, read_tile):
    batch = Batch()
    for block in range(packed_count(tiles)):
        place = slice(at + block * rows, at + (block + 1) * rows), slice(None)
        batch.add(out_ref, place, pack_block(read_tile, tiles, block, rows))
    batch.flush()


def unpack_tiles(ref, at, rows, tiles, write):
    batch = Batch()
    for index in range(tiles):
        tile = unpack_tile(lambda t: ref[at + t * rows : at + (t + 1) * rows, :], index, rows)
        for store in write(index, tile):
            batch.add(*store)
    batch.flush()


class Sizes:
    def __init__(self, loads, nx, ny, count_x, count_y):
        self.loads, self.nx, self.ny = loads, nx, ny
        self.count_x, self.count_y = count_x, count_y
        self.mx, self.my = nx + 4, ny + 4
        self.pitch = -(-(ny + 6) // SUB) * SUB
        self.y_dens = packed_count(2 * nx) * loads
        self.y_rows = self.y_dens + 3 * nx
        self.x_dens = packed_count(2 * ny) * loads
        self.x_rows = self.x_dens + 3 * ny
        self.c_dens = packed_count(8) * loads
        self.c_rows = self.c_dens + -(-18 // SUB) * SUB


class Tiles:
    def __init__(self, ref, columns, loads):
        self.ref, self.columns, self.loads = ref, columns, loads

    def rows(self, at):
        start = (at[0] * self.columns + at[1]) * self.loads
        if not isinstance(start, int):
            start = pl.multiple_of(start, SUB)
        return pl.ds(start, self.loads)

    def __getitem__(self, at):
        return self.ref[self.rows(at), :]

    def __setitem__(self, at, tile):
        self.ref[self.rows(at), :] = tile


class Rows:
    def __init__(self, ref, pitch, loads):
        self.ref, self.pitch, self.loads = ref, pitch, loads

    def __getitem__(self, at):
        row = self.ref[pl.ds(at[0] * self.pitch + at[1], 1), :]
        return jnp.broadcast_to(row, (self.loads, LANES))

    def put(self, x, values):
        self.ref[x * self.pitch : x * self.pitch + values.shape[0], :] = values


class Joined:
    def __init__(self, first, second, own):
        self.first, self.second, self.own = first, second, own

    def __getitem__(self, at):
        if at[0] in self.own:
            return self.first[self.own.index(at[0]), at[1]]
        return self.second[at]

    def __setitem__(self, at, tile):
        self.first[self.own.index(at[0]), at[1]] = tile

    def put(self, x, values):
        self.first.put(self.own.index(x), values)


class Halves:
    def __init__(self, outer_ref, middle_ref, ny, loads):
        self.edge = (0, 1, ny - 2, ny - 1)
        self.outer, self.middle = Tiles(outer_ref, 4, loads), Tiles(middle_ref, ny - 4, loads)

    def __getitem__(self, at):
        if at[1] in self.edge:
            return self.outer[at[0], self.edge.index(at[1])]
        return self.middle[at[0], at[1] - 2]


class Inside:
    def __init__(self, inner, own, outer):
        self.inner, self.own, self.outer = inner, own, outer

    def __getitem__(self, at):
        if at[1] in self.own:
            return self.inner[at[0] - 2, at[1] - 2]
        return self.outer[at]

    def __setitem__(self, at, tile):
        self.outer[at] = tile


def is_even(axis):
    return lax.rem(lax.axis_index(axis), 2) == 0


def is_alone(axis, count, start):
    place = lax.axis_index(axis)
    last = (count - start) % 2
    alone = place < start
    return jnp.logical_or(alone, place == count - 1) if last else alone


def pick(even, if_even, if_odd):
    return jnp.where(even, if_even, if_odd)


def pack_x_kernel(s, b_hbm, d_hbm, b_ref, dt_ref, x1_ref, x2_ref, d_ref, sems):
    loads, nx, ny = s.loads, s.nx, s.ny
    blocks = packed_count(ny)
    d_copy = pltpu.make_async_copy(d_hbm, d_ref, sems.at[blocks])
    d_copy.start()
    copies = []
    for block in range(blocks):
        lanes = pl.ds(block * LANES, LANES)
        copies.append(
            pltpu.make_async_copy(b_hbm.at[:, lanes], b_ref.at[block], sems.at[block])
        )
        copies[-1].start()
    d_copy.wait()
    batch = Batch(16)
    for x0 in range(0, nx, SUB):
        for y in range(ny):
            tile = unpack_tile(
                lambda t: d_ref[x0 : x0 + SUB, t * LANES : (t + 1) * LANES], y, SUB
            )
            batch.add(dt_ref, (pl.ds(x0 * ny + y, SUB, stride=ny), slice(None)), tile)
    batch.flush()
    even_x = is_even("gx")
    for ref, upper in ((x2_ref, jnp.logical_not(even_x)), (x1_ref, even_x)):
        rows = pl.ds(pl.multiple_of(pick(upper, nx - 3, 0) * ny, SUB), 3 * ny)
        ref[s.x_dens :, :] = dt_ref[rows, :]
    for copy in copies:
        copy.wait()
    batch = Batch()
    for ref, upper in ((x2_ref, jnp.logical_not(even_x)), (x1_ref, even_x)):
        x0 = pick(upper, nx - 2, 0)
        for dx in range(2):
            for block in range(blocks):
                tile = b_ref[block, pl.ds(x0 + dx, loads, stride=nx), :]
                at = (dx * blocks + block) * loads
                batch.add(ref, (slice(at, at + loads), slice(None)), tile)
    batch.flush()


def lay_out(s, b_ref, columns, out_ref):
    loads, nx, count = s.loads, s.nx, len(columns)
    batch = Batch(16)
    for load in range(loads):
        for x0 in range(0, nx, SUB):
            at = load * nx + x0
            for place, y in enumerate(columns):
                tile = unpack_tile(lambda t: b_ref[t, at : at + SUB, :], y, SUB)
                rows = pl.ds((x0 * count + place) * loads + load, SUB, stride=count * loads)
                batch.add(out_ref, (rows, slice(None)), tile)
    batch.flush()


def pack_far_kernel(s, b_ref, dt_ref, be_ref, y2_ref):
    lay_out(s, b_ref, (0, 1, s.ny - 2, s.ny - 1), be_ref)
    pack_y_face(s, jnp.logical_not(is_even("gy")), be_ref, dt_ref, y2_ref)


def pack_near_kernel(s, be_ref, dt_ref, y1_ref):
    pack_y_face(s, is_even("gy"), be_ref, dt_ref, y1_ref)


def pack_y_face(s, upper, be_ref, dt_ref, out_ref):
    loads, nx, ny = s.loads, s.nx, s.ny
    tiles = Tiles(be_ref, 4, loads)
    y0 = pick(upper, 2, 0)
    pack_tiles(out_ref, 0, loads, 2 * nx, lambda i: tiles[i // 2, y0 + i % 2])
    y0 = pick(upper, ny - 3, 0)
    batch = Batch()
    for dy in range(3):
        for x0 in range(0, nx, SUB):
            at = s.y_dens + dy * nx + x0
            tile = dt_ref[pl.ds(x0 * ny + y0 + dy, SUB, stride=ny), :]
            batch.add(out_ref, (slice(at, at + SUB), slice(None)), tile)
    batch.flush()


def open_y_kernel(s, y_ref, t_ref):
    tiles = Tiles(t_ref, 2, s.loads)
    unpack_tiles(
        y_ref, 0, s.loads, 2 * s.nx, lambda i, tile: [(tiles, (i // 2, i % 2), tile)]
    )


def open_x_kernel(s, x_ref, t_ref):
    tiles = Tiles(t_ref, s.ny, s.loads)
    unpack_tiles(
        x_ref, 0, s.loads, 2 * s.ny, lambda i, tile: [(tiles, (i // s.ny, i % s.ny), tile)]
    )


def corner_kernel(s, x2_ref, t2_ref, x1_ref, t1_ref, c1_ref, c2_ref):
    loads, ny = s.loads, s.ny
    open_x_kernel(s, x1_ref, t1_ref)
    halves = Tiles(t1_ref, ny, loads), Tiles(t2_ref, ny, loads)
    even_y = is_even("gy")
    for out_ref, upper in ((c2_ref, jnp.logical_not(even_y)), (c1_ref, even_y)):
        y0 = pick(upper, ny - 2, 0)
        pack_tiles(out_ref, 0, loads, 8, lambda i: halves[i // 4][i // 2 % 2, y0 + i % 2])
        y0 = pick(upper, ny - 3, 0)
        batch, at = Batch(18), s.c_dens
        for ref in (x1_ref, x2_ref):
            for t in range(3):
                for dy in range(3):
                    row = ref[pl.ds(s.x_dens + t * ny + y0 + dy, 1), :]
                    batch.add(out_ref, (slice(at, at + 1), slice(None)), row)
                    at += 1
        batch.flush()
        out_ref[at:, :] = jnp.zeros((s.c_rows - at, LANES), jnp.float32)


def join_density(s, dt_ref, y1_ref, y2_ref, dens_ref):
    nx, ny, pitch = s.nx, s.ny, s.pitch
    even_y = is_even("gy")
    yd = (pick(even_y, ny + 3, 0), pick(even_y, 0, ny + 3))
    batch = Batch(16)
    for x in range(nx):
        at = x * pitch
        batch.add(
            dens_ref, (slice(at + 3, at + 3 + ny), slice(None)), dt_ref[x * ny : (x + 1) * ny, :]
        )
    batch.flush()
    for side, ref in enumerate((y1_ref, y2_ref)):
        alone = is_alone("gy", s.count_y, side)
        for dy in range(3):
            for x0 in range(0, nx, SUB):
                at = s.y_dens + dy * nx + x0
                to = x0 * pitch + yd[side] + dy
                batch.add(
                    dens_ref,
                    (pl.ds(to, SUB, stride=pitch), slice(None)),
                    jnp.where(alone, 0.0, ref[at : at + SUB, :]),
                )
    batch.flush()


def conduct_of(dens):
    return jnp.where(
        dens > 0.0, (KMIN + (1.0 - KMIN) * (dens * dens * dens)) * (1.0 / 12.0), 0.0
    )


def inverse_of(s, before, after):
    pair = before + after
    pair = pair[: s.pitch - 1] + pair[1:]
    total = 4.0 * (pair + pltpu.roll(pair, 1, 1))
    return jnp.where(after[1:] > 0.0, 1.0 / total, 0.0)


def up(tile):
    return pltpu.roll(tile, LANES - 1, 1)


def element_planes(cond, carry, a, count, y0, columns, field, field_up, emitter, keep=True):
    def loads_of(step):
        y = y0 + step
        right = [(field[a + u, y + 1], field_up[a + u, y + 1]) for u in range(count + 1)]
        conduct = [cond[a + u, y] for u in range(count)]
        above = extra = None
        if step and emitter:
            above = (carry[0, y], carry[1, y])
            extra = [emitter.fetch(a + u, y) for u in range(count)]
        return right, conduct, above, extra

    left = [(field[a + u, y0], field_up[a + u, y0]) for u in range(count + 1)]
    ahead = loads_of(0)
    old, waiting = [None] * count, []
    for step in range(columns):
        y = y0 + step
        right, conduct, above, extra = ahead
        if step + 1 < columns:
            ahead = loads_of(step + 1)
        if len(waiting) > 1:
            for into, at, tile in waiting.pop(0):
                into[at] = tile
        stores = []
        for u in range(count):
            (p0, p0s), (p1, p1s) = left[u], left[u + 1]
            (r0, r0s), (r1, r1s) = right[u], right[u + 1]
            c = conduct[u]
            even = (p0 + r1) + (r0s + p1s)
            odd = (r0 + p1) + (p0s + r1s)
            pass_on = keep or u + 1 < count
            lower = upper = None
            if emitter:
                lower = (c * (odd + p1s), c * (even + p1))
            if pass_on:
                upper = (c * (even + p0s), c * (odd + p0))
            if step and emitter:
                low = (c * (even + r1s) + old[u][0][0]) + above[0]
                high = (c * (odd + r1) + old[u][0][1]) + above[1]
                total = low + pltpu.roll(high, 1, 1)
                stores += emitter.finish(a + u, y, p0, total, extra[u])
            if step and pass_on:
                above = (
                    c * (odd + r0s) + old[u][1][0],
                    c * (even + r0) + old[u][1][1],
                )
            old[u] = (lower, upper)
        if step and keep:
            stores += [(carry, (0, y), above[0]), (carry, (1, y), above[1])]
        waiting.append(stores)
        left = right
    for stores in waiting:
        for into, at, tile in stores:
            into[at] = tile


class First:
    def __init__(self, bx, invx, qx, wx, wu):
        self.bx, self.invx, self.qx, self.wx, self.wu = bx, invx, qx, wx, wu

    def fetch(self, x, y):
        return self.bx[x, y], self.invx[x, y]

    def finish(self, x, y, node, total, extra):
        source, inverse = extra
        image = 1.25 * source - total
        weighted = image * inverse
        at = x, y
        return [(self.qx, at, image), (self.wx, at, weighted), (self.wu, at, up(weighted))]


class Second:
    def __init__(self, bx, zx, qx, q_out, v_out, sums):
        self.bx, self.zx, self.qx, self.sums = bx, zx, qx, sums
        self.q_out, self.v_out = q_out, v_out

    def fetch(self, x, y):
        return self.bx[x, y], self.zx[x, y], self.qx[x, y]

    def finish(self, x, y, weighted, total, extra):
        source, scaled, image = extra
        again = 1.25 * image - total
        change = scaled - weighted
        sums = self.sums
        sums[0] = sums[0] + source * scaled
        sums[1] = sums[1] + source * change
        sums[2] = sums[2] + (source - image) * change
        sums[3] = sums[3] + (image - again) * change
        at = x - 2, y - 2
        return [(self.q_out, at, image), (self.v_out, at, again)]


def over_planes(start, stop, body, state):
    pairs = (stop - start) // 2
    state = lax.fori_loop(0, pairs, lambda i, st: body(start + 2 * i, 2, st), state)
    if (stop - start) % 2:
        state = body(stop - 1, 1, state)
    return state


def inside_fields(s, be_ref, bm_ref, zt_ref, ut_ref, bx, zx, zu):
    brick = [Halves(be_ref, bm_ref, s.ny, s.loads)]
    brick += [Tiles(ref, s.ny, s.loads) for ref in (zt_ref, ut_ref)]
    starts = (2, 3, 3)
    return tuple(
        Inside(inner, range(start, s.ny + 2), outer)
        for inner, start, outer in zip(brick, starts, (bx, zx, zu))
    )


def scale_kernel(
    s, b_ref, be_ref, dt_ref, bm_ref, zt_ref, ut_ref, ct_ref, it_ref, cond_ref, inv_ref
):
    loads, nx, ny = s.loads, s.nx, s.ny
    lay_out(s, b_ref, range(2, ny - 2), bm_ref)
    inner = Halves(be_ref, bm_ref, ny, loads)
    scaled, shifted, cond_t, inv_t = (
        Tiles(ref, ny, loads) for ref in (zt_ref, ut_ref, ct_ref, it_ref)
    )
    cond, inverse = Rows(cond_ref, ny, loads), Rows(inv_ref, ny, loads)
    before = None
    for x in range(nx):
        after = conduct_of(dt_ref[x * ny : (x + 1) * ny, :])
        cond.put(x, after)
        if x:
            pair = before + after
            pair = pair[: ny - 1] + pair[1:]
            total = 4.0 * (pair + pltpu.roll(pair, 1, 1))
            inverse.put(x, jnp.where(after[1:] > 0.0, 1.0 / total, 0.0))
        before = after
    batch = Batch(16)
    for x in range(nx):
        for y in range(ny):
            batch.add(cond_t, (x, y), cond[x, y])
            if x and y:
                row = inverse[x, y - 1]
                tile = inner[x, y] * row
                batch.add(inv_t, (x, y), row)
                batch.add(scaled, (x, y), tile)
                batch.add(shifted, (x, y), up(tile))
    batch.flush()


def inner_kernel(
    s, be_ref, bm_ref, zt_ref, ut_ref, ct_ref, it_ref, dt_ref, y1_ref, y2_ref, t1_ref,
    dens_ref, cond, invx, bx, zx, zu, qx, wx, wu, q_out, v_out, carry1, carry2, sums_ref,
):
    loads, nx, ny, my, pitch = s.loads, s.nx, s.ny, s.my, s.pitch
    bx, zx, zu, qx, wx, wu, carry1, carry2 = (
        Tiles(ref, my, loads) for ref in (bx, zx, zu, qx, wx, wu, carry1, carry2)
    )
    q_out, v_out = Tiles(q_out, ny, loads), Tiles(v_out, ny, loads)
    cond, invx = Rows(cond, pitch, loads), Rows(invx, pitch, loads)
    join_density(s, dt_ref, y1_ref, y2_ref, dens_ref)
    even_y = is_even("gy")
    ys = (pick(even_y, ny + 2, 0), pick(even_y, 0, ny + 2))
    before = None
    for x in range(nx):
        after = conduct_of(dens_ref[x * pitch : (x + 1) * pitch, :])
        cond.put(x + 2, after[1:])
        if x:
            invx.put(x + 2, inverse_of(s, before, after))
        before = after

    bx, zx, zu = inside_fields(s, be_ref, bm_ref, zt_ref, ut_ref, bx, zx, zu)

    def stage(x, y, tile):
        stores = [(bx, (x + 2, y), tile)]
        if x:
            scaled = tile * invx[x + 2, y]
            stores += [(zx, (x + 2, y), scaled), (zu, (x + 2, y), up(scaled))]
        return stores

    batch = Batch(16)
    for x in range(1, nx):
        scaled = bx[x + 2, 2] * invx[x + 2, 2]
        batch.add(zx, (x + 2, 2), scaled)
        batch.add(zu, (x + 2, 2), up(scaled))
    batch.flush()
    unpack_tiles(
        y2_ref, 0, loads, 2 * nx, lambda i, tile: stage(i // 2, ys[1] + i % 2, tile)
    )
    near = Tiles(t1_ref, 2, loads)
    batch = Batch(16)
    for x in range(nx):
        for dy in range(2):
            for store in stage(x, ys[0] + dy, near[x, dy]):
                batch.add(*store)
    batch.flush()

    cond = Inside(Tiles(ct_ref, ny, loads), range(2, ny + 2), cond)
    invx = Inside(Tiles(it_ref, ny, loads), range(3, ny + 2), invx)
    element_planes(cond, carry1, 3, 1, 0, my - 1, zx, zu, None)

    def first(a, count, state):
        emitter = First(bx, invx, qx, wx, wu)
        element_planes(cond, carry1, a, count, 0, my - 1, zx, zu, emitter)
        return state

    over_planes(4, nx + 1, first, 0)
    element_planes(cond, carry2, 4, 1, 1, my - 3, wx, wu, None)

    def second(a, count, sums):
        sums = list(sums)
        emitter = Second(bx, zx, qx, q_out, v_out, sums)
        element_planes(cond, carry2, a, count, 1, my - 3, wx, wu, emitter)
        return tuple(sums)

    zero = jnp.zeros((loads, LANES), jnp.float32)
    sums = over_planes(5, nx, second, (zero,) * 4)
    for place, part in enumerate(sums):
        sums_ref[place * loads : (place + 1) * loads, :] = part


def outer_kernel(
    s, be_ref, bm_ref, zt_ref, ut_ref, dens_ref, x1_ref, x2_ref, t1_ref, t2_ref, c1_ref, c2_ref,
    cond1, invx1, bx1, zx1, zu1, qx1, wx1, wu1, carry1, carry2, sums1,
    q_out, v_out, inv_out, sums_ref,
    low_ref, high_ref, low_d, high_d, cond2, invx2, bx2, zx2, zu2, qx2, wx2, wu2, carry3,
):
    loads, nx, ny, mx, my, pitch = s.loads, s.nx, s.ny, s.mx, s.my, s.pitch
    even_x = is_even("gx")

    even_y = is_even("gy")
    ys = (pick(even_y, ny + 2, 0), pick(even_y, 0, ny + 2))
    yd = (pick(even_y, ny + 3, 0), pick(even_y, 0, ny + 3))

    def take(near, far):
        faces = (x1_ref, t1_ref, near), (x2_ref, t2_ref, far)
        for side, (ref, face_ref, (tiles_ref, into)) in enumerate(faces):
            face, tiles = Tiles(face_ref, ny, loads), Tiles(tiles_ref, my, loads)
            alone_x = is_alone("gx", s.count_x, side)
            batch = Batch(18)
            for dx in range(2):
                for y in range(ny):
                    batch.add(tiles, (dx, y + 2), face[dx, y])
            for t in range(3):
                at = s.x_dens + t * ny
                rows = jnp.where(alone_x, 0.0, ref[at : at + ny, :])
                to = t * pitch + 3
                batch.add(into, (slice(to, to + ny), slice(None)), rows)
            batch.flush()
            for end, corner in enumerate((c1_ref, c2_ref)):
                alone = jnp.logical_or(alone_x, is_alone("gy", s.count_y, end))
                for i in range(4):
                    tile = unpack_tile(
                        lambda t: corner[t * loads : (t + 1) * loads, :], 4 * side + i, loads
                    )
                    batch.add(tiles, (i // 2, ys[end] + i % 2), tile)
                for i in range(9):
                    at = s.c_dens + 9 * side + i
                    row = jnp.where(alone, 0.0, corner[at : at + 1, :])
                    to = i // 3 * pitch + yd[end] + i % 3
                    batch.add(into, (pl.ds(to, 1), slice(None)), row)
            batch.flush()

    @pl.when(even_x)
    def _():
        take((high_ref, high_d), (low_ref, low_d))

    @pl.when(jnp.logical_not(even_x))
    def _():
        take((low_ref, low_d), (high_ref, high_d))

    def joined(first, second, own):
        return Joined(Tiles(first, my, loads), Tiles(second, my, loads), own)

    def joined_rows(first, second, own):
        return Joined(Rows(first, pitch, loads), Rows(second, pitch, loads), own)

    outside = (0, 1, nx + 2, nx + 3)
    scaled_own = outside + (2,)
    image_own = (1, 2, 3, nx + 1, nx + 2)
    cond, invx = joined_rows(cond2, cond1, outside), joined_rows(invx2, invx1, scaled_own)
    bx1, zx1, zu1 = inside_fields(
        s, be_ref, bm_ref, zt_ref, ut_ref, *(Tiles(ref, my, loads) for ref in (bx1, zx1, zu1))
    )
    bx = Joined(Tiles(bx2, my, loads), bx1, outside)
    zx = Joined(Tiles(zx2, my, loads), zx1, scaled_own)
    zu = Joined(Tiles(zu2, my, loads), zu1, scaled_own)
    qx, wx = joined(qx2, qx1, image_own), joined(wx2, wx1, image_own)
    wu = joined(wu2, wu1, image_own)
    own = [x - 2 for x in outer_planes(nx)]
    q_out, v_out = (Joined(Tiles(ref, ny, loads), None, own) for ref in (q_out, v_out))
    carry1, carry2, carry3 = (Tiles(ref, my, loads) for ref in (carry1, carry2, carry3))

    def conduct(ref, x):
        return conduct_of(ref[x * pitch : (x + 1) * pitch, :])

    low = [conduct(low_d, t) for t in range(3)] + [conduct(dens_ref, 0)]
    high = [conduct(dens_ref, nx - 1)] + [conduct(high_d, t) for t in range(2)]
    for x in range(3):
        inverse = inverse_of(s, low[x], low[x + 1])
        invx.put(x, inverse)
        if x < 2:
            cond.put(x, low[x + 1][1:])
    inv_out[...] = inverse[2 : 2 + ny]
    for x in range(2):
        invx.put(nx + 2 + x, inverse_of(s, high[x], high[x + 1]))
    cond.put(nx + 2, high[1][1:])

    batch = Batch(16)
    for ref, x0 in ((low_ref, 0), (high_ref, nx + 2)):
        tiles = Tiles(ref, my, loads)
        for dx in range(2):
            for y in range(my):
                tile = tiles[dx, y]
                batch.add(bx, (x0 + dx, y), tile)
                scaled = tile * invx[x0 + dx, y]
                batch.add(zx, (x0 + dx, y), scaled)
                batch.add(zu, (x0 + dx, y), up(scaled))
    for y in range(my):
        scaled = bx[2, y] * invx[2, y]
        batch.add(zx, (2, y), scaled)
        batch.add(zu, (2, y), up(scaled))
    batch.flush()

    emitter = First(bx, invx, qx, wx, wu)
    element_planes(cond, carry3, 0, 1, 0, my - 1, zx, zu, None)
    element_planes(cond, carry3, 1, 2, 0, my - 1, zx, zu, emitter)
    element_planes(cond, carry3, 3, 1, 0, my - 1, zx, zu, emitter, keep=False)
    element_planes(cond, carry1, nx + 1, 2, 0, my - 1, zx, zu, emitter, keep=False)
    sums = [sums1[place * loads : (place + 1) * loads, :] for place in range(4)]
    emitter = Second(bx, zx, qx, q_out, v_out, sums)
    element_planes(cond, carry3, 1, 1, 1, my - 3, wx, wu, None)
    element_planes(cond, carry3, 2, 2, 1, my - 3, wx, wu, emitter)
    element_planes(cond, carry3, 4, 1, 1, my - 3, wx, wu, emitter, keep=False)
    element_planes(cond, carry2, nx, 2, 1, my - 3, wx, wu, emitter, keep=False)
    lane = lane_ids(loads)
    load = lax.broadcasted_iota(jnp.int32, (loads, LANES), 0)
    packed = jnp.zeros((loads, LANES), jnp.float32)
    for place, part in enumerate(sums):
        total = jnp.sum(part, axis=1, keepdims=True)
        packed = packed + jnp.where(lane == place * loads + load, total, 0.0)
    row = jnp.sum(packed, axis=0, keepdims=True)
    sums_ref[...] = jnp.broadcast_to(row[None], sums_ref.shape)


def outer_planes(nx):
    return (2, 3, 4, nx, nx + 1)


def unpack_kernel(
    s, q1_ref, q2_ref, v1_ref, v2_ref, inv1_ref, inv2_ref, qo_ref, vo_ref, io_ref, q_ref, v_ref
):
    loads, nx, ny = s.loads, s.nx, s.ny
    batch = Batch()
    planes = outer_planes(nx)
    for first, second, whole in ((q1_ref, q2_ref, q_ref), (v1_ref, v2_ref, v_ref)):
        first, second = Tiles(first, ny, loads), Tiles(second, ny, loads)
        whole = Tiles(whole, ny, loads)
        for x in range(nx):
            for y in range(ny):
                if x + 2 in planes:
                    batch.add(whole, (x, y), second[planes.index(x + 2), y])
                else:
                    batch.add(whole, (x, y), first[x, y])
    batch.flush()
    batch = Batch()
    for x0 in range(0, nx, SUB):
        for ref, out in ((q_ref, qo_ref), (v_ref, vo_ref)):
            for load in range(loads):
                for block in range(packed_count(ny)):
                    tile = pack_block(
                        lambda y: ref[
                            pl.ds((x0 * ny + y) * loads + load, SUB, stride=ny * loads), :
                        ],
                        ny, block, SUB,
                    )
                    lanes = slice(block * LANES, (block + 1) * LANES)
                    batch.add(out, (load, slice(x0, x0 + SUB), lanes), tile)
        for block in range(packed_count(ny)):
            tile = pack_block(
                lambda y: inv1_ref[
                    pl.ds((x0 + 2) * s.pitch + y + 2, SUB, stride=s.pitch), :
                ],
                ny, block, SUB,
            )
            lanes = slice(block * LANES, (block + 1) * LANES)
            batch.add(io_ref, (slice(x0, x0 + SUB), lanes), tile)
    batch.flush()
    for block in range(packed_count(ny)):
        io_ref[0:1, block * LANES : (block + 1) * LANES] = pack_block(
            lambda y: inv2_ref[y : y + 1, :], ny, block, 1
        )


def finish_kernel(s, parts_ref, b_ref, q_ref, v_ref, inv_ref, x_hbm, r_hbm, x_ref, r_ref, sems):
    loads = s.loads
    totals = jnp.sum(parts_ref[...], axis=0)

    def part(place):
        return pltpu.roll(totals, (LANES - place * loads) % LANES, 1) if place else totals

    rz, near, square, last = (part(place) for place in range(4))
    direct = rz - near
    alpha = rz / direct
    short = -near / direct
    rz_next = short * short * rz + 2.0 * alpha * short * near + alpha * alpha * square
    beta = rz_next / rz
    grown = short + beta
    curved = (
        grown * grown * direct
        + 2.0 * alpha * grown * (near - square)
        + alpha * alpha * last
    )
    alpha_next = rz_next / curved
    first_row = alpha + alpha_next * (1.0 + beta)
    second_row = alpha_next * alpha
    inverse = inv_ref[...]
    copies = []
    for load in range(loads):
        first = first_row[:, load : load + 1]
        second = second_row[:, load : load + 1]
        source, image = b_ref[load], q_ref[load]
        x_ref[load] = (first * source - second * image) * inverse
        copies.append(pltpu.make_async_copy(x_ref.at[load], x_hbm.at[load], sems.at[0, load]))
        copies[-1].start()
        r_ref[load] = source - first * image + second * v_ref[load]
        copies.append(pltpu.make_async_copy(r_ref.at[load], r_hbm.at[load], sems.at[1, load]))
        copies[-1].start()
    for copy in copies:
        copy.wait()


def swap(array, axis, start):
    counts = {name: lax.axis_size(name) for name in ("gx", "gy")}
    other = "gy" if axis == "gx" else "gx"
    pairs = []
    for at in np.ndindex(counts["gx"], counts["gy"]):
        place = dict(zip(("gx", "gy"), at))
        partner = place[axis] + (1 if (place[axis] - start) % 2 == 0 else -1)
        if 0 <= partner < counts[axis]:
            place[axis] = partner
        elif place[other] ^ 1 < counts[other]:
            place[other] ^= 1
        pairs.append((at[0] * counts["gy"] + at[1], place["gx"] * counts["gy"] + place["gy"]))
    return lax.ppermute(array, ("gx", "gy"), pairs)


def per_device(heat_source, density):
    loads, nx, flat = heat_source.shape
    ny = flat // NZ
    s = Sizes(loads, nx, ny, lax.axis_size("gx"), lax.axis_size("gy"))
    nodes = nx * ny * loads
    devices = lax.axis_size("gx") * lax.axis_size("gy")

    def shape(*dims):
        return jax.ShapeDtypeStruct(dims, jnp.float32)

    def scratch(*dims):
        return pltpu.VMEM(dims, jnp.float32)

    def call(kernel, out_shape, **more):
        params = pltpu.CompilerParams(vmem_limit_bytes=20 * 1024 * 1024)
        return pl.pallas_call(
            functools.partial(kernel, s), out_shape=out_shape, compiler_params=params, **more
        )

    hbm = pl.BlockSpec(memory_space=pltpu.HBM)
    y_face, x_face, corner = (shape(rows, LANES) for rows in (s.y_rows, s.x_rows, s.c_rows))
    b, dt, x1, x2 = call(
        pack_x_kernel,
        (shape(packed_count(ny), loads * nx, LANES), shape(nx * ny, LANES), x_face, x_face),
        in_specs=[hbm, hbm],
        scratch_shapes=[scratch(nx, flat), pltpu.SemaphoreType.DMA((packed_count(ny) + 1,))],
    )(
        pltpu.with_memory_space_constraint(heat_source.reshape(loads * nx, flat), pltpu.HBM),
        pltpu.with_memory_space_constraint(density, pltpu.HBM),
    )
    x2, x1 = swap(x2, "gx", 1), swap(x1, "gx", 0)
    outer_columns = shape(nx * 4 * loads, LANES)
    be, y2 = call(pack_far_kernel, (outer_columns, y_face))(b, dt)
    y2 = swap(y2, "gy", 1)
    xt = shape(2 * ny * loads, LANES)
    xt2 = call(open_x_kernel, xt)(x2)
    xt2, be_later, dt_later = lax.optimization_barrier((xt2, be, dt))
    y1 = swap(call(pack_near_kernel, y_face)(be_later, dt_later), "gy", 0)
    t1 = call(open_y_kernel, shape(2 * nx * loads, LANES))(y1)
    inside = shape(nodes, LANES)
    bm, zt, ut, ct, it = call(
        scale_kernel,
        (shape(nx * (ny - 4) * loads, LANES),) + (inside,) * 4,
        scratch_shapes=[scratch(nx * ny, LANES)] * 2,
    )(b, be, dt_later)
    xt1, c1, c2 = call(
        corner_kernel,
        (xt, corner, corner),
        cost_estimate=pl.CostEstimate(flops=2 * 10**9, transcendentals=0, bytes_accessed=0),
    )(x2, xt2, x1)
    xt1, dt = lax.optimization_barrier((xt1, dt))
    c2, c1 = swap(c2, "gy", 1), swap(c1, "gy", 0)
    plane = s.my * loads
    rows, field = shape(s.mx * s.pitch, LANES), shape(s.mx * plane, LANES)
    edge = shape(2 * plane, LANES)
    dens, cond, inv_1, bx, zx, zu, q_x, w_x, w_u, q_1, v_1, carry1, carry2, sums = call(
        inner_kernel,
        (shape(nx * s.pitch, LANES),)
        + (rows,) * 2
        + (field,) * 6
        + (inside,) * 2
        + (edge,) * 2
        + (shape(4 * loads, LANES),),
    )(be, bm, zt, ut, ct, it, dt, y1, y2, t1)
    ends = shape(len(outer_planes(nx)) * ny * loads, LANES)
    q_2, v_2, inv_2, sums = call(
        outer_kernel,
        (ends, ends, shape(ny, LANES), shape(devices, 1, LANES)),
        scratch_shapes=[scratch(2 * plane, LANES)] * 2
        + [scratch(3 * s.pitch, LANES)] * 2
        + [scratch(5 * s.pitch, LANES)] * 2
        + [scratch(5 * plane, LANES)] * 6
        + [scratch(2 * plane, LANES)],
    )(be, bm, zt, ut, dens, x1, x2, xt1, xt2, c1, c2, cond, inv_1, bx, zx, zu, q_x, w_x, w_u, carry1, carry2, sums)
    parts = lax.all_to_all(sums, ("gx", "gy"), 0, 0, tiled=True)
    whole = shape(loads, nx, flat)
    image, again, inverse = call(
        unpack_kernel,
        (whole, whole, shape(nx, flat)),
        scratch_shapes=[scratch(nodes, LANES)] * 2,
    )(q_1, q_2, v_1, v_2, inv_1, inv_2)
    return call(
        finish_kernel,
        (whole, whole),
        out_specs=(hbm, hbm),
        scratch_shapes=[
            scratch(loads, nx, flat),
            scratch(loads, nx, flat),
            pltpu.SemaphoreType.DMA((2, loads)),
        ],
    )(parts, heat_source, image, again, inverse)


def solution(mesh):
    placed = (P(None, "gx", "gy"), P("gx", "gy"))
    return jax.shard_map(
        per_device,
        mesh=mesh,
        in_specs=placed,
        out_specs=(P(None, "gx", "gy"), P(None, "gx", "gy")),
        check_vma=False,
    )
```

```python
import functools

import jax
import jax.numpy as jnp
import numpy as np
from jax import lax
from jax.experimental import pallas as pl
from jax.experimental.pallas import tpu as pltpu
from jax.sharding import PartitionSpec as P

NZ = 96
KMIN = 0.001
LANES = 128
SUB = 8


class Batch:
    def __init__(self, size=12):
        self.size, self.held = size, []

    def add(self, into, at, tile):
        self.held.append((into, at, tile))
        if len(self.held) >= self.size:
            self.flush()

    def flush(self):
        for into, at, tile in self.held:
            into[at] = tile
        self.held = []


def packed_count(tiles):
    return -(-tiles * NZ // LANES)


def lane_ids(rows):
    return lax.broadcasted_iota(jnp.int32, (rows, LANES), 1)


def unpack_tile(read, index, rows):
    start = index * NZ
    block, offset = start // LANES, start % LANES
    lane = lane_ids(rows)
    first = read(block)
    if offset:
        first = pltpu.roll(first, LANES - offset, 1)
    if offset + NZ > LANES:
        second = pltpu.roll(read(block + 1), LANES - offset, 1)
        first = jnp.where(lane < LANES - offset, first, second)
    return jnp.where(lane < NZ, first, 0.0)


def pack_block(read_tile, tiles, block, rows):
    lane = lane_ids(rows)
    start = block * LANES
    out, at = None, start
    while at < start + LANES and at // NZ < tiles:
        index, z = at // NZ, at % NZ
        here = at - start
        piece = read_tile(index)
        shift = (here - z) % LANES
        if shift:
            piece = pltpu.roll(piece, shift, 1)
        out = piece if out is None else jnp.where(lane < here, out, piece)
        at += NZ - z
    return out


def pack_tiles(out_ref, at, rows, tiles, read_tile):
    batch = Batch()
    for block in range(packed_count(tiles)):
        place = slice(at + block * rows, at + (block + 1) * rows), slice(None)
        batch.add(out_ref, place, pack_block(read_tile, tiles, block, rows))
    batch.flush()


def unpack_tiles(ref, at, rows, tiles, write):
    batch = Batch()
    for index in range(tiles):
        tile = unpack_tile(lambda t: ref[at + t * rows : at + (t + 1) * rows, :], index, rows)
        for store in write(index, tile):
            batch.add(*store)
    batch.flush()


class Sizes:
    def __init__(self, loads, nx, ny, count_x, count_y):
        self.loads, self.nx, self.ny = loads, nx, ny
        self.count_x, self.count_y = count_x, count_y
        self.mx, self.my = nx + 4, ny + 4
        self.pitch = -(-(ny + 6) // SUB) * SUB
        self.y_dens = packed_count(2 * nx) * loads
        self.y_rows = self.y_dens + 3 * nx
        self.x_dens = packed_count(2 * ny) * loads
        self.x_rows = self.x_dens + 3 * ny
        self.c_dens = packed_count(8) * loads
        self.c_rows = self.c_dens + -(-18 // SUB) * SUB


class Tiles:
    def __init__(self, ref, columns, loads):
        self.ref, self.columns, self.loads = ref, columns, loads

    def rows(self, at):
        start = (at[0] * self.columns + at[1]) * self.loads
        if not isinstance(start, int):
            start = pl.multiple_of(start, SUB)
        return pl.ds(start, self.loads)

    def __getitem__(self, at):
        return self.ref[self.rows(at), :]

    def __setitem__(self, at, tile):
        self.ref[self.rows(at), :] = tile


class Rows:
    def __init__(self, ref, pitch, loads):
        self.ref, self.pitch, self.loads = ref, pitch, loads

    def __getitem__(self, at):
        row = self.ref[pl.ds(at[0] * self.pitch + at[1], 1), :]
        return jnp.broadcast_to(row, (self.loads, LANES))

    def put(self, x, values):
        self.ref[x * self.pitch : x * self.pitch + values.shape[0], :] = values


class Joined:
    def __init__(self, first, second, own):
        self.first, self.second, self.own = first, second, own

    def __getitem__(self, at):
        if at[0] in self.own:
            return self.first[self.own.index(at[0]), at[1]]
        return self.second[at]

    def __setitem__(self, at, tile):
        self.first[self.own.index(at[0]), at[1]] = tile

    def put(self, x, values):
        self.first.put(self.own.index(x), values)


class Halves:
    def __init__(self, outer_ref, middle_ref, ny, loads):
        self.edge = (0, 1, ny - 2, ny - 1)
        self.outer, self.middle = Tiles(outer_ref, 4, loads), Tiles(middle_ref, ny - 4, loads)

    def __getitem__(self, at):
        if at[1] in self.edge:
            return self.outer[at[0], self.edge.index(at[1])]
        return self.middle[at[0], at[1] - 2]


class Inside:
    def __init__(self, inner, own, outer):
        self.inner, self.own, self.outer = inner, own, outer

    def __getitem__(self, at):
        if at[1] in self.own:
            return self.inner[at[0] - 2, at[1] - 2]
        return self.outer[at]

    def __setitem__(self, at, tile):
        self.outer[at] = tile


def is_even(axis):
    return lax.rem(lax.axis_index(axis), 2) == 0


def is_alone(axis, count, start):
    place = lax.axis_index(axis)
    last = (count - start) % 2
    alone = place < start
    return jnp.logical_or(alone, place == count - 1) if last else alone


def pick(even, if_even, if_odd):
    return jnp.where(even, if_even, if_odd)


def pack_x_kernel(s, b_hbm, d_hbm, b_ref, dt_ref, x1_ref, x2_ref, d_ref, sems):
    loads, nx, ny = s.loads, s.nx, s.ny
    blocks = packed_count(ny)
    d_copy = pltpu.make_async_copy(d_hbm, d_ref, sems.at[blocks])
    d_copy.start()
    copies = []
    for block in range(blocks):
        lanes = pl.ds(block * LANES, LANES)
        copies.append(
            pltpu.make_async_copy(b_hbm.at[:, lanes], b_ref.at[block], sems.at[block])
        )
        copies[-1].start()
    d_copy.wait()
    batch = Batch(16)
    for x0 in range(0, nx, SUB):
        for y in range(ny):
            tile = unpack_tile(
                lambda t: d_ref[x0 : x0 + SUB, t * LANES : (t + 1) * LANES], y, SUB
            )
            batch.add(dt_ref, (pl.ds(x0 * ny + y, SUB, stride=ny), slice(None)), tile)
    batch.flush()
    even_x = is_even("gx")
    for ref, upper in ((x2_ref, jnp.logical_not(even_x)), (x1_ref, even_x)):
        rows = pl.ds(pl.multiple_of(pick(upper, nx - 3, 0) * ny, SUB), 3 * ny)
        ref[s.x_dens :, :] = dt_ref[rows, :]
    for copy in copies:
        copy.wait()
    batch = Batch()
    for ref, upper in ((x2_ref, jnp.logical_not(even_x)), (x1_ref, even_x)):
        x0 = pick(upper, nx - 2, 0)
        for dx in range(2):
            for block in range(blocks):
                tile = b_ref[block, pl.ds(x0 + dx, loads, stride=nx), :]
                at = (dx * blocks + block) * loads
                batch.add(ref, (slice(at, at + loads), slice(None)), tile)
    batch.flush()


def lay_out(s, b_ref, columns, out_ref):
    loads, nx, count = s.loads, s.nx, len(columns)
    batch = Batch(16)
    for load in range(loads):
        for x0 in range(0, nx, SUB):
            at = load * nx + x0
            for place, y in enumerate(columns):
                tile = unpack_tile(lambda t: b_ref[t, at : at + SUB, :], y, SUB)
                rows = pl.ds((x0 * count + place) * loads + load, SUB, stride=count * loads)
                batch.add(out_ref, (rows, slice(None)), tile)
    batch.flush()


def pack_far_kernel(s, b_ref, dt_ref, be_ref, y2_ref):
    lay_out(s, b_ref, (0, 1, s.ny - 2, s.ny - 1), be_ref)
    pack_y_face(s, jnp.logical_not(is_even("gy")), be_ref, dt_ref, y2_ref)


def pack_near_kernel(s, be_ref, dt_ref, y1_ref):
    pack_y_face(s, is_even("gy"), be_ref, dt_ref, y1_ref)


def pack_y_face(s, upper, be_ref, dt_ref, out_ref):
    loads, nx, ny = s.loads, s.nx, s.ny
    tiles = Tiles(be_ref, 4, loads)
    y0 = pick(upper, 2, 0)
    pack_tiles(out_ref, 0, loads, 2 * nx, lambda i: tiles[i // 2, y0 + i % 2])
    y0 = pick(upper, ny - 3, 0)
    batch = Batch()
    for dy in range(3):
        for x0 in range(0, nx, SUB):
            at = s.y_dens + dy * nx + x0
            tile = dt_ref[pl.ds(x0 * ny + y0 + dy, SUB, stride=ny), :]
            batch.add(out_ref, (slice(at, at + SUB), slice(None)), tile)
    batch.flush()


def open_y_kernel(s, y_ref, t_ref):
    tiles = Tiles(t_ref, 2, s.loads)
    unpack_tiles(
        y_ref, 0, s.loads, 2 * s.nx, lambda i, tile: [(tiles, (i // 2, i % 2), tile)]
    )


def open_x_kernel(s, x_ref, t_ref):
    tiles = Tiles(t_ref, s.ny, s.loads)
    unpack_tiles(
        x_ref, 0, s.loads, 2 * s.ny, lambda i, tile: [(tiles, (i // s.ny, i % s.ny), tile)]
    )


def corner_kernel(s, x2_ref, t2_ref, x1_ref, t1_ref, c1_ref, c2_ref):
    loads, ny = s.loads, s.ny
    open_x_kernel(s, x1_ref, t1_ref)
    halves = Tiles(t1_ref, ny, loads), Tiles(t2_ref, ny, loads)
    even_y = is_even("gy")
    for out_ref, upper in ((c2_ref, jnp.logical_not(even_y)), (c1_ref, even_y)):
        y0 = pick(upper, ny - 2, 0)
        pack_tiles(out_ref, 0, loads, 8, lambda i: halves[i // 4][i // 2 % 2, y0 + i % 2])
        y0 = pick(upper, ny - 3, 0)
        batch, at = Batch(18), s.c_dens
        for ref in (x1_ref, x2_ref):
            for t in range(3):
                for dy in range(3):
                    row = ref[pl.ds(s.x_dens + t * ny + y0 + dy, 1), :]
                    batch.add(out_ref, (slice(at, at + 1), slice(None)), row)
                    at += 1
        batch.flush()
        out_ref[at:, :] = jnp.zeros((s.c_rows - at, LANES), jnp.float32)


def join_density(s, dt_ref, y1_ref, y2_ref, dens_ref):
    nx, ny, pitch = s.nx, s.ny, s.pitch
    even_y = is_even("gy")
    yd = (pick(even_y, ny + 3, 0), pick(even_y, 0, ny + 3))
    batch = Batch(16)
    for x in range(nx):
        at = x * pitch
        batch.add(
            dens_ref, (slice(at + 3, at + 3 + ny), slice(None)), dt_ref[x * ny : (x + 1) * ny, :]
        )
    batch.flush()
    for side, ref in enumerate((y1_ref, y2_ref)):
        alone = is_alone("gy", s.count_y, side)
        for dy in range(3):
            for x0 in range(0, nx, SUB):
                at = s.y_dens + dy * nx + x0
                to = x0 * pitch + yd[side] + dy
                batch.add(
                    dens_ref,
                    (pl.ds(to, SUB, stride=pitch), slice(None)),
                    jnp.where(alone, 0.0, ref[at : at + SUB, :]),
                )
    batch.flush()


def conduct_of(dens):
    return jnp.where(
        dens > 0.0, (KMIN + (1.0 - KMIN) * (dens * dens * dens)) * (1.0 / 12.0), 0.0
    )


def inverse_of(s, before, after):
    pair = before + after
    pair = pair[: s.pitch - 1] + pair[1:]
    total = 4.0 * (pair + pltpu.roll(pair, 1, 1))
    return jnp.where(after[1:] > 0.0, 1.0 / total, 0.0)


def up(tile):
    return pltpu.roll(tile, LANES - 1, 1)


def element_planes(cond, carry, a, count, y0, columns, field, field_up, emitter, keep=True):
    def loads_of(step):
        y = y0 + step
        right = [(field[a + u, y + 1], field_up[a + u, y + 1]) for u in range(count + 1)]
        conduct = [cond[a + u, y] for u in range(count)]
        above = extra = None
        if step and emitter:
            above = (carry[0, y], carry[1, y])
            extra = [emitter.fetch(a + u, y) for u in range(count)]
        return right, conduct, above, extra

    left = [(field[a + u, y0], field_up[a + u, y0]) for u in range(count + 1)]
    ahead = loads_of(0)
    old, waiting = [None] * count, []
    for step in range(columns):
        y = y0 + step
        right, conduct, above, extra = ahead
        if step + 1 < columns:
            ahead = loads_of(step + 1)
        if len(waiting) > 1:
            for into, at, tile in waiting.pop(0):
                into[at] = tile
        stores = []
        for u in range(count):
            (p0, p0s), (p1, p1s) = left[u], left[u + 1]
            (r0, r0s), (r1, r1s) = right[u], right[u + 1]
            c = conduct[u]
            even = (p0 + r1) + (r0s + p1s)
            odd = (r0 + p1) + (p0s + r1s)
            pass_on = keep or u + 1 < count
            lower = upper = None
            if emitter:
                lower = (c * (odd + p1s), c * (even + p1))
            if pass_on:
                upper = (c * (even + p0s), c * (odd + p0))
            if step and emitter:
                low = (c * (even + r1s) + old[u][0][0]) + above[0]
                high = (c * (odd + r1) + old[u][0][1]) + above[1]
                total = low + pltpu.roll(high, 1, 1)
                stores += emitter.finish(a + u, y, p0, total, extra[u])
            if step and pass_on:
                above = (
                    c * (odd + r0s) + old[u][1][0],
                    c * (even + r0) + old[u][1][1],
                )
            old[u] = (lower, upper)
        if step and keep:
            stores += [(carry, (0, y), above[0]), (carry, (1, y), above[1])]
        waiting.append(stores)
        left = right
    for stores in waiting:
        for into, at, tile in stores:
            into[at] = tile


class First:
    def __init__(self, bx, invx, qx, wx, wu):
        self.bx, self.invx, self.qx, self.wx, self.wu = bx, invx, qx, wx, wu

    def fetch(self, x, y):
        return self.bx[x, y], self.invx[x, y]

    def finish(self, x, y, node, total, extra):
        source, inverse = extra
        image = 1.25 * source - total
        weighted = image * inverse
        at = x, y
        return [(self.qx, at, image), (self.wx, at, weighted), (self.wu, at, up(weighted))]


class Second:
    def __init__(self, bx, zx, qx, q_out, v_out, sums):
        self.bx, self.zx, self.qx, self.sums = bx, zx, qx, sums
        self.q_out, self.v_out = q_out, v_out

    def fetch(self, x, y):
        return self.bx[x, y], self.zx[x, y], self.qx[x, y]

    def finish(self, x, y, weighted, total, extra):
        source, scaled, image = extra
        again = 1.25 * image - total
        change = scaled - weighted
        sums = self.sums
        sums[0] = sums[0] + source * scaled
        sums[1] = sums[1] + source * change
        sums[2] = sums[2] + (source - image) * change
        sums[3] = sums[3] + (image - again) * change
        at = x - 2, y - 2
        return [(self.q_out, at, image), (self.v_out, at, again)]


def over_planes(start, stop, body, state):
    groups, rest = (stop - start) // 3, (stop - start) % 3
    state = lax.fori_loop(0, groups, lambda i, st: body(start + 3 * i, 3, st), state)
    if rest:
        state = body(stop - rest, rest, state)
    return state


def inside_fields(s, be_ref, bm_ref, zt_ref, ut_ref, bx, zx, zu):
    brick = [Halves(be_ref, bm_ref, s.ny, s.loads)]
    brick += [Tiles(ref, s.ny, s.loads) for ref in (zt_ref, ut_ref)]
    starts = (2, 3, 3)
    return tuple(
        Inside(inner, range(start, s.ny + 2), outer)
        for inner, start, outer in zip(brick, starts, (bx, zx, zu))
    )


def scale_kernel(
    s, b_ref, be_ref, dt_ref, bm_ref, zt_ref, ut_ref, ct_ref, it_ref, cond_ref, inv_ref
):
    loads, nx, ny = s.loads, s.nx, s.ny
    lay_out(s, b_ref, range(2, ny - 2), bm_ref)
    inner = Halves(be_ref, bm_ref, ny, loads)
    scaled, shifted, cond_t, inv_t = (
        Tiles(ref, ny, loads) for ref in (zt_ref, ut_ref, ct_ref, it_ref)
    )
    cond, inverse = Rows(cond_ref, ny, loads), Rows(inv_ref, ny, loads)
    before = None
    for x in range(nx):
        after = conduct_of(dt_ref[x * ny : (x + 1) * ny, :])
        cond.put(x, after)
        if x:
            pair = before + after
            pair = pair[: ny - 1] + pair[1:]
            total = 4.0 * (pair + pltpu.roll(pair, 1, 1))
            inverse.put(x, jnp.where(after[1:] > 0.0, 1.0 / total, 0.0))
        before = after
    batch = Batch(16)
    for x in range(nx):
        for y in range(ny):
            batch.add(cond_t, (x, y), cond[x, y])
            if x and y:
                row = inverse[x, y - 1]
                tile = inner[x, y] * row
                batch.add(inv_t, (x, y), row)
                batch.add(scaled, (x, y), tile)
                batch.add(shifted, (x, y), up(tile))
    batch.flush()


def inner_kernel(
    s, be_ref, bm_ref, zt_ref, ut_ref, ct_ref, it_ref, dt_ref, y1_ref, y2_ref, t1_ref,
    dens_ref, cond, invx, bx, zx, zu, qx, wx, wu, q_out, v_out, carry1, carry2, sums_ref,
):
    loads, nx, ny, my, pitch = s.loads, s.nx, s.ny, s.my, s.pitch
    bx, zx, zu, qx, wx, wu, carry1, carry2 = (
        Tiles(ref, my, loads) for ref in (bx, zx, zu, qx, wx, wu, carry1, carry2)
    )
    q_out, v_out = Tiles(q_out, ny, loads), Tiles(v_out, ny, loads)
    cond, invx = Rows(cond, pitch, loads), Rows(invx, pitch, loads)
    join_density(s, dt_ref, y1_ref, y2_ref, dens_ref)
    even_y = is_even("gy")
    ys = (pick(even_y, ny + 2, 0), pick(even_y, 0, ny + 2))
    before = None
    for x in range(nx):
        after = conduct_of(dens_ref[x * pitch : (x + 1) * pitch, :])
        cond.put(x + 2, after[1:])
        if x:
            invx.put(x + 2, inverse_of(s, before, after))
        before = after

    bx, zx, zu = inside_fields(s, be_ref, bm_ref, zt_ref, ut_ref, bx, zx, zu)

    def stage(x, y, tile):
        stores = [(bx, (x + 2, y), tile)]
        if x:
            scaled = tile * invx[x + 2, y]
            stores += [(zx, (x + 2, y), scaled), (zu, (x + 2, y), up(scaled))]
        return stores

    batch = Batch(16)
    for x in range(1, nx):
        scaled = bx[x + 2, 2] * invx[x + 2, 2]
        batch.add(zx, (x + 2, 2), scaled)
        batch.add(zu, (x + 2, 2), up(scaled))
    batch.flush()
    unpack_tiles(
        y2_ref, 0, loads, 2 * nx, lambda i, tile: stage(i // 2, ys[1] + i % 2, tile)
    )
    near = Tiles(t1_ref, 2, loads)
    batch = Batch(16)
    for x in range(nx):
        for dy in range(2):
            for store in stage(x, ys[0] + dy, near[x, dy]):
                batch.add(*store)
    batch.flush()

    cond = Inside(Tiles(ct_ref, ny, loads), range(2, ny + 2), cond)
    invx = Inside(Tiles(it_ref, ny, loads), range(3, ny + 2), invx)
    element_planes(cond, carry1, 3, 1, 0, my - 1, zx, zu, None)

    def first(a, count, state):
        emitter = First(bx, invx, qx, wx, wu)
        element_planes(cond, carry1, a, count, 0, my - 1, zx, zu, emitter)
        return state

    over_planes(4, nx + 1, first, 0)
    element_planes(cond, carry2, 4, 1, 1, my - 3, wx, wu, None)

    def second(a, count, sums):
        sums = list(sums)
        emitter = Second(bx, zx, qx, q_out, v_out, sums)
        element_planes(cond, carry2, a, count, 1, my - 3, wx, wu, emitter)
        return tuple(sums)

    zero = jnp.zeros((loads, LANES), jnp.float32)
    sums = over_planes(5, nx, second, (zero,) * 4)
    for place, part in enumerate(sums):
        sums_ref[place * loads : (place + 1) * loads, :] = part


def outer_kernel(
    s, be_ref, bm_ref, zt_ref, ut_ref, dens_ref, x1_ref, x2_ref, t1_ref, t2_ref, c1_ref, c2_ref,
    cond1, invx1, bx1, zx1, zu1, qx1, wx1, wu1, carry1, carry2, sums1,
    q_out, v_out, inv_out, sums_ref,
    low_ref, high_ref, low_d, high_d, cond2, invx2, bx2, zx2, zu2, qx2, wx2, wu2, carry3,
):
    loads, nx, ny, mx, my, pitch = s.loads, s.nx, s.ny, s.mx, s.my, s.pitch
    even_x = is_even("gx")

    even_y = is_even("gy")
    ys = (pick(even_y, ny + 2, 0), pick(even_y, 0, ny + 2))
    yd = (pick(even_y, ny + 3, 0), pick(even_y, 0, ny + 3))

    def take(near, far):
        faces = (x1_ref, t1_ref, near), (x2_ref, t2_ref, far)
        for side, (ref, face_ref, (tiles_ref, into)) in enumerate(faces):
            face, tiles = Tiles(face_ref, ny, loads), Tiles(tiles_ref, my, loads)
            alone_x = is_alone("gx", s.count_x, side)
            batch = Batch(18)
            for dx in range(2):
                for y in range(ny):
                    batch.add(tiles, (dx, y + 2), face[dx, y])
            for t in range(3):
                at = s.x_dens + t * ny
                rows = jnp.where(alone_x, 0.0, ref[at : at + ny, :])
                to = t * pitch + 3
                batch.add(into, (slice(to, to + ny), slice(None)), rows)
            batch.flush()
            for end, corner in enumerate((c1_ref, c2_ref)):
                alone = jnp.logical_or(alone_x, is_alone("gy", s.count_y, end))
                for i in range(4):
                    tile = unpack_tile(
                        lambda t: corner[t * loads : (t + 1) * loads, :], 4 * side + i, loads
                    )
                    batch.add(tiles, (i // 2, ys[end] + i % 2), tile)
                for i in range(9):
                    at = s.c_dens + 9 * side + i
                    row = jnp.where(alone, 0.0, corner[at : at + 1, :])
                    to = i // 3 * pitch + yd[end] + i % 3
                    batch.add(into, (pl.ds(to, 1), slice(None)), row)
            batch.flush()

    @pl.when(even_x)
    def _():
        take((high_ref, high_d), (low_ref, low_d))

    @pl.when(jnp.logical_not(even_x))
    def _():
        take((low_ref, low_d), (high_ref, high_d))

    def joined(first, second, own):
        return Joined(Tiles(first, my, loads), Tiles(second, my, loads), own)

    def joined_rows(first, second, own):
        return Joined(Rows(first, pitch, loads), Rows(second, pitch, loads), own)

    outside = (0, 1, nx + 2, nx + 3)
    scaled_own = outside + (2,)
    image_own = (1, 2, 3, nx + 1, nx + 2)
    cond, invx = joined_rows(cond2, cond1, outside), joined_rows(invx2, invx1, scaled_own)
    bx1, zx1, zu1 = inside_fields(
        s, be_ref, bm_ref, zt_ref, ut_ref, *(Tiles(ref, my, loads) for ref in (bx1, zx1, zu1))
    )
    bx = Joined(Tiles(bx2, my, loads), bx1, outside)
    zx = Joined(Tiles(zx2, my, loads), zx1, scaled_own)
    zu = Joined(Tiles(zu2, my, loads), zu1, scaled_own)
    qx, wx = joined(qx2, qx1, image_own), joined(wx2, wx1, image_own)
    wu = joined(wu2, wu1, image_own)
    own = [x - 2 for x in outer_planes(nx)]
    q_out, v_out = (Joined(Tiles(ref, ny, loads), None, own) for ref in (q_out, v_out))
    carry1, carry2, carry3 = (Tiles(ref, my, loads) for ref in (carry1, carry2, carry3))

    def conduct(ref, x):
        return conduct_of(ref[x * pitch : (x + 1) * pitch, :])

    low = [conduct(low_d, t) for t in range(3)] + [conduct(dens_ref, 0)]
    high = [conduct(dens_ref, nx - 1)] + [conduct(high_d, t) for t in range(2)]
    for x in range(3):
        inverse = inverse_of(s, low[x], low[x + 1])
        invx.put(x, inverse)
        if x < 2:
            cond.put(x, low[x + 1][1:])
    inv_out[...] = inverse[2 : 2 + ny]
    for x in range(2):
        invx.put(nx + 2 + x, inverse_of(s, high[x], high[x + 1]))
    cond.put(nx + 2, high[1][1:])

    batch = Batch(16)
    for ref, x0 in ((low_ref, 0), (high_ref, nx + 2)):
        tiles = Tiles(ref, my, loads)
        for dx in range(2):
            for y in range(my):
                tile = tiles[dx, y]
                batch.add(bx, (x0 + dx, y), tile)
                scaled = tile * invx[x0 + dx, y]
                batch.add(zx, (x0 + dx, y), scaled)
                batch.add(zu, (x0 + dx, y), up(scaled))
    for y in range(my):
        scaled = bx[2, y] * invx[2, y]
        batch.add(zx, (2, y), scaled)
        batch.add(zu, (2, y), up(scaled))
    batch.flush()

    emitter = First(bx, invx, qx, wx, wu)
    element_planes(cond, carry3, 0, 1, 0, my - 1, zx, zu, None)
    element_planes(cond, carry3, 1, 2, 0, my - 1, zx, zu, emitter)
    element_planes(cond, carry3, 3, 1, 0, my - 1, zx, zu, emitter, keep=False)
    element_planes(cond, carry1, nx + 1, 2, 0, my - 1, zx, zu, emitter, keep=False)
    sums = [sums1[place * loads : (place + 1) * loads, :] for place in range(4)]
    emitter = Second(bx, zx, qx, q_out, v_out, sums)
    element_planes(cond, carry3, 1, 1, 1, my - 3, wx, wu, None)
    element_planes(cond, carry3, 2, 2, 1, my - 3, wx, wu, emitter)
    element_planes(cond, carry3, 4, 1, 1, my - 3, wx, wu, emitter, keep=False)
    element_planes(cond, carry2, nx, 2, 1, my - 3, wx, wu, emitter, keep=False)
    lane = lane_ids(loads)
    load = lax.broadcasted_iota(jnp.int32, (loads, LANES), 0)
    packed = jnp.zeros((loads, LANES), jnp.float32)
    for place, part in enumerate(sums):
        total = jnp.sum(part, axis=1, keepdims=True)
        packed = packed + jnp.where(lane == place * loads + load, total, 0.0)
    row = jnp.sum(packed, axis=0, keepdims=True)
    sums_ref[...] = jnp.broadcast_to(row[None], sums_ref.shape)


def outer_planes(nx):
    return (2, 3, 4, nx, nx + 1)


def unpack_kernel(
    s, q1_ref, q2_ref, v1_ref, v2_ref, inv1_ref, inv2_ref, qo_ref, vo_ref, io_ref, q_ref, v_ref
):
    loads, nx, ny = s.loads, s.nx, s.ny
    batch = Batch()
    planes = outer_planes(nx)
    for first, second, whole in ((q1_ref, q2_ref, q_ref), (v1_ref, v2_ref, v_ref)):
        first, second = Tiles(first, ny, loads), Tiles(second, ny, loads)
        whole = Tiles(whole, ny, loads)
        for x in range(nx):
            for y in range(ny):
                if x + 2 in planes:
                    batch.add(whole, (x, y), second[planes.index(x + 2), y])
                else:
                    batch.add(whole, (x, y), first[x, y])
    batch.flush()
    batch = Batch()
    for x0 in range(0, nx, SUB):
        for ref, out in ((q_ref, qo_ref), (v_ref, vo_ref)):
            for load in range(loads):
                for block in range(packed_count(ny)):
                    tile = pack_block(
                        lambda y: ref[
                            pl.ds((x0 * ny + y) * loads + load, SUB, stride=ny * loads), :
                        ],
                        ny, block, SUB,
                    )
                    lanes = slice(block * LANES, (block + 1) * LANES)
                    batch.add(out, (load, slice(x0, x0 + SUB), lanes), tile)
        for block in range(packed_count(ny)):
            tile = pack_block(
                lambda y: inv1_ref[
                    pl.ds((x0 + 2) * s.pitch + y + 2, SUB, stride=s.pitch), :
                ],
                ny, block, SUB,
            )
            lanes = slice(block * LANES, (block + 1) * LANES)
            batch.add(io_ref, (slice(x0, x0 + SUB), lanes), tile)
    batch.flush()
    for block in range(packed_count(ny)):
        io_ref[0:1, block * LANES : (block + 1) * LANES] = pack_block(
            lambda y: inv2_ref[y : y + 1, :], ny, block, 1
        )


def finish_kernel(s, parts_ref, b_ref, q_ref, v_ref, inv_ref, x_hbm, r_hbm, x_ref, r_ref, sems):
    loads = s.loads
    totals = jnp.sum(parts_ref[...], axis=0)

    def part(place):
        return pltpu.roll(totals, (LANES - place * loads) % LANES, 1) if place else totals

    rz, near, square, last = (part(place) for place in range(4))
    direct = rz - near
    alpha = rz / direct
    short = -near / direct
    rz_next = short * short * rz + 2.0 * alpha * short * near + alpha * alpha * square
    beta = rz_next / rz
    grown = short + beta
    curved = (
        grown * grown * direct
        + 2.0 * alpha * grown * (near - square)
        + alpha * alpha * last
    )
    alpha_next = rz_next / curved
    first_row = alpha + alpha_next * (1.0 + beta)
    second_row = alpha_next * alpha
    inverse = inv_ref[...]
    copies = []
    for load in range(loads):
        first = first_row[:, load : load + 1]
        second = second_row[:, load : load + 1]
        source, image = b_ref[load], q_ref[load]
        x_ref[load] = (first * source - second * image) * inverse
        copies.append(pltpu.make_async_copy(x_ref.at[load], x_hbm.at[load], sems.at[0, load]))
        copies[-1].start()
        r_ref[load] = source - first * image + second * v_ref[load]
        copies.append(pltpu.make_async_copy(r_ref.at[load], r_hbm.at[load], sems.at[1, load]))
        copies[-1].start()
    for copy in copies:
        copy.wait()


def swap(array, axis, start):
    counts = {name: lax.axis_size(name) for name in ("gx", "gy")}
    other = "gy" if axis == "gx" else "gx"
    pairs = []
    for at in np.ndindex(counts["gx"], counts["gy"]):
        place = dict(zip(("gx", "gy"), at))
        partner = place[axis] + (1 if (place[axis] - start) % 2 == 0 else -1)
        if 0 <= partner < counts[axis]:
            place[axis] = partner
        elif place[other] ^ 1 < counts[other]:
            place[other] ^= 1
        pairs.append((at[0] * counts["gy"] + at[1], place["gx"] * counts["gy"] + place["gy"]))
    return lax.ppermute(array, ("gx", "gy"), pairs)


def per_device(heat_source, density):
    loads, nx, flat = heat_source.shape
    ny = flat // NZ
    s = Sizes(loads, nx, ny, lax.axis_size("gx"), lax.axis_size("gy"))
    nodes = nx * ny * loads
    devices = lax.axis_size("gx") * lax.axis_size("gy")

    def shape(*dims):
        return jax.ShapeDtypeStruct(dims, jnp.float32)

    def scratch(*dims):
        return pltpu.VMEM(dims, jnp.float32)

    def call(kernel, out_shape, **more):
        params = pltpu.CompilerParams(vmem_limit_bytes=20 * 1024 * 1024)
        return pl.pallas_call(
            functools.partial(kernel, s), out_shape=out_shape, compiler_params=params, **more
        )

    hbm = pl.BlockSpec(memory_space=pltpu.HBM)
    y_face, x_face, corner = (shape(rows, LANES) for rows in (s.y_rows, s.x_rows, s.c_rows))
    b, dt, x1, x2 = call(
        pack_x_kernel,
        (shape(packed_count(ny), loads * nx, LANES), shape(nx * ny, LANES), x_face, x_face),
        in_specs=[hbm, hbm],
        scratch_shapes=[scratch(nx, flat), pltpu.SemaphoreType.DMA((packed_count(ny) + 1,))],
    )(
        pltpu.with_memory_space_constraint(heat_source.reshape(loads * nx, flat), pltpu.HBM),
        pltpu.with_memory_space_constraint(density, pltpu.HBM),
    )
    x2, x1 = swap(x2, "gx", 1), swap(x1, "gx", 0)
    outer_columns = shape(nx * 4 * loads, LANES)
    be, y2 = call(pack_far_kernel, (outer_columns, y_face))(b, dt)
    y2 = swap(y2, "gy", 1)
    xt = shape(2 * ny * loads, LANES)
    xt2 = call(open_x_kernel, xt)(x2)
    xt2, be_later, dt_later = lax.optimization_barrier((xt2, be, dt))
    y1 = swap(call(pack_near_kernel, y_face)(be_later, dt_later), "gy", 0)
    t1 = call(open_y_kernel, shape(2 * nx * loads, LANES))(y1)
    inside = shape(nodes, LANES)
    bm, zt, ut, ct, it = call(
        scale_kernel,
        (shape(nx * (ny - 4) * loads, LANES),) + (inside,) * 4,
        scratch_shapes=[scratch(nx * ny, LANES)] * 2,
    )(b, be, dt_later)
    xt1, c1, c2 = call(
        corner_kernel,
        (xt, corner, corner),
        cost_estimate=pl.CostEstimate(flops=2 * 10**9, transcendentals=0, bytes_accessed=0),
    )(x2, xt2, x1)
    xt1, dt = lax.optimization_barrier((xt1, dt))
    c2, c1 = swap(c2, "gy", 1), swap(c1, "gy", 0)
    plane = s.my * loads
    rows, field = shape(s.mx * s.pitch, LANES), shape(s.mx * plane, LANES)
    edge = shape(2 * plane, LANES)
    dens, cond, inv_1, bx, zx, zu, q_x, w_x, w_u, q_1, v_1, carry1, carry2, sums = call(
        inner_kernel,
        (shape(nx * s.pitch, LANES),)
        + (rows,) * 2
        + (field,) * 6
        + (inside,) * 2
        + (edge,) * 2
        + (shape(4 * loads, LANES),),
    )(be, bm, zt, ut, ct, it, dt, y1, y2, t1)
    ends = shape(len(outer_planes(nx)) * ny * loads, LANES)
    q_2, v_2, inv_2, sums = call(
        outer_kernel,
        (ends, ends, shape(ny, LANES), shape(devices, 1, LANES)),
        scratch_shapes=[scratch(2 * plane, LANES)] * 2
        + [scratch(3 * s.pitch, LANES)] * 2
        + [scratch(5 * s.pitch, LANES)] * 2
        + [scratch(5 * plane, LANES)] * 6
        + [scratch(2 * plane, LANES)],
    )(be, bm, zt, ut, dens, x1, x2, xt1, xt2, c1, c2, cond, inv_1, bx, zx, zu, q_x, w_x, w_u, carry1, carry2, sums)
    parts = lax.all_to_all(sums, ("gx", "gy"), 0, 0, tiled=True)
    whole = shape(loads, nx, flat)
    image, again, inverse = call(
        unpack_kernel,
        (whole, whole, shape(nx, flat)),
        scratch_shapes=[scratch(nodes, LANES)] * 2,
    )(q_1, q_2, v_1, v_2, inv_1, inv_2)
    return call(
        finish_kernel,
        (whole, whole),
        out_specs=(hbm, hbm),
        scratch_shapes=[
            scratch(loads, nx, flat),
            scratch(loads, nx, flat),
            pltpu.SemaphoreType.DMA((2, loads)),
        ],
    )(parts, heat_source, image, again, inverse)


def solution(mesh):
    placed = (P(None, "gx", "gy"), P("gx", "gy"))
    return jax.shard_map(
        per_device,
        mesh=mesh,
        in_specs=placed,
        out_specs=(P(None, "gx", "gy"), P(None, "gx", "gy")),
        check_vma=False,
    )
```

```python
import functools

import jax
import jax.numpy as jnp
import numpy as np
from jax import lax
from jax.experimental import pallas as pl
from jax.experimental.pallas import tpu as pltpu
from jax.sharding import PartitionSpec as P

NZ = 96
KMIN = 0.001
LANES = 128
SUB = 8


class Batch:
    def __init__(self, size=12):
        self.size, self.held = size, []

    def add(self, into, at, tile):
        self.held.append((into, at, tile))
        if len(self.held) >= self.size:
            self.flush()

    def flush(self):
        for into, at, tile in self.held:
            into[at] = tile
        self.held = []


def packed_count(tiles):
    return -(-tiles * NZ // LANES)


def lane_ids(rows):
    return lax.broadcasted_iota(jnp.int32, (rows, LANES), 1)


def unpack_tile(read, index, rows):
    start = index * NZ
    block, offset = start // LANES, start % LANES
    lane = lane_ids(rows)
    first = read(block)
    if offset:
        first = pltpu.roll(first, LANES - offset, 1)
    if offset + NZ > LANES:
        second = pltpu.roll(read(block + 1), LANES - offset, 1)
        first = jnp.where(lane < LANES - offset, first, second)
    return jnp.where(lane < NZ, first, 0.0)


def pack_block(read_tile, tiles, block, rows):
    lane = lane_ids(rows)
    start = block * LANES
    out, at = None, start
    while at < start + LANES and at // NZ < tiles:
        index, z = at // NZ, at % NZ
        here = at - start
        piece = read_tile(index)
        shift = (here - z) % LANES
        if shift:
            piece = pltpu.roll(piece, shift, 1)
        out = piece if out is None else jnp.where(lane < here, out, piece)
        at += NZ - z
    return out


def pack_tiles(out_ref, at, rows, tiles, read_tile):
    batch = Batch()
    for block in range(packed_count(tiles)):
        place = slice(at + block * rows, at + (block + 1) * rows), slice(None)
        batch.add(out_ref, place, pack_block(read_tile, tiles, block, rows))
    batch.flush()


def unpack_tiles(ref, at, rows, tiles, write):
    batch = Batch()
    for index in range(tiles):
        tile = unpack_tile(lambda t: ref[at + t * rows : at + (t + 1) * rows, :], index, rows)
        for store in write(index, tile):
            batch.add(*store)
    batch.flush()


class Sizes:
    def __init__(self, loads, nx, ny, count_x, count_y):
        self.loads, self.nx, self.ny = loads, nx, ny
        self.count_x, self.count_y = count_x, count_y
        self.mx, self.my = nx + 4, ny + 4
        self.pitch = -(-(ny + 6) // SUB) * SUB
        self.y_dens = packed_count(2 * nx) * loads
        self.y_rows = self.y_dens + 3 * nx
        self.x_dens = packed_count(2 * ny) * loads
        self.x_rows = self.x_dens + 3 * ny
        self.c_dens = packed_count(8) * loads
        self.c_rows = self.c_dens + -(-18 // SUB) * SUB


class Tiles:
    def __init__(self, ref, columns, loads):
        self.ref, self.columns, self.loads = ref, columns, loads

    def rows(self, at):
        start = (at[0] * self.columns + at[1]) * self.loads
        if not isinstance(start, int):
            start = pl.multiple_of(start, SUB)
        return pl.ds(start, self.loads)

    def __getitem__(self, at):
        return self.ref[self.rows(at), :]

    def __setitem__(self, at, tile):
        self.ref[self.rows(at), :] = tile


class Rows:
    def __init__(self, ref, pitch, loads):
        self.ref, self.pitch, self.loads = ref, pitch, loads

    def __getitem__(self, at):
        row = self.ref[pl.ds(at[0] * self.pitch + at[1], 1), :]
        return jnp.broadcast_to(row, (self.loads, LANES))

    def put(self, x, values):
        self.ref[x * self.pitch : x * self.pitch + values.shape[0], :] = values


class Joined:
    def __init__(self, first, second, own):
        self.first, self.second, self.own = first, second, own

    def __getitem__(self, at):
        if at[0] in self.own:
            return self.first[self.own.index(at[0]), at[1]]
        return self.second[at]

    def __setitem__(self, at, tile):
        self.first[self.own.index(at[0]), at[1]] = tile

    def put(self, x, values):
        self.first.put(self.own.index(x), values)


class Halves:
    def __init__(self, outer_ref, middle_ref, ny, loads):
        self.edge = (0, 1, ny - 2, ny - 1)
        self.outer, self.middle = Tiles(outer_ref, 4, loads), Tiles(middle_ref, ny - 4, loads)

    def __getitem__(self, at):
        if at[1] in self.edge:
            return self.outer[at[0], self.edge.index(at[1])]
        return self.middle[at[0], at[1] - 2]


class Inside:
    def __init__(self, inner, own, outer):
        self.inner, self.own, self.outer = inner, own, outer

    def __getitem__(self, at):
        if at[1] in self.own:
            return self.inner[at[0] - 2, at[1] - 2]
        return self.outer[at]

    def __setitem__(self, at, tile):
        self.outer[at] = tile


def is_even(axis):
    return lax.rem(lax.axis_index(axis), 2) == 0


def is_alone(axis, count, start):
    place = lax.axis_index(axis)
    last = (count - start) % 2
    alone = place < start
    return jnp.logical_or(alone, place == count - 1) if last else alone


def pick(even, if_even, if_odd):
    return jnp.where(even, if_even, if_odd)


def pack_x_kernel(s, b_hbm, d_hbm, b_ref, dt_ref, x1_ref, x2_ref, d_ref, sems):
    loads, nx, ny = s.loads, s.nx, s.ny
    blocks = packed_count(ny)
    d_copy = pltpu.make_async_copy(d_hbm, d_ref, sems.at[blocks])
    d_copy.start()
    copies = []
    for block in range(blocks):
        lanes = pl.ds(block * LANES, LANES)
        copies.append(
            pltpu.make_async_copy(b_hbm.at[:, lanes], b_ref.at[block], sems.at[block])
        )
        copies[-1].start()
    d_copy.wait()
    batch = Batch(16)
    for x0 in range(0, nx, SUB):
        for y in range(ny):
            tile = unpack_tile(
                lambda t: d_ref[x0 : x0 + SUB, t * LANES : (t + 1) * LANES], y, SUB
            )
            batch.add(dt_ref, (pl.ds(x0 * ny + y, SUB, stride=ny), slice(None)), tile)
    batch.flush()
    even_x = is_even("gx")
    for ref, upper in ((x2_ref, jnp.logical_not(even_x)), (x1_ref, even_x)):
        rows = pl.ds(pl.multiple_of(pick(upper, nx - 3, 0) * ny, SUB), 3 * ny)
        ref[s.x_dens :, :] = dt_ref[rows, :]
    for copy in copies:
        copy.wait()
    batch = Batch()
    for ref, upper in ((x2_ref, jnp.logical_not(even_x)), (x1_ref, even_x)):
        x0 = pick(upper, nx - 2, 0)
        for dx in range(2):
            for block in range(blocks):
                tile = b_ref[block, pl.ds(x0 + dx, loads, stride=nx), :]
                at = (dx * blocks + block) * loads
                batch.add(ref, (slice(at, at + loads), slice(None)), tile)
    batch.flush()


def lay_out(s, b_ref, columns, out_ref):
    loads, nx, count = s.loads, s.nx, len(columns)
    batch = Batch(16)
    for load in range(loads):
        for x0 in range(0, nx, SUB):
            at = load * nx + x0
            for place, y in enumerate(columns):
                tile = unpack_tile(lambda t: b_ref[t, at : at + SUB, :], y, SUB)
                rows = pl.ds((x0 * count + place) * loads + load, SUB, stride=count * loads)
                batch.add(out_ref, (rows, slice(None)), tile)
    batch.flush()


def pack_far_kernel(s, b_ref, dt_ref, be_ref, y2_ref):
    lay_out(s, b_ref, (0, 1, s.ny - 2, s.ny - 1), be_ref)
    pack_y_face(s, jnp.logical_not(is_even("gy")), be_ref, dt_ref, y2_ref)


def pack_near_kernel(s, be_ref, dt_ref, y1_ref):
    pack_y_face(s, is_even("gy"), be_ref, dt_ref, y1_ref)


def pack_y_face(s, upper, be_ref, dt_ref, out_ref):
    loads, nx, ny = s.loads, s.nx, s.ny
    tiles = Tiles(be_ref, 4, loads)
    y0 = pick(upper, 2, 0)
    pack_tiles(out_ref, 0, loads, 2 * nx, lambda i: tiles[i // 2, y0 + i % 2])
    y0 = pick(upper, ny - 3, 0)
    batch = Batch()
    for dy in range(3):
        for x0 in range(0, nx, SUB):
            at = s.y_dens + dy * nx + x0
            tile = dt_ref[pl.ds(x0 * ny + y0 + dy, SUB, stride=ny), :]
            batch.add(out_ref, (slice(at, at + SUB), slice(None)), tile)
    batch.flush()


def open_y_kernel(s, y_ref, t_ref):
    tiles = Tiles(t_ref, 2, s.loads)
    unpack_tiles(
        y_ref, 0, s.loads, 2 * s.nx, lambda i, tile: [(tiles, (i // 2, i % 2), tile)]
    )


def open_x_kernel(s, x_ref, t_ref):
    tiles = Tiles(t_ref, s.ny, s.loads)
    unpack_tiles(
        x_ref, 0, s.loads, 2 * s.ny, lambda i, tile: [(tiles, (i // s.ny, i % s.ny), tile)]
    )


def corner_kernel(s, x2_ref, t2_ref, x1_ref, t1_ref, c1_ref, c2_ref):
    loads, ny = s.loads, s.ny
    open_x_kernel(s, x1_ref, t1_ref)
    halves = Tiles(t1_ref, ny, loads), Tiles(t2_ref, ny, loads)
    even_y = is_even("gy")
    for out_ref, upper in ((c2_ref, jnp.logical_not(even_y)), (c1_ref, even_y)):
        y0 = pick(upper, ny - 2, 0)
        pack_tiles(out_ref, 0, loads, 8, lambda i: halves[i // 4][i // 2 % 2, y0 + i % 2])
        y0 = pick(upper, ny - 3, 0)
        batch, at = Batch(18), s.c_dens
        for ref in (x1_ref, x2_ref):
            for t in range(3):
                for dy in range(3):
                    row = ref[pl.ds(s.x_dens + t * ny + y0 + dy, 1), :]
                    batch.add(out_ref, (slice(at, at + 1), slice(None)), row)
                    at += 1
        batch.flush()
        out_ref[at:, :] = jnp.zeros((s.c_rows - at, LANES), jnp.float32)


def join_density(s, dt_ref, y1_ref, y2_ref, dens_ref):
    nx, ny, pitch = s.nx, s.ny, s.pitch
    even_y = is_even("gy")
    yd = (pick(even_y, ny + 3, 0), pick(even_y, 0, ny + 3))
    batch = Batch(16)
    for x in range(nx):
        at = x * pitch
        batch.add(
            dens_ref, (slice(at + 3, at + 3 + ny), slice(None)), dt_ref[x * ny : (x + 1) * ny, :]
        )
    batch.flush()
    for side, ref in enumerate((y1_ref, y2_ref)):
        alone = is_alone("gy", s.count_y, side)
        for dy in range(3):
            for x0 in range(0, nx, SUB):
                at = s.y_dens + dy * nx + x0
                to = x0 * pitch + yd[side] + dy
                batch.add(
                    dens_ref,
                    (pl.ds(to, SUB, stride=pitch), slice(None)),
                    jnp.where(alone, 0.0, ref[at : at + SUB, :]),
                )
    batch.flush()


def conduct_of(dens):
    return jnp.where(
        dens > 0.0, (KMIN + (1.0 - KMIN) * (dens * dens * dens)) * (1.0 / 12.0), 0.0
    )


def inverse_of(s, before, after):
    pair = before + after
    pair = pair[: s.pitch - 1] + pair[1:]
    total = 4.0 * (pair + pltpu.roll(pair, 1, 1))
    return jnp.where(after[1:] > 0.0, 1.0 / total, 0.0)


def up(tile):
    return pltpu.roll(tile, LANES - 1, 1)


def element_planes(cond, carry, a, count, y0, columns, field, field_up, emitter, keep=True):
    def loads_of(step):
        y = y0 + step
        right = [(field[a + u, y + 1], field_up[a + u, y + 1]) for u in range(count + 1)]
        conduct = [cond[a + u, y] for u in range(count)]
        above = extra = None
        if step and emitter:
            above = (carry[0, y], carry[1, y])
            extra = [emitter.fetch(a + u, y) for u in range(count)]
        return right, conduct, above, extra

    left = [(field[a + u, y0], field_up[a + u, y0]) for u in range(count + 1)]
    ahead = loads_of(0)
    old, waiting = [None] * count, []
    for step in range(columns):
        y = y0 + step
        right, conduct, above, extra = ahead
        if step + 1 < columns:
            ahead = loads_of(step + 1)
        if len(waiting) > 1:
            for into, at, tile in waiting.pop(0):
                into[at] = tile
        stores = []
        for u in range(count):
            (p0, p0s), (p1, p1s) = left[u], left[u + 1]
            (r0, r0s), (r1, r1s) = right[u], right[u + 1]
            c = conduct[u]
            even = (p0 + r1) + (r0s + p1s)
            odd = (r0 + p1) + (p0s + r1s)
            pass_on = keep or u + 1 < count
            lower = upper = None
            if emitter:
                lower = (c * (odd + p1s), c * (even + p1))
            if pass_on:
                upper = (c * (even + p0s), c * (odd + p0))
            if step and emitter:
                low = (c * (even + r1s) + old[u][0][0]) + above[0]
                high = (c * (odd + r1) + old[u][0][1]) + above[1]
                total = low + pltpu.roll(high, 1, 1)
                stores += emitter.finish(a + u, y, p0, total, extra[u])
            if step and pass_on:
                above = (
                    c * (odd + r0s) + old[u][1][0],
                    c * (even + r0) + old[u][1][1],
                )
            old[u] = (lower, upper)
        if step and keep:
            stores += [(carry, (0, y), above[0]), (carry, (1, y), above[1])]
        waiting.append(stores)
        left = right
    for stores in waiting:
        for into, at, tile in stores:
            into[at] = tile


class First:
    def __init__(self, bx, invx, qx, wx, wu):
        self.bx, self.invx, self.qx, self.wx, self.wu = bx, invx, qx, wx, wu

    def fetch(self, x, y):
        return self.bx[x, y], self.invx[x, y]

    def finish(self, x, y, node, total, extra):
        source, inverse = extra
        image = 1.25 * source - total
        weighted = image * inverse
        at = x, y
        return [(self.qx, at, image), (self.wx, at, weighted), (self.wu, at, up(weighted))]


class Second:
    def __init__(self, bx, zx, qx, q_out, v_out, sums):
        self.bx, self.zx, self.qx, self.sums = bx, zx, qx, sums
        self.q_out, self.v_out = q_out, v_out

    def fetch(self, x, y):
        return self.bx[x, y], self.zx[x, y], self.qx[x, y]

    def finish(self, x, y, weighted, total, extra):
        source, scaled, image = extra
        again = 1.25 * image - total
        change = scaled - weighted
        sums = self.sums
        sums[0] = sums[0] + source * scaled
        sums[1] = sums[1] + source * change
        sums[2] = sums[2] + (source - image) * change
        sums[3] = sums[3] + (image - again) * change
        at = x - 2, y - 2
        return [(self.q_out, at, image), (self.v_out, at, again)]


def over_planes(start, stop, body, state):
    groups, rest = (stop - start) // 4, (stop - start) % 4
    state = lax.fori_loop(0, groups, lambda i, st: body(start + 4 * i, 4, st), state)
    if rest:
        state = body(stop - rest, rest, state)
    return state


def inside_fields(s, be_ref, bm_ref, zt_ref, ut_ref, bx, zx, zu):
    brick = [Halves(be_ref, bm_ref, s.ny, s.loads)]
    brick += [Tiles(ref, s.ny, s.loads) for ref in (zt_ref, ut_ref)]
    starts = (2, 3, 3)
    return tuple(
        Inside(inner, range(start, s.ny + 2), outer)
        for inner, start, outer in zip(brick, starts, (bx, zx, zu))
    )


def scale_kernel(
    s, b_ref, be_ref, dt_ref, bm_ref, zt_ref, ut_ref, ct_ref, it_ref, cond_ref, inv_ref
):
    loads, nx, ny = s.loads, s.nx, s.ny
    lay_out(s, b_ref, range(2, ny - 2), bm_ref)
    inner = Halves(be_ref, bm_ref, ny, loads)
    scaled, shifted, cond_t, inv_t = (
        Tiles(ref, ny, loads) for ref in (zt_ref, ut_ref, ct_ref, it_ref)
    )
    cond, inverse = Rows(cond_ref, ny, loads), Rows(inv_ref, ny, loads)
    before = None
    for x in range(nx):
        after = conduct_of(dt_ref[x * ny : (x + 1) * ny, :])
        cond.put(x, after)
        if x:
            pair = before + after
            pair = pair[: ny - 1] + pair[1:]
            total = 4.0 * (pair + pltpu.roll(pair, 1, 1))
            inverse.put(x, jnp.where(after[1:] > 0.0, 1.0 / total, 0.0))
        before = after
    batch = Batch(16)
    for x in range(nx):
        for y in range(ny):
            batch.add(cond_t, (x, y), cond[x, y])
            if x and y:
                row = inverse[x, y - 1]
                tile = inner[x, y] * row
                batch.add(inv_t, (x, y), row)
                batch.add(scaled, (x, y), tile)
                batch.add(shifted, (x, y), up(tile))
    batch.flush()


def inner_kernel(
    s, be_ref, bm_ref, zt_ref, ut_ref, ct_ref, it_ref, dt_ref, y1_ref, y2_ref, t1_ref,
    dens_ref, cond, invx, bx, zx, zu, qx, wx, wu, q_out, v_out, carry1, carry2, sums_ref,
):
    loads, nx, ny, my, pitch = s.loads, s.nx, s.ny, s.my, s.pitch
    bx, zx, zu, qx, wx, wu, carry1, carry2 = (
        Tiles(ref, my, loads) for ref in (bx, zx, zu, qx, wx, wu, carry1, carry2)
    )
    q_out, v_out = Tiles(q_out, ny, loads), Tiles(v_out, ny, loads)
    cond, invx = Rows(cond, pitch, loads), Rows(invx, pitch, loads)
    join_density(s, dt_ref, y1_ref, y2_ref, dens_ref)
    even_y = is_even("gy")
    ys = (pick(even_y, ny + 2, 0), pick(even_y, 0, ny + 2))
    before = None
    for x in range(nx):
        after = conduct_of(dens_ref[x * pitch : (x + 1) * pitch, :])
        cond.put(x + 2, after[1:])
        if x:
            invx.put(x + 2, inverse_of(s, before, after))
        before = after

    bx, zx, zu = inside_fields(s, be_ref, bm_ref, zt_ref, ut_ref, bx, zx, zu)

    def stage(x, y, tile):
        stores = [(bx, (x + 2, y), tile)]
        if x:
            scaled = tile * invx[x + 2, y]
            stores += [(zx, (x + 2, y), scaled), (zu, (x + 2, y), up(scaled))]
        return stores

    batch = Batch(16)
    for x in range(1, nx):
        scaled = bx[x + 2, 2] * invx[x + 2, 2]
        batch.add(zx, (x + 2, 2), scaled)
        batch.add(zu, (x + 2, 2), up(scaled))
    batch.flush()
    unpack_tiles(
        y2_ref, 0, loads, 2 * nx, lambda i, tile: stage(i // 2, ys[1] + i % 2, tile)
    )
    near = Tiles(t1_ref, 2, loads)
    batch = Batch(16)
    for x in range(nx):
        for dy in range(2):
            for store in stage(x, ys[0] + dy, near[x, dy]):
                batch.add(*store)
    batch.flush()

    cond = Inside(Tiles(ct_ref, ny, loads), range(2, ny + 2), cond)
    invx = Inside(Tiles(it_ref, ny, loads), range(3, ny + 2), invx)
    element_planes(cond, carry1, 3, 1, 0, my - 1, zx, zu, None)

    def first(a, count, state):
        emitter = First(bx, invx, qx, wx, wu)
        element_planes(cond, carry1, a, count, 0, my - 1, zx, zu, emitter)
        return state

    over_planes(4, nx + 1, first, 0)
    element_planes(cond, carry2, 4, 1, 1, my - 3, wx, wu, None)

    def second(a, count, sums):
        sums = list(sums)
        emitter = Second(bx, zx, qx, q_out, v_out, sums)
        element_planes(cond, carry2, a, count, 1, my - 3, wx, wu, emitter)
        return tuple(sums)

    zero = jnp.zeros((loads, LANES), jnp.float32)
    sums = over_planes(5, nx, second, (zero,) * 4)
    for place, part in enumerate(sums):
        sums_ref[place * loads : (place + 1) * loads, :] = part


def outer_kernel(
    s, be_ref, bm_ref, zt_ref, ut_ref, dens_ref, x1_ref, x2_ref, t1_ref, t2_ref, c1_ref, c2_ref,
    cond1, invx1, bx1, zx1, zu1, qx1, wx1, wu1, carry1, carry2, sums1,
    q_out, v_out, inv_out, sums_ref,
    low_ref, high_ref, low_d, high_d, cond2, invx2, bx2, zx2, zu2, qx2, wx2, wu2, carry3,
):
    loads, nx, ny, mx, my, pitch = s.loads, s.nx, s.ny, s.mx, s.my, s.pitch
    even_x = is_even("gx")

    even_y = is_even("gy")
    ys = (pick(even_y, ny + 2, 0), pick(even_y, 0, ny + 2))
    yd = (pick(even_y, ny + 3, 0), pick(even_y, 0, ny + 3))

    def take(near, far):
        faces = (x1_ref, t1_ref, near), (x2_ref, t2_ref, far)
        for side, (ref, face_ref, (tiles_ref, into)) in enumerate(faces):
            face, tiles = Tiles(face_ref, ny, loads), Tiles(tiles_ref, my, loads)
            alone_x = is_alone("gx", s.count_x, side)
            batch = Batch(18)
            for dx in range(2):
                for y in range(ny):
                    batch.add(tiles, (dx, y + 2), face[dx, y])
            for t in range(3):
                at = s.x_dens + t * ny
                rows = jnp.where(alone_x, 0.0, ref[at : at + ny, :])
                to = t * pitch + 3
                batch.add(into, (slice(to, to + ny), slice(None)), rows)
            batch.flush()
            for end, corner in enumerate((c1_ref, c2_ref)):
                alone = jnp.logical_or(alone_x, is_alone("gy", s.count_y, end))
                for i in range(4):
                    tile = unpack_tile(
                        lambda t: corner[t * loads : (t + 1) * loads, :], 4 * side + i, loads
                    )
                    batch.add(tiles, (i // 2, ys[end] + i % 2), tile)
                for i in range(9):
                    at = s.c_dens + 9 * side + i
                    row = jnp.where(alone, 0.0, corner[at : at + 1, :])
                    to = i // 3 * pitch + yd[end] + i % 3
                    batch.add(into, (pl.ds(to, 1), slice(None)), row)
            batch.flush()

    @pl.when(even_x)
    def _():
        take((high_ref, high_d), (low_ref, low_d))

    @pl.when(jnp.logical_not(even_x))
    def _():
        take((low_ref, low_d), (high_ref, high_d))

    def joined(first, second, own):
        return Joined(Tiles(first, my, loads), Tiles(second, my, loads), own)

    def joined_rows(first, second, own):
        return Joined(Rows(first, pitch, loads), Rows(second, pitch, loads), own)

    outside = (0, 1, nx + 2, nx + 3)
    scaled_own = outside + (2,)
    image_own = (1, 2, 3, nx + 1, nx + 2)
    cond, invx = joined_rows(cond2, cond1, outside), joined_rows(invx2, invx1, scaled_own)
    bx1, zx1, zu1 = inside_fields(
        s, be_ref, bm_ref, zt_ref, ut_ref, *(Tiles(ref, my, loads) for ref in (bx1, zx1, zu1))
    )
    bx = Joined(Tiles(bx2, my, loads), bx1, outside)
    zx = Joined(Tiles(zx2, my, loads), zx1, scaled_own)
    zu = Joined(Tiles(zu2, my, loads), zu1, scaled_own)
    qx, wx = joined(qx2, qx1, image_own), joined(wx2, wx1, image_own)
    wu = joined(wu2, wu1, image_own)
    own = [x - 2 for x in outer_planes(nx)]
    q_out, v_out = (Joined(Tiles(ref, ny, loads), None, own) for ref in (q_out, v_out))
    carry1, carry2, carry3 = (Tiles(ref, my, loads) for ref in (carry1, carry2, carry3))

    def conduct(ref, x):
        return conduct_of(ref[x * pitch : (x + 1) * pitch, :])

    low = [conduct(low_d, t) for t in range(3)] + [conduct(dens_ref, 0)]
    high = [conduct(dens_ref, nx - 1)] + [conduct(high_d, t) for t in range(2)]
    for x in range(3):
        inverse = inverse_of(s, low[x], low[x + 1])
        invx.put(x, inverse)
        if x < 2:
            cond.put(x, low[x + 1][1:])
    inv_out[...] = inverse[2 : 2 + ny]
    for x in range(2):
        invx.put(nx + 2 + x, inverse_of(s, high[x], high[x + 1]))
    cond.put(nx + 2, high[1][1:])

    batch = Batch(16)
    for ref, x0 in ((low_ref, 0), (high_ref, nx + 2)):
        tiles = Tiles(ref, my, loads)
        for dx in range(2):
            for y in range(my):
                tile = tiles[dx, y]
                batch.add(bx, (x0 + dx, y), tile)
                scaled = tile * invx[x0 + dx, y]
                batch.add(zx, (x0 + dx, y), scaled)
                batch.add(zu, (x0 + dx, y), up(scaled))
    for y in range(my):
        scaled = bx[2, y] * invx[2, y]
        batch.add(zx, (2, y), scaled)
        batch.add(zu, (2, y), up(scaled))
    batch.flush()

    emitter = First(bx, invx, qx, wx, wu)
    element_planes(cond, carry3, 0, 1, 0, my - 1, zx, zu, None)
    element_planes(cond, carry3, 1, 3, 0, my - 1, zx, zu, emitter, keep=False)
    element_planes(cond, carry1, nx + 1, 2, 0, my - 1, zx, zu, emitter, keep=False)
    sums = [sums1[place * loads : (place + 1) * loads, :] for place in range(4)]
    emitter = Second(bx, zx, qx, q_out, v_out, sums)
    element_planes(cond, carry3, 1, 1, 1, my - 3, wx, wu, None)
    element_planes(cond, carry3, 2, 3, 1, my - 3, wx, wu, emitter, keep=False)
    element_planes(cond, carry2, nx, 2, 1, my - 3, wx, wu, emitter, keep=False)
    lane = lane_ids(loads)
    load = lax.broadcasted_iota(jnp.int32, (loads, LANES), 0)
    packed = jnp.zeros((loads, LANES), jnp.float32)
    for place, part in enumerate(sums):
        total = jnp.sum(part, axis=1, keepdims=True)
        packed = packed + jnp.where(lane == place * loads + load, total, 0.0)
    row = jnp.sum(packed, axis=0, keepdims=True)
    sums_ref[...] = jnp.broadcast_to(row[None], sums_ref.shape)


def outer_planes(nx):
    return (2, 3, 4, nx, nx + 1)


def unpack_kernel(
    s, q1_ref, q2_ref, v1_ref, v2_ref, inv1_ref, inv2_ref, qo_ref, vo_ref, io_ref, q_ref, v_ref
):
    loads, nx, ny = s.loads, s.nx, s.ny
    batch = Batch()
    planes = outer_planes(nx)
    for first, second, whole in ((q1_ref, q2_ref, q_ref), (v1_ref, v2_ref, v_ref)):
        first, second = Tiles(first, ny, loads), Tiles(second, ny, loads)
        whole = Tiles(whole, ny, loads)
        for x in range(nx):
            for y in range(ny):
                if x + 2 in planes:
                    batch.add(whole, (x, y), second[planes.index(x + 2), y])
                else:
                    batch.add(whole, (x, y), first[x, y])
    batch.flush()
    batch = Batch()
    for x0 in range(0, nx, SUB):
        for ref, out in ((q_ref, qo_ref), (v_ref, vo_ref)):
            for load in range(loads):
                for block in range(packed_count(ny)):
                    tile = pack_block(
                        lambda y: ref[
                            pl.ds((x0 * ny + y) * loads + load, SUB, stride=ny * loads), :
                        ],
                        ny, block, SUB,
                    )
                    lanes = slice(block * LANES, (block + 1) * LANES)
                    batch.add(out, (load, slice(x0, x0 + SUB), lanes), tile)
        for block in range(packed_count(ny)):
            tile = pack_block(
                lambda y: inv1_ref[
                    pl.ds((x0 + 2) * s.pitch + y + 2, SUB, stride=s.pitch), :
                ],
                ny, block, SUB,
            )
            lanes = slice(block * LANES, (block + 1) * LANES)
            batch.add(io_ref, (slice(x0, x0 + SUB), lanes), tile)
    batch.flush()
    for block in range(packed_count(ny)):
        io_ref[0:1, block * LANES : (block + 1) * LANES] = pack_block(
            lambda y: inv2_ref[y : y + 1, :], ny, block, 1
        )


def finish_kernel(s, parts_ref, b_ref, q_ref, v_ref, inv_ref, x_hbm, r_hbm, x_ref, r_ref, sems):
    loads = s.loads
    totals = jnp.sum(parts_ref[...], axis=0)

    def part(place):
        return pltpu.roll(totals, (LANES - place * loads) % LANES, 1) if place else totals

    rz, near, square, last = (part(place) for place in range(4))
    direct = rz - near
    alpha = rz / direct
    short = -near / direct
    rz_next = short * short * rz + 2.0 * alpha * short * near + alpha * alpha * square
    beta = rz_next / rz
    grown = short + beta
    curved = (
        grown * grown * direct
        + 2.0 * alpha * grown * (near - square)
        + alpha * alpha * last
    )
    alpha_next = rz_next / curved
    first_row = alpha + alpha_next * (1.0 + beta)
    second_row = alpha_next * alpha
    inverse = inv_ref[...]
    copies = []
    for load in range(loads):
        first = first_row[:, load : load + 1]
        second = second_row[:, load : load + 1]
        source, image = b_ref[load], q_ref[load]
        x_ref[load] = (first * source - second * image) * inverse
        copies.append(pltpu.make_async_copy(x_ref.at[load], x_hbm.at[load], sems.at[0, load]))
        copies[-1].start()
        r_ref[load] = source - first * image + second * v_ref[load]
        copies.append(pltpu.make_async_copy(r_ref.at[load], r_hbm.at[load], sems.at[1, load]))
        copies[-1].start()
    for copy in copies:
        copy.wait()


def swap(array, axis, start):
    counts = {name: lax.axis_size(name) for name in ("gx", "gy")}
    other = "gy" if axis == "gx" else "gx"
    pairs = []
    for at in np.ndindex(counts["gx"], counts["gy"]):
        place = dict(zip(("gx", "gy"), at))
        partner = place[axis] + (1 if (place[axis] - start) % 2 == 0 else -1)
        if 0 <= partner < counts[axis]:
            place[axis] = partner
        elif place[other] ^ 1 < counts[other]:
            place[other] ^= 1
        pairs.append((at[0] * counts["gy"] + at[1], place["gx"] * counts["gy"] + place["gy"]))
    return lax.ppermute(array, ("gx", "gy"), pairs)


def per_device(heat_source, density):
    loads, nx, flat = heat_source.shape
    ny = flat // NZ
    s = Sizes(loads, nx, ny, lax.axis_size("gx"), lax.axis_size("gy"))
    nodes = nx * ny * loads
    devices = lax.axis_size("gx") * lax.axis_size("gy")

    def shape(*dims):
        return jax.ShapeDtypeStruct(dims, jnp.float32)

    def scratch(*dims):
        return pltpu.VMEM(dims, jnp.float32)

    def call(kernel, out_shape, **more):
        params = pltpu.CompilerParams(vmem_limit_bytes=20 * 1024 * 1024)
        return pl.pallas_call(
            functools.partial(kernel, s), out_shape=out_shape, compiler_params=params, **more
        )

    hbm = pl.BlockSpec(memory_space=pltpu.HBM)
    y_face, x_face, corner = (shape(rows, LANES) for rows in (s.y_rows, s.x_rows, s.c_rows))
    b, dt, x1, x2 = call(
        pack_x_kernel,
        (shape(packed_count(ny), loads * nx, LANES), shape(nx * ny, LANES), x_face, x_face),
        in_specs=[hbm, hbm],
        scratch_shapes=[scratch(nx, flat), pltpu.SemaphoreType.DMA((packed_count(ny) + 1,))],
    )(
        pltpu.with_memory_space_constraint(heat_source.reshape(loads * nx, flat), pltpu.HBM),
        pltpu.with_memory_space_constraint(density, pltpu.HBM),
    )
    x2, x1 = swap(x2, "gx", 1), swap(x1, "gx", 0)
    outer_columns = shape(nx * 4 * loads, LANES)
    be, y2 = call(pack_far_kernel, (outer_columns, y_face))(b, dt)
    y2 = swap(y2, "gy", 1)
    xt = shape(2 * ny * loads, LANES)
    xt2 = call(open_x_kernel, xt)(x2)
    xt2, be_later, dt_later = lax.optimization_barrier((xt2, be, dt))
    y1 = swap(call(pack_near_kernel, y_face)(be_later, dt_later), "gy", 0)
    t1 = call(open_y_kernel, shape(2 * nx * loads, LANES))(y1)
    inside = shape(nodes, LANES)
    bm, zt, ut, ct, it = call(
        scale_kernel,
        (shape(nx * (ny - 4) * loads, LANES),) + (inside,) * 4,
        scratch_shapes=[scratch(nx * ny, LANES)] * 2,
    )(b, be, dt_later)
    xt1, c1, c2 = call(
        corner_kernel,
        (xt, corner, corner),
        cost_estimate=pl.CostEstimate(flops=2 * 10**9, transcendentals=0, bytes_accessed=0),
    )(x2, xt2, x1)
    xt1, dt = lax.optimization_barrier((xt1, dt))
    c2, c1 = swap(c2, "gy", 1), swap(c1, "gy", 0)
    plane = s.my * loads
    rows, field = shape(s.mx * s.pitch, LANES), shape(s.mx * plane, LANES)
    edge = shape(2 * plane, LANES)
    dens, cond, inv_1, bx, zx, zu, q_x, w_x, w_u, q_1, v_1, carry1, carry2, sums = call(
        inner_kernel,
        (shape(nx * s.pitch, LANES),)
        + (rows,) * 2
        + (field,) * 6
        + (inside,) * 2
        + (edge,) * 2
        + (shape(4 * loads, LANES),),
    )(be, bm, zt, ut, ct, it, dt, y1, y2, t1)
    ends = shape(len(outer_planes(nx)) * ny * loads, LANES)
    q_2, v_2, inv_2, sums = call(
        outer_kernel,
        (ends, ends, shape(ny, LANES), shape(devices, 1, LANES)),
        scratch_shapes=[scratch(2 * plane, LANES)] * 2
        + [scratch(3 * s.pitch, LANES)] * 2
        + [scratch(5 * s.pitch, LANES)] * 2
        + [scratch(5 * plane, LANES)] * 6
        + [scratch(2 * plane, LANES)],
    )(be, bm, zt, ut, dens, x1, x2, xt1, xt2, c1, c2, cond, inv_1, bx, zx, zu, q_x, w_x, w_u, carry1, carry2, sums)
    parts = lax.all_to_all(sums, ("gx", "gy"), 0, 0, tiled=True)
    whole = shape(loads, nx, flat)
    image, again, inverse = call(
        unpack_kernel,
        (whole, whole, shape(nx, flat)),
        scratch_shapes=[scratch(nodes, LANES)] * 2,
    )(q_1, q_2, v_1, v_2, inv_1, inv_2)
    return call(
        finish_kernel,
        (whole, whole),
        out_specs=(hbm, hbm),
        scratch_shapes=[
            scratch(loads, nx, flat),
            scratch(loads, nx, flat),
            pltpu.SemaphoreType.DMA((2, loads)),
        ],
    )(parts, heat_source, image, again, inverse)


def solution(mesh):
    placed = (P(None, "gx", "gy"), P("gx", "gy"))
    return jax.shard_map(
        per_device,
        mesh=mesh,
        in_specs=placed,
        out_specs=(P(None, "gx", "gy"), P(None, "gx", "gy")),
        check_vma=False,
    )
```

```python
import functools

import jax
import jax.numpy as jnp
import numpy as np
from jax import lax
from jax.experimental import pallas as pl
from jax.experimental.pallas import tpu as pltpu
from jax.sharding import PartitionSpec as P

NZ = 96
KMIN = 0.001
LANES = 128
SUB = 8


class Batch:
    def __init__(self, size=12):
        self.size, self.held = size, []

    def add(self, into, at, tile):
        self.held.append((into, at, tile))
        if len(self.held) >= self.size:
            self.flush()

    def flush(self):
        for into, at, tile in self.held:
            into[at] = tile
        self.held = []


def packed_count(tiles):
    return -(-tiles * NZ // LANES)


def lane_ids(rows):
    return lax.broadcasted_iota(jnp.int32, (rows, LANES), 1)


def unpack_tile(read, index, rows):
    start = index * NZ
    block, offset = start // LANES, start % LANES
    lane = lane_ids(rows)
    first = read(block)
    if offset:
        first = pltpu.roll(first, LANES - offset, 1)
    if offset + NZ > LANES:
        second = pltpu.roll(read(block + 1), LANES - offset, 1)
        first = jnp.where(lane < LANES - offset, first, second)
    return jnp.where(lane < NZ, first, 0.0)


def pack_block(read_tile, tiles, block, rows):
    lane = lane_ids(rows)
    start = block * LANES
    out, at = None, start
    while at < start + LANES and at // NZ < tiles:
        index, z = at // NZ, at % NZ
        here = at - start
        piece = read_tile(index)
        shift = (here - z) % LANES
        if shift:
            piece = pltpu.roll(piece, shift, 1)
        out = piece if out is None else jnp.where(lane < here, out, piece)
        at += NZ - z
    return out


def pack_tiles(out_ref, at, rows, tiles, read_tile):
    batch = Batch()
    for block in range(packed_count(tiles)):
        place = slice(at + block * rows, at + (block + 1) * rows), slice(None)
        batch.add(out_ref, place, pack_block(read_tile, tiles, block, rows))
    batch.flush()


def unpack_tiles(ref, at, rows, tiles, write):
    batch = Batch()
    for index in range(tiles):
        tile = unpack_tile(lambda t: ref[at + t * rows : at + (t + 1) * rows, :], index, rows)
        for store in write(index, tile):
            batch.add(*store)
    batch.flush()


class Sizes:
    def __init__(self, loads, nx, ny, count_x, count_y):
        self.loads, self.nx, self.ny = loads, nx, ny
        self.count_x, self.count_y = count_x, count_y
        self.mx, self.my = nx + 4, ny + 4
        self.pitch = -(-(ny + 6) // SUB) * SUB
        self.y_dens = packed_count(2 * nx) * loads
        self.y_rows = self.y_dens + 3 * nx
        self.x_dens = packed_count(2 * ny) * loads
        self.x_rows = self.x_dens + 3 * ny
        self.c_dens = packed_count(8) * loads
        self.c_rows = self.c_dens + -(-18 // SUB) * SUB


class Tiles:
    def __init__(self, ref, columns, loads):
        self.ref, self.columns, self.loads = ref, columns, loads

    def rows(self, at):
        start = (at[0] * self.columns + at[1]) * self.loads
        if not isinstance(start, int):
            start = pl.multiple_of(start, SUB)
        return pl.ds(start, self.loads)

    def __getitem__(self, at):
        return self.ref[self.rows(at), :]

    def __setitem__(self, at, tile):
        self.ref[self.rows(at), :] = tile


class Rows:
    def __init__(self, ref, pitch, loads):
        self.ref, self.pitch, self.loads = ref, pitch, loads

    def __getitem__(self, at):
        row = self.ref[pl.ds(at[0] * self.pitch + at[1], 1), :]
        return jnp.broadcast_to(row, (self.loads, LANES))

    def put(self, x, values):
        self.ref[x * self.pitch : x * self.pitch + values.shape[0], :] = values


class Joined:
    def __init__(self, first, second, own):
        self.first, self.second, self.own = first, second, own

    def __getitem__(self, at):
        if at[0] in self.own:
            return self.first[self.own.index(at[0]), at[1]]
        return self.second[at]

    def __setitem__(self, at, tile):
        self.first[self.own.index(at[0]), at[1]] = tile

    def put(self, x, values):
        self.first.put(self.own.index(x), values)


class Halves:
    def __init__(self, outer_ref, middle_ref, ny, loads):
        self.edge = (0, 1, ny - 2, ny - 1)
        self.outer, self.middle = Tiles(outer_ref, 4, loads), Tiles(middle_ref, ny - 4, loads)

    def __getitem__(self, at):
        if at[1] in self.edge:
            return self.outer[at[0], self.edge.index(at[1])]
        return self.middle[at[0], at[1] - 2]


class Inside:
    def __init__(self, inner, own, outer):
        self.inner, self.own, self.outer = inner, own, outer

    def __getitem__(self, at):
        if at[1] in self.own:
            return self.inner[at[0] - 2, at[1] - 2]
        return self.outer[at]

    def __setitem__(self, at, tile):
        self.outer[at] = tile


def is_even(axis):
    return lax.rem(lax.axis_index(axis), 2) == 0


def is_alone(axis, count, start):
    place = lax.axis_index(axis)
    last = (count - start) % 2
    alone = place < start
    return jnp.logical_or(alone, place == count - 1) if last else alone


def pick(even, if_even, if_odd):
    return jnp.where(even, if_even, if_odd)


def pack_x_kernel(s, b_hbm, d_hbm, b_ref, dt_ref, x1_ref, x2_ref, d_ref, sems):
    loads, nx, ny = s.loads, s.nx, s.ny
    blocks = packed_count(ny)
    d_copy = pltpu.make_async_copy(d_hbm, d_ref, sems.at[blocks])
    d_copy.start()
    copies = []
    for block in range(blocks):
        lanes = pl.ds(block * LANES, LANES)
        copies.append(
            pltpu.make_async_copy(b_hbm.at[:, lanes], b_ref.at[block], sems.at[block])
        )
        copies[-1].start()
    d_copy.wait()
    batch = Batch(16)
    for x0 in range(0, nx, SUB):
        for y in range(ny):
            tile = unpack_tile(
                lambda t: d_ref[x0 : x0 + SUB, t * LANES : (t + 1) * LANES], y, SUB
            )
            batch.add(dt_ref, (pl.ds(x0 * ny + y, SUB, stride=ny), slice(None)), tile)
    batch.flush()
    even_x = is_even("gx")
    for ref, upper in ((x2_ref, jnp.logical_not(even_x)), (x1_ref, even_x)):
        rows = pl.ds(pl.multiple_of(pick(upper, nx - 3, 0) * ny, SUB), 3 * ny)
        ref[s.x_dens :, :] = dt_ref[rows, :]
    for copy in copies:
        copy.wait()
    batch = Batch()
    for ref, upper in ((x2_ref, jnp.logical_not(even_x)), (x1_ref, even_x)):
        x0 = pick(upper, nx - 2, 0)
        for dx in range(2):
            for block in range(blocks):
                tile = b_ref[block, pl.ds(x0 + dx, loads, stride=nx), :]
                at = (dx * blocks + block) * loads
                batch.add(ref, (slice(at, at + loads), slice(None)), tile)
    batch.flush()


def lay_out(s, b_ref, columns, out_ref):
    loads, nx, count = s.loads, s.nx, len(columns)
    batch = Batch(16)
    for load in range(loads):
        for x0 in range(0, nx, SUB):
            at = load * nx + x0
            for place, y in enumerate(columns):
                tile = unpack_tile(lambda t: b_ref[t, at : at + SUB, :], y, SUB)
                rows = pl.ds((x0 * count + place) * loads + load, SUB, stride=count * loads)
                batch.add(out_ref, (rows, slice(None)), tile)
    batch.flush()


def pack_far_kernel(s, b_ref, dt_ref, be_ref, y2_ref):
    lay_out(s, b_ref, (0, 1, s.ny - 2, s.ny - 1), be_ref)
    pack_y_face(s, jnp.logical_not(is_even("gy")), be_ref, dt_ref, y2_ref)


def pack_near_kernel(s, be_ref, dt_ref, y1_ref):
    pack_y_face(s, is_even("gy"), be_ref, dt_ref, y1_ref)


def pack_y_face(s, upper, be_ref, dt_ref, out_ref):
    loads, nx, ny = s.loads, s.nx, s.ny
    tiles = Tiles(be_ref, 4, loads)
    y0 = pick(upper, 2, 0)
    pack_tiles(out_ref, 0, loads, 2 * nx, lambda i: tiles[i // 2, y0 + i % 2])
    y0 = pick(upper, ny - 3, 0)
    batch = Batch()
    for dy in range(3):
        for x0 in range(0, nx, SUB):
            at = s.y_dens + dy * nx + x0
            tile = dt_ref[pl.ds(x0 * ny + y0 + dy, SUB, stride=ny), :]
            batch.add(out_ref, (slice(at, at + SUB), slice(None)), tile)
    batch.flush()


def open_y_kernel(s, y_ref, t_ref):
    tiles = Tiles(t_ref, 2, s.loads)
    unpack_tiles(
        y_ref, 0, s.loads, 2 * s.nx, lambda i, tile: [(tiles, (i // 2, i % 2), tile)]
    )


def open_x_kernel(s, x_ref, t_ref):
    tiles = Tiles(t_ref, s.ny, s.loads)
    unpack_tiles(
        x_ref, 0, s.loads, 2 * s.ny, lambda i, tile: [(tiles, (i // s.ny, i % s.ny), tile)]
    )


def corner_kernel(s, x2_ref, t2_ref, x1_ref, t1_ref, c1_ref, c2_ref):
    loads, ny = s.loads, s.ny
    open_x_kernel(s, x1_ref, t1_ref)
    halves = Tiles(t1_ref, ny, loads), Tiles(t2_ref, ny, loads)
    even_y = is_even("gy")
    for out_ref, upper in ((c2_ref, jnp.logical_not(even_y)), (c1_ref, even_y)):
        y0 = pick(upper, ny - 2, 0)
        pack_tiles(out_ref, 0, loads, 8, lambda i: halves[i // 4][i // 2 % 2, y0 + i % 2])
        y0 = pick(upper, ny - 3, 0)
        batch, at = Batch(18), s.c_dens
        for ref in (x1_ref, x2_ref):
            for t in range(3):
                for dy in range(3):
                    row = ref[pl.ds(s.x_dens + t * ny + y0 + dy, 1), :]
                    batch.add(out_ref, (slice(at, at + 1), slice(None)), row)
                    at += 1
        batch.flush()
        out_ref[at:, :] = jnp.zeros((s.c_rows - at, LANES), jnp.float32)


def join_density(s, dt_ref, y1_ref, y2_ref, dens_ref):
    nx, ny, pitch = s.nx, s.ny, s.pitch
    even_y = is_even("gy")
    yd = (pick(even_y, ny + 3, 0), pick(even_y, 0, ny + 3))
    batch = Batch(16)
    for x in range(nx):
        at = x * pitch
        batch.add(
            dens_ref, (slice(at + 3, at + 3 + ny), slice(None)), dt_ref[x * ny : (x + 1) * ny, :]
        )
    batch.flush()
    for side, ref in enumerate((y1_ref, y2_ref)):
        alone = is_alone("gy", s.count_y, side)
        for dy in range(3):
            for x0 in range(0, nx, SUB):
                at = s.y_dens + dy * nx + x0
                to = x0 * pitch + yd[side] + dy
                batch.add(
                    dens_ref,
                    (pl.ds(to, SUB, stride=pitch), slice(None)),
                    jnp.where(alone, 0.0, ref[at : at + SUB, :]),
                )
    batch.flush()


def conduct_of(dens):
    return jnp.where(
        dens > 0.0, (KMIN + (1.0 - KMIN) * (dens * dens * dens)) * (1.0 / 12.0), 0.0
    )


def inverse_of(s, before, after):
    pair = before + after
    pair = pair[: s.pitch - 1] + pair[1:]
    total = 4.0 * (pair + pltpu.roll(pair, 1, 1))
    return jnp.where(after[1:] > 0.0, 1.0 / total, 0.0)


def up(tile):
    return pltpu.roll(tile, LANES - 1, 1)


def element_planes(cond, carry, a, count, y0, columns, field, field_up, emitter, keep=True):
    def loads_of(step):
        y = y0 + step
        right = [(field[a + u, y + 1], field_up[a + u, y + 1]) for u in range(count + 1)]
        conduct = [cond[a + u, y] for u in range(count)]
        above = extra = None
        if step and emitter:
            above = (carry[0, y], carry[1, y])
            extra = [emitter.fetch(a + u, y) for u in range(count)]
        return right, conduct, above, extra

    left = [(field[a + u, y0], field_up[a + u, y0]) for u in range(count + 1)]
    ahead = loads_of(0)
    old, waiting = [None] * count, []
    for step in range(columns):
        y = y0 + step
        right, conduct, above, extra = ahead
        if step + 1 < columns:
            ahead = loads_of(step + 1)
        if len(waiting) > 1:
            for into, at, tile in waiting.pop(0):
                into[at] = tile
        stores = []
        for u in range(count):
            (p0, p0s), (p1, p1s) = left[u], left[u + 1]
            (r0, r0s), (r1, r1s) = right[u], right[u + 1]
            c = conduct[u]
            even = (p0 + r1) + (r0s + p1s)
            odd = (r0 + p1) + (p0s + r1s)
            pass_on = keep or u + 1 < count
            lower = upper = None
            if emitter:
                lower = (c * (odd + p1s), c * (even + p1))
            if pass_on:
                upper = (c * (even + p0s), c * (odd + p0))
            if step and emitter:
                low = (c * (even + r1s) + old[u][0][0]) + above[0]
                high = (c * (odd + r1) + old[u][0][1]) + above[1]
                total = low + pltpu.roll(high, 1, 1)
                stores += emitter.finish(a + u, y, p0, total, extra[u])
            if step and pass_on:
                above = (
                    c * (odd + r0s) + old[u][1][0],
                    c * (even + r0) + old[u][1][1],
                )
            old[u] = (lower, upper)
        if step and keep:
            stores += [(carry, (0, y), above[0]), (carry, (1, y), above[1])]
        waiting.append(stores)
        left = right
    for stores in waiting:
        for into, at, tile in stores:
            into[at] = tile


class First:
    def __init__(self, bx, invx, qx, wx, wu):
        self.bx, self.invx, self.qx, self.wx, self.wu = bx, invx, qx, wx, wu

    def fetch(self, x, y):
        return self.bx[x, y], self.invx[x, y]

    def finish(self, x, y, node, total, extra):
        source, inverse = extra
        image = 1.25 * source - total
        weighted = image * inverse
        at = x, y
        return [(self.qx, at, image), (self.wx, at, weighted), (self.wu, at, up(weighted))]


class Second:
    def __init__(self, bx, zx, qx, q_out, v_out, sums):
        self.bx, self.zx, self.qx, self.sums = bx, zx, qx, sums
        self.q_out, self.v_out = q_out, v_out

    def fetch(self, x, y):
        return self.bx[x, y], self.zx[x, y], self.qx[x, y]

    def finish(self, x, y, weighted, total, extra):
        source, scaled, image = extra
        again = 1.25 * image - total
        change = scaled - weighted
        sums = self.sums
        sums[0] = sums[0] + source * scaled
        sums[1] = sums[1] + source * change
        sums[2] = sums[2] + (source - image) * change
        sums[3] = sums[3] + (image - again) * change
        at = x - 2, y - 2
        return [(self.q_out, at, image), (self.v_out, at, again)]


def over_planes(start, stop, body, state):
    groups, rest = (stop - start) // 4, (stop - start) % 4
    state = lax.fori_loop(0, groups, lambda i, st: body(start + 4 * i, 4, st), state)
    if rest:
        state = body(stop - rest, rest, state)
    return state


def inside_fields(s, be_ref, bm_ref, zt_ref, ut_ref, bx, zx, zu):
    brick = [Halves(be_ref, bm_ref, s.ny, s.loads)]
    brick += [Tiles(ref, s.ny, s.loads) for ref in (zt_ref, ut_ref)]
    starts = (2, 3, 3)
    return tuple(
        Inside(inner, range(start, s.ny + 2), outer)
        for inner, start, outer in zip(brick, starts, (bx, zx, zu))
    )


def scale_kernel(
    s, b_ref, be_ref, dt_ref, bm_ref, zt_ref, ut_ref, ct_ref, it_ref, cond_ref, inv_ref
):
    loads, nx, ny = s.loads, s.nx, s.ny
    lay_out(s, b_ref, range(2, ny - 2), bm_ref)
    inner = Halves(be_ref, bm_ref, ny, loads)
    scaled, shifted, cond_t, inv_t = (
        Tiles(ref, ny, loads) for ref in (zt_ref, ut_ref, ct_ref, it_ref)
    )
    cond, inverse = Rows(cond_ref, ny, loads), Rows(inv_ref, ny, loads)
    before = None
    for x in range(nx):
        after = conduct_of(dt_ref[x * ny : (x + 1) * ny, :])
        cond.put(x, after)
        if x:
            pair = before + after
            pair = pair[: ny - 1] + pair[1:]
            total = 4.0 * (pair + pltpu.roll(pair, 1, 1))
            inverse.put(x, jnp.where(after[1:] > 0.0, 1.0 / total, 0.0))
        before = after
    batch = Batch(16)
    for x in range(nx):
        for y in range(ny):
            batch.add(cond_t, (x, y), cond[x, y])
            if x and y:
                row = inverse[x, y - 1]
                tile = inner[x, y] * row
                batch.add(inv_t, (x, y), row)
                batch.add(scaled, (x, y), tile)
                batch.add(shifted, (x, y), up(tile))
    batch.flush()


def inner_kernel(
    s, be_ref, bm_ref, zt_ref, ut_ref, ct_ref, it_ref, dt_ref, y1_ref, y2_ref, t1_ref,
    dens_ref, cond, invx, bx, zx, zu, qx, wx, wu, q_out, v_out, carry1, carry2, sums_ref,
):
    loads, nx, ny, my, pitch = s.loads, s.nx, s.ny, s.my, s.pitch
    bx, zx, zu, qx, wx, wu, carry1, carry2 = (
        Tiles(ref, my, loads) for ref in (bx, zx, zu, qx, wx, wu, carry1, carry2)
    )
    q_out, v_out = Tiles(q_out, ny, loads), Tiles(v_out, ny, loads)
    cond, invx = Rows(cond, pitch, loads), Rows(invx, pitch, loads)
    join_density(s, dt_ref, y1_ref, y2_ref, dens_ref)
    even_y = is_even("gy")
    ys = (pick(even_y, ny + 2, 0), pick(even_y, 0, ny + 2))
    before = None
    for x in range(nx):
        after = conduct_of(dens_ref[x * pitch : (x + 1) * pitch, :])
        cond.put(x + 2, after[1:])
        if x:
            invx.put(x + 2, inverse_of(s, before, after))
        before = after

    bx, zx, zu = inside_fields(s, be_ref, bm_ref, zt_ref, ut_ref, bx, zx, zu)

    def stage(x, y, tile):
        stores = [(bx, (x + 2, y), tile)]
        if x:
            scaled = tile * invx[x + 2, y]
            stores += [(zx, (x + 2, y), scaled), (zu, (x + 2, y), up(scaled))]
        return stores

    batch = Batch(16)
    for x in range(1, nx):
        scaled = bx[x + 2, 2] * invx[x + 2, 2]
        batch.add(zx, (x + 2, 2), scaled)
        batch.add(zu, (x + 2, 2), up(scaled))
    batch.flush()
    unpack_tiles(
        y2_ref, 0, loads, 2 * nx, lambda i, tile: stage(i // 2, ys[1] + i % 2, tile)
    )
    near = Tiles(t1_ref, 2, loads)
    batch = Batch(16)
    for x in range(nx):
        for dy in range(2):
            for store in stage(x, ys[0] + dy, near[x, dy]):
                batch.add(*store)
    batch.flush()

    cond = Inside(Tiles(ct_ref, ny, loads), range(2, ny + 2), cond)
    invx = Inside(Tiles(it_ref, ny, loads), range(3, ny + 2), invx)
    element_planes(cond, carry1, 3, 1, 0, my - 1, zx, zu, None)

    def first(a, count, state):
        emitter = First(bx, invx, qx, wx, wu)
        element_planes(cond, carry1, a, count, 0, my - 1, zx, zu, emitter)
        return state

    over_planes(4, nx + 1, first, 0)
    element_planes(cond, carry2, 4, 1, 1, my - 3, wx, wu, None)

    def second(a, count, sums):
        sums = list(sums)
        emitter = Second(bx, zx, qx, q_out, v_out, sums)
        element_planes(cond, carry2, a, count, 1, my - 3, wx, wu, emitter)
        return tuple(sums)

    zero = jnp.zeros((loads, LANES), jnp.float32)
    sums = over_planes(5, nx, second, (zero,) * 4)
    for place, part in enumerate(sums):
        sums_ref[place * loads : (place + 1) * loads, :] = part


def outer_kernel(
    s, be_ref, bm_ref, zt_ref, ut_ref, dens_ref, x1_ref, x2_ref, t1_ref, t2_ref, c2_ref, c1_ref,
    cond1, invx1, bx1, zx1, zu1, qx1, wx1, wu1, carry1, carry2, sums1,
    q_out, v_out, inv_out, sums_ref,
    low_ref, high_ref, low_d, high_d, cond2, invx2, bx2, zx2, zu2, qx2, wx2, wu2, carry3,
):
    loads, nx, ny, mx, my, pitch = s.loads, s.nx, s.ny, s.mx, s.my, s.pitch
    even_x = is_even("gx")

    even_y = is_even("gy")
    ys = (pick(even_y, ny + 2, 0), pick(even_y, 0, ny + 2))
    yd = (pick(even_y, ny + 3, 0), pick(even_y, 0, ny + 3))

    def take(near, far):
        faces = (x1_ref, t1_ref, near), (x2_ref, t2_ref, far)
        for side, (ref, face_ref, (tiles_ref, into)) in enumerate(faces):
            face, tiles = Tiles(face_ref, ny, loads), Tiles(tiles_ref, my, loads)
            alone_x = is_alone("gx", s.count_x, side)
            batch = Batch(18)
            for dx in range(2):
                for y in range(ny):
                    batch.add(tiles, (dx, y + 2), face[dx, y])
            for t in range(3):
                at = s.x_dens + t * ny
                rows = jnp.where(alone_x, 0.0, ref[at : at + ny, :])
                to = t * pitch + 3
                batch.add(into, (slice(to, to + ny), slice(None)), rows)
            batch.flush()
            for end, corner in enumerate((c1_ref, c2_ref)):
                alone = jnp.logical_or(alone_x, is_alone("gy", s.count_y, end))
                for i in range(4):
                    tile = unpack_tile(
                        lambda t: corner[t * loads : (t + 1) * loads, :], 4 * side + i, loads
                    )
                    batch.add(tiles, (i // 2, ys[end] + i % 2), tile)
                for i in range(9):
                    at = s.c_dens + 9 * side + i
                    row = jnp.where(alone, 0.0, corner[at : at + 1, :])
                    to = i // 3 * pitch + yd[end] + i % 3
                    batch.add(into, (pl.ds(to, 1), slice(None)), row)
            batch.flush()

    @pl.when(even_x)
    def _():
        take((high_ref, high_d), (low_ref, low_d))

    @pl.when(jnp.logical_not(even_x))
    def _():
        take((low_ref, low_d), (high_ref, high_d))

    def joined(first, second, own):
        return Joined(Tiles(first, my, loads), Tiles(second, my, loads), own)

    def joined_rows(first, second, own):
        return Joined(Rows(first, pitch, loads), Rows(second, pitch, loads), own)

    outside = (0, 1, nx + 2, nx + 3)
    scaled_own = outside + (2,)
    image_own = (1, 2, 3, nx + 1, nx + 2)
    cond, invx = joined_rows(cond2, cond1, outside), joined_rows(invx2, invx1, scaled_own)
    bx1, zx1, zu1 = inside_fields(
        s, be_ref, bm_ref, zt_ref, ut_ref, *(Tiles(ref, my, loads) for ref in (bx1, zx1, zu1))
    )
    bx = Joined(Tiles(bx2, my, loads), bx1, outside)
    zx = Joined(Tiles(zx2, my, loads), zx1, scaled_own)
    zu = Joined(Tiles(zu2, my, loads), zu1, scaled_own)
    qx, wx = joined(qx2, qx1, image_own), joined(wx2, wx1, image_own)
    wu = joined(wu2, wu1, image_own)
    own = [x - 2 for x in outer_planes(nx)]
    q_out, v_out = (Joined(Tiles(ref, ny, loads), None, own) for ref in (q_out, v_out))
    carry1, carry2, carry3 = (Tiles(ref, my, loads) for ref in (carry1, carry2, carry3))

    def conduct(ref, x):
        return conduct_of(ref[x * pitch : (x + 1) * pitch, :])

    low = [conduct(low_d, t) for t in range(3)] + [conduct(dens_ref, 0)]
    high = [conduct(dens_ref, nx - 1)] + [conduct(high_d, t) for t in range(2)]
    for x in range(3):
        inverse = inverse_of(s, low[x], low[x + 1])
        invx.put(x, inverse)
        if x < 2:
            cond.put(x, low[x + 1][1:])
    inv_out[...] = inverse[2 : 2 + ny]
    for x in range(2):
        invx.put(nx + 2 + x, inverse_of(s, high[x], high[x + 1]))
    cond.put(nx + 2, high[1][1:])

    batch = Batch(16)
    for ref, x0 in ((low_ref, 0), (high_ref, nx + 2)):
        tiles = Tiles(ref, my, loads)
        for dx in range(2):
            for y in range(my):
                tile = tiles[dx, y]
                batch.add(bx, (x0 + dx, y), tile)
                scaled = tile * invx[x0 + dx, y]
                batch.add(zx, (x0 + dx, y), scaled)
                batch.add(zu, (x0 + dx, y), up(scaled))
    for y in range(my):
        scaled = bx[2, y] * invx[2, y]
        batch.add(zx, (2, y), scaled)
        batch.add(zu, (2, y), up(scaled))
    batch.flush()

    emitter = First(bx, invx, qx, wx, wu)
    element_planes(cond, carry3, 0, 1, 0, my - 1, zx, zu, None)
    element_planes(cond, carry3, 1, 3, 0, my - 1, zx, zu, emitter, keep=False)
    element_planes(cond, carry1, nx + 1, 2, 0, my - 1, zx, zu, emitter, keep=False)
    sums = [sums1[place * loads : (place + 1) * loads, :] for place in range(4)]
    emitter = Second(bx, zx, qx, q_out, v_out, sums)
    element_planes(cond, carry3, 1, 1, 1, my - 3, wx, wu, None)
    element_planes(cond, carry3, 2, 3, 1, my - 3, wx, wu, emitter, keep=False)
    element_planes(cond, carry2, nx, 2, 1, my - 3, wx, wu, emitter, keep=False)
    lane = lane_ids(loads)
    load = lax.broadcasted_iota(jnp.int32, (loads, LANES), 0)
    packed = jnp.zeros((loads, LANES), jnp.float32)
    for place, part in enumerate(sums):
        total = jnp.sum(part, axis=1, keepdims=True)
        packed = packed + jnp.where(lane == place * loads + load, total, 0.0)
    row = jnp.sum(packed, axis=0, keepdims=True)
    sums_ref[...] = jnp.broadcast_to(row[None], sums_ref.shape)


def outer_planes(nx):
    return (2, 3, 4, nx, nx + 1)


def unpack_kernel(
    s, q1_ref, q2_ref, v1_ref, v2_ref, inv1_ref, inv2_ref, qo_ref, vo_ref, io_ref, q_ref, v_ref
):
    loads, nx, ny = s.loads, s.nx, s.ny
    batch = Batch()
    planes = outer_planes(nx)
    for first, second, whole in ((q1_ref, q2_ref, q_ref), (v1_ref, v2_ref, v_ref)):
        first, second = Tiles(first, ny, loads), Tiles(second, ny, loads)
        whole = Tiles(whole, ny, loads)
        for x in range(nx):
            for y in range(ny):
                if x + 2 in planes:
                    batch.add(whole, (x, y), second[planes.index(x + 2), y])
                else:
                    batch.add(whole, (x, y), first[x, y])
    batch.flush()
    batch = Batch()
    for x0 in range(0, nx, SUB):
        for ref, out in ((q_ref, qo_ref), (v_ref, vo_ref)):
            for load in range(loads):
                for block in range(packed_count(ny)):
                    tile = pack_block(
                        lambda y: ref[
                            pl.ds((x0 * ny + y) * loads + load, SUB, stride=ny * loads), :
                        ],
                        ny, block, SUB,
                    )
                    lanes = slice(block * LANES, (block + 1) * LANES)
                    batch.add(out, (load, slice(x0, x0 + SUB), lanes), tile)
        for block in range(packed_count(ny)):
            tile = pack_block(
                lambda y: inv1_ref[
                    pl.ds((x0 + 2) * s.pitch + y + 2, SUB, stride=s.pitch), :
                ],
                ny, block, SUB,
            )
            lanes = slice(block * LANES, (block + 1) * LANES)
            batch.add(io_ref, (slice(x0, x0 + SUB), lanes), tile)
    batch.flush()
    for block in range(packed_count(ny)):
        io_ref[0:1, block * LANES : (block + 1) * LANES] = pack_block(
            lambda y: inv2_ref[y : y + 1, :], ny, block, 1
        )


def finish_kernel(s, parts_ref, b_ref, q_ref, v_ref, inv_ref, x_hbm, r_hbm, x_ref, r_ref, sems):
    loads = s.loads
    totals = jnp.sum(parts_ref[...], axis=0)

    def part(place):
        return pltpu.roll(totals, (LANES - place * loads) % LANES, 1) if place else totals

    rz, near, square, last = (part(place) for place in range(4))
    direct = rz - near
    alpha = rz / direct
    short = -near / direct
    rz_next = short * short * rz + 2.0 * alpha * short * near + alpha * alpha * square
    beta = rz_next / rz
    grown = short + beta
    curved = (
        grown * grown * direct
        + 2.0 * alpha * grown * (near - square)
        + alpha * alpha * last
    )
    alpha_next = rz_next / curved
    first_row = alpha + alpha_next * (1.0 + beta)
    second_row = alpha_next * alpha
    inverse = inv_ref[...]
    copies = []
    for load in range(loads):
        first = first_row[:, load : load + 1]
        second = second_row[:, load : load + 1]
        source, image = b_ref[load], q_ref[load]
        x_ref[load] = (first * source - second * image) * inverse
        copies.append(pltpu.make_async_copy(x_ref.at[load], x_hbm.at[load], sems.at[0, load]))
        copies[-1].start()
        r_ref[load] = source - first * image + second * v_ref[load]
        copies.append(pltpu.make_async_copy(r_ref.at[load], r_hbm.at[load], sems.at[1, load]))
        copies[-1].start()
    for copy in copies:
        copy.wait()


def swap(array, axis, start):
    counts = {name: lax.axis_size(name) for name in ("gx", "gy")}
    other = "gy" if axis == "gx" else "gx"
    pairs = []
    for at in np.ndindex(counts["gx"], counts["gy"]):
        place = dict(zip(("gx", "gy"), at))
        partner = place[axis] + (1 if (place[axis] - start) % 2 == 0 else -1)
        if 0 <= partner < counts[axis]:
            place[axis] = partner
        elif place[other] ^ 1 < counts[other]:
            place[other] ^= 1
        pairs.append((at[0] * counts["gy"] + at[1], place["gx"] * counts["gy"] + place["gy"]))
    return lax.ppermute(array, ("gx", "gy"), pairs)


def per_device(heat_source, density):
    loads, nx, flat = heat_source.shape
    ny = flat // NZ
    s = Sizes(loads, nx, ny, lax.axis_size("gx"), lax.axis_size("gy"))
    nodes = nx * ny * loads
    devices = lax.axis_size("gx") * lax.axis_size("gy")

    def shape(*dims):
        return jax.ShapeDtypeStruct(dims, jnp.float32)

    def scratch(*dims):
        return pltpu.VMEM(dims, jnp.float32)

    def call(kernel, out_shape, **more):
        params = pltpu.CompilerParams(vmem_limit_bytes=20 * 1024 * 1024)
        return pl.pallas_call(
            functools.partial(kernel, s), out_shape=out_shape, compiler_params=params, **more
        )

    hbm = pl.BlockSpec(memory_space=pltpu.HBM)
    y_face, x_face, corner = (shape(rows, LANES) for rows in (s.y_rows, s.x_rows, s.c_rows))
    b, dt, x1, x2 = call(
        pack_x_kernel,
        (shape(packed_count(ny), loads * nx, LANES), shape(nx * ny, LANES), x_face, x_face),
        in_specs=[hbm, hbm],
        scratch_shapes=[scratch(nx, flat), pltpu.SemaphoreType.DMA((packed_count(ny) + 1,))],
    )(
        pltpu.with_memory_space_constraint(heat_source.reshape(loads * nx, flat), pltpu.HBM),
        pltpu.with_memory_space_constraint(density, pltpu.HBM),
    )
    x2, x1 = swap(x2, "gx", 1), swap(x1, "gx", 0)
    outer_columns = shape(nx * 4 * loads, LANES)
    be, y2 = call(pack_far_kernel, (outer_columns, y_face))(b, dt)
    y2 = swap(y2, "gy", 1)
    xt = shape(2 * ny * loads, LANES)
    xt2 = call(open_x_kernel, xt)(x2)
    xt2, be_later, dt_later = lax.optimization_barrier((xt2, be, dt))
    y1 = swap(call(pack_near_kernel, y_face)(be_later, dt_later), "gy", 0)
    t1 = call(open_y_kernel, shape(2 * nx * loads, LANES))(y1)
    inside = shape(nodes, LANES)
    bm, zt, ut, ct, it = call(
        scale_kernel,
        (shape(nx * (ny - 4) * loads, LANES),) + (inside,) * 4,
        scratch_shapes=[scratch(nx * ny, LANES)] * 2,
    )(b, be, dt_later)
    xt1, c1, c2 = call(
        corner_kernel,
        (xt, corner, corner),
        cost_estimate=pl.CostEstimate(flops=2 * 10**9, transcendentals=0, bytes_accessed=0),
    )(x2, xt2, x1)
    xt1, dt = lax.optimization_barrier((xt1, dt))
    c1, c2 = swap(c1, "gy", 0), swap(c2, "gy", 1)
    plane = s.my * loads
    rows, field = shape(s.mx * s.pitch, LANES), shape(s.mx * plane, LANES)
    edge = shape(2 * plane, LANES)
    dens, cond, inv_1, bx, zx, zu, q_x, w_x, w_u, q_1, v_1, carry1, carry2, sums = call(
        inner_kernel,
        (shape(nx * s.pitch, LANES),)
        + (rows,) * 2
        + (field,) * 6
        + (inside,) * 2
        + (edge,) * 2
        + (shape(4 * loads, LANES),),
    )(be, bm, zt, ut, ct, it, dt, y1, y2, t1)
    ends = shape(len(outer_planes(nx)) * ny * loads, LANES)
    q_2, v_2, inv_2, sums = call(
        outer_kernel,
        (ends, ends, shape(ny, LANES), shape(devices, 1, LANES)),
        scratch_shapes=[scratch(2 * plane, LANES)] * 2
        + [scratch(3 * s.pitch, LANES)] * 2
        + [scratch(5 * s.pitch, LANES)] * 2
        + [scratch(5 * plane, LANES)] * 6
        + [scratch(2 * plane, LANES)],
    )(be, bm, zt, ut, dens, x1, x2, xt1, xt2, c2, c1, cond, inv_1, bx, zx, zu, q_x, w_x, w_u, carry1, carry2, sums)
    parts = lax.all_to_all(sums, ("gx", "gy"), 0, 0, tiled=True)
    whole = shape(loads, nx, flat)
    image, again, inverse = call(
        unpack_kernel,
        (whole, whole, shape(nx, flat)),
        scratch_shapes=[scratch(nodes, LANES)] * 2,
    )(q_1, q_2, v_1, v_2, inv_1, inv_2)
    return call(
        finish_kernel,
        (whole, whole),
        out_specs=(hbm, hbm),
        scratch_shapes=[
            scratch(loads, nx, flat),
            scratch(loads, nx, flat),
            pltpu.SemaphoreType.DMA((2, loads)),
        ],
    )(parts, heat_source, image, again, inverse)


def solution(mesh):
    placed = (P(None, "gx", "gy"), P("gx", "gy"))
    return jax.shard_map(
        per_device,
        mesh=mesh,
        in_specs=placed,
        out_specs=(P(None, "gx", "gy"), P(None, "gx", "gy")),
        check_vma=False,
    )
```

```python
import functools

import jax
import jax.numpy as jnp
import numpy as np
from jax import lax
from jax.experimental import pallas as pl
from jax.experimental.pallas import tpu as pltpu
from jax.sharding import PartitionSpec as P

NZ = 96
KMIN = 0.001
LANES = 128
SUB = 8


class Batch:
    def __init__(self, size=12):
        self.size, self.held = size, []

    def add(self, into, at, tile):
        self.held.append((into, at, tile))
        if len(self.held) >= self.size:
            self.flush()

    def flush(self):
        for into, at, tile in self.held:
            into[at] = tile
        self.held = []


def packed_count(tiles):
    return -(-tiles * NZ // LANES)


def lane_ids(rows):
    return lax.broadcasted_iota(jnp.int32, (rows, LANES), 1)


def unpack_tile(read, index, rows):
    start = index * NZ
    block, offset = start // LANES, start % LANES
    lane = lane_ids(rows)
    first = read(block)
    if offset:
        first = pltpu.roll(first, LANES - offset, 1)
    if offset + NZ > LANES:
        second = pltpu.roll(read(block + 1), LANES - offset, 1)
        first = jnp.where(lane < LANES - offset, first, second)
    return jnp.where(lane < NZ, first, 0.0)


def pack_block(read_tile, tiles, block, rows):
    lane = lane_ids(rows)
    start = block * LANES
    out, at = None, start
    while at < start + LANES and at // NZ < tiles:
        index, z = at // NZ, at % NZ
        here = at - start
        piece = read_tile(index)
        shift = (here - z) % LANES
        if shift:
            piece = pltpu.roll(piece, shift, 1)
        out = piece if out is None else jnp.where(lane < here, out, piece)
        at += NZ - z
    return out


def pack_tiles(out_ref, at, rows, tiles, read_tile):
    batch = Batch()
    for block in range(packed_count(tiles)):
        place = slice(at + block * rows, at + (block + 1) * rows), slice(None)
        batch.add(out_ref, place, pack_block(read_tile, tiles, block, rows))
    batch.flush()


def unpack_tiles(ref, at, rows, tiles, write):
    batch = Batch()
    for index in range(tiles):
        tile = unpack_tile(lambda t: ref[at + t * rows : at + (t + 1) * rows, :], index, rows)
        for store in write(index, tile):
            batch.add(*store)
    batch.flush()


class Sizes:
    def __init__(self, loads, nx, ny, count_x, count_y):
        self.loads, self.nx, self.ny = loads, nx, ny
        self.count_x, self.count_y = count_x, count_y
        self.mx, self.my = nx + 4, ny + 4
        self.pitch = -(-(ny + 6) // SUB) * SUB
        self.y_dens = packed_count(2 * nx) * loads
        self.y_rows = self.y_dens + 3 * nx
        self.x_dens = packed_count(2 * ny) * loads
        self.x_rows = self.x_dens + 3 * ny
        self.c_dens = packed_count(8) * loads
        self.c_rows = self.c_dens + -(-18 // SUB) * SUB


class Tiles:
    def __init__(self, ref, columns, loads):
        self.ref, self.columns, self.loads = ref, columns, loads

    def rows(self, at):
        start = (at[0] * self.columns + at[1]) * self.loads
        if not isinstance(start, int):
            start = pl.multiple_of(start, SUB)
        return pl.ds(start, self.loads)

    def __getitem__(self, at):
        return self.ref[self.rows(at), :]

    def __setitem__(self, at, tile):
        self.ref[self.rows(at), :] = tile


class Rows:
    def __init__(self, ref, pitch, loads):
        self.ref, self.pitch, self.loads = ref, pitch, loads

    def __getitem__(self, at):
        row = self.ref[pl.ds(at[0] * self.pitch + at[1], 1), :]
        return jnp.broadcast_to(row, (self.loads, LANES))

    def put(self, x, values):
        self.ref[x * self.pitch : x * self.pitch + values.shape[0], :] = values


class Joined:
    def __init__(self, first, second, own):
        self.first, self.second, self.own = first, second, own

    def __getitem__(self, at):
        if at[0] in self.own:
            return self.first[self.own.index(at[0]), at[1]]
        return self.second[at]

    def __setitem__(self, at, tile):
        self.first[self.own.index(at[0]), at[1]] = tile

    def put(self, x, values):
        self.first.put(self.own.index(x), values)


class Halves:
    def __init__(self, outer_ref, middle_ref, ny, loads):
        self.edge = (0, 1, ny - 2, ny - 1)
        self.outer, self.middle = Tiles(outer_ref, 4, loads), Tiles(middle_ref, ny - 4, loads)

    def __getitem__(self, at):
        if at[1] in self.edge:
            return self.outer[at[0], self.edge.index(at[1])]
        return self.middle[at[0], at[1] - 2]


class Inside:
    def __init__(self, inner, own, outer):
        self.inner, self.own, self.outer = inner, own, outer

    def __getitem__(self, at):
        if at[1] in self.own:
            return self.inner[at[0] - 2, at[1] - 2]
        return self.outer[at]

    def __setitem__(self, at, tile):
        self.outer[at] = tile


def is_even(axis):
    return lax.rem(lax.axis_index(axis), 2) == 0


def is_alone(axis, count, start):
    place = lax.axis_index(axis)
    last = (count - start) % 2
    alone = place < start
    return jnp.logical_or(alone, place == count - 1) if last else alone


def pick(even, if_even, if_odd):
    return jnp.where(even, if_even, if_odd)


def pack_x_kernel(s, b_hbm, d_hbm, b_ref, dt_ref, x1_ref, x2_ref, d_ref, sems):
    loads, nx, ny = s.loads, s.nx, s.ny
    blocks = packed_count(ny)
    d_copy = pltpu.make_async_copy(d_hbm, d_ref, sems.at[blocks])
    d_copy.start()
    copies = []
    for block in range(blocks):
        lanes = pl.ds(block * LANES, LANES)
        copies.append(
            pltpu.make_async_copy(b_hbm.at[:, lanes], b_ref.at[block], sems.at[block])
        )
        copies[-1].start()
    d_copy.wait()
    batch = Batch(16)
    for x0 in range(0, nx, SUB):
        for y in range(ny):
            tile = unpack_tile(
                lambda t: d_ref[x0 : x0 + SUB, t * LANES : (t + 1) * LANES], y, SUB
            )
            batch.add(dt_ref, (pl.ds(x0 * ny + y, SUB, stride=ny), slice(None)), tile)
    batch.flush()
    even_x = is_even("gx")
    for ref, upper in ((x2_ref, jnp.logical_not(even_x)), (x1_ref, even_x)):
        rows = pl.ds(pl.multiple_of(pick(upper, nx - 3, 0) * ny, SUB), 3 * ny)
        ref[s.x_dens :, :] = dt_ref[rows, :]
    for copy in copies:
        copy.wait()
    batch = Batch()
    for ref, upper in ((x2_ref, jnp.logical_not(even_x)), (x1_ref, even_x)):
        x0 = pick(upper, nx - 2, 0)
        for dx in range(2):
            for block in range(blocks):
                tile = b_ref[block, pl.ds(x0 + dx, loads, stride=nx), :]
                at = (dx * blocks + block) * loads
                batch.add(ref, (slice(at, at + loads), slice(None)), tile)
    batch.flush()


def lay_out(s, b_ref, columns, out_ref):
    loads, nx, count = s.loads, s.nx, len(columns)
    batch = Batch(16)
    for load in range(loads):
        for x0 in range(0, nx, SUB):
            at = load * nx + x0
            for place, y in enumerate(columns):
                tile = unpack_tile(lambda t: b_ref[t, at : at + SUB, :], y, SUB)
                rows = pl.ds((x0 * count + place) * loads + load, SUB, stride=count * loads)
                batch.add(out_ref, (rows, slice(None)), tile)
    batch.flush()


def pack_far_kernel(s, b_ref, dt_ref, be_ref, y2_ref):
    lay_out(s, b_ref, (0, 1, s.ny - 2, s.ny - 1), be_ref)
    pack_y_face(s, jnp.logical_not(is_even("gy")), be_ref, dt_ref, y2_ref)


def pack_near_kernel(s, be_ref, dt_ref, y1_ref):
    pack_y_face(s, is_even("gy"), be_ref, dt_ref, y1_ref)


def pack_y_face(s, upper, be_ref, dt_ref, out_ref):
    loads, nx, ny = s.loads, s.nx, s.ny
    tiles = Tiles(be_ref, 4, loads)
    y0 = pick(upper, 2, 0)
    pack_tiles(out_ref, 0, loads, 2 * nx, lambda i: tiles[i // 2, y0 + i % 2])
    y0 = pick(upper, ny - 3, 0)
    batch = Batch()
    for dy in range(3):
        for x0 in range(0, nx, SUB):
            at = s.y_dens + dy * nx + x0
            tile = dt_ref[pl.ds(x0 * ny + y0 + dy, SUB, stride=ny), :]
            batch.add(out_ref, (slice(at, at + SUB), slice(None)), tile)
    batch.flush()


def open_y_kernel(s, y_ref, t_ref):
    tiles = Tiles(t_ref, 2, s.loads)
    unpack_tiles(
        y_ref, 0, s.loads, 2 * s.nx, lambda i, tile: [(tiles, (i // 2, i % 2), tile)]
    )


def open_x_kernel(s, x_ref, t_ref):
    tiles = Tiles(t_ref, s.ny, s.loads)
    unpack_tiles(
        x_ref, 0, s.loads, 2 * s.ny, lambda i, tile: [(tiles, (i // s.ny, i % s.ny), tile)]
    )


def corner_kernel(s, x2_ref, t2_ref, x1_ref, t1_ref, c1_ref, c2_ref):
    loads, ny = s.loads, s.ny
    open_x_kernel(s, x1_ref, t1_ref)
    halves = Tiles(t1_ref, ny, loads), Tiles(t2_ref, ny, loads)
    even_y = is_even("gy")
    for out_ref, upper in ((c2_ref, jnp.logical_not(even_y)), (c1_ref, even_y)):
        y0 = pick(upper, ny - 2, 0)
        pack_tiles(out_ref, 0, loads, 8, lambda i: halves[i // 4][i // 2 % 2, y0 + i % 2])
        y0 = pick(upper, ny - 3, 0)
        batch, at = Batch(18), s.c_dens
        for ref in (x1_ref, x2_ref):
            for t in range(3):
                for dy in range(3):
                    row = ref[pl.ds(s.x_dens + t * ny + y0 + dy, 1), :]
                    batch.add(out_ref, (slice(at, at + 1), slice(None)), row)
                    at += 1
        batch.flush()
        out_ref[at:, :] = jnp.zeros((s.c_rows - at, LANES), jnp.float32)


def join_density(s, dt_ref, y1_ref, y2_ref, dens_ref):
    nx, ny, pitch = s.nx, s.ny, s.pitch
    even_y = is_even("gy")
    yd = (pick(even_y, ny + 3, 0), pick(even_y, 0, ny + 3))
    batch = Batch(16)
    for x in range(nx):
        at = x * pitch
        batch.add(
            dens_ref, (slice(at + 3, at + 3 + ny), slice(None)), dt_ref[x * ny : (x + 1) * ny, :]
        )
    batch.flush()
    for side, ref in enumerate((y1_ref, y2_ref)):
        alone = is_alone("gy", s.count_y, side)
        for dy in range(3):
            for x0 in range(0, nx, SUB):
                at = s.y_dens + dy * nx + x0
                to = x0 * pitch + yd[side] + dy
                batch.add(
                    dens_ref,
                    (pl.ds(to, SUB, stride=pitch), slice(None)),
                    jnp.where(alone, 0.0, ref[at : at + SUB, :]),
                )
    batch.flush()


def conduct_of(dens):
    return jnp.where(
        dens > 0.0, (KMIN + (1.0 - KMIN) * (dens * dens * dens)) * (1.0 / 12.0), 0.0
    )


def inverse_of(s, before, after):
    pair = before + after
    pair = pair[: s.pitch - 1] + pair[1:]
    total = 4.0 * (pair + pltpu.roll(pair, 1, 1))
    return jnp.where(after[1:] > 0.0, 1.0 / total, 0.0)


def up(tile):
    return pltpu.roll(tile, LANES - 1, 1)


def element_planes(cond, carry, a, count, y0, columns, field, field_up, emitter, keep=True):
    def loads_of(step):
        y = y0 + step
        right = [(field[a + u, y + 1], field_up[a + u, y + 1]) for u in range(count + 1)]
        conduct = [cond[a + u, y] for u in range(count)]
        above = extra = None
        if step and emitter:
            above = (carry[0, y], carry[1, y])
            extra = [emitter.fetch(a + u, y) for u in range(count)]
        return right, conduct, above, extra

    left = [(field[a + u, y0], field_up[a + u, y0]) for u in range(count + 1)]
    ahead = loads_of(0)
    old, waiting = [None] * count, []
    for step in range(columns):
        y = y0 + step
        right, conduct, above, extra = ahead
        if step + 1 < columns:
            ahead = loads_of(step + 1)
        if len(waiting) > 1:
            for into, at, tile in waiting.pop(0):
                into[at] = tile
        stores = []
        for u in range(count):
            (p0, p0s), (p1, p1s) = left[u], left[u + 1]
            (r0, r0s), (r1, r1s) = right[u], right[u + 1]
            c = conduct[u]
            even = (p0 + r1) + (r0s + p1s)
            odd = (r0 + p1) + (p0s + r1s)
            pass_on = keep or u + 1 < count
            lower = upper = None
            if emitter:
                lower = (c * (odd + p1s), c * (even + p1))
            if pass_on:
                upper = (c * (even + p0s), c * (odd + p0))
            if step and emitter:
                low = (c * (even + r1s) + old[u][0][0]) + above[0]
                high = (c * (odd + r1) + old[u][0][1]) + above[1]
                total = low + pltpu.roll(high, 1, 1)
                stores += emitter.finish(a + u, y, p0, total, extra[u])
            if step and pass_on:
                above = (
                    c * (odd + r0s) + old[u][1][0],
                    c * (even + r0) + old[u][1][1],
                )
            old[u] = (lower, upper)
        if step and keep:
            stores += [(carry, (0, y), above[0]), (carry, (1, y), above[1])]
        waiting.append(stores)
        left = right
    for stores in waiting:
        for into, at, tile in stores:
            into[at] = tile


class First:
    def __init__(self, bx, invx, qx, wx, wu):
        self.bx, self.invx, self.qx, self.wx, self.wu = bx, invx, qx, wx, wu

    def fetch(self, x, y):
        return self.bx[x, y], self.invx[x, y]

    def finish(self, x, y, node, total, extra):
        source, inverse = extra
        image = 1.25 * source - total
        weighted = image * inverse
        at = x, y
        return [(self.qx, at, image), (self.wx, at, weighted), (self.wu, at, up(weighted))]


class Second:
    def __init__(self, bx, zx, qx, q_out, v_out, sums):
        self.bx, self.zx, self.qx, self.sums = bx, zx, qx, sums
        self.q_out, self.v_out = q_out, v_out

    def fetch(self, x, y):
        return self.bx[x, y], self.zx[x, y], self.qx[x, y]

    def finish(self, x, y, weighted, total, extra):
        source, scaled, image = extra
        again = 1.25 * image - total
        change = scaled - weighted
        sums = self.sums
        sums[0] = sums[0] + source * scaled
        sums[1] = sums[1] + source * change
        sums[2] = sums[2] + (source - image) * change
        sums[3] = sums[3] + (image - again) * change
        at = x - 2, y - 2
        return [(self.q_out, at, image), (self.v_out, at, again)]


def over_planes(start, stop, body, state):
    groups, rest = (stop - start) // 4, (stop - start) % 4
    if rest == 1 and groups:
        groups, rest = groups - 1, 5
    state = lax.fori_loop(0, groups, lambda i, st: body(start + 4 * i, 4, st), state)
    if rest:
        state = body(stop - rest, rest, state)
    return state


def inside_fields(s, be_ref, bm_ref, zt_ref, ut_ref, bx, zx, zu):
    brick = [Halves(be_ref, bm_ref, s.ny, s.loads)]
    brick += [Tiles(ref, s.ny, s.loads) for ref in (zt_ref, ut_ref)]
    starts = (2, 3, 3)
    return tuple(
        Inside(inner, range(start, s.ny + 2), outer)
        for inner, start, outer in zip(brick, starts, (bx, zx, zu))
    )


def scale_kernel(
    s, b_ref, be_ref, dt_ref, bm_ref, zt_ref, ut_ref, ct_ref, it_ref, cond_ref, inv_ref
):
    loads, nx, ny = s.loads, s.nx, s.ny
    lay_out(s, b_ref, range(2, ny - 2), bm_ref)
    inner = Halves(be_ref, bm_ref, ny, loads)
    scaled, shifted, cond_t, inv_t = (
        Tiles(ref, ny, loads) for ref in (zt_ref, ut_ref, ct_ref, it_ref)
    )
    cond, inverse = Rows(cond_ref, ny, loads), Rows(inv_ref, ny, loads)
    before = None
    for x in range(nx):
        after = conduct_of(dt_ref[x * ny : (x + 1) * ny, :])
        cond.put(x, after)
        if x:
            pair = before + after
            pair = pair[: ny - 1] + pair[1:]
            total = 4.0 * (pair + pltpu.roll(pair, 1, 1))
            inverse.put(x, jnp.where(after[1:] > 0.0, 1.0 / total, 0.0))
        before = after
    batch = Batch(16)
    for x in range(nx):
        for y in range(ny):
            batch.add(cond_t, (x, y), cond[x, y])
            if x and y:
                row = inverse[x, y - 1]
                tile = inner[x, y] * row
                batch.add(inv_t, (x, y), row)
                batch.add(scaled, (x, y), tile)
                batch.add(shifted, (x, y), up(tile))
    batch.flush()


def inner_kernel(
    s, be_ref, bm_ref, zt_ref, ut_ref, ct_ref, it_ref, dt_ref, y1_ref, y2_ref, t1_ref,
    dens_ref, cond, invx, bx, zx, zu, qx, wx, wu, q_out, v_out, carry1, carry2, sums_ref,
):
    loads, nx, ny, my, pitch = s.loads, s.nx, s.ny, s.my, s.pitch
    bx, zx, zu, qx, wx, wu, carry1, carry2 = (
        Tiles(ref, my, loads) for ref in (bx, zx, zu, qx, wx, wu, carry1, carry2)
    )
    q_out, v_out = Tiles(q_out, ny, loads), Tiles(v_out, ny, loads)
    cond, invx = Rows(cond, pitch, loads), Rows(invx, pitch, loads)
    join_density(s, dt_ref, y1_ref, y2_ref, dens_ref)
    even_y = is_even("gy")
    ys = (pick(even_y, ny + 2, 0), pick(even_y, 0, ny + 2))
    before = None
    for x in range(nx):
        after = conduct_of(dens_ref[x * pitch : (x + 1) * pitch, :])
        cond.put(x + 2, after[1:])
        if x:
            invx.put(x + 2, inverse_of(s, before, after))
        before = after

    bx, zx, zu = inside_fields(s, be_ref, bm_ref, zt_ref, ut_ref, bx, zx, zu)

    def stage(x, y, tile):
        stores = [(bx, (x + 2, y), tile)]
        if x:
            scaled = tile * invx[x + 2, y]
            stores += [(zx, (x + 2, y), scaled), (zu, (x + 2, y), up(scaled))]
        return stores

    batch = Batch(16)
    for x in range(1, nx):
        scaled = bx[x + 2, 2] * invx[x + 2, 2]
        batch.add(zx, (x + 2, 2), scaled)
        batch.add(zu, (x + 2, 2), up(scaled))
    batch.flush()
    unpack_tiles(
        y2_ref, 0, loads, 2 * nx, lambda i, tile: stage(i // 2, ys[1] + i % 2, tile)
    )
    near = Tiles(t1_ref, 2, loads)
    batch = Batch(16)
    for x in range(nx):
        for dy in range(2):
            for store in stage(x, ys[0] + dy, near[x, dy]):
                batch.add(*store)
    batch.flush()

    cond = Inside(Tiles(ct_ref, ny, loads), range(2, ny + 2), cond)
    invx = Inside(Tiles(it_ref, ny, loads), range(3, ny + 2), invx)
    element_planes(cond, carry1, 3, 1, 0, my - 1, zx, zu, None)

    def first(a, count, state):
        emitter = First(bx, invx, qx, wx, wu)
        element_planes(cond, carry1, a, count, 0, my - 1, zx, zu, emitter)
        return state

    over_planes(4, nx + 1, first, 0)
    element_planes(cond, carry2, 4, 1, 1, my - 3, wx, wu, None)

    def second(a, count, sums):
        sums = list(sums)
        emitter = Second(bx, zx, qx, q_out, v_out, sums)
        element_planes(cond, carry2, a, count, 1, my - 3, wx, wu, emitter)
        return tuple(sums)

    zero = jnp.zeros((loads, LANES), jnp.float32)
    sums = over_planes(5, nx, second, (zero,) * 4)
    for place, part in enumerate(sums):
        sums_ref[place * loads : (place + 1) * loads, :] = part


def outer_kernel(
    s, be_ref, bm_ref, zt_ref, ut_ref, dens_ref, x1_ref, x2_ref, t1_ref, t2_ref, c2_ref, c1_ref,
    cond1, invx1, bx1, zx1, zu1, qx1, wx1, wu1, carry1, carry2, sums1,
    q_out, v_out, inv_out, sums_ref,
    low_ref, high_ref, low_d, high_d, cond2, invx2, bx2, zx2, zu2, qx2, wx2, wu2, carry3,
):
    loads, nx, ny, mx, my, pitch = s.loads, s.nx, s.ny, s.mx, s.my, s.pitch
    even_x = is_even("gx")

    even_y = is_even("gy")
    ys = (pick(even_y, ny + 2, 0), pick(even_y, 0, ny + 2))
    yd = (pick(even_y, ny + 3, 0), pick(even_y, 0, ny + 3))

    def take(near, far):
        faces = (x1_ref, t1_ref, near), (x2_ref, t2_ref, far)
        for side, (ref, face_ref, (tiles_ref, into)) in enumerate(faces):
            face, tiles = Tiles(face_ref, ny, loads), Tiles(tiles_ref, my, loads)
            alone_x = is_alone("gx", s.count_x, side)
            batch = Batch(18)
            for dx in range(2):
                for y in range(ny):
                    batch.add(tiles, (dx, y + 2), face[dx, y])
            for t in range(3):
                at = s.x_dens + t * ny
                rows = jnp.where(alone_x, 0.0, ref[at : at + ny, :])
                to = t * pitch + 3
                batch.add(into, (slice(to, to + ny), slice(None)), rows)
            batch.flush()
            for end, corner in enumerate((c1_ref, c2_ref)):
                alone = jnp.logical_or(alone_x, is_alone("gy", s.count_y, end))
                for i in range(4):
                    tile = unpack_tile(
                        lambda t: corner[t * loads : (t + 1) * loads, :], 4 * side + i, loads
                    )
                    batch.add(tiles, (i // 2, ys[end] + i % 2), tile)
                for i in range(9):
                    at = s.c_dens + 9 * side + i
                    row = jnp.where(alone, 0.0, corner[at : at + 1, :])
                    to = i // 3 * pitch + yd[end] + i % 3
                    batch.add(into, (pl.ds(to, 1), slice(None)), row)
            batch.flush()

    @pl.when(even_x)
    def _():
        take((high_ref, high_d), (low_ref, low_d))

    @pl.when(jnp.logical_not(even_x))
    def _():
        take((low_ref, low_d), (high_ref, high_d))

    def joined(first, second, own):
        return Joined(Tiles(first, my, loads), Tiles(second, my, loads), own)

    def joined_rows(first, second, own):
        return Joined(Rows(first, pitch, loads), Rows(second, pitch, loads), own)

    outside = (0, 1, nx + 2, nx + 3)
    scaled_own = outside + (2,)
    image_own = (1, 2, 3, nx + 1, nx + 2)
    cond, invx = joined_rows(cond2, cond1, outside), joined_rows(invx2, invx1, scaled_own)
    bx1, zx1, zu1 = inside_fields(
        s, be_ref, bm_ref, zt_ref, ut_ref, *(Tiles(ref, my, loads) for ref in (bx1, zx1, zu1))
    )
    bx = Joined(Tiles(bx2, my, loads), bx1, outside)
    zx = Joined(Tiles(zx2, my, loads), zx1, scaled_own)
    zu = Joined(Tiles(zu2, my, loads), zu1, scaled_own)
    qx, wx = joined(qx2, qx1, image_own), joined(wx2, wx1, image_own)
    wu = joined(wu2, wu1, image_own)
    own = [x - 2 for x in outer_planes(nx)]
    q_out, v_out = (Joined(Tiles(ref, ny, loads), None, own) for ref in (q_out, v_out))
    carry1, carry2, carry3 = (Tiles(ref, my, loads) for ref in (carry1, carry2, carry3))

    def conduct(ref, x):
        return conduct_of(ref[x * pitch : (x + 1) * pitch, :])

    low = [conduct(low_d, t) for t in range(3)] + [conduct(dens_ref, 0)]
    high = [conduct(dens_ref, nx - 1)] + [conduct(high_d, t) for t in range(2)]
    for x in range(3):
        inverse = inverse_of(s, low[x], low[x + 1])
        invx.put(x, inverse)
        if x < 2:
            cond.put(x, low[x + 1][1:])
    inv_out[...] = inverse[2 : 2 + ny]
    for x in range(2):
        invx.put(nx + 2 + x, inverse_of(s, high[x], high[x + 1]))
    cond.put(nx + 2, high[1][1:])

    batch = Batch(16)
    for ref, x0 in ((low_ref, 0), (high_ref, nx + 2)):
        tiles = Tiles(ref, my, loads)
        for dx in range(2):
            for y in range(my):
                tile = tiles[dx, y]
                batch.add(bx, (x0 + dx, y), tile)
                scaled = tile * invx[x0 + dx, y]
                batch.add(zx, (x0 + dx, y), scaled)
                batch.add(zu, (x0 + dx, y), up(scaled))
    for y in range(my):
        scaled = bx[2, y] * invx[2, y]
        batch.add(zx, (2, y), scaled)
        batch.add(zu, (2, y), up(scaled))
    batch.flush()

    emitter = First(bx, invx, qx, wx, wu)
    element_planes(cond, carry3, 0, 1, 0, my - 1, zx, zu, None)
    element_planes(cond, carry3, 1, 3, 0, my - 1, zx, zu, emitter, keep=False)
    element_planes(cond, carry1, nx + 1, 2, 0, my - 1, zx, zu, emitter, keep=False)
    sums = [sums1[place * loads : (place + 1) * loads, :] for place in range(4)]
    emitter = Second(bx, zx, qx, q_out, v_out, sums)
    element_planes(cond, carry3, 1, 1, 1, my - 3, wx, wu, None)
    element_planes(cond, carry3, 2, 3, 1, my - 3, wx, wu, emitter, keep=False)
    element_planes(cond, carry2, nx, 2, 1, my - 3, wx, wu, emitter, keep=False)
    lane = lane_ids(loads)
    load = lax.broadcasted_iota(jnp.int32, (loads, LANES), 0)
    packed = jnp.zeros((loads, LANES), jnp.float32)
    for place, part in enumerate(sums):
        total = jnp.sum(part, axis=1, keepdims=True)
        packed = packed + jnp.where(lane == place * loads + load, total, 0.0)
    row = jnp.sum(packed, axis=0, keepdims=True)
    sums_ref[...] = jnp.broadcast_to(row[None], sums_ref.shape)


def outer_planes(nx):
    return (2, 3, 4, nx, nx + 1)


def unpack_kernel(
    s, q1_ref, q2_ref, v1_ref, v2_ref, inv1_ref, inv2_ref, qo_ref, vo_ref, io_ref, q_ref, v_ref
):
    loads, nx, ny = s.loads, s.nx, s.ny
    batch = Batch()
    planes = outer_planes(nx)
    for first, second, whole in ((q1_ref, q2_ref, q_ref), (v1_ref, v2_ref, v_ref)):
        first, second = Tiles(first, ny, loads), Tiles(second, ny, loads)
        whole = Tiles(whole, ny, loads)
        for x in range(nx):
            for y in range(ny):
                if x + 2 in planes:
                    batch.add(whole, (x, y), second[planes.index(x + 2), y])
                else:
                    batch.add(whole, (x, y), first[x, y])
    batch.flush()
    batch = Batch()
    for x0 in range(0, nx, SUB):
        for ref, out in ((q_ref, qo_ref), (v_ref, vo_ref)):
            for load in range(loads):
                for block in range(packed_count(ny)):
                    tile = pack_block(
                        lambda y: ref[
                            pl.ds((x0 * ny + y) * loads + load, SUB, stride=ny * loads), :
                        ],
                        ny, block, SUB,
                    )
                    lanes = slice(block * LANES, (block + 1) * LANES)
                    batch.add(out, (load, slice(x0, x0 + SUB), lanes), tile)
        for block in range(packed_count(ny)):
            tile = pack_block(
                lambda y: inv1_ref[
                    pl.ds((x0 + 2) * s.pitch + y + 2, SUB, stride=s.pitch), :
                ],
                ny, block, SUB,
            )
            lanes = slice(block * LANES, (block + 1) * LANES)
            batch.add(io_ref, (slice(x0, x0 + SUB), lanes), tile)
    batch.flush()
    for block in range(packed_count(ny)):
        io_ref[0:1, block * LANES : (block + 1) * LANES] = pack_block(
            lambda y: inv2_ref[y : y + 1, :], ny, block, 1
        )


def finish_kernel(s, parts_ref, b_ref, q_ref, v_ref, inv_ref, x_hbm, r_hbm, x_ref, r_ref, sems):
    loads = s.loads
    totals = jnp.sum(parts_ref[...], axis=0)

    def part(place):
        return pltpu.roll(totals, (LANES - place * loads) % LANES, 1) if place else totals

    rz, near, square, last = (part(place) for place in range(4))
    direct = rz - near
    alpha = rz / direct
    short = -near / direct
    rz_next = short * short * rz + 2.0 * alpha * short * near + alpha * alpha * square
    beta = rz_next / rz
    grown = short + beta
    curved = (
        grown * grown * direct
        + 2.0 * alpha * grown * (near - square)
        + alpha * alpha * last
    )
    alpha_next = rz_next / curved
    first_row = alpha + alpha_next * (1.0 + beta)
    second_row = alpha_next * alpha
    inverse = inv_ref[...]
    copies = []
    for load in range(loads):
        first = first_row[:, load : load + 1]
        second = second_row[:, load : load + 1]
        source, image = b_ref[load], q_ref[load]
        x_ref[load] = (first * source - second * image) * inverse
        copies.append(pltpu.make_async_copy(x_ref.at[load], x_hbm.at[load], sems.at[0, load]))
        copies[-1].start()
        r_ref[load] = source - first * image + second * v_ref[load]
        copies.append(pltpu.make_async_copy(r_ref.at[load], r_hbm.at[load], sems.at[1, load]))
        copies[-1].start()
    for copy in copies:
        copy.wait()


def swap(array, axis, start):
    counts = {name: lax.axis_size(name) for name in ("gx", "gy")}
    other = "gy" if axis == "gx" else "gx"
    pairs = []
    for at in np.ndindex(counts["gx"], counts["gy"]):
        place = dict(zip(("gx", "gy"), at))
        partner = place[axis] + (1 if (place[axis] - start) % 2 == 0 else -1)
        if 0 <= partner < counts[axis]:
            place[axis] = partner
        elif place[other] ^ 1 < counts[other]:
            place[other] ^= 1
        pairs.append((at[0] * counts["gy"] + at[1], place["gx"] * counts["gy"] + place["gy"]))
    return lax.ppermute(array, ("gx", "gy"), pairs)


def per_device(heat_source, density):
    loads, nx, flat = heat_source.shape
    ny = flat // NZ
    s = Sizes(loads, nx, ny, lax.axis_size("gx"), lax.axis_size("gy"))
    nodes = nx * ny * loads
    devices = lax.axis_size("gx") * lax.axis_size("gy")

    def shape(*dims):
        return jax.ShapeDtypeStruct(dims, jnp.float32)

    def scratch(*dims):
        return pltpu.VMEM(dims, jnp.float32)

    def call(kernel, out_shape, **more):
        params = pltpu.CompilerParams(vmem_limit_bytes=20 * 1024 * 1024)
        return pl.pallas_call(
            functools.partial(kernel, s), out_shape=out_shape, compiler_params=params, **more
        )

    hbm = pl.BlockSpec(memory_space=pltpu.HBM)
    y_face, x_face, corner = (shape(rows, LANES) for rows in (s.y_rows, s.x_rows, s.c_rows))
    b, dt, x1, x2 = call(
        pack_x_kernel,
        (shape(packed_count(ny), loads * nx, LANES), shape(nx * ny, LANES), x_face, x_face),
        in_specs=[hbm, hbm],
        scratch_shapes=[scratch(nx, flat), pltpu.SemaphoreType.DMA((packed_count(ny) + 1,))],
    )(
        pltpu.with_memory_space_constraint(heat_source.reshape(loads * nx, flat), pltpu.HBM),
        pltpu.with_memory_space_constraint(density, pltpu.HBM),
    )
    x2, x1 = swap(x2, "gx", 1), swap(x1, "gx", 0)
    outer_columns = shape(nx * 4 * loads, LANES)
    be, y2 = call(pack_far_kernel, (outer_columns, y_face))(b, dt)
    y2 = swap(y2, "gy", 1)
    xt = shape(2 * ny * loads, LANES)
    xt2 = call(open_x_kernel, xt)(x2)
    xt2, be_later, dt_later = lax.optimization_barrier((xt2, be, dt))
    y1 = swap(call(pack_near_kernel, y_face)(be_later, dt_later), "gy", 0)
    t1 = call(open_y_kernel, shape(2 * nx * loads, LANES))(y1)
    inside = shape(nodes, LANES)
    bm, zt, ut, ct, it = call(
        scale_kernel,
        (shape(nx * (ny - 4) * loads, LANES),) + (inside,) * 4,
        scratch_shapes=[scratch(nx * ny, LANES)] * 2,
    )(b, be, dt_later)
    xt1, c1, c2 = call(
        corner_kernel,
        (xt, corner, corner),
        cost_estimate=pl.CostEstimate(flops=2 * 10**9, transcendentals=0, bytes_accessed=0),
    )(x2, xt2, x1)
    xt1, dt = lax.optimization_barrier((xt1, dt))
    c1, c2 = swap(c1, "gy", 0), swap(c2, "gy", 1)
    plane = s.my * loads
    rows, field = shape(s.mx * s.pitch, LANES), shape(s.mx * plane, LANES)
    edge = shape(2 * plane, LANES)
    dens, cond, inv_1, bx, zx, zu, q_x, w_x, w_u, q_1, v_1, carry1, carry2, sums = call(
        inner_kernel,
        (shape(nx * s.pitch, LANES),)
        + (rows,) * 2
        + (field,) * 6
        + (inside,) * 2
        + (edge,) * 2
        + (shape(4 * loads, LANES),),
    )(be, bm, zt, ut, ct, it, dt, y1, y2, t1)
    ends = shape(len(outer_planes(nx)) * ny * loads, LANES)
    q_2, v_2, inv_2, sums = call(
        outer_kernel,
        (ends, ends, shape(ny, LANES), shape(devices, 1, LANES)),
        scratch_shapes=[scratch(2 * plane, LANES)] * 2
        + [scratch(3 * s.pitch, LANES)] * 2
        + [scratch(5 * s.pitch, LANES)] * 2
        + [scratch(5 * plane, LANES)] * 6
        + [scratch(2 * plane, LANES)],
    )(be, bm, zt, ut, dens, x1, x2, xt1, xt2, c2, c1, cond, inv_1, bx, zx, zu, q_x, w_x, w_u, carry1, carry2, sums)
    parts = lax.all_to_all(sums, ("gx", "gy"), 0, 0, tiled=True)
    whole = shape(loads, nx, flat)
    image, again, inverse = call(
        unpack_kernel,
        (whole, whole, shape(nx, flat)),
        scratch_shapes=[scratch(nodes, LANES)] * 2,
    )(q_1, q_2, v_1, v_2, inv_1, inv_2)
    return call(
        finish_kernel,
        (whole, whole),
        out_specs=(hbm, hbm),
        scratch_shapes=[
            scratch(loads, nx, flat),
            scratch(loads, nx, flat),
            pltpu.SemaphoreType.DMA((2, loads)),
        ],
    )(parts, heat_source, image, again, inverse)


def solution(mesh):
    placed = (P(None, "gx", "gy"), P("gx", "gy"))
    return jax.shard_map(
        per_device,
        mesh=mesh,
        in_specs=placed,
        out_specs=(P(None, "gx", "gy"), P(None, "gx", "gy")),
        check_vma=False,
    )
```
